32 devices in a mesh: fsdp: 4 (over z), context: 2 (over y), tensor: 4 (over x, core).
Axes of the slice: x: 2, y: 2, z: 4, core: 2. Of those that a mesh axis runs over, the one named last changes fastest.
Arguments:
- patches: bfloat16 [10240, 768], P(('fsdp', 'context')), may hold values from -6 to 6
- out_grad: bfloat16 [10240, 768], P(('fsdp', 'context')), may hold values from -6 to 6
- block_order: int32 [4, 20], P('fsdp'), may hold values from 0 to 19, as said below
- first_gain: float32 [768], replicated, may hold values from 0.25 to 1.75
- first_shift: float32 [768], replicated, may hold values from -2 to 2
- attn_proj: bfloat16 [3, 768, 768], P(None, 'fsdp', 'tensor'), may hold values from -0.21875 to 0.21875
- attn_bias: float32 [2, 768], P(None, 'tensor'), may hold values from -3 to 3
- out_proj: bfloat16 [768, 768], P('tensor', 'fsdp'), may hold values from -0.875 to 0.875
- out_bias: float32 [768], replicated, may hold values from -2 to 2
- second_gain: float32 [768], replicated, may hold values from 0.25 to 1.75
- second_shift: float32 [768], replicated, may hold values from -2 to 2
- up_proj: bfloat16 [768, 3072], P('fsdp', 'tensor'), may hold values from -0.21875 to 0.21875
- up_bias: float32 [3072], P('tensor'), may hold values from -3 to 3
- down_proj: bfloat16 [3072, 768], P('tensor', 'fsdp'), may hold values from -0.109375 to 0.109375
- down_bias: float32 [768], replicated, may hold values from -2 to 2
Outputs:
- result: bfloat16 [10240, 768], P(('fsdp', 'context'))
- patch_grad: float32 [10240, 768], P(('fsdp', 'context'))
- grad_first_gain: float32 [768], replicated
- grad_first_shift: float32 [768], replicated
- grad_attn_proj: float32 [3, 768, 768], P(None, 'fsdp', 'tensor')
- grad_attn_bias: float32 [2, 768], P(None, 'tensor')
- grad_out_proj: float32 [768, 768], P('tensor', 'fsdp')
- grad_out_bias: float32 [768], replicated
- grad_second_gain: float32 [768], replicated
- grad_second_shift: float32 [768], replicated
- grad_up_proj: float32 [768, 3072], P('fsdp', 'tensor')
- grad_up_bias: float32 [3072], P('tensor')
- grad_down_proj: float32 [3072, 768], P('tensor', 'fsdp')
- grad_down_bias: float32 [768], replicated
The draws below stay inside these ranges and needn't reach their ends.
Inputs may be any that keep to these rules, and one draw needn't show every extreme that they name: `block_order`: each row lists every block number of its group once. In every group, each device of context holds 20 // 2 blocks of every tree, or one more.
All inputs are finite; a program needn't handle non-finite values.
Results may differ from the reference program's by a relative error of at most 0.0098.
Values may be sent and summed in bfloat16 or wider, within the bound.
A program may use at most 128 MiB of HBM per device.

```python
import jax
import jax.numpy as jnp
from jax import lax

D = 768
HEADS = 12
HEAD_DIM = 64
FF = 3072
BLOCK = 128
TRUNK_BLK = 8
BRANCHES = 4
LEAVES = 2
TREE_BLK = 20
BLOCKS_GRP = 20
BLK_DEV = 10
GROUPS = 4
TOKENS = 10240


def deal_group(group_key):
    tree_count = BLOCKS_GRP // TREE_BLK
    context_count = BLOCKS_GRP // BLK_DEV
    order_key, inner_key = jax.random.split(group_key)
    tree_order = jax.random.permutation(order_key, tree_count)
    inner_keys = jax.random.split(inner_key, tree_count)
    inner_order = jax.vmap(shuffle_tree)(inner_keys)
    dealt_blocks = (tree_order[:, None] * TREE_BLK + inner_order).reshape(-1).astype(jnp.int32)
    position = jnp.arange(BLOCKS_GRP)
    slot_index = position % context_count * BLK_DEV + position // context_count
    return jnp.zeros((BLOCKS_GRP,), jnp.int32).at[slot_index].set(dealt_blocks)


def shuffle_tree(tree_key):
    return jax.random.permutation(tree_key, TREE_BLK)


def draw_block_order(key, part):
    return jax.vmap(deal_group)(jax.random.split(key, GROUPS))


def shard_levels(rng, dims, cuts, low, largest):
    level = 1.0
    for dim, blocks in cuts:
        heights = jax.random.uniform(jax.random.fold_in(jax.random.fold_in(rng, 6), dim), (blocks,), jnp.float32, low / len(cuts), largest / len(cuts))
        level = level * jnp.repeat(jnp.exp(heights), dims[dim] // blocks).reshape((-1,) + (1,) * (len(dims) - 1 - dim))
    return level


def scatter_about(stream_key, shape, spread, bound, cuts=(), dtype=jnp.bfloat16):
    drawn = jax.random.normal(stream_key, shape, jnp.float32) * spread
    if len(cuts) > 0:
        drawn = shard_levels(stream_key, shape, cuts, -0.22, 0.18) * drawn
    return jnp.clip(drawn, min=-bound, max=bound).astype(dtype)


def setup_inputs(seed: int = 0) -> dict:
    arg_keys = jax.random.split(jax.random.key(seed), 16)
    patches = scatter_about(arg_keys[0], (TOKENS, D), 1.0, 6.0, ((0, 8),))
    out_grad = scatter_about(arg_keys[1], (TOKENS, D), 1.0, 6.0, ((0, 8),))
    block_order = draw_block_order(jax.random.fold_in(arg_keys[15], 71), 0)
    first_gain = jnp.clip(1.0 + 0.15 * jax.random.normal(arg_keys[3], (D,), jnp.float32), 0.25, 1.75)
    first_shift = scatter_about(arg_keys[4], (D,), 0.3, 2.0, (), jnp.float32)
    attn_proj = scatter_about(arg_keys[5], (3, D, D), D ** -0.5, 0.21875, ((1, 4), (2, 4)))
    attn_bias = scatter_about(arg_keys[6], (2, D), 0.5, 3.0, ((1, 4),), jnp.float32)
    out_proj = scatter_about(arg_keys[7], (D, D), (D // 16) ** -0.5, 0.875, ((0, 4), (1, 4)))
    out_bias = scatter_about(arg_keys[8], (D,), 0.3, 2.0, (), jnp.float32)
    second_gain = jnp.clip(1.0 + 0.15 * jax.random.normal(arg_keys[9], (D,), jnp.float32), 0.25, 1.75)
    second_shift = scatter_about(arg_keys[10], (D,), 0.3, 2.0, (), jnp.float32)
    up_proj = scatter_about(arg_keys[11], (D, FF), D ** -0.5, 0.21875, ((0, 4), (1, 4)))
    up_bias = scatter_about(arg_keys[12], (FF,), 0.5, 3.0, ((0, 4),), jnp.float32)
    down_proj = scatter_about(arg_keys[13], (FF, D), FF ** -0.5, 0.109375, ((0, 4), (1, 4)))
    down_bias = scatter_about(arg_keys[14], (D,), 0.3, 2.0, (), jnp.float32)
    return {"patches": patches, "out_grad": out_grad, "block_order": block_order, "first_gain": first_gain, "first_shift": first_shift, "attn_proj": attn_proj, "attn_bias": attn_bias, "out_proj": out_proj, "out_bias": out_bias, "second_gain": second_gain, "second_shift": second_shift, "up_proj": up_proj, "up_bias": up_bias, "down_proj": down_proj, "down_bias": down_bias}


@jax.custom_vjp
def low(v):
    return lax.optimization_barrier(v.astype(jnp.bfloat16)).astype(jnp.float32)

@jax.custom_vjp
def low_back(v):
    return v

def low_keep(v):
    return (low(v), None)

def low_pass(kept, grad):
    return (grad,)

def back_keep(v):
    return (v, None)

def back_low(kept, grad):
    return (low(grad),)
low.defvjp(low_keep, low_pass)
low_back.defvjp(back_keep, back_low)
epsilon = 1e-05
far_below = -1e+30
highest = lax.Precision.HIGHEST

def layer_norm(values, norm_gain, norm_shift):
    center = values - lax.optimization_barrier(jnp.mean(values, axis=1, keepdims=True))
    inverse = lax.rsqrt(lax.optimization_barrier(jnp.mean(center * center, axis=1, keepdims=True)) + epsilon)
    return center * inverse * norm_gain + norm_shift

def slot_labels(block_order):
    position = block_order % TREE_BLK
    segment = jnp.where(position < TRUNK_BLK, 0, position - TRUNK_BLK + 1)
    return (block_order // TREE_BLK, segment)

def spread_rows(values):
    return jnp.broadcast_to(values[:, None], (values.shape[0], BLOCK)).reshape(-1)

def visible(query_labels, key_labels):
    query_tree, query_seg = query_labels
    key_tree, key_seg = key_labels
    parent = jnp.where(query_seg > BRANCHES, 1 + (query_seg - BRANCHES - 1) // LEAVES, 0)
    reaches = (key_seg[None, :] == 0) | (key_seg[None, :] == query_seg[:, None]) | (key_seg[None, :] == parent[:, None])
    return (query_tree[:, None] == key_tree[None, :]) & reaches

def group_attention(operands):
    queries, keys, values, tree_slot, seg_slot = operands
    row_total = queries.shape[0]
    block_rows = 4 * BLOCK
    key_tree = spread_rows(tree_slot)
    key_seg = spread_rows(seg_slot)
    key_heads = keys.reshape(row_total, HEADS, HEAD_DIM)
    value_heads = values.reshape(row_total, HEADS, HEAD_DIM)

    def one_block(block_operands):
        query_block, query_tree, query_seg = block_operands
        raw = jnp.einsum('qhd,khd->hqk', query_block.reshape(block_rows, HEADS, HEAD_DIM), key_heads, precision=highest)
        scores = low_back(raw * HEAD_DIM ** (-0.5))
        allowed = visible((query_tree, query_seg), (key_tree, key_seg))
        masked = jnp.where(allowed[None], scores, far_below)
        running_top = lax.optimization_barrier(jnp.max(masked, axis=2, keepdims=True))
        kept_exp = jnp.where(allowed[None], jnp.exp(masked - running_top), 0.0)
        weights = kept_exp / lax.optimization_barrier(jnp.sum(kept_exp, axis=2, keepdims=True))
        mixed = jnp.einsum('hqk,khd->qhd', low(weights), value_heads, precision=highest)
        return mixed.reshape(block_rows, HEADS * HEAD_DIM)
    block_count = row_total // block_rows
    attended_blocks = lax.map(jax.checkpoint(one_block), (queries.reshape(block_count, block_rows, HEADS * HEAD_DIM), key_tree.reshape(block_count, block_rows), key_seg.reshape(block_count, block_rows)))
    return attended_blocks.reshape(row_total, HEADS * HEAD_DIM)

def forward(inputs, first_gain, first_shift, attn_proj, attn_bias, out_proj, out_bias, second_gain, second_shift, up_proj, up_bias, down_proj, down_bias, tree_tab, seg_tab):
    first_low = low(layer_norm(inputs, first_gain, first_shift))
    projected = jnp.einsum('rd,cde->cre', first_low, attn_proj, precision=highest)
    queries = low(low_back(projected[0] + attn_bias[0]))
    keys = low(low_back(projected[1]))
    values = low(low_back(projected[2] + attn_bias[1]))
    group_rows = BLOCKS_GRP * BLOCK
    attended = lax.map(group_attention, (queries.reshape(GROUPS, group_rows, D), keys.reshape(GROUPS, group_rows, D), values.reshape(GROUPS, group_rows, D), tree_tab, seg_tab))
    attended = low(low_back(attended.reshape(GROUPS * group_rows, D)))
    middle = inputs + low_back(jnp.dot(attended, out_proj, precision=highest) + out_bias)
    second_low = low(layer_norm(middle, second_gain, second_shift))
    pre_act = low_back(jnp.dot(second_low, up_proj, precision=highest) + up_bias)
    hidden = low(jax.nn.gelu(pre_act, approximate=False))
    return middle + low_back(jnp.dot(hidden, down_proj, precision=highest) + down_bias)

def reference(patches, out_grad, block_order, first_gain, first_shift, attn_proj, attn_bias, out_proj, out_bias, second_gain, second_shift, up_proj, up_bias, down_proj, down_bias):
    tree_tab, seg_tab = slot_labels(block_order)
    float_args = (patches.astype(jnp.float32), first_gain.astype(jnp.float32), first_shift.astype(jnp.float32), attn_proj.astype(jnp.float32), attn_bias.astype(jnp.float32), out_proj.astype(jnp.float32), out_bias.astype(jnp.float32), second_gain.astype(jnp.float32), second_shift.astype(jnp.float32), up_proj.astype(jnp.float32), up_bias.astype(jnp.float32), down_proj.astype(jnp.float32), down_bias.astype(jnp.float32))

    def run_layer(*values):
        return forward(*values, tree_tab, seg_tab)
    result, pull_back = jax.vjp(run_layer, *float_args)
    gradients = pull_back(out_grad.astype(jnp.float32))
    return (result.astype(jnp.bfloat16), gradients[0], gradients[1], gradients[2], gradients[3], gradients[4], gradients[5], gradients[6], gradients[7], gradients[8], gradients[9], gradients[10], gradients[11], gradients[12])
```

```python
from functools import partial

import jax
import jax.numpy as jnp
from jax import lax
from jax.experimental import pallas as pl
from jax.experimental.pallas import tpu as pltpu
from jax.sharding import PartitionSpec as P

HEAD_DIM = 64
BLOCK = 128
TRUNK_BLK = 8
BRANCHES = 4
LEAVES = 2
TREE_BLK = 20


epsilon = 1e-05
far_below = -1e30


def layer_norm(values, norm_gain, norm_shift):
    center = values - jnp.mean(values, axis=1, keepdims=True)
    inverse = lax.rsqrt(jnp.mean(center * center, axis=1, keepdims=True) + epsilon)
    normed = center * inverse
    return (normed * norm_gain + norm_shift, normed, inverse)


def norm_back(gradient, normed, inverse, norm_gain):
    scaled = gradient * norm_gain
    return inverse * (
        scaled
        - jnp.mean(scaled, axis=1, keepdims=True)
        - normed * jnp.mean(scaled * normed, axis=1, keepdims=True)
    )


def slot_labels(order_row):
    position = order_row % TREE_BLK
    return (order_row // TREE_BLK, jnp.where(position < TRUNK_BLK, 0, position - TRUNK_BLK + 1))


def spread_rows(values):
    return jnp.broadcast_to(values[:, None], (values.shape[0], BLOCK)).reshape(-1)


def row_labels(labels, first_slot, slot_count):
    return tuple(
        (
            spread_rows(lax.dynamic_slice_in_dim(label_table, first_slot, slot_count))
            for label_table in labels
        )
    )


def visible(query_labels, key_labels):
    query_tree, query_seg = query_labels
    key_tree, key_seg = key_labels
    parent = jnp.where(query_seg > BRANCHES, 1 + (query_seg - BRANCHES - 1) // LEAVES, 0)
    reaches = (
        (key_seg[None, :] == 0)
        | (key_seg[None, :] == query_seg[:, None])
        | (key_seg[None, :] == parent[:, None])
    )
    return (query_tree[:, None] == key_tree[None, :]) & reaches


def head_view(matrix):
    return matrix.reshape(matrix.shape[0], matrix.shape[1] // HEAD_DIM, HEAD_DIM)


def scores_of(query_heads, key_heads):
    return jnp.einsum(
        "qhd,khd->hqk", query_heads, key_heads, preferred_element_type=jnp.float32
    ) * HEAD_DIM ** (-0.5)


def weights_of(scores, log_total, allowed):
    return jnp.where(allowed[None], jnp.exp(scores - log_total[:, :, None]), 0.0)


def score_grads(query_heads, grad_heads, key_heads, value_heads, log_total, row_delta, allowed):
    weights = weights_of(scores_of(query_heads, key_heads), log_total, allowed)
    prob_grad = jnp.einsum(
        "qhd,khd->hqk", grad_heads, value_heads, preferred_element_type=jnp.float32
    )
    return (
        (weights * (prob_grad - row_delta[:, :, None])).astype(jnp.bfloat16),
        weights.astype(jnp.bfloat16),
    )


def shards(
    patches,
    out_grad,
    block_order,
    first_gain,
    first_shift,
    attn_proj,
    attn_bias,
    out_proj,
    out_bias,
    second_gain,
    second_shift,
    up_proj,
    up_bias,
    down_proj,
    down_bias,
):
    attn_full, out_full, up_full, down_full = (
        lax.all_gather(attn_proj, "fsdp", axis=1, tiled=True),
        lax.all_gather(out_proj, "fsdp", axis=1, tiled=True),
        lax.all_gather(up_proj, "fsdp", axis=0, tiled=True),
        lax.all_gather(down_proj, "fsdp", axis=1, tiled=True),
    )
    labels = slot_labels(block_order[0])
    row_count = patches.shape[0]
    own_slots = row_count // BLOCK
    query_labels = row_labels(labels, lax.axis_index("context") * own_slots, own_slots)
    head_width = attn_full.shape[2]
    head_count = head_width // HEAD_DIM
    key_block = 4 * BLOCK
    block_slots = key_block // BLOCK
    score_scale = HEAD_DIM ** (-0.5)
    inputs = patches.astype(jnp.float32)
    first_norm, first_normed, first_inverse = layer_norm(inputs, first_gain, first_shift)
    first_low = first_norm.astype(jnp.bfloat16)
    projected = jnp.einsum("rd,cde->cre", first_low, attn_full, preferred_element_type=jnp.float32)
    queries = (projected[0] + attn_bias[0]).astype(jnp.bfloat16)
    keys_low = projected[1].astype(jnp.bfloat16)
    values_low = (projected[2] + attn_bias[1]).astype(jnp.bfloat16)
    keys_all = lax.all_gather(
        jnp.concatenate([keys_low, values_low], axis=1), "context", axis=0, tiled=True
    )
    block_count = keys_all.shape[0] // key_block
    query_heads = head_view(queries)

    def key_piece(step_index):
        key_slab = lax.dynamic_slice_in_dim(keys_all, step_index * key_block, key_block, 0)
        allowed = visible(query_labels, row_labels(labels, step_index * block_slots, block_slots))
        return (head_view(key_slab[:, :head_width]), head_view(key_slab[:, head_width:]), allowed)

    def total_step(step_index, carried):
        running_top, running_sum = carried
        key_heads, value_heads, allowed = key_piece(step_index)
        masked = jnp.where(allowed[None], scores_of(query_heads, key_heads), far_below)
        new_top = jnp.maximum(running_top, jnp.max(masked, axis=2))
        kept_exp = jnp.where(allowed[None], jnp.exp(masked - new_top[:, :, None]), 0.0)
        return (new_top, running_sum * jnp.exp(running_top - new_top) + jnp.sum(kept_exp, axis=2))

    start_top = jnp.full((head_count, row_count), far_below, jnp.float32)
    running_top, running_sum = lax.fori_loop(
        0, block_count, total_step, (start_top, jnp.zeros((head_count, row_count), jnp.float32))
    )
    log_total = running_top + jnp.log(running_sum)

    def mix_step(step_index, mixed):
        key_heads, value_heads, allowed = key_piece(step_index)
        weights = weights_of(scores_of(query_heads, key_heads), log_total, allowed).astype(
            jnp.bfloat16
        )
        return mixed + jnp.einsum(
            "hqk,khd->qhd", weights, value_heads, preferred_element_type=jnp.float32
        )

    attended = lax.fori_loop(
        0, block_count, mix_step, jnp.zeros((row_count, head_count, HEAD_DIM), jnp.float32)
    )
    attended_low = attended.reshape(row_count, head_width).astype(jnp.bfloat16)
    attn_part = jnp.dot(attended_low, out_full, preferred_element_type=jnp.float32)
    middle = inputs + (lax.psum(attn_part, "tensor") + out_bias)
    second_norm, second_normed, second_inverse = layer_norm(middle, second_gain, second_shift)
    second_low = second_norm.astype(jnp.bfloat16)
    pre_act = jnp.dot(second_low, up_full, preferred_element_type=jnp.float32) + up_bias
    hidden, gelu_back = jax.vjp(partial(jax.nn.gelu, approximate=False), pre_act)
    hidden_low = hidden.astype(jnp.bfloat16)
    mlp_part = jnp.dot(hidden_low, down_full, preferred_element_type=jnp.float32)
    result = (
        middle + (lax.psum(mlp_part.astype(jnp.bfloat16), "tensor").astype(jnp.float32) + down_bias)
    ).astype(jnp.bfloat16)
    top_grad = out_grad.astype(jnp.float32)
    grad_down_bias = jnp.sum(top_grad, axis=0)
    grad_down = jnp.einsum("rf,rd->fd", hidden_low, out_grad, preferred_element_type=jnp.float32)
    hidden_grad = jnp.einsum("rd,fd->rf", out_grad, down_full, preferred_element_type=jnp.float32)
    pre_grad = gelu_back(hidden_grad)[0].astype(jnp.bfloat16)
    grad_up_bias = jnp.sum(pre_grad.astype(jnp.float32), axis=0)
    grad_up = jnp.einsum("rd,rf->df", second_low, pre_grad, preferred_element_type=jnp.float32)
    second_part = jnp.einsum("rf,df->rd", pre_grad, up_full, preferred_element_type=jnp.float32)
    second_grad = lax.psum(second_part, "tensor")
    grad_second_gain = jnp.sum(second_grad * second_normed, axis=0)
    grad_second_shift = jnp.sum(second_grad, axis=0)
    middle_grad = top_grad + norm_back(second_grad, second_normed, second_inverse, second_gain)
    branch_grad = middle_grad.astype(jnp.bfloat16)
    grad_out_bias = jnp.sum(branch_grad.astype(jnp.float32), axis=0)
    grad_out = jnp.einsum(
        "re,rd->ed", attended_low, branch_grad, preferred_element_type=jnp.float32
    )
    attended_grad = jnp.einsum(
        "rd,ed->re", branch_grad, out_full, preferred_element_type=jnp.float32
    ).astype(jnp.bfloat16)
    grad_heads = head_view(attended_grad)

    def delta_step(step_index, row_delta):
        key_heads, value_heads, allowed = key_piece(step_index)
        weights = weights_of(scores_of(query_heads, key_heads), log_total, allowed)
        prob_grad = jnp.einsum(
            "qhd,khd->hqk", grad_heads, value_heads, preferred_element_type=jnp.float32
        )
        return row_delta + jnp.sum(weights * prob_grad, axis=2)

    row_delta = lax.fori_loop(
        0, block_count, delta_step, jnp.zeros((head_count, row_count), jnp.float32)
    )
    query_start = jnp.zeros((row_count, head_count, HEAD_DIM), jnp.float32)

    def back_step(step_index, carried):
        query_acc, key_acc = carried
        key_heads, value_heads, allowed = key_piece(step_index)
        score_low, weights_low = score_grads(
            query_heads, grad_heads, key_heads, value_heads, log_total, row_delta, allowed
        )
        query_acc = query_acc + jnp.einsum(
            "hqk,khd->qhd", score_low, key_heads, preferred_element_type=jnp.float32
        )
        key_part = jnp.einsum(
            "hqk,qhd->khd", score_low, query_heads, preferred_element_type=jnp.float32
        )
        value_part = jnp.einsum(
            "hqk,qhd->khd", weights_low, grad_heads, preferred_element_type=jnp.float32
        )
        joined = jnp.concatenate(
            [key_part.reshape(key_block, head_width), value_part.reshape(key_block, head_width)],
            axis=1,
        )
        return (
            query_acc,
            lax.dynamic_update_slice_in_dim(key_acc, joined, step_index * key_block, 0),
        )

    key_start = jnp.zeros((keys_all.shape[0], 2 * head_width), jnp.float32)
    query_acc, key_acc = lax.fori_loop(0, block_count, back_step, (query_start, key_start))
    key_value_grad = lax.psum_scatter(key_acc, "context", scatter_dimension=0, tiled=True)
    query_grad = (query_acc.reshape(row_count, head_width) * score_scale).astype(jnp.bfloat16)
    key_grad = (key_value_grad[:, :head_width] * score_scale).astype(jnp.bfloat16)
    value_grad = key_value_grad[:, head_width:].astype(jnp.bfloat16)
    stacked = jnp.stack([query_grad, key_grad, value_grad])
    grad_attn_bias = jnp.stack(
        [
            jnp.sum(query_grad.astype(jnp.float32), axis=0),
            jnp.sum(value_grad.astype(jnp.float32), axis=0),
        ]
    )
    grad_attn = jnp.einsum("rd,cre->cde", first_low, stacked, preferred_element_type=jnp.float32)
    first_grad = lax.psum(
        jnp.einsum("cre,cde->rd", stacked, attn_full, preferred_element_type=jnp.float32), "tensor"
    )
    grad_first_gain = jnp.sum(first_grad * first_normed, axis=0)
    grad_first_shift = jnp.sum(first_grad, axis=0)
    patch_grad = middle_grad + norm_back(first_grad, first_normed, first_inverse, first_gain)
    wide_attn, wide_out, wide_up, wide_down = (
        lax.psum_scatter(grad_attn, ("fsdp", "context"), scatter_dimension=1, tiled=True),
        lax.psum_scatter(grad_out, ("fsdp", "context"), scatter_dimension=1, tiled=True),
        lax.psum_scatter(grad_up, ("fsdp", "context"), scatter_dimension=0, tiled=True),
        lax.psum_scatter(grad_down, ("fsdp", "context"), scatter_dimension=1, tiled=True),
    )
    grad_attn, grad_out, grad_up, grad_down = (
        lax.all_gather(wide_attn, "context", axis=1, tiled=True),
        lax.all_gather(wide_out, "context", axis=1, tiled=True),
        lax.all_gather(wide_up, "context", axis=0, tiled=True),
        lax.all_gather(wide_down, "context", axis=1, tiled=True),
    )
    small_grads = lax.psum(
        (
            grad_first_gain,
            grad_first_shift,
            grad_attn_bias,
            grad_out_bias,
            grad_second_gain,
            grad_second_shift,
            grad_up_bias,
            grad_down_bias,
        ),
        ("fsdp", "context"),
    )
    return (
        result,
        patch_grad,
        small_grads[0],
        small_grads[1],
        grad_attn,
        small_grads[2],
        grad_out,
        small_grads[3],
        small_grads[4],
        small_grads[5],
        grad_up,
        small_grads[6],
        grad_down,
        small_grads[7],
    )


bf16 = jnp.bfloat16
f32 = jnp.float32
VMEM = pl.BlockSpec(memory_space=pltpu.VMEM)
SMEM = pl.BlockSpec(memory_space=pltpu.SMEM)
ANY = pl.BlockSpec(memory_space=pl.ANY)
MESH = pl.DeviceIdType.MESH
LIMIT = 60 * 1024 * 1024


def dot_nn(a, b):
    return lax.dot_general(a, b, (((1,), (0,)), ((), ())), preferred_element_type=f32)


def dot_nt(a, b):
    return lax.dot_general(a, b, (((1,), (1,)), ((), ())), preferred_element_type=f32)


def dot_tn(a, b):
    return lax.dot_general(a, b, (((0,), (0,)), ((), ())), preferred_element_type=f32)


class Here:
    def __init__(self, fsdp_count):
        self.f = lax.axis_index("fsdp")
        self.c = lax.axis_index("context")
        self.t = lax.axis_index("tensor")
        self.x = self.t // 2
        self.k = self.t % 2
        self.core = (self.f, self.c, 2 * self.x + 1 - self.k)
        self.xp = (self.f, self.c, 2 * (1 - self.x) + self.k)
        self.yp = (self.f, 1 - self.c, self.t)
        self.z = [((self.f + i) % fsdp_count, self.c, self.t) for i in range(1, fsdp_count)]
        self.back = [(self.f + fsdp_count - i) % fsdp_count for i in range(1, fsdp_count)]


def greet(devices):
    barrier = pltpu.get_barrier_semaphore()
    for device in devices:
        pl.semaphore_signal(barrier, inc=1, device_id=device, device_id_type=MESH)
    pl.semaphore_wait(barrier, len(devices))


class Post:
    def __init__(self, send_sem, recv_sem):
        self.send_sem, self.recv_sem = send_sem, recv_sem
        self.sent, self.open = [], []

    def send(self, src, dst, device):
        index = len(self.sent)
        copy = pltpu.make_async_remote_copy(
            src_ref=src,
            dst_ref=dst,
            send_sem=self.send_sem.at[index],
            recv_sem=self.recv_sem.at[index],
            device_id=device,
            device_id_type=MESH,
        )
        copy.start()
        self.sent.append(copy)
        self.open.append(copy)
        return copy

    def got(self, copy):
        copy.wait_recv()
        self.open = [other for other in self.open if other is not copy]

    def close(self):
        for copy in self.open:
            copy.wait_recv()
        for copy in self.sent:
            copy.wait_send()


def ds(start, size, step=16):
    return pl.ds(pl.multiple_of(start, step), size)


def gather_kernel(
    fsdp_count, patches, grads, wa, wu, wd, bias, rows_all, grads_all, wa_all, wu_all, wd_all, bias_all, local, ss, rs
):
    me = Here(fsdp_count)
    f, c, t, k = me.f, me.c, me.t, me.k
    rows = patches.shape[0]
    part = rows // 4
    deep = wa.shape[0]
    half = deep // 2
    greet([me.core, me.xp, me.yp] + me.z)
    post = Post(ss, rs)
    keep = [
        (patches, rows_all.at[ds(rows * c, rows)]),
        (grads, grads_all.at[ds(rows * c, rows)]),
        (wa, wa_all.at[k, ds(deep * f, deep)]),
        (wu, wu_all.at[k, ds(deep * f, deep)]),
        (wd, wd_all.at[k, ds(deep * f, deep)]),
        (bias, bias_all.at[k]),
    ]
    own = []
    for index, (src, dst) in enumerate(keep):
        copy = pltpu.make_async_copy(src, dst, local.at[index])
        copy.start()
        own.append(copy)
    from_y = []
    for src, dst in ((patches, rows_all), (grads, grads_all)):
        from_y.append(post.send(src.at[ds(part * t, part)], dst.at[ds(rows * c + part * t, part)], me.yp))
    from_z = []
    for device in me.z:
        from_z.append(post.send(wa, wa_all.at[k, ds(deep * f, deep)], device))
    strips = []
    for device in me.z:
        for src, dst in ((wu, wu_all), (wd, wd_all)):
            strips.append(
                post.send(src.at[ds(half * c, half)], dst.at[k, ds(deep * f + half * c, half)], device)
            )
    for src, dst in keep[2:]:
        post.send(src, dst, me.core)
    from_x = []
    there = rows * (1 - c)
    for copy, dst in zip(from_y, (rows_all, grads_all)):
        post.got(copy)
        piece = dst.at[ds(there + part * t, part)]
        from_x.append(post.send(piece, piece, me.xp))
        post.send(piece, piece, me.core)
    for copy, source in zip(from_z, me.back):
        post.got(copy)
        piece = wa_all.at[k, ds(deep * source, deep)]
        post.send(piece, piece, me.core)
    passed = []
    for index, source in enumerate(me.back):
        for copy, dst in zip(strips[2 * index : 2 * index + 2], (wu_all, wd_all)):
            post.got(copy)
            piece = dst.at[k, ds(deep * source + half * c, half)]
            passed.append(post.send(piece, piece, me.yp))
            post.send(piece, piece, me.core)
    other = (t + 2) % 4
    for copy, dst in zip(from_x, (rows_all, grads_all)):
        post.got(copy)
        piece = dst.at[ds(there + part * other, part)]
        post.send(piece, piece, me.core)
    for index, source in enumerate(me.back):
        for copy, dst in zip(passed[2 * index : 2 * index + 2], (wu_all, wd_all)):
            post.got(copy)
            piece = dst.at[k, ds(deep * source + half * (1 - c), half)]
            post.send(piece, piece, me.core)
    post.close()
    for copy in own:
        copy.wait()


def gather(fsdp_count, patches, grads, wa, wu, wd, bias):
    rows, width = patches.shape
    deep = wa.shape[0]
    whole = jax.ShapeDtypeStruct((2 * rows, width), bf16)
    weight = lambda w: jax.ShapeDtypeStruct((2, deep * fsdp_count, w.shape[1]), bf16)
    return pl.pallas_call(
        partial(gather_kernel, fsdp_count),
        out_shape=(whole, whole, weight(wa), weight(wu), weight(wd), jax.ShapeDtypeStruct((2,) + bias.shape, f32)),
        in_specs=[ANY] * 6,
        out_specs=(ANY,) * 6,
        scratch_shapes=[pltpu.SemaphoreType.DMA((6,)), pltpu.SemaphoreType.DMA((64,)), pltpu.SemaphoreType.DMA((64,))],
        compiler_params=pltpu.CompilerParams(collective_id=0, has_side_effects=True, vmem_limit_bytes=LIMIT),
        name="gather",
    )(patches, grads, wa, wu, wd, bias)


TRUNK = TRUNK_BLK * BLOCK
SUB = (1 + LEAVES) * BLOCK
KEYS = TRUNK + SUB
OWN = 2 * BLOCK + SUB
PIECES = (
    (2 * BLOCK, TRUNK, 2 * BLOCK),
    (3 * BLOCK, TRUNK + BLOCK, BLOCK),
    (4 * BLOCK, TRUNK + BLOCK, 2 * BLOCK),
)


def own_places(s):
    return [2 * s, 2 * s + 1, 12 + 2 * s, 8 + s, 13 + 2 * s]


def row_norm(values):
    center = values - jnp.mean(values, axis=1, keepdims=True)
    inverse = lax.rsqrt(jnp.mean(center * center, axis=1, keepdims=True) + epsilon)
    return center * inverse, inverse


def front_kernel(
    where, rows_all, grads_all, wa, bias, gain, shift,
    x_own, g_own, low_own, q_out, k_out, v_out, kt_out, attended, lse_out, wh,
    low, vt, att_t, st, pt,
):
    c, t = lax.axis_index("context"), lax.axis_index("tensor")
    s = 2 * c + t % 2
    places = [*range(TRUNK_BLK)] + own_places(s)[2:]
    gain_row, shift_row = gain[...], shift[...]

    def norm_block(place, dst, dst_row):
        values = rows_all[ds(where[place] * BLOCK, BLOCK), :]
        normed, _ = row_norm(values.astype(f32))
        dst[ds(dst_row, BLOCK), :] = (normed * gain_row + shift_row).astype(bf16)

    def trunk_step(j, carried):
        norm_block(j, low, j * BLOCK)
        return carried

    lax.fori_loop(0, TRUNK_BLK, trunk_step, 0)
    for j in range(TRUNK_BLK, len(places)):
        norm_block(places[j], low, j * BLOCK)
    for j, place in enumerate(own_places(s)):
        x_own[pl.ds(j * BLOCK, BLOCK), :] = rows_all[ds(where[place] * BLOCK, BLOCK), :]
        g_own[pl.ds(j * BLOCK, BLOCK), :] = grads_all[ds(where[place] * BLOCK, BLOCK), :]
    low_own[0 : 2 * BLOCK, :] = low[ds(2 * BLOCK * s, 2 * BLOCK), :]
    low_own[2 * BLOCK :, :] = low[TRUNK:, :]
    for i, slab in enumerate((0, 1, 2, 5)):
        wh[i, :, 0:128] = wa[0, :, 128 * slab : 128 * slab + 128]
        wh[i, :, 128:256] = wa[1, :, 128 * slab : 128 * slab + 128]
        start = 384 + 64 * i
        wh[i, :, 256:384] = jnp.concatenate(
            [wa[0, :, start : start + 64], wa[1, :, start : start + 64]], axis=1
        )

    def heads_row(row):
        a, b = bias[0, row : row + 1, :], bias[1, row : row + 1, :]
        return jnp.concatenate([a[:, 0:128], b[:, 0:128], a[:, 128:192], b[:, 128:192]], axis=1)

    q_out[...] = ((dot_nn(low_own[...], wh[0]) + heads_row(1)).astype(bf16) * HEAD_DIM ** (-0.5)).astype(bf16)
    value_bias = heads_row(2)

    def project(j, carried):
        rows = ds(j * (KEYS // 2), KEYS // 2)
        k_out[rows, :] = dot_nn(low[rows, :], wh[1]).astype(bf16)
        v_out[rows, :] = (dot_nn(low[rows, :], wh[2]) + value_bias).astype(bf16)
        return carried

    lax.fori_loop(0, 2, project, 0)
    kt_out[...] = k_out[...].T
    vt[...] = v_out[...].T
    lane = lax.broadcasted_iota(jnp.int32, (OWN, 128), 1) // HEAD_DIM

    def head(h, carried):
        slab, part = h // 2, h % 2
        lanes = pl.ds(pl.multiple_of(slab * 128, 128), 128)
        own_q = q_out[:, lanes]
        q_part = jnp.where(lane == part, own_q, jnp.zeros_like(own_q))
        st[0:TRUNK, :] = dot_nt(k_out[0:TRUNK, lanes], q_part)
        for q_row, k_row, count in PIECES:
            st[TRUNK : TRUNK + count, q_row : q_row + BLOCK] = dot_nt(
                k_out[k_row : k_row + count, lanes], q_part[q_row : q_row + BLOCK]
            )
        tops, totals = [], []
        for j in range(OWN // BLOCK):
            cols = slice(j * BLOCK, (j + 1) * BLOCK)
            count = TRUNK + (0 if j < 2 else PIECES[j - 2][2])
            top = jnp.full((8, BLOCK), far_below, f32)
            for r in range(0, count, BLOCK):
                piece = st[r : r + BLOCK, cols].reshape(BLOCK // 8, 8, BLOCK)
                top = jnp.maximum(top, jnp.max(piece, axis=0))
            top = jnp.max(top, axis=0, keepdims=True)
            total = jnp.zeros((8, BLOCK), f32)
            for r in range(0, count, BLOCK):
                weight = jnp.exp(st[r : r + BLOCK, cols] - top)
                total = total + jnp.sum(weight.reshape(BLOCK // 8, 8, BLOCK), axis=0)
                pt[r : r + BLOCK, cols] = weight.astype(bf16)
            tops.append(top)
            totals.append(jnp.sum(total, axis=0, keepdims=True))
        total = jnp.concatenate(totals, axis=1)
        head_rows = ds(h * HEAD_DIM, HEAD_DIM)
        att_t[head_rows, :] = dot_nn(vt[head_rows, 0:TRUNK], pt[0:TRUNK, :])
        for q_row, k_row, count in PIECES:
            cols = slice(q_row, q_row + BLOCK)
            att_t[head_rows, cols] += dot_nn(
                vt[head_rows, k_row : k_row + count], pt[TRUNK : TRUNK + count, cols]
            )
        att_t[head_rows, :] = att_t[head_rows, :] / total
        lse_out[pl.ds(h, 1), :] = jnp.concatenate(tops, axis=1) + jnp.log(total)
        return carried

    lax.fori_loop(0, 6, head, 0)
    attended[...] = att_t[...].T.astype(bf16)


def front(where, rows_all, grads_all, wa, bias, gain, shift):
    width = rows_all.shape[1]
    shape = jax.ShapeDtypeStruct
    return pl.pallas_call(
        front_kernel,
        out_shape=(
            shape((OWN, width), bf16),
            shape((OWN, width), bf16),
            shape((OWN, width), bf16),
            shape((OWN, 384), bf16),
            shape((KEYS, 384), bf16),
            shape((KEYS, 384), bf16),
            shape((384, KEYS), bf16),
            shape((OWN, 384), bf16),
            shape((8, OWN), f32),
            shape((4, width, 384), bf16),
        ),
        in_specs=[SMEM] + [VMEM] * 6,
        out_specs=(VMEM,) * 10,
        scratch_shapes=[
            pltpu.VMEM((KEYS, width), bf16),
            pltpu.VMEM((384, KEYS), bf16),
            pltpu.VMEM((384, OWN), f32),
            pltpu.VMEM((TRUNK + 2 * BLOCK, OWN), f32),
            pltpu.VMEM((TRUNK + 2 * BLOCK, OWN), bf16),
        ],
        compiler_params=pltpu.CompilerParams(vmem_limit_bytes=LIMIT),
        name="front",
    )(where, rows_all, grads_all, wa, bias, gain, shift)


HALF = OWN // 2


def middle_kernel(
    fsdp_count, attended, wo, x_own, g_own, wu_in, wd_in, bias, gain, shift, out_bias, down_bias,
    result_half, middle_grad, da, g_up, g_down, g_out, stats, up_stats,
    wu, wd, att_x, wo_x, middle, normed, inverse, low, hidden, pre_grad, second, second_send, second_x,
    mlp_send, mlp_x, da_send, g_out_send, g_out_x, local, ss, rs,
):
    me = Here(fsdp_count)
    x, k = me.x, me.k
    width = x_own.shape[1]
    mine, far = HALF * x, HALF * (1 - x)
    here_rows, far_rows = ds(mine, HALF), ds(far, HALF)
    copies = [pltpu.make_async_copy(wu_in, wu, local.at[0]), pltpu.make_async_copy(wd_in, wd, local.at[1])]
    for copy in copies:
        copy.start()
    greet([me.core, me.xp])
    post = Post(ss, rs)
    att_copy = post.send(attended.at[far_rows], att_x, me.xp)
    part = ds(width // 2 * k, width // 2)
    wo_copy = post.send(wo.at[part], wo_x.at[part], me.xp)
    middle[...] = (
        x_own[here_rows, :].astype(f32) + out_bias[...] + dot_nt(attended[here_rows, :], wo[...])
    )
    post.got(wo_copy)
    wo_core = post.send(wo_x.at[part], wo_x.at[part], me.core)
    post.got(wo_core)
    post.got(att_copy)
    middle[...] += dot_nt(att_x[...], wo_x[...])
    n2, s2 = row_norm(middle[...])
    normed[...] = n2
    inverse[...] = s2
    low[here_rows, :] = (n2 * gain[...] + shift[...]).astype(bf16)
    low_copy = post.send(low.at[here_rows], low.at[here_rows], me.xp)
    for copy in copies:
        copy.wait()
    tile = 256

    def feed(rows):
        second[rows, :] = jnp.zeros((HALF, width), f32)

        def step(j, carried):
            shard, lanes = j // 3, pl.ds(pl.multiple_of(j % 3 * tile, 128), tile)
            out = pl.ds(pl.multiple_of(j * tile, 128), tile)
            pre = dot_nn(low[rows, :], wu[shard, :, lanes]) + bias[shard, 0:1, lanes]
            below = 0.5 * (1.0 + lax.erf(pre * (2.0**-0.5)))
            density = jnp.exp(-0.5 * pre * pre) * (2.0 * jnp.pi) ** -0.5
            hidden[rows, out] = (pre * below).astype(bf16)
            back = dot_nn(g_own[rows, :], wd[shard, :, lanes])
            low_back = (back * (below + pre * density)).astype(bf16)
            pre_grad[rows, out] = low_back
            second[rows, :] += dot_nt(low_back, wu[shard, :, lanes])
            return carried

        lax.fori_loop(0, 6, step, 0)

    def mlp(rows):
        return dot_nt(hidden[rows, 0:width], wd[0]) + dot_nt(hidden[rows, width:], wd[1])

    feed(here_rows)
    post.got(low_copy)
    feed(far_rows)
    second_send[...] = second[far_rows, :].astype(bf16)
    second_copy = post.send(second_send, second_x, me.xp)
    mlp_send[...] = mlp(far_rows).astype(bf16)
    mlp_copy = post.send(mlp_send, mlp_x, me.xp)

    def weight_step(j, carried):
        lanes = pl.ds(pl.multiple_of(j * tile, 128), tile)
        g_up[:, lanes] = dot_tn(low[...], pre_grad[:, lanes]).astype(bf16)
        g_down[:, lanes] = dot_tn(g_own[...], hidden[:, lanes]).astype(bf16)
        return carried

    lax.fori_loop(0, 6, weight_step, 0)
    up_stats[0:1, :] = jnp.sum(pre_grad[:, 0:width].astype(f32), axis=0, keepdims=True)
    up_stats[1:2, :] = jnp.sum(pre_grad[:, width:].astype(f32), axis=0, keepdims=True)
    own_result = middle[...] + mlp(here_rows) + down_bias[...]
    middle[...] = own_result
    post.got(second_copy)
    second_grad = second[here_rows, :] + second_x[...].astype(f32)
    n2 = normed[...]
    dy = g_own[here_rows, :].astype(f32)
    stats[0:1, :] = jnp.sum(second_grad * n2, axis=0, keepdims=True)
    stats[1:2, :] = jnp.sum(second_grad, axis=0, keepdims=True)
    stats[2:3, :] = jnp.sum(dy, axis=0, keepdims=True)
    grad = dy + norm_back(second_grad, n2, inverse[...], gain[...])
    middle_grad[...] = grad
    branch = grad.astype(bf16)
    stats[3:4, :] = jnp.sum(branch.astype(f32), axis=0, keepdims=True)
    da_send[...] = dot_nn(branch, wo_x[...]).astype(bf16)
    da_copy = post.send(da_send, da.at[here_rows], me.xp)
    da[here_rows, :] = dot_nn(branch, wo[...]).astype(bf16)
    g_out_send[...] = dot_tn(branch, att_x[...]).astype(bf16)
    g_out_copy = post.send(g_out_send, g_out_x, me.xp)
    g_out_own = dot_tn(branch, attended[here_rows, :])
    post.got(mlp_copy)
    result_half[...] = (middle[...] + mlp_x[...].astype(f32)).astype(bf16)
    post.got(g_out_copy)
    g_out[...] = (g_out_own + g_out_x[...].astype(f32)).astype(bf16)
    post.close()


def middle_layer(fsdp_count, attended, wo, x_own, g_own, wu, wd, bias, gain, shift, out_bias, down_bias):
    width = x_own.shape[1]
    shape = jax.ShapeDtypeStruct
    units = 2 * wu.shape[2]
    return pl.pallas_call(
        partial(middle_kernel, fsdp_count),
        out_shape=(
            shape((HALF, width), bf16),
            shape((HALF, width), f32),
            shape((OWN, 384), bf16),
            shape((width, units), bf16),
            shape((width, units), bf16),
            shape((width, 384), bf16),
            shape((4, width), f32),
            shape((2, width), f32),
        ),
        in_specs=[VMEM] * 4 + [ANY] * 2 + [VMEM] * 5,
        out_specs=(VMEM,) * 8,
        scratch_shapes=[
            pltpu.VMEM(wu.shape, bf16),
            pltpu.VMEM(wd.shape, bf16),
            pltpu.VMEM((HALF, 384), bf16),
            pltpu.VMEM((width, 384), bf16),
            pltpu.VMEM((HALF, width), f32),
            pltpu.VMEM((HALF, width), f32),
            pltpu.VMEM((HALF, 1), f32),
            pltpu.VMEM((OWN, width), bf16),
            pltpu.VMEM((OWN, units), bf16),
            pltpu.VMEM((OWN, units), bf16),
            pltpu.VMEM((OWN, width), f32),
            pltpu.VMEM((HALF, width), bf16),
            pltpu.VMEM((HALF, width), bf16),
            pltpu.VMEM((HALF, width), bf16),
            pltpu.VMEM((HALF, width), bf16),
            pltpu.VMEM((HALF, 384), bf16),
            pltpu.VMEM((width, 384), bf16),
            pltpu.VMEM((width, 384), bf16),
            pltpu.SemaphoreType.DMA((2,)),
            pltpu.SemaphoreType.DMA((8,)),
            pltpu.SemaphoreType.DMA((8,)),
        ],
        compiler_params=pltpu.CompilerParams(collective_id=1, has_side_effects=True, vmem_limit_bytes=LIMIT),
        name="middle",
    )(attended, wo, x_own, g_own, wu, wd, bias, gain, shift, out_bias, down_bias)


def back_kernel(da, attended, q, k, v, kt, lse, dq, dkv, delta, st, dpt, pt, dst, dk_acc, dv_acc, dq_t):
    product = (da[...].astype(f32) * attended[...].astype(f32)).T
    for h in range(6):
        delta[h : h + 1, :] = jnp.sum(product[h * HEAD_DIM : (h + 1) * HEAD_DIM], axis=0, keepdims=True)
    dk_acc[...] = jnp.zeros_like(dk_acc)
    dv_acc[...] = jnp.zeros_like(dv_acc)
    lane = lax.broadcasted_iota(jnp.int32, (OWN, 128), 1) // HEAD_DIM

    def head(h, carried):
        slab, part = h // 2, h % 2
        lanes = pl.ds(pl.multiple_of(slab * 128, 128), 128)
        q_slab, da_slab = q[:, lanes], da[:, lanes]
        q_part = jnp.where(lane == part, q_slab, jnp.zeros_like(q_slab))
        da_part = jnp.where(lane == part, da_slab, jnp.zeros_like(da_slab))
        st[0:TRUNK, :] = dot_nt(k[0:TRUNK, lanes], q_part)
        dpt[0:TRUNK, :] = dot_nt(v[0:TRUNK, lanes], da_part)
        for q_row, k_row, count in PIECES:
            cols, rows = slice(q_row, q_row + BLOCK), slice(TRUNK, TRUNK + count)
            st[rows, cols] = dot_nt(k[k_row : k_row + count, lanes], q_part[q_row : q_row + BLOCK])
            dpt[rows, cols] = dot_nt(v[k_row : k_row + count, lanes], da_part[q_row : q_row + BLOCK])
        log_total, row_delta = lse[pl.ds(h, 1), :], delta[pl.ds(h, 1), :]
        for j in range(OWN // BLOCK):
            cols = slice(j * BLOCK, (j + 1) * BLOCK)
            count = TRUNK + (0 if j < 2 else PIECES[j - 2][2])
            for r in range(0, count, BLOCK):
                weight = jnp.exp(st[r : r + BLOCK, cols] - log_total[:, cols])
                pt[r : r + BLOCK, cols] = weight.astype(bf16)
                dst[r : r + BLOCK, cols] = (
                    weight * (dpt[r : r + BLOCK, cols] - row_delta[:, cols])
                ).astype(bf16)
        dk_acc[0:TRUNK, lanes] += dot_nn(dst[0:TRUNK, :], q_part)
        dv_acc[0:TRUNK, lanes] += dot_nn(pt[0:TRUNK, :], da_part)
        head_rows = ds(h * HEAD_DIM, HEAD_DIM)
        dq_t[head_rows, :] = dot_nn(kt[head_rows, 0:TRUNK], dst[0:TRUNK, :])
        for q_row, k_row, count in PIECES:
            cols, rows = slice(q_row, q_row + BLOCK), slice(TRUNK, TRUNK + count)
            own = slice(k_row, k_row + count)
            dk_acc[own, lanes] += dot_nn(dst[rows, cols], q_part[q_row : q_row + BLOCK])
            dv_acc[own, lanes] += dot_nn(pt[rows, cols], da_part[q_row : q_row + BLOCK])
            dq_t[head_rows, cols] += dot_nn(kt[head_rows, own], dst[rows, cols])
        return carried

    lax.fori_loop(0, 6, head, 0)
    dq[...] = (dq_t[...].T * HEAD_DIM ** (-0.5)).astype(bf16)
    dkv[:, 0:384] = dk_acc[...].astype(bf16)
    dkv[:, 384:768] = dv_acc[...].astype(bf16)


def back(da, attended, q, k, v, kt, lse):
    shape = jax.ShapeDtypeStruct
    tall = TRUNK + 2 * BLOCK
    return pl.pallas_call(
        back_kernel,
        out_shape=(shape((OWN, 384), bf16), shape((KEYS, 768), bf16)),
        in_specs=[VMEM] * 7,
        out_specs=(VMEM, VMEM),
        scratch_shapes=[
            pltpu.VMEM((8, OWN), f32),
            pltpu.VMEM((tall, OWN), f32),
            pltpu.VMEM((tall, OWN), f32),
            pltpu.VMEM((tall, OWN), bf16),
            pltpu.VMEM((tall, OWN), bf16),
            pltpu.VMEM((KEYS, 384), f32),
            pltpu.VMEM((KEYS, 384), f32),
            pltpu.VMEM((384, OWN), f32),
        ],
        compiler_params=pltpu.CompilerParams(vmem_limit_bytes=LIMIT),
        name="back",
    )(da, attended, q, k, v, kt, lse)


UNIT = 32


def finish_kernel(
    fsdp_count, where, dq, dkv, wh, low_own, x_own, middle_grad, result_half, gain,
    result, patch_grad, g_attn, stats, attn_stats,
    trunk_core, trunk_far, trunk_send, trunk_y, dkv_own, first_send, first_x, all_rows, local, ss, rs,
):
    me = Here(fsdp_count)
    c, x, k = me.c, me.x, me.k
    s = 2 * c + k
    pair = 2 * BLOCK
    units = HALF // UNIT
    mine, far = HALF * x, HALF * (1 - x)
    here_rows, far_rows = ds(mine, HALF), ds(far, HALF)
    greet([me.core, me.xp, me.yp])
    post = Post(ss, rs)

    all_rows[0, pl.ds(units * (2 * s + x), units)] = result_half[...].reshape(units, UNIT, -1)
    far_core = post.send(dkv.at[ds(pair * (2 * (1 - c) + 1 - k), pair)], trunk_far, me.core)
    own_core = post.send(dkv.at[ds(pair * (2 * c + 1 - k), pair)], trunk_core, me.core)
    post.got(far_core)
    trunk_send[...] = (
        dkv[ds(pair * (2 * (1 - c) + k), pair), :].astype(f32) + trunk_far[...].astype(f32)
    ).astype(bf16)
    y_copy = post.send(trunk_send, trunk_y, me.yp)
    dkv_own[pair:, :] = dkv[TRUNK:, :]
    post.got(own_core)
    post.got(y_copy)
    dkv_own[0:pair, :] = (
        dkv[ds(pair * s, pair), :].astype(f32) + trunk_core[...].astype(f32) + trunk_y[...].astype(f32)
    ).astype(bf16)

    def first(rows):
        return (
            dot_nt(dq[rows, :], wh[0])
            + dot_nt(dkv_own[rows, 0:384], wh[1])
            + dot_nt(dkv_own[rows, 384:768], wh[2])
        )

    first_send[...] = first(far_rows).astype(bf16)
    first_copy = post.send(first_send, first_x, me.xp)
    own_first = first(here_rows)
    g_attn[0] = dot_tn(low_own[...], dq[...]).astype(bf16)
    g_attn[1] = dot_tn(low_own[...], dkv_own[:, 0:384]).astype(bf16)
    g_attn[2] = dot_tn(low_own[...], dkv_own[:, 384:768]).astype(bf16)
    attn_stats[0:1, 0:384] = jnp.sum(dq[...].astype(f32), axis=0, keepdims=True)
    attn_stats[0:1, 384:768] = jnp.sum(dkv_own[:, 384:768].astype(f32), axis=0, keepdims=True)
    post.got(first_copy)
    first_grad = own_first + first_x[...].astype(f32)
    n1, s1 = row_norm(x_own[here_rows, :].astype(f32))
    stats[0:1, :] = jnp.sum(first_grad * n1, axis=0, keepdims=True)
    stats[1:2, :] = jnp.sum(first_grad, axis=0, keepdims=True)
    grad = middle_grad[...] + norm_back(first_grad, n1, s1, gain[...])
    all_rows[1, pl.ds(units * (2 * s + x), units)] = grad.astype(bf16).reshape(units, UNIT, -1)
    there = (2 * s + 1 - x, 2 * (2 * (1 - c) + k) + x)
    for index in (1, 0):
        own = all_rows.at[index, pl.ds(units * (2 * s + x), units)]
        from_x = post.send(own, own, me.xp)
        from_y = post.send(own, own, me.yp)
        post.send(own, own, me.core)
        post.got(from_x)
        quarter = units // 2
        beside = all_rows.at[index, pl.ds(units * there[0], units)]
        first_part = all_rows.at[index, pl.ds(units * there[0], quarter)]
        diagonal = [post.send(first_part, first_part, me.yp)]
        post.send(beside, beside, me.core)
        post.got(from_y)
        beyond = all_rows.at[index, pl.ds(units * there[1], units)]
        last_part = all_rows.at[index, pl.ds(units * there[1] + quarter, units - quarter)]
        diagonal.append(post.send(last_part, last_part, me.xp))
        post.send(beyond, beyond, me.core)
        for copy in diagonal:
            post.got(copy)
        corner = all_rows.at[index, pl.ds(units * (2 * (2 * (1 - c) + k) + 1 - x), units)]
        post.send(corner, corner, me.core)
    post.close()
    for j in range(result.shape[0] // BLOCK):
        first_unit = where[j]
        to = slice(j * BLOCK, (j + 1) * BLOCK)
        result[to, :] = all_rows[0, pl.ds(first_unit, BLOCK // UNIT)].reshape(BLOCK, -1)
        patch_grad[to, :] = all_rows[1, pl.ds(first_unit, BLOCK // UNIT)].reshape(BLOCK, -1).astype(f32)


def finish(fsdp_count, where, dq, dkv, wh, low_own, x_own, middle_grad, result_half, gain):
    width = x_own.shape[1]
    shape = jax.ShapeDtypeStruct
    rows = where.shape[0] * BLOCK
    pair = 2 * BLOCK
    return pl.pallas_call(
        partial(finish_kernel, fsdp_count),
        out_shape=(
            shape((rows, width), bf16),
            shape((rows, width), f32),
            shape((3, width, 384), bf16),
            shape((2, width), f32),
            shape((1, width), f32),
        ),
        in_specs=[SMEM] + [VMEM] * 8,
        out_specs=(VMEM,) * 5,
        scratch_shapes=[
            pltpu.VMEM((pair, 768), bf16),
            pltpu.VMEM((pair, 768), bf16),
            pltpu.VMEM((pair, 768), bf16),
            pltpu.VMEM((pair, 768), bf16),
            pltpu.VMEM((OWN, 768), bf16),
            pltpu.VMEM((HALF, width), bf16),
            pltpu.VMEM((HALF, width), bf16),
            pltpu.VMEM((2, 2 * rows // UNIT, UNIT, width), bf16),
            pltpu.SemaphoreType.DMA((2,)),
            pltpu.SemaphoreType.DMA((24,)),
            pltpu.SemaphoreType.DMA((24,)),
        ],
        compiler_params=pltpu.CompilerParams(collective_id=2, has_side_effects=True, vmem_limit_bytes=LIMIT),
        name="finish",
    )(where, dq, dkv, wh, low_own, x_own, middle_grad, result_half, gain)


def total_kernel(
    fsdp_count, g_up, g_down, g_attn, g_out, all_stats, part_stats,
    final, all_total, part_total,
    packed, from_core, summed, from_y, strips, from_z, final_f32, stat_buf, stat_in, stat_z, ss, rs,
):
    me = Here(fsdp_count)
    f, c, x, k = me.f, me.c, me.x, me.k
    width = g_up.shape[0]
    deep = width // fsdp_count
    half = deep // 2
    greet([me.core, me.xp, me.yp] + me.z)
    post = Post(ss, rs)
    for j in (0, 1):
        packed[j, :, 0:768] = g_up[:, 768 * j : 768 * j + 768]
        packed[j, :, 768:1536] = g_down[:, 768 * j : 768 * j + 768]
        parts = [g_attn[0], g_attn[1], g_attn[2], g_out[...]]
        lanes = slice(128 * j, 128 * j + 128)
        tails = [p[:, 256 + 64 * j : 320 + 64 * j] for p in parts]
        for i, p in enumerate(parts):
            packed[j, :, 1536 + 128 * i : 1664 + 128 * i] = p[:, lanes]
        packed[j, :, 2048:2176] = jnp.concatenate(tails[0:2], axis=1)
        packed[j, :, 2176:2304] = jnp.concatenate(tails[2:4], axis=1)
    core_copy = post.send(packed.at[1 - k], from_core, me.core)
    rows_all, rows_part = all_stats.shape[0], part_stats.shape[0]
    stat_buf[0:rows_all, :] = all_stats[...]
    stat_buf[8 : 8 + rows_part, :] = part_stats[...]
    stat_copy = post.send(stat_buf.at[pl.ds(0, 16)], stat_in.at[0], me.core)
    post.got(stat_copy)
    post.got(core_copy)

    def add_core(j, carried):
        rows = ds(j * half, half)
        summed[rows, :] = (packed[k, rows, :].astype(f32) + from_core[rows, :].astype(f32)).astype(bf16)
        return carried

    lax.fori_loop(0, 2 * fsdp_count, add_core, 0)
    y_copies = []
    for g in range(fsdp_count):
        y_copies.append(post.send(summed.at[ds(deep * g + half * (1 - c), half)], from_y.at[g], me.yp))
    stat_buf[16:32, :] = stat_buf[0:16, :] + stat_in[0]
    stat_copy = post.send(stat_buf.at[pl.ds(16, 16)], stat_in.at[1], me.yp)
    for copy in y_copies:
        post.got(copy)

    def add_y(g, carried):
        rows = ds(deep * g + half * c, half)
        strips[g] = (summed[rows, :].astype(f32) + from_y[g].astype(f32)).astype(bf16)
        return carried

    lax.fori_loop(0, fsdp_count, add_y, 0)
    z_copies = []
    for i, device in enumerate(me.z):
        z_copies.append(post.send(strips.at[(f + i + 1) % fsdp_count], from_z.at[i], device))
    post.got(stat_copy)
    stat_buf[32:48, :] = stat_buf[16:32, :] + stat_in[1]
    stat_copy = post.send(stat_buf.at[pl.ds(32, 16)], stat_in.at[2], me.xp)
    post.got(stat_copy)
    stat_buf[48:56, :] = stat_buf[32:40, :] + stat_in[2, 0:8]
    stat_buf[56:64, :] = stat_buf[40:48, :]
    stat_z[f] = stat_buf[48:64, :]
    stat_copies = []
    for device in me.z:
        stat_copies.append(post.send(stat_buf.at[pl.ds(48, 16)], stat_z.at[f], device))
    for copy in z_copies:
        post.got(copy)
    final_f32[...] = strips[f].astype(f32)
    for i in range(len(me.z)):
        final_f32[...] += from_z[i].astype(f32)
    final[c] = final_f32[...].astype(bf16)
    post.send(final.at[c], final.at[c], me.yp)
    for copy in stat_copies:
        post.got(copy)
    total = stat_z[0]
    for g in range(1, fsdp_count):
        total = total + stat_z[g]
    all_total[...] = total[0:rows_all]
    part_total[...] = total[8 : 8 + rows_part]
    post.close()


def totals(fsdp_count, g_up, g_down, g_attn, g_out, all_stats, part_stats):
    width = g_up.shape[0]
    wide = 2304
    half = width // fsdp_count // 2
    shape = jax.ShapeDtypeStruct
    return pl.pallas_call(
        partial(total_kernel, fsdp_count),
        out_shape=(shape((2, half, wide), bf16), shape(all_stats.shape, f32), shape(part_stats.shape, f32)),
        in_specs=[VMEM] * 6,
        out_specs=(VMEM,) * 3,
        scratch_shapes=[
            pltpu.VMEM((2, width, wide), bf16),
            pltpu.VMEM((width, wide), bf16),
            pltpu.VMEM((width, wide), bf16),
            pltpu.VMEM((fsdp_count, half, wide), bf16),
            pltpu.VMEM((fsdp_count, half, wide), bf16),
            pltpu.VMEM((fsdp_count - 1, half, wide), bf16),
            pltpu.VMEM((half, wide), f32),
            pltpu.VMEM((64, width), f32),
            pltpu.VMEM((3, 16, width), f32),
            pltpu.VMEM((fsdp_count, 16, width), f32),
            pltpu.SemaphoreType.DMA((24,)),
            pltpu.SemaphoreType.DMA((24,)),
        ],
        compiler_params=pltpu.CompilerParams(collective_id=3, has_side_effects=True, vmem_limit_bytes=LIMIT),
        name="totals",
    )(g_up, g_down, g_attn, g_out, all_stats, part_stats)


def tree_shards(
    fsdp_count, patches, out_grad, block_order, first_gain, first_shift, attn_proj, attn_bias, out_proj, out_bias,
    second_gain, second_shift, up_proj, up_bias, down_proj, down_bias,
):
    row = lambda vector: vector.reshape(1, -1)
    order = block_order[0]
    slots = jnp.arange(order.shape[0], dtype=jnp.int32)
    where = jnp.sum(jnp.where(order[None, :] == slots[:, None], slots[None, :], 0), axis=1, dtype=jnp.int32)
    q, k, v = attn_proj[0], attn_proj[1], attn_proj[2]
    out_t = out_proj.T
    wa = jnp.concatenate(
        [q[:, :128], k[:, :128], v[:, :128], q[:, 128:], k[:, 128:], v[:, 128:], out_t[:, 128:], out_t[:, :128]],
        axis=1,
    )
    head_width = attn_bias.shape[1]
    bias = jnp.zeros((8, up_bias.shape[0]), f32)
    bias = bias.at[0].set(up_bias).at[1:3, :head_width].set(attn_bias)
    rows_all, grads_all, wa, wu, wd, bias = gather(
        fsdp_count, patches, out_grad, wa, up_proj, down_proj.T, bias
    )
    x_own, g_own, low_own, q, k, v, kt, attended, lse, wh = front(
        where, rows_all, grads_all, wa, bias, row(first_gain), row(first_shift)
    )
    result_half, middle_grad, da, g_up, g_down, g_out, stats, up_stats = middle_layer(
        fsdp_count, attended, wh[3], x_own, g_own, wu, wd, bias,
        row(second_gain), row(second_shift), row(out_bias), row(down_bias),
    )
    dq, dkv = back(da, attended, q, k, v, kt, lse)
    trunk, branch, leaf = order, order - TRUNK_BLK, order - TRUNK_BLK - BRANCHES
    gathered = jnp.where(
        order < TRUNK_BLK,
        5 * (trunk // 2) + trunk % 2,
        jnp.where(branch < BRANCHES, 5 * branch + 3, 5 * (leaf // 2) + 2 + 2 * (leaf % 2)),
    )
    own = patches.shape[0] // BLOCK
    gathered = lax.dynamic_slice_in_dim(gathered, lax.axis_index("context") * own, own)
    result, patch_grad, g_attn, first_stats, attn_stats = finish(
        fsdp_count, gathered * (BLOCK // UNIT), dq, dkv, wh, low_own, x_own, middle_grad, result_half, row(first_gain)
    )
    final, all_total, part_total = totals(
        fsdp_count, g_up, g_down, g_attn, g_out,
        jnp.concatenate([first_stats, stats], axis=0), jnp.concatenate([up_stats, attn_stats], axis=0),
    )
    final = final.reshape(-1, final.shape[2]).astype(f32)
    slab = lambda i: final[:, 1536 + 128 * i : 1664 + 128 * i]
    half_slab = lambda i: final[:, 2048 + 64 * i : 2112 + 64 * i]
    joined = [jnp.concatenate([slab(i), half_slab(i)], axis=1) for i in range(4)]
    core = lax.axis_index("tensor") % 2
    part_total = part_total.reshape(-1)
    up_total = lax.dynamic_slice_in_dim(part_total, core * 768, 768)
    attn_total = part_total[1536:].reshape(2, 384)
    attn_total = jnp.concatenate(
        [
            lax.dynamic_slice_in_dim(attn_total, core * 128, 128, 1),
            lax.dynamic_slice_in_dim(attn_total, 256 + core * 64, 64, 1),
        ],
        axis=1,
    )
    return (
        result,
        patch_grad,
        all_total[0],
        all_total[1],
        jnp.stack(joined[0:3]),
        attn_total,
        joined[3].T,
        all_total[5],
        all_total[2],
        all_total[3],
        final[:, 0:768],
        up_total,
        final[:, 768:1536].T,
        all_total[4],
    )


def solution(mesh):
    fits = mesh.shape["context"] * 2 == BRANCHES and mesh.shape["tensor"] == 4 and mesh.shape["fsdp"] == 4
    body = partial(tree_shards, mesh.shape["fsdp"]) if fits else shards
    return jax.shard_map(
        body,
        mesh=mesh,
        in_specs=(
            P(("fsdp", "context"), None),
            P(("fsdp", "context"), None),
            P("fsdp", None),
            P(),
            P(),
            P(None, "fsdp", "tensor"),
            P(None, "tensor"),
            P("tensor", "fsdp"),
            P(),
            P(),
            P(),
            P("fsdp", "tensor"),
            P("tensor"),
            P("tensor", "fsdp"),
            P(),
        ),
        out_specs=(
            P(("fsdp", "context"), None),
            P(("fsdp", "context"), None),
            P(),
            P(),
            P(None, "fsdp", "tensor"),
            P(None, "tensor"),
            P("tensor", "fsdp"),
            P(),
            P(),
            P(),
            P("fsdp", "tensor"),
            P("tensor"),
            P("tensor", "fsdp"),
            P(),
        ),
        check_vma=False,
    )
```

```python
from functools import partial

import jax
import jax.numpy as jnp
from jax import lax
from jax.experimental import pallas as pl
from jax.experimental.pallas import tpu as pltpu
from jax.sharding import PartitionSpec as P

HEAD_DIM = 64
BLOCK = 128
TRUNK_BLK = 8
BRANCHES = 4
LEAVES = 2
TREE_BLK = 20


epsilon = 1e-05
far_below = -1e30


def layer_norm(values, norm_gain, norm_shift):
    center = values - jnp.mean(values, axis=1, keepdims=True)
    inverse = lax.rsqrt(jnp.mean(center * center, axis=1, keepdims=True) + epsilon)
    normed = center * inverse
    return (normed * norm_gain + norm_shift, normed, inverse)


def norm_back(gradient, normed, inverse, norm_gain):
    scaled = gradient * norm_gain
    return inverse * (
        scaled
        - jnp.mean(scaled, axis=1, keepdims=True)
        - normed * jnp.mean(scaled * normed, axis=1, keepdims=True)
    )


def slot_labels(order_row):
    position = order_row % TREE_BLK
    return (order_row // TREE_BLK, jnp.where(position < TRUNK_BLK, 0, position - TRUNK_BLK + 1))


def spread_rows(values):
    return jnp.broadcast_to(values[:, None], (values.shape[0], BLOCK)).reshape(-1)


def row_labels(labels, first_slot, slot_count):
    return tuple(
        (
            spread_rows(lax.dynamic_slice_in_dim(label_table, first_slot, slot_count))
            for label_table in labels
        )
    )


def visible(query_labels, key_labels):
    query_tree, query_seg = query_labels
    key_tree, key_seg = key_labels
    parent = jnp.where(query_seg > BRANCHES, 1 + (query_seg - BRANCHES - 1) // LEAVES, 0)
    reaches = (
        (key_seg[None, :] == 0)
        | (key_seg[None, :] == query_seg[:, None])
        | (key_seg[None, :] == parent[:, None])
    )
    return (query_tree[:, None] == key_tree[None, :]) & reaches


def head_view(matrix):
    return matrix.reshape(matrix.shape[0], matrix.shape[1] // HEAD_DIM, HEAD_DIM)


def scores_of(query_heads, key_heads):
    return jnp.einsum(
        "qhd,khd->hqk", query_heads, key_heads, preferred_element_type=jnp.float32
    ) * HEAD_DIM ** (-0.5)


def weights_of(scores, log_total, allowed):
    return jnp.where(allowed[None], jnp.exp(scores - log_total[:, :, None]), 0.0)


def score_grads(query_heads, grad_heads, key_heads, value_heads, log_total, row_delta, allowed):
    weights = weights_of(scores_of(query_heads, key_heads), log_total, allowed)
    prob_grad = jnp.einsum(
        "qhd,khd->hqk", grad_heads, value_heads, preferred_element_type=jnp.float32
    )
    return (
        (weights * (prob_grad - row_delta[:, :, None])).astype(jnp.bfloat16),
        weights.astype(jnp.bfloat16),
    )


def shards(
    patches,
    out_grad,
    block_order,
    first_gain,
    first_shift,
    attn_proj,
    attn_bias,
    out_proj,
    out_bias,
    second_gain,
    second_shift,
    up_proj,
    up_bias,
    down_proj,
    down_bias,
):
    attn_full, out_full, up_full, down_full = (
        lax.all_gather(attn_proj, "fsdp", axis=1, tiled=True),
        lax.all_gather(out_proj, "fsdp", axis=1, tiled=True),
        lax.all_gather(up_proj, "fsdp", axis=0, tiled=True),
        lax.all_gather(down_proj, "fsdp", axis=1, tiled=True),
    )
    labels = slot_labels(block_order[0])
    row_count = patches.shape[0]
    own_slots = row_count // BLOCK
    query_labels = row_labels(labels, lax.axis_index("context") * own_slots, own_slots)
    head_width = attn_full.shape[2]
    head_count = head_width // HEAD_DIM
    key_block = 4 * BLOCK
    block_slots = key_block // BLOCK
    score_scale = HEAD_DIM ** (-0.5)
    inputs = patches.astype(jnp.float32)
    first_norm, first_normed, first_inverse = layer_norm(inputs, first_gain, first_shift)
    first_low = first_norm.astype(jnp.bfloat16)
    projected = jnp.einsum("rd,cde->cre", first_low, attn_full, preferred_element_type=jnp.float32)
    queries = (projected[0] + attn_bias[0]).astype(jnp.bfloat16)
    keys_low = projected[1].astype(jnp.bfloat16)
    values_low = (projected[2] + attn_bias[1]).astype(jnp.bfloat16)
    keys_all = lax.all_gather(
        jnp.concatenate([keys_low, values_low], axis=1), "context", axis=0, tiled=True
    )
    block_count = keys_all.shape[0] // key_block
    query_heads = head_view(queries)

    def key_piece(step_index):
        key_slab = lax.dynamic_slice_in_dim(keys_all, step_index * key_block, key_block, 0)
        allowed = visible(query_labels, row_labels(labels, step_index * block_slots, block_slots))
        return (head_view(key_slab[:, :head_width]), head_view(key_slab[:, head_width:]), allowed)

    def total_step(step_index, carried):
        running_top, running_sum = carried
        key_heads, value_heads, allowed = key_piece(step_index)
        masked = jnp.where(allowed[None], scores_of(query_heads, key_heads), far_below)
        new_top = jnp.maximum(running_top, jnp.max(masked, axis=2))
        kept_exp = jnp.where(allowed[None], jnp.exp(masked - new_top[:, :, None]), 0.0)
        return (new_top, running_sum * jnp.exp(running_top - new_top) + jnp.sum(kept_exp, axis=2))

    start_top = jnp.full((head_count, row_count), far_below, jnp.float32)
    running_top, running_sum = lax.fori_loop(
        0, block_count, total_step, (start_top, jnp.zeros((head_count, row_count), jnp.float32))
    )
    log_total = running_top + jnp.log(running_sum)

    def mix_step(step_index, mixed):
        key_heads, value_heads, allowed = key_piece(step_index)
        weights = weights_of(scores_of(query_heads, key_heads), log_total, allowed).astype(
            jnp.bfloat16
        )
        return mixed + jnp.einsum(
            "hqk,khd->qhd", weights, value_heads, preferred_element_type=jnp.float32
        )

    attended = lax.fori_loop(
        0, block_count, mix_step, jnp.zeros((row_count, head_count, HEAD_DIM), jnp.float32)
    )
    attended_low = attended.reshape(row_count, head_width).astype(jnp.bfloat16)
    attn_part = jnp.dot(attended_low, out_full, preferred_element_type=jnp.float32)
    middle = inputs + (lax.psum(attn_part, "tensor") + out_bias)
    second_norm, second_normed, second_inverse = layer_norm(middle, second_gain, second_shift)
    second_low = second_norm.astype(jnp.bfloat16)
    pre_act = jnp.dot(second_low, up_full, preferred_element_type=jnp.float32) + up_bias
    hidden, gelu_back = jax.vjp(partial(jax.nn.gelu, approximate=False), pre_act)
    hidden_low = hidden.astype(jnp.bfloat16)
    mlp_part = jnp.dot(hidden_low, down_full, preferred_element_type=jnp.float32)
    result = (
        middle + (lax.psum(mlp_part.astype(jnp.bfloat16), "tensor").astype(jnp.float32) + down_bias)
    ).astype(jnp.bfloat16)
    top_grad = out_grad.astype(jnp.float32)
    grad_down_bias = jnp.sum(top_grad, axis=0)
    grad_down = jnp.einsum("rf,rd->fd", hidden_low, out_grad, preferred_element_type=jnp.float32)
    hidden_grad = jnp.einsum("rd,fd->rf", out_grad, down_full, preferred_element_type=jnp.float32)
    pre_grad = gelu_back(hidden_grad)[0].astype(jnp.bfloat16)
    grad_up_bias = jnp.sum(pre_grad.astype(jnp.float32), axis=0)
    grad_up = jnp.einsum("rd,rf->df", second_low, pre_grad, preferred_element_type=jnp.float32)
    second_part = jnp.einsum("rf,df->rd", pre_grad, up_full, preferred_element_type=jnp.float32)
    second_grad = lax.psum(second_part, "tensor")
    grad_second_gain = jnp.sum(second_grad * second_normed, axis=0)
    grad_second_shift = jnp.sum(second_grad, axis=0)
    middle_grad = top_grad + norm_back(second_grad, second_normed, second_inverse, second_gain)
    branch_grad = middle_grad.astype(jnp.bfloat16)
    grad_out_bias = jnp.sum(branch_grad.astype(jnp.float32), axis=0)
    grad_out = jnp.einsum(
        "re,rd->ed", attended_low, branch_grad, preferred_element_type=jnp.float32
    )
    attended_grad = jnp.einsum(
        "rd,ed->re", branch_grad, out_full, preferred_element_type=jnp.float32
    ).astype(jnp.bfloat16)
    grad_heads = head_view(attended_grad)

    def delta_step(step_index, row_delta):
        key_heads, value_heads, allowed = key_piece(step_index)
        weights = weights_of(scores_of(query_heads, key_heads), log_total, allowed)
        prob_grad = jnp.einsum(
            "qhd,khd->hqk", grad_heads, value_heads, preferred_element_type=jnp.float32
        )
        return row_delta + jnp.sum(weights * prob_grad, axis=2)

    row_delta = lax.fori_loop(
        0, block_count, delta_step, jnp.zeros((head_count, row_count), jnp.float32)
    )
    query_start = jnp.zeros((row_count, head_count, HEAD_DIM), jnp.float32)

    def back_step(step_index, carried):
        query_acc, key_acc = carried
        key_heads, value_heads, allowed = key_piece(step_index)
        score_low, weights_low = score_grads(
            query_heads, grad_heads, key_heads, value_heads, log_total, row_delta, allowed
        )
        query_acc = query_acc + jnp.einsum(
            "hqk,khd->qhd", score_low, key_heads, preferred_element_type=jnp.float32
        )
        key_part = jnp.einsum(
            "hqk,qhd->khd", score_low, query_heads, preferred_element_type=jnp.float32
        )
        value_part = jnp.einsum(
            "hqk,qhd->khd", weights_low, grad_heads, preferred_element_type=jnp.float32
        )
        joined = jnp.concatenate(
            [key_part.reshape(key_block, head_width), value_part.reshape(key_block, head_width)],
            axis=1,
        )
        return (
            query_acc,
            lax.dynamic_update_slice_in_dim(key_acc, joined, step_index * key_block, 0),
        )

    key_start = jnp.zeros((keys_all.shape[0], 2 * head_width), jnp.float32)
    query_acc, key_acc = lax.fori_loop(0, block_count, back_step, (query_start, key_start))
    key_value_grad = lax.psum_scatter(key_acc, "context", scatter_dimension=0, tiled=True)
    query_grad = (query_acc.reshape(row_count, head_width) * score_scale).astype(jnp.bfloat16)
    key_grad = (key_value_grad[:, :head_width] * score_scale).astype(jnp.bfloat16)
    value_grad = key_value_grad[:, head_width:].astype(jnp.bfloat16)
    stacked = jnp.stack([query_grad, key_grad, value_grad])
    grad_attn_bias = jnp.stack(
        [
            jnp.sum(query_grad.astype(jnp.float32), axis=0),
            jnp.sum(value_grad.astype(jnp.float32), axis=0),
        ]
    )
    grad_attn = jnp.einsum("rd,cre->cde", first_low, stacked, preferred_element_type=jnp.float32)
    first_grad = lax.psum(
        jnp.einsum("cre,cde->rd", stacked, attn_full, preferred_element_type=jnp.float32), "tensor"
    )
    grad_first_gain = jnp.sum(first_grad * first_normed, axis=0)
    grad_first_shift = jnp.sum(first_grad, axis=0)
    patch_grad = middle_grad + norm_back(first_grad, first_normed, first_inverse, first_gain)
    wide_attn, wide_out, wide_up, wide_down = (
        lax.psum_scatter(grad_attn, ("fsdp", "context"), scatter_dimension=1, tiled=True),
        lax.psum_scatter(grad_out, ("fsdp", "context"), scatter_dimension=1, tiled=True),
        lax.psum_scatter(grad_up, ("fsdp", "context"), scatter_dimension=0, tiled=True),
        lax.psum_scatter(grad_down, ("fsdp", "context"), scatter_dimension=1, tiled=True),
    )
    grad_attn, grad_out, grad_up, grad_down = (
        lax.all_gather(wide_attn, "context", axis=1, tiled=True),
        lax.all_gather(wide_out, "context", axis=1, tiled=True),
        lax.all_gather(wide_up, "context", axis=0, tiled=True),
        lax.all_gather(wide_down, "context", axis=1, tiled=True),
    )
    small_grads = lax.psum(
        (
            grad_first_gain,
            grad_first_shift,
            grad_attn_bias,
            grad_out_bias,
            grad_second_gain,
            grad_second_shift,
            grad_up_bias,
            grad_down_bias,
        ),
        ("fsdp", "context"),
    )
    return (
        result,
        patch_grad,
        small_grads[0],
        small_grads[1],
        grad_attn,
        small_grads[2],
        grad_out,
        small_grads[3],
        small_grads[4],
        small_grads[5],
        grad_up,
        small_grads[6],
        grad_down,
        small_grads[7],
    )


bf16 = jnp.bfloat16
f32 = jnp.float32
VMEM = pl.BlockSpec(memory_space=pltpu.VMEM)
SMEM = pl.BlockSpec(memory_space=pltpu.SMEM)
ANY = pl.BlockSpec(memory_space=pl.ANY)
MESH = pl.DeviceIdType.MESH
LIMIT = 60 * 1024 * 1024


def dot_nn(a, b):
    return lax.dot_general(a, b, (((1,), (0,)), ((), ())), preferred_element_type=f32)


def dot_nt(a, b):
    return lax.dot_general(a, b, (((1,), (1,)), ((), ())), preferred_element_type=f32)


def dot_tn(a, b):
    return lax.dot_general(a, b, (((0,), (0,)), ((), ())), preferred_element_type=f32)


class Here:
    def __init__(self, fsdp_count):
        self.f = lax.axis_index("fsdp")
        self.c = lax.axis_index("context")
        self.t = lax.axis_index("tensor")
        self.x = self.t // 2
        self.k = self.t % 2
        self.core = (self.f, self.c, 2 * self.x + 1 - self.k)
        self.xp = (self.f, self.c, 2 * (1 - self.x) + self.k)
        self.yp = (self.f, 1 - self.c, self.t)
        self.z = [((self.f + i) % fsdp_count, self.c, self.t) for i in range(1, fsdp_count)]
        self.back = [(self.f + fsdp_count - i) % fsdp_count for i in range(1, fsdp_count)]


def greet(devices):
    barrier = pltpu.get_barrier_semaphore()
    for device in devices:
        pl.semaphore_signal(barrier, inc=1, device_id=device, device_id_type=MESH)
    pl.semaphore_wait(barrier, len(devices))


class Post:
    def __init__(self, send_sem, recv_sem):
        self.send_sem, self.recv_sem = send_sem, recv_sem
        self.sent, self.open = [], []

    def send(self, src, dst, device):
        index = len(self.sent)
        copy = pltpu.make_async_remote_copy(
            src_ref=src,
            dst_ref=dst,
            send_sem=self.send_sem.at[index],
            recv_sem=self.recv_sem.at[index],
            device_id=device,
            device_id_type=MESH,
        )
        copy.start()
        self.sent.append(copy)
        self.open.append((copy, device))
        return copy

    def got(self, copy):
        copy.wait_recv()
        self.open = [entry for entry in self.open if entry[0] is not copy]

    def got_from(self, device):
        for copy, to in self.open:
            if to is device:
                self.got(copy)

    def close(self):
        for copy, _ in self.open:
            copy.wait_recv()
        for copy in self.sent:
            copy.wait_send()


def ds(start, size, step=16):
    return pl.ds(pl.multiple_of(start, step), size)


TRUNK = TRUNK_BLK * BLOCK
SUB = (1 + LEAVES) * BLOCK
KEYS = TRUNK + SUB
OWN = 2 * BLOCK + SUB
PIECES = (
    (2 * BLOCK, TRUNK, 2 * BLOCK),
    (3 * BLOCK, TRUNK + BLOCK, BLOCK),
    (4 * BLOCK, TRUNK + BLOCK, 2 * BLOCK),
)


def own_places(s):
    return [2 * s, 2 * s + 1, 12 + 2 * s, 8 + s, 13 + 2 * s]


def row_norm(values):
    center = values - jnp.mean(values, axis=1, keepdims=True)
    inverse = lax.rsqrt(jnp.mean(center * center, axis=1, keepdims=True) + epsilon)
    return center * inverse, inverse

HALF = OWN // 2
UNIT = 32


def first_kernel(
    fsdp_count, where, patches, grads, attn_proj, out_proj, up, down, bias, gain1, shift1, gain2, shift2, out_bias, down_bias,
    q_out, k_out, v_out, kt_out, att_out, low_out, x_out, wh_out, g_up_out, g_down_out,
    lse, da, middle_grad, mlp_own, mlp_send, g_out_own, g_out_send, stats, up_stats,
    a_own, d_own, rows_all, grads_all, wa, wh, wo_x, wu, wd, bias_all,
    low, low_own, x_own, g_own, q, k, v, kt, vt, attended, att_t, att_x, st, pt,
    middle, normed, inverse, low2, hidden, pre_grad, second, second_send, second_x, da_send, g_up, g_down,
    local, ss, rs,
):
    me = Here(fsdp_count)
    f, c, x, core, t = me.f, me.c, me.x, me.k, me.t
    s = 2 * c + core
    units = patches.shape[0]
    part = units // 4
    width = patches.shape[2]
    deep = up.shape[0]
    half = deep // 2
    head_width = attn_proj.shape[2]
    early = 640
    own_copies = []

    def keep(src, dst):
        copy = pltpu.make_async_copy(src, dst, local.at[len(own_copies)])
        copy.start()
        own_copies.append(copy)

    keep(patches, rows_all.at[pl.ds(units * c, units)])
    keep(grads, grads_all.at[pl.ds(units * c, units)])
    keep(up, wu.at[core, ds(deep * f, deep)])
    a_own[:, 0:128] = attn_proj[0, :, 0:128]
    a_own[:, 128:256] = attn_proj[1, :, 0:128]
    a_own[:, 256:384] = attn_proj[2, :, 0:128]
    out_t = out_proj[...].T
    a_own[:, 384:512] = jnp.concatenate([attn_proj[0, :, 128:head_width], attn_proj[1, :, 128:head_width]], axis=1)
    a_own[:, 512:640] = jnp.concatenate([attn_proj[2, :, 128:head_width], out_t[:, 128:head_width]], axis=1)
    a_own[:, 640:768] = out_t[:, 0:128]
    greet([me.core, me.xp, me.yp] + me.z)
    post = Post(ss, rs)
    there = units * (1 - c)
    strip, other_strip = half * c, half * (1 - c)

    def quarter(array, index, piece, count=2):
        size = part // count
        return array.at[pl.ds(there + part * index + size * piece, size)]

    def to_y(src, dst, piece, count=2):
        size = part // count
        return post.send(
            src.at[pl.ds(part * t + size * piece, size)],
            dst.at[pl.ds(units * c + part * t + size * piece, size)],
            me.yp,
        )

    def relay(piece, device):
        return post.send(piece, piece, device)

    a_dst = lambda shard, row, lanes: wa.at[shard, ds(row, half), lanes]
    lo, hi = pl.ds(0, early), pl.ds(early, width - early)
    patches_y = [to_y(patches, rows_all, i) for i in range(2)]
    a1_z = [
        post.send(a_own.at[ds(strip, half), lo], a_dst(core, deep * f + strip, lo), device) for device in me.z
    ]
    a_core = post.send(a_own, wa.at[core, ds(deep * f, deep)], me.core)
    bias_core = post.send(bias, bias_all.at[core], me.core)
    u_core = post.send(up, wu.at[core, ds(deep * f, deep)], me.core)
    wa[core, ds(deep * f, deep), :] = a_own[...]
    bias_all[core] = bias[...]
    d_own[...] = down[...].T
    wd[core, ds(deep * f, deep), :] = d_own[...]
    d_core = post.send(d_own, wd.at[core, ds(deep * f, deep)], me.core)
    patches_x = []
    for i in range(2):
        post.got(patches_y[i])
        patches_x.append(relay(quarter(rows_all, t, i), me.xp))
        relay(quarter(rows_all, t, i), me.core)
    a1_y = []
    for copy, source in zip(a1_z, me.back):
        post.got(copy)
        piece = a_dst(core, deep * source + strip, lo)
        a1_y.append(relay(piece, me.yp))
        relay(piece, me.core)
    a2_z = [
        post.send(a_own.at[ds(strip, half), hi], a_dst(core, deep * f + strip, hi), device) for device in me.z
    ]
    u_z = [
        post.send(up.at[ds(strip, half)], wu.at[core, ds(deep * f + strip, half)], device) for device in me.z
    ]
    over = (t + 2) % 4
    for i in range(2):
        post.got(patches_x[i])
        relay(quarter(rows_all, over, i), me.core)
    post.got_from(me.core)
    own_copies[0].wait()

    gain_row, shift_row = gain1[...], shift1[...]

    def block_of(array, place):
        return array[pl.ds(where[place], BLOCK // UNIT)].reshape(BLOCK, width)

    def norm_block(place, row):
        normed_rows, _ = row_norm(block_of(rows_all, place).astype(f32))
        low[ds(row, BLOCK), :] = (normed_rows * gain_row + shift_row).astype(bf16)

    def trunk_step(j, carried):
        norm_block(j, j * BLOCK)
        return carried

    lax.fori_loop(0, TRUNK_BLK, trunk_step, 0)
    places = own_places(s)
    for j in range(2, 5):
        norm_block(places[j], TRUNK + (j - 2) * BLOCK)
    for j, place in enumerate(places):
        x_own[pl.ds(j * BLOCK, BLOCK), :] = block_of(rows_all, place)
    low_own[0 : 2 * BLOCK, :] = low[ds(2 * BLOCK * s, 2 * BLOCK), :]
    low_own[2 * BLOCK :, :] = low[TRUNK:, :]
    for copy, source in zip(a1_y, me.back):
        post.got(copy)
        relay(a_dst(core, deep * source + other_strip, lo), me.core)
    grads_y = [to_y(grads, grads_all, i) for i in range(2)]
    post.got_from(me.core)

    def assemble(i):
        slab = (0, 1, 2, 5)[i]
        wh[i, :, 0:128] = wa[0, :, 128 * slab : 128 * slab + 128]
        wh[i, :, 128:256] = wa[1, :, 128 * slab : 128 * slab + 128]
        start = 384 + 64 * i
        wh[i, :, 256:384] = jnp.concatenate(
            [wa[0, :, start : start + 64], wa[1, :, start : start + 64]], axis=1
        )

    for i in range(3):
        assemble(i)

    def heads_row(row):
        a, b = bias_all[0, row : row + 1, :], bias_all[1, row : row + 1, :]
        return jnp.concatenate([a[:, 0:128], b[:, 0:128], a[:, 128:192], b[:, 128:192]], axis=1)

    q[...] = ((dot_nn(low_own[...], wh[0]) + heads_row(1)).astype(bf16) * HEAD_DIM ** (-0.5)).astype(bf16)
    value_bias = heads_row(2)

    def project(j, carried):
        rows = ds(j * (KEYS // 2), KEYS // 2)
        k[rows, :] = dot_nn(low[rows, :], wh[1]).astype(bf16)
        v[rows, :] = (dot_nn(low[rows, :], wh[2]) + value_bias).astype(bf16)
        return carried

    lax.fori_loop(0, 2, project, 0)
    kt[...] = k[...].T
    vt[...] = v[...].T
    for src, dst in ((q, q_out), (k, k_out), (v, v_out), (kt, kt_out), (low_own, low_out), (x_own, x_out)):
        keep(src, dst)
    lane = lax.broadcasted_iota(jnp.int32, (OWN, 128), 1) // HEAD_DIM

    def head(h, carried):
        slab, side = h // 2, h % 2
        lanes = pl.ds(pl.multiple_of(slab * 128, 128), 128)
        own_q = q[:, lanes]
        q_part = jnp.where(lane == side, own_q, jnp.zeros_like(own_q))
        st[0:TRUNK, :] = dot_nt(k[0:TRUNK, lanes], q_part)
        for q_row, k_row, count in PIECES:
            st[TRUNK : TRUNK + count, q_row : q_row + BLOCK] = dot_nt(
                k[k_row : k_row + count, lanes], q_part[q_row : q_row + BLOCK]
            )
        tops, sums = [], []
        for j in range(OWN // BLOCK):
            cols = slice(j * BLOCK, (j + 1) * BLOCK)
            count = TRUNK + (0 if j < 2 else PIECES[j - 2][2])
            top = jnp.full((8, BLOCK), far_below, f32)
            for r in range(0, count, BLOCK):
                piece = st[r : r + BLOCK, cols].reshape(BLOCK // 8, 8, BLOCK)
                top = jnp.maximum(top, jnp.max(piece, axis=0))
            top = jnp.max(top, axis=0, keepdims=True)
            total = jnp.zeros((8, BLOCK), f32)
            for r in range(0, count, BLOCK):
                weight = jnp.exp(st[r : r + BLOCK, cols] - top)
                total = total + jnp.sum(weight.reshape(BLOCK // 8, 8, BLOCK), axis=0)
                pt[r : r + BLOCK, cols] = weight.astype(bf16)
            tops.append(top)
            sums.append(jnp.sum(total, axis=0, keepdims=True))
        total = jnp.concatenate(sums, axis=1)
        head_rows = ds(h * HEAD_DIM, HEAD_DIM)
        att_t[head_rows, :] = dot_nn(vt[head_rows, 0:TRUNK], pt[0:TRUNK, :])
        for q_row, k_row, count in PIECES:
            cols = slice(q_row, q_row + BLOCK)
            att_t[head_rows, cols] += dot_nn(
                vt[head_rows, k_row : k_row + count], pt[TRUNK : TRUNK + count, cols]
            )
        att_t[head_rows, :] = att_t[head_rows, :] / total
        lse[pl.ds(h, 1), :] = jnp.concatenate(tops, axis=1) + jnp.log(total)
        return carried

    lax.fori_loop(0, 2, head, 0)
    a2_y, u_y, grads_x = [], [], []
    for copy, source in zip(a2_z, me.back):
        post.got(copy)
        piece = a_dst(core, deep * source + strip, hi)
        a2_y.append(relay(piece, me.yp))
        relay(piece, me.core)
    post.got(grads_y[0])
    grads_x.append(relay(quarter(grads_all, t, 0), me.xp))
    relay(quarter(grads_all, t, 0), me.core)
    for copy, source in zip(u_z, me.back):
        post.got(copy)
        piece = wu.at[core, ds(deep * source + strip, half)]
        u_y.append(relay(piece, me.yp))
        relay(piece, me.core)
    d_z = [
        post.send(d_own.at[ds(strip, half)], wd.at[core, ds(deep * f + strip, half)], device) for device in me.z
    ]
    lax.fori_loop(2, 4, head, 0)
    post.got(grads_y[1])
    grads_x.append(relay(quarter(grads_all, t, 1), me.xp))
    relay(quarter(grads_all, t, 1), me.core)
    for copy, source in zip(a2_y, me.back):
        post.got(copy)
        relay(a_dst(core, deep * source + other_strip, hi), me.core)
    lax.fori_loop(4, 6, head, 0)
    attended[...] = att_t[...].T.astype(bf16)
    mine, far = HALF * x, HALF * (1 - x)
    here_rows, far_rows = ds(mine, HALF), ds(far, HALF)
    att_copy = post.send(attended.at[far_rows], att_x, me.xp)
    keep(attended, att_out)
    post.got_from(me.core)
    assemble(3)
    keep(wh, wh_out)
    wo_rows = ds(width // 2 * core, width // 2)
    wo_copy = post.send(wh.at[3, wo_rows], wo_x.at[wo_rows], me.xp)
    middle[...] = (
        x_own[here_rows, :].astype(f32) + out_bias[...] + dot_nt(attended[here_rows, :], wh[3])
    )
    d_y = []
    for copy, source in zip(d_z, me.back):
        post.got(copy)
        piece = wd.at[core, ds(deep * source + strip, half)]
        d_y.append(relay(piece, me.yp))
        relay(piece, me.core)
    post.got(wo_copy)
    relay(wo_x.at[wo_rows], me.core)
    for i in range(2):
        post.got(grads_x[i])
        relay(quarter(grads_all, over, i), me.core)
    post.got_from(me.core)
    post.got(att_copy)
    middle[...] += dot_nt(att_x[...], wo_x[...])
    n2, s2 = row_norm(middle[...])
    normed[...] = n2
    inverse[...] = s2
    low2[here_rows, :] = (n2 * gain2[...] + shift2[...]).astype(bf16)
    low_copy = post.send(low2.at[here_rows], low2.at[here_rows], me.xp)
    own_copies[1].wait()
    for j, place in enumerate(places):
        g_own[pl.ds(j * BLOCK, BLOCK), :] = block_of(grads_all, place)
    for copy, source in zip(u_y, me.back):
        post.got(copy)
        relay(wu.at[core, ds(deep * source + other_strip, half)], me.core)
    for copy, source in zip(d_y, me.back):
        post.got(copy)
        relay(wd.at[core, ds(deep * source + other_strip, half)], me.core)
    post.got_from(me.core)
    own_copies[2].wait()
    tile = 256

    def feed(rows):
        second[rows, :] = jnp.zeros((HALF, width), f32)

        def step(j, carried):
            shard, lanes = j // 3, pl.ds(pl.multiple_of(j % 3 * tile, 128), tile)
            out = pl.ds(pl.multiple_of(j * tile, 128), tile)
            pre = dot_nn(low2[rows, :], wu[shard, :, lanes]) + bias_all[shard, 0:1, lanes]
            below = 0.5 * (1.0 + lax.erf(pre * (2.0**-0.5)))
            density = jnp.exp(-0.5 * pre * pre) * (2.0 * jnp.pi) ** -0.5
            hidden[rows, out] = (pre * below).astype(bf16)
            back = dot_nn(g_own[rows, :], wd[shard, :, lanes])
            low_back = (back * (below + pre * density)).astype(bf16)
            pre_grad[rows, out] = low_back
            second[rows, :] += dot_nt(low_back, wu[shard, :, lanes])
            return carried

        lax.fori_loop(0, 6, step, 0)

    def mlp(rows):
        return dot_nt(hidden[rows, 0:width], wd[0]) + dot_nt(hidden[rows, width:], wd[1])

    feed(here_rows)
    post.got(low_copy)
    feed(far_rows)
    second_send[...] = second[far_rows, :].astype(bf16)
    second_copy = post.send(second_send, second_x, me.xp)

    def weight_step(j, carried):
        lanes = pl.ds(pl.multiple_of(j * tile, 128), tile)
        g_up[:, lanes] = dot_tn(low2[...], pre_grad[:, lanes]).astype(bf16)
        g_down[:, lanes] = dot_tn(g_own[...], hidden[:, lanes]).astype(bf16)
        return carried

    lax.fori_loop(0, 6, weight_step, 0)
    keep(g_up, g_up_out)
    keep(g_down, g_down_out)
    up_stats[0:1, :] = jnp.sum(pre_grad[:, 0:width].astype(f32), axis=0, keepdims=True)
    up_stats[1:2, :] = jnp.sum(pre_grad[:, width:].astype(f32), axis=0, keepdims=True)
    mlp_send[...] = mlp(far_rows).astype(bf16)
    mlp_own[...] = middle[...] + mlp(here_rows) + down_bias[...]
    dy = g_own[here_rows, :].astype(f32)
    stats[2:3, :] = jnp.sum(dy, axis=0, keepdims=True)
    post.got(second_copy)
    second_grad = second[here_rows, :] + second_x[...].astype(f32)
    n2 = normed[...]
    stats[0:1, :] = jnp.sum(second_grad * n2, axis=0, keepdims=True)
    stats[1:2, :] = jnp.sum(second_grad, axis=0, keepdims=True)
    grad = dy + norm_back(second_grad, n2, inverse[...], gain2[...])
    middle_grad[...] = grad
    branch = grad.astype(bf16)
    da_send[...] = dot_nn(branch, wo_x[...]).astype(bf16)
    post.send(da_send, da.at[here_rows], me.xp)
    stats[3:4, :] = jnp.sum(branch.astype(f32), axis=0, keepdims=True)
    da[here_rows, :] = dot_nn(branch, wh[3]).astype(bf16)
    g_out_send[...] = dot_tn(branch, att_x[...]).astype(bf16)
    g_out_own[...] = dot_tn(branch, attended[here_rows, :]).astype(bf16)
    post.close()
    for copy in own_copies[3:]:
        copy.wait()


def first_half(fsdp_count, where, patches, grads, attn_proj, out_proj, up, down, bias, *rows):
    width = patches.shape[1]
    shape = jax.ShapeDtypeStruct
    vmem = pltpu.VMEM
    units = 2 * up.shape[1]
    all_units = 2 * patches.shape[0] // UNIT
    deep = up.shape[0]
    fold = lambda a: a.reshape(-1, UNIT, width)
    return pl.pallas_call(
        partial(first_kernel, fsdp_count),
        out_shape=(
            shape((OWN, 384), bf16),
            shape((KEYS, 384), bf16),
            shape((KEYS, 384), bf16),
            shape((384, KEYS), bf16),
            shape((OWN, 384), bf16),
            shape((OWN, width), bf16),
            shape((OWN, width), bf16),
            shape((4, width, 384), bf16),
            shape((width, units), bf16),
            shape((width, units), bf16),
            shape((8, OWN), f32),
            shape((OWN, 384), bf16),
            shape((HALF, width), f32),
            shape((HALF, width), f32),
            shape((HALF, width), bf16),
            shape((width, 384), bf16),
            shape((width, 384), bf16),
            shape((4, width), f32),
            shape((2, width), f32),
        ),
        in_specs=[SMEM, ANY, ANY, VMEM, VMEM, ANY, VMEM] + [VMEM] * 7,
        out_specs=(ANY,) * 10 + (VMEM,) * 9,
        scratch_shapes=[
            vmem((deep, width), bf16),
            vmem((deep, down.shape[0]), bf16),
            vmem((all_units, UNIT, width), bf16),
            vmem((all_units, UNIT, width), bf16),
            vmem((2, width, width), bf16),
            vmem((4, width, 384), bf16),
            vmem((width, 384), bf16),
            vmem((2, width, up.shape[1]), bf16),
            vmem((2, width, up.shape[1]), bf16),
            vmem((2,) + bias.shape, f32),
            vmem((KEYS, width), bf16),
            vmem((OWN, width), bf16),
            vmem((OWN, width), bf16),
            vmem((OWN, width), bf16),
            vmem((OWN, 384), bf16),
            vmem((KEYS, 384), bf16),
            vmem((KEYS, 384), bf16),
            vmem((384, KEYS), bf16),
            vmem((384, KEYS), bf16),
            vmem((OWN, 384), bf16),
            vmem((384, OWN), f32),
            vmem((HALF, 384), bf16),
            vmem((TRUNK + 2 * BLOCK, OWN), f32),
            vmem((TRUNK + 2 * BLOCK, OWN), bf16),
            vmem((HALF, width), f32),
            vmem((HALF, width), f32),
            vmem((HALF, 1), f32),
            vmem((OWN, width), bf16),
            vmem((OWN, units), bf16),
            vmem((OWN, units), bf16),
            vmem((OWN, width), f32),
            vmem((HALF, width), bf16),
            vmem((HALF, width), bf16),
            vmem((HALF, 384), bf16),
            vmem((width, units), bf16),
            vmem((width, units), bf16),
            pltpu.SemaphoreType.DMA((16,)),
            pltpu.SemaphoreType.DMA((80,)),
            pltpu.SemaphoreType.DMA((80,)),
        ],
        compiler_params=pltpu.CompilerParams(collective_id=0, has_side_effects=True, vmem_limit_bytes=LIMIT),
        name="first_half",
    )(where, fold(patches), fold(grads), attn_proj, out_proj, up, down, bias, *rows)


class StripSum:
    def __init__(self, me, post, fsdp_count, held, from_core, buffers):
        self.me, self.post, self.count = me, post, fsdp_count
        self.held, self.from_core = held, from_core
        self.from_y, self.from_z, self.done = buffers
        self.half = from_core.shape[0] // fsdp_count // 2

    def from_sibling(self, src):
        self.core_copy = self.post.send(src, self.from_core, self.me.core)

    def add_sibling(self):
        self.post.got(self.core_copy)
        half = self.half

        def step(j, carried):
            rows = ds(j * half, half)
            self.held[rows, :] = (self.held[rows, :].astype(f32) + self.from_core[rows, :].astype(f32)).astype(bf16)
            return carried

        lax.fori_loop(0, 2 * self.count, step, 0)

    def strip(self, g, side):
        return ds(self.half * (2 * g + side), self.half)

    def over_y(self):
        me = self.me
        self.y_copies = [
            self.post.send(self.held.at[self.strip(g, 1 - me.c)], self.from_y.at[g], me.yp)
            for g in range(self.count)
        ]

    def over_z(self):
        me = self.me
        for copy in self.y_copies:
            self.post.got(copy)

        def step(g, carried):
            rows = self.strip(g, me.c)
            self.held[rows, :] = (self.held[rows, :].astype(f32) + self.from_y[g].astype(f32)).astype(bf16)
            return carried

        lax.fori_loop(0, self.count, step, 0)
        self.z_copies = [
            self.post.send(self.held.at[self.strip((me.f + i + 1) % self.count, me.c)], self.from_z.at[i], device)
            for i, device in enumerate(me.z)
        ]

    def finish(self):
        me = self.me
        for copy in self.z_copies:
            self.post.got(copy)
        total = self.held[self.strip(me.f, me.c), :].astype(f32)
        for i in range(self.count - 1):
            total = total + self.from_z[i].astype(f32)
        self.done[me.c] = total.astype(bf16)
        self.last = self.post.send(self.done.at[me.c], self.done.at[me.c], me.yp)

    def value(self):
        self.post.got(self.last)
        return self.done[...].reshape(2 * self.half, -1).astype(f32)


def second_kernel(
    fsdp_count, where, q_in, k_in, v_in, kt_in, att_in, low_in, x_in, wh_in, g_up, g_down,
    lse, da, middle_grad, mlp_own, mlp_send, g_out_own, g_out_send, mid_stats, up_stats, gain1,
    result, patch_grad, grad_attn, grad_out, grad_up, grad_down, all_total, part_total,
    q, k, v, kt, attended, low_own, x_own, wh, up_own, down_own,
    delta, st, dpt, pt, dst, dk_acc, dv_acc, dq_t, dq, trunk, trunk_own, trunk_far, trunk_send, trunk_y, dkv_own,
    mlp_x, first_send, first_x, rows_out, out_core, out_sum, out_x, packed,
    from_core, from_y, from_z, done, result_stage, patch_stage, stat_buf, stat_in, stat_z, local, stage_sem, ss, rs,
):
    me = Here(fsdp_count)
    f, c, x, core = me.f, me.c, me.x, me.k
    s = 2 * c + core
    pair = 2 * BLOCK
    units = HALF // UNIT
    width = x_in.shape[1]
    shard = width
    mine, far = HALF * x, HALF * (1 - x)
    here_rows, far_rows = ds(mine, HALF), ds(far, HALF)
    loads = []
    own_lanes, sibling_lanes = pl.ds(pl.multiple_of(shard * core, 128), shard), pl.ds(
        pl.multiple_of(shard * (1 - core), 128), shard
    )
    for src, held in (
        (k_in, k), (q_in, q), (v_in, v), (att_in, attended), (kt_in, kt),
        (g_up.at[:, own_lanes], up_own), (g_down.at[:, own_lanes], down_own),
        (low_in, low_own), (x_in, x_own), (wh_in.at[pl.ds(0, 3)], wh),
    ):
        copy = pltpu.make_async_copy(src, held, local.at[len(loads)])
        copy.start()
        loads.append(copy)
    greet([me.core, me.xp, me.yp] + me.z)
    post = Post(ss, rs)
    mlp_copy = post.send(mlp_send, mlp_x, me.xp)
    sums = [
        StripSum(me, post, fsdp_count, held, from_core.at[i], (from_y.at[i], from_z.at[i], done.at[i]))
        for i, held in enumerate((up_own, down_own, packed.at[core]))
    ]
    sums[0].from_sibling(g_up.at[:, sibling_lanes])
    sums[1].from_sibling(g_down.at[:, sibling_lanes])
    slab_own = pl.ds(pl.multiple_of(128 * core, 128), 128)
    slab_sibling = pl.ds(pl.multiple_of(128 * (1 - core), 128), 128)
    slab_both = pl.ds(256, 128)
    out_copies = []
    for i, src in enumerate((g_out_own, g_out_send)):
        for j, lanes in enumerate((slab_sibling, slab_both)):
            out_copies.append(post.send(src.at[:, lanes], out_core.at[i, j], me.core))
    for copy in loads[:5]:
        copy.wait()
    product = (da[...].astype(f32) * attended[...].astype(f32)).T
    for h in range(6):
        delta[h : h + 1, :] = jnp.sum(product[h * HEAD_DIM : (h + 1) * HEAD_DIM], axis=0, keepdims=True)
    lane = lax.broadcasted_iota(jnp.int32, (OWN, 128), 1) // HEAD_DIM

    def head(h, carried):
        slab, part = h // 2, h % 2
        lanes = pl.ds(pl.multiple_of(slab * 128, 128), 128)
        q_slab, da_slab = q[:, lanes], da[:, lanes]
        q_part = jnp.where(lane == part, q_slab, jnp.zeros_like(q_slab))
        da_part = jnp.where(lane == part, da_slab, jnp.zeros_like(da_slab))
        st[0:TRUNK, :] = dot_nt(k[0:TRUNK, lanes], q_part)
        dpt[0:TRUNK, :] = dot_nt(v[0:TRUNK, lanes], da_part)
        for q_row, k_row, count in PIECES:
            cols, rows = slice(q_row, q_row + BLOCK), slice(TRUNK, TRUNK + count)
            st[rows, cols] = dot_nt(k[k_row : k_row + count, lanes], q_part[q_row : q_row + BLOCK])
            dpt[rows, cols] = dot_nt(v[k_row : k_row + count, lanes], da_part[q_row : q_row + BLOCK])
        log_total, row_delta = lse[pl.ds(h, 1), :], delta[pl.ds(h, 1), :]
        for j in range(OWN // BLOCK):
            cols = slice(j * BLOCK, (j + 1) * BLOCK)
            count = TRUNK + (0 if j < 2 else PIECES[j - 2][2])
            for r in range(0, count, BLOCK):
                weight = jnp.exp(st[r : r + BLOCK, cols] - log_total[:, cols])
                pt[r : r + BLOCK, cols] = weight.astype(bf16)
                dst[r : r + BLOCK, cols] = (
                    weight * (dpt[r : r + BLOCK, cols] - row_delta[:, cols])
                ).astype(bf16)
        dk_acc[0:TRUNK, :] += dot_nn(dst[0:TRUNK, :], q_part)
        dv_acc[0:TRUNK, :] += dot_nn(pt[0:TRUNK, :], da_part)
        head_rows = ds(h * HEAD_DIM, HEAD_DIM)
        dq_t[head_rows, :] = dot_nn(kt[head_rows, 0:TRUNK], dst[0:TRUNK, :])
        for q_row, k_row, count in PIECES:
            cols, rows = slice(q_row, q_row + BLOCK), slice(TRUNK, TRUNK + count)
            own = slice(k_row, k_row + count)
            dk_acc[own, :] += dot_nn(dst[rows, cols], q_part[q_row : q_row + BLOCK])
            dv_acc[own, :] += dot_nn(pt[rows, cols], da_part[q_row : q_row + BLOCK])
            dq_t[head_rows, cols] += dot_nn(kt[head_rows, own], dst[rows, cols])
        return carried

    chip_rows = lambda chip, side: ds(pair * (2 * chip + side), pair)
    trunk_copies, y_copies = [], []

    def slab_heads(slab):
        dk_acc[...] = jnp.zeros_like(dk_acc)
        dv_acc[...] = jnp.zeros_like(dv_acc)
        lax.fori_loop(2 * slab, 2 * slab + 2, head, 0)

    def trunk_out(slab):
        trunk[slab, 0] = dk_acc[0:TRUNK, :].astype(bf16)
        trunk[slab, 1] = dv_acc[0:TRUNK, :].astype(bf16)
        for i, total in enumerate((dk_acc, dv_acc)):
            lanes = slice(384 * i + 128 * slab, 384 * i + 128 * slab + 128)
            dkv_own[pair:, lanes] = total[TRUNK:, :].astype(bf16)
        trunk_copies.append(
            (
                post.send(trunk.at[slab, :, chip_rows(1 - c, 1 - core), :], trunk_far.at[slab], me.core),
                post.send(trunk.at[slab, :, chip_rows(c, 1 - core), :], trunk_own.at[slab], me.core),
            )
        )

    def trunk_over(slab):
        post.got(trunk_copies[slab][0])
        trunk_send[slab] = (
            trunk[slab, :, chip_rows(1 - c, core), :].astype(f32) + trunk_far[slab].astype(f32)
        ).astype(bf16)
        y_copies.append(post.send(trunk_send.at[slab], trunk_y.at[slab], me.yp))

    def trunk_in(slab):
        post.got(trunk_copies[slab][1])
        post.got(y_copies[slab])
        total = (
            trunk[slab, :, chip_rows(c, core), :].astype(f32)
            + trunk_own[slab].astype(f32)
            + trunk_y[slab].astype(f32)
        ).astype(bf16)
        for i in range(2):
            lanes = slice(384 * i + 128 * slab, 384 * i + 128 * slab + 128)
            dkv_own[0:pair, lanes] = total[i]

    slab_heads(0)
    trunk_out(0)
    for copy in loads[5:]:
        copy.wait()
    sums[0].add_sibling()
    sums[0].over_y()
    trunk_over(0)
    slab_heads(1)
    trunk_out(1)
    for copy in out_copies:
        post.got(copy)
    for i, src in enumerate((g_out_own, g_out_send)):
        for j, lanes in enumerate((slab_own, slab_both)):
            out_sum[i, j] = (src[:, lanes].astype(f32) + out_core[i, j].astype(f32)).astype(bf16)
    out_copy = post.send(out_sum.at[1], out_x, me.xp)
    trunk_over(1)
    sums[1].add_sibling()
    slab_heads(2)
    trunk_out(2)
    dq[...] = (dq_t[...].T * HEAD_DIM ** (-0.5)).astype(bf16)
    trunk_over(2)
    sums[0].over_z()
    for slab in range(3):
        trunk_in(slab)

    def first(rows):
        return (
            dot_nt(dq[rows, :], wh[0])
            + dot_nt(dkv_own[rows, 0:384], wh[1])
            + dot_nt(dkv_own[rows, 384:768], wh[2])
        )

    first_send[...] = first(far_rows).astype(bf16)
    first_copy = post.send(first_send, first_x, me.xp)
    sums[1].over_y()
    own_first = first(here_rows)
    post.got(mlp_copy)
    own_units = pl.ds(units * (2 * s + x), units)
    rows_out[0, own_units] = (mlp_own[...] + mlp_x[...].astype(f32)).astype(bf16).reshape(units, UNIT, width)
    post.got(out_copy)
    g_attn = [
        dot_tn(low_own[...], dq[...]),
        dot_tn(low_own[...], dkv_own[:, 0:384]),
        dot_tn(low_own[...], dkv_own[:, 384:768]),
    ]
    tails = []
    for j in (0, 1):
        for i in range(3):
            packed[j, :, 128 * i : 128 * i + 128] = g_attn[i][:, 128 * j : 128 * j + 128].astype(bf16)
        tail = [g[:, 256 + 64 * j : 320 + 64 * j] for g in g_attn]
        packed[j, :, 512:640] = jnp.concatenate(tail[0:2], axis=1).astype(bf16)
        packed[j, :, 640:768] = jnp.concatenate([tail[2], jnp.zeros_like(tail[2])], axis=1).astype(bf16)
    attn_stats = jnp.concatenate(
        [
            jnp.sum(dq[...].astype(f32), axis=0, keepdims=True),
            jnp.sum(dkv_own[:, 384:768].astype(f32), axis=0, keepdims=True),
        ],
        axis=1,
    )
    sums[2].from_sibling(packed.at[1 - core])
    sums[2].add_sibling()
    packed[core, :, 384:512] = (out_sum[0, 0].astype(f32) + out_x[0].astype(f32)).astype(bf16)
    last = out_sum[0, 1].astype(f32) + out_x[1].astype(f32)
    side = lax.broadcasted_iota(jnp.int32, last.shape, 1) // HEAD_DIM
    turned = jnp.concatenate([last[:, HEAD_DIM:], last[:, :HEAD_DIM]], axis=1)
    tail = jnp.where(core == 0, turned, last)
    packed[core, :, 640:768] = jnp.where(side == 0, packed[core, :, 640:768].astype(f32), tail).astype(bf16)
    post.got(first_copy)
    first_grad = own_first + first_x[...].astype(f32)
    n1, s1 = row_norm(x_own[here_rows, :].astype(f32))
    grad = middle_grad[...] + norm_back(first_grad, n1, s1, gain1[...])
    rows_out[1, own_units] = grad.astype(bf16).reshape(units, UNIT, width)
    beside = 2 * s + 1 - x
    beyond = 2 * (2 * (1 - c) + core) + x
    corner = 2 * (2 * (1 - c) + core) + 1 - x
    near, over = {}, {}

    def piece(index, owner, start, count):
        return rows_out.at[index, pl.ds(units * owner + start, count)]

    def spread(index):
        own = piece(index, 2 * s + x, 0, units)
        near[index] = (post.send(own, own, me.xp), post.send(own, own, me.yp))
        post.send(own, own, me.core)

    def pass_on(index):
        quarter = units // 2
        post.got(near[index][0])
        part = piece(index, beside, 0, quarter)
        diagonal = [post.send(part, part, me.yp)]
        whole = piece(index, beside, 0, units)
        post.send(whole, whole, me.core)
        post.got(near[index][1])
        part = piece(index, beyond, quarter, units - quarter)
        diagonal.append(post.send(part, part, me.xp))
        whole = piece(index, beyond, 0, units)
        post.send(whole, whole, me.core)
        over[index] = diagonal

    def corner_on(index):
        for copy in over[index]:
            post.got(copy)
        whole = piece(index, corner, 0, units)
        post.send(whole, whole, me.core)

    spread(1)
    rows_mid, rows_up = mid_stats.shape[0], up_stats.shape[0]
    stat_buf[0:1, :] = jnp.sum(first_grad * n1, axis=0, keepdims=True)
    stat_buf[1:2, :] = jnp.sum(first_grad, axis=0, keepdims=True)
    stat_buf[2 : 2 + rows_mid, :] = mid_stats[...]
    stat_buf[2 + rows_mid : 8, :] = jnp.zeros((6 - rows_mid, width), f32)
    stat_buf[8 : 8 + rows_up, :] = up_stats[...]
    stat_buf[8 + rows_up : 9 + rows_up, :] = attn_stats
    stat_buf[9 + rows_up : 16, :] = jnp.zeros((7 - rows_up, width), f32)
    level = lambda i: pl.ds(16 * i, 16)
    stat_copy = post.send(stat_buf.at[level(0)], stat_in.at[0], me.core)
    sums[2].over_y()
    post.got(stat_copy)
    stat_buf[level(1), :] = stat_buf[level(0), :] + stat_in[0]
    stat_copy = post.send(stat_buf.at[level(1)], stat_in.at[1], me.yp)
    sums[1].over_z()
    sums[0].finish()
    pass_on(1)
    spread(0)
    post.got(stat_copy)
    stat_buf[level(2), :] = stat_buf[level(1), :] + stat_in[1]
    stat_copy = post.send(stat_buf.at[level(2)], stat_in.at[2], me.xp)
    sums[2].over_z()
    corner_on(1)
    pass_on(0)
    post.got(stat_copy)
    stat_buf[48:56, :] = stat_buf[32:40, :] + stat_in[2, 0:8]
    stat_buf[56:64, :] = stat_buf[40:48, :]
    stat_z[f] = stat_buf[level(3), :]
    stat_copies = [post.send(stat_buf.at[level(3)], stat_z.at[f], device) for device in me.z]
    sums[1].finish()
    corner_on(0)
    sums[2].finish()
    for copy in stat_copies:
        post.got(copy)
    total = stat_z[0]
    for g in range(1, fsdp_count):
        total = total + stat_z[g]
    all_total[...] = total[0 : 2 + rows_mid]
    part_total[...] = total[8 : 9 + rows_up]
    grad_up[...] = sums[0].value()
    grad_down[...] = sums[1].value().T
    value = sums[2].value()
    tails = [value[:, 512:576], value[:, 576:640], value[:, 640:704], value[:, 704:768]]
    for i in range(3):
        grad_attn[i, :, 0:128] = value[:, 128 * i : 128 * i + 128]
        grad_attn[i, :, 128:192] = tails[i]
    grad_out[...] = jnp.concatenate([value[:, 384:512], tails[3]], axis=1).T
    post.close()
    out = []
    for j in range(result.shape[0] // BLOCK):
        for copy in out[max(0, 2 * j - 4) : max(0, 2 * j - 2)]:
            copy.wait()
        rows = pl.ds(where[j], BLOCK // UNIT)
        result_stage[j % 2] = rows_out[0, rows].reshape(BLOCK, -1)
        patch_stage[j % 2] = rows_out[1, rows].reshape(BLOCK, -1).astype(f32)
        to = pl.ds(j * BLOCK, BLOCK)
        for i, (stage, dest) in enumerate(((result_stage, result), (patch_stage, patch_grad))):
            copy = pltpu.make_async_copy(stage.at[j % 2], dest.at[to], stage_sem.at[i, j % 2])
            copy.start()
            out.append(copy)
    for copy in out[-4:]:
        copy.wait()


def second_half(fsdp_count, where, *operands):
    shape = jax.ShapeDtypeStruct
    vmem = pltpu.VMEM
    width = operands[5].shape[1]
    rows = where.shape[0] * BLOCK
    tall = TRUNK + 2 * BLOCK
    pair = 2 * BLOCK
    deep = width // fsdp_count
    half = deep // 2
    return pl.pallas_call(
        partial(second_kernel, fsdp_count),
        out_shape=(
            shape((rows, width), bf16),
            shape((rows, width), f32),
            shape((3, deep, 192), f32),
            shape((192, deep), f32),
            shape((deep, width), f32),
            shape((width, deep), f32),
            shape((6, width), f32),
            shape((3, width), f32),
        ),
        in_specs=[SMEM] + [ANY] * 10 + [VMEM] * 10,
        out_specs=(ANY,) * 2 + (VMEM,) * 6,
        scratch_shapes=[
            vmem((OWN, 384), bf16),
            vmem((KEYS, 384), bf16),
            vmem((KEYS, 384), bf16),
            vmem((384, KEYS), bf16),
            vmem((OWN, 384), bf16),
            vmem((OWN, width), bf16),
            vmem((OWN, width), bf16),
            vmem((3, width, 384), bf16),
            vmem((width, width), bf16),
            vmem((width, width), bf16),
            vmem((8, OWN), f32),
            vmem((tall, OWN), f32),
            vmem((tall, OWN), f32),
            vmem((tall, OWN), bf16),
            vmem((tall, OWN), bf16),
            vmem((KEYS, 128), f32),
            vmem((KEYS, 128), f32),
            vmem((384, OWN), f32),
            vmem((OWN, 384), bf16),
            vmem((3, 2, TRUNK, 128), bf16),
            vmem((3, 2, pair, 128), bf16),
            vmem((3, 2, pair, 128), bf16),
            vmem((3, 2, pair, 128), bf16),
            vmem((3, 2, pair, 128), bf16),
            vmem((OWN, 768), bf16),
            vmem((HALF, width), bf16),
            vmem((HALF, width), bf16),
            vmem((HALF, width), bf16),
            vmem((2, 2 * rows // UNIT, UNIT, width), bf16),
            vmem((2, 2, width, 128), bf16),
            vmem((2, 2, width, 128), bf16),
            vmem((2, width, 128), bf16),
            vmem((2, width, width), bf16),
            vmem((3, width, width), bf16),
            vmem((3, fsdp_count, half, width), bf16),
            vmem((3, fsdp_count - 1, half, width), bf16),
            vmem((3, 2, half, width), bf16),
            vmem((2, BLOCK, width), bf16),
            vmem((2, BLOCK, width), f32),
            vmem((64, width), f32),
            vmem((3, 16, width), f32),
            vmem((fsdp_count, 16, width), f32),
            pltpu.SemaphoreType.DMA((10,)),
            pltpu.SemaphoreType.DMA((2, 2)),
            pltpu.SemaphoreType.DMA((80,)),
            pltpu.SemaphoreType.DMA((80,)),
        ],
        compiler_params=pltpu.CompilerParams(collective_id=1, has_side_effects=True, vmem_limit_bytes=LIMIT),
        name="second_half",
    )(where, *operands)


def tree_shards(
    fsdp_count, patches, out_grad, block_order, first_gain, first_shift, attn_proj, attn_bias, out_proj, out_bias,
    second_gain, second_shift, up_proj, up_bias, down_proj, down_bias,
):
    row = lambda vector: vector.reshape(1, -1)
    order = block_order[0]
    slots = jnp.arange(order.shape[0], dtype=jnp.int32)
    unit_count = BLOCK // UNIT
    where = unit_count * jnp.sum(
        jnp.where(order[None, :] == slots[:, None], slots[None, :], 0), axis=1, dtype=jnp.int32
    )
    branch, leaf = order - TRUNK_BLK, order - TRUNK_BLK - BRANCHES
    gathered = unit_count * jnp.where(
        order < TRUNK_BLK,
        5 * (order // 2) + order % 2,
        jnp.where(branch < BRANCHES, 5 * branch + 3, 5 * (leaf // 2) + 2 + 2 * (leaf % 2)),
    )
    own = patches.shape[0] // BLOCK
    gathered = lax.dynamic_slice_in_dim(gathered, lax.axis_index("context") * own, own)
    head_width = attn_bias.shape[1]
    bias = jnp.zeros((8, up_bias.shape[0]), f32)
    bias = bias.at[0].set(up_bias).at[1:3, :head_width].set(attn_bias)
    middle = first_half(
        fsdp_count, where, patches, out_grad, attn_proj, out_proj, up_proj, down_proj, bias,
        row(first_gain), row(first_shift), row(second_gain), row(second_shift), row(out_bias), row(down_bias),
    )
    result, patch_grad, grad_attn, grad_out, grad_up, grad_down, all_total, part_total = second_half(
        fsdp_count, gathered, *middle, row(first_gain)
    )
    core = lax.axis_index("tensor") % 2
    up_total = lax.dynamic_index_in_dim(part_total, core, 0, keepdims=False)
    attn_total = part_total[2].reshape(2, 384)
    attn_total = jnp.concatenate(
        [
            lax.dynamic_slice_in_dim(attn_total, core * 128, 128, 1),
            lax.dynamic_slice_in_dim(attn_total, 256 + core * 64, 64, 1),
        ],
        axis=1,
    )
    return (
        result,
        patch_grad,
        all_total[0],
        all_total[1],
        grad_attn,
        attn_total,
        grad_out,
        all_total[5],
        all_total[2],
        all_total[3],
        grad_up,
        up_total,
        grad_down,
        all_total[4],
    )


def solution(mesh):
    fits = mesh.shape["context"] * 2 == BRANCHES and mesh.shape["tensor"] == 4 and mesh.shape["fsdp"] == 4
    body = partial(tree_shards, mesh.shape["fsdp"]) if fits else shards
    return jax.shard_map(
        body,
        mesh=mesh,
        in_specs=(
            P(("fsdp", "context"), None),
            P(("fsdp", "context"), None),
            P("fsdp", None),
            P(),
            P(),
            P(None, "fsdp", "tensor"),
            P(None, "tensor"),
            P("tensor", "fsdp"),
            P(),
            P(),
            P(),
            P("fsdp", "tensor"),
            P("tensor"),
            P("tensor", "fsdp"),
            P(),
        ),
        out_specs=(
            P(("fsdp", "context"), None),
            P(("fsdp", "context"), None),
            P(),
            P(),
            P(None, "fsdp", "tensor"),
            P(None, "tensor"),
            P("tensor", "fsdp"),
            P(),
            P(),
            P(),
            P("fsdp", "tensor"),
            P("tensor"),
            P("tensor", "fsdp"),
            P(),
        ),
        check_vma=False,
    )
```

```python
from functools import partial

import jax
import jax.numpy as jnp
from jax import lax
from jax.experimental import pallas as pl
from jax.experimental.pallas import tpu as pltpu
from jax.sharding import PartitionSpec as P

HEAD_DIM = 64
BLOCK = 128
TRUNK_BLK = 8
BRANCHES = 4
LEAVES = 2
TREE_BLK = 20


epsilon = 1e-05
far_below = -1e30


def layer_norm(values, norm_gain, norm_shift):
    center = values - jnp.mean(values, axis=1, keepdims=True)
    inverse = lax.rsqrt(jnp.mean(center * center, axis=1, keepdims=True) + epsilon)
    normed = center * inverse
    return (normed * norm_gain + norm_shift, normed, inverse)


def norm_back(gradient, normed, inverse, norm_gain):
    scaled = gradient * norm_gain
    return inverse * (
        scaled
        - jnp.mean(scaled, axis=1, keepdims=True)
        - normed * jnp.mean(scaled * normed, axis=1, keepdims=True)
    )


def slot_labels(order_row):
    position = order_row % TREE_BLK
    return (order_row // TREE_BLK, jnp.where(position < TRUNK_BLK, 0, position - TRUNK_BLK + 1))


def spread_rows(values):
    return jnp.broadcast_to(values[:, None], (values.shape[0], BLOCK)).reshape(-1)


def row_labels(labels, first_slot, slot_count):
    return tuple(
        (
            spread_rows(lax.dynamic_slice_in_dim(label_table, first_slot, slot_count))
            for label_table in labels
        )
    )


def visible(query_labels, key_labels):
    query_tree, query_seg = query_labels
    key_tree, key_seg = key_labels
    parent = jnp.where(query_seg > BRANCHES, 1 + (query_seg - BRANCHES - 1) // LEAVES, 0)
    reaches = (
        (key_seg[None, :] == 0)
        | (key_seg[None, :] == query_seg[:, None])
        | (key_seg[None, :] == parent[:, None])
    )
    return (query_tree[:, None] == key_tree[None, :]) & reaches


def head_view(matrix):
    return matrix.reshape(matrix.shape[0], matrix.shape[1] // HEAD_DIM, HEAD_DIM)


def scores_of(query_heads, key_heads):
    return jnp.einsum(
        "qhd,khd->hqk", query_heads, key_heads, preferred_element_type=jnp.float32
    ) * HEAD_DIM ** (-0.5)


def weights_of(scores, log_total, allowed):
    return jnp.where(allowed[None], jnp.exp(scores - log_total[:, :, None]), 0.0)


def score_grads(query_heads, grad_heads, key_heads, value_heads, log_total, row_delta, allowed):
    weights = weights_of(scores_of(query_heads, key_heads), log_total, allowed)
    prob_grad = jnp.einsum(
        "qhd,khd->hqk", grad_heads, value_heads, preferred_element_type=jnp.float32
    )
    return (
        (weights * (prob_grad - row_delta[:, :, None])).astype(jnp.bfloat16),
        weights.astype(jnp.bfloat16),
    )


def shards(
    patches,
    out_grad,
    block_order,
    first_gain,
    first_shift,
    attn_proj,
    attn_bias,
    out_proj,
    out_bias,
    second_gain,
    second_shift,
    up_proj,
    up_bias,
    down_proj,
    down_bias,
):
    attn_full, out_full, up_full, down_full = (
        lax.all_gather(attn_proj, "fsdp", axis=1, tiled=True),
        lax.all_gather(out_proj, "fsdp", axis=1, tiled=True),
        lax.all_gather(up_proj, "fsdp", axis=0, tiled=True),
        lax.all_gather(down_proj, "fsdp", axis=1, tiled=True),
    )
    labels = slot_labels(block_order[0])
    row_count = patches.shape[0]
    own_slots = row_count // BLOCK
    query_labels = row_labels(labels, lax.axis_index("context") * own_slots, own_slots)
    head_width = attn_full.shape[2]
    head_count = head_width // HEAD_DIM
    key_block = 4 * BLOCK
    block_slots = key_block // BLOCK
    score_scale = HEAD_DIM ** (-0.5)
    inputs = patches.astype(jnp.float32)
    first_norm, first_normed, first_inverse = layer_norm(inputs, first_gain, first_shift)
    first_low = first_norm.astype(jnp.bfloat16)
    projected = jnp.einsum("rd,cde->cre", first_low, attn_full, preferred_element_type=jnp.float32)
    queries = (projected[0] + attn_bias[0]).astype(jnp.bfloat16)
    keys_low = projected[1].astype(jnp.bfloat16)
    values_low = (projected[2] + attn_bias[1]).astype(jnp.bfloat16)
    keys_all = lax.all_gather(
        jnp.concatenate([keys_low, values_low], axis=1), "context", axis=0, tiled=True
    )
    block_count = keys_all.shape[0] // key_block
    query_heads = head_view(queries)

    def key_piece(step_index):
        key_slab = lax.dynamic_slice_in_dim(keys_all, step_index * key_block, key_block, 0)
        allowed = visible(query_labels, row_labels(labels, step_index * block_slots, block_slots))
        return (head_view(key_slab[:, :head_width]), head_view(key_slab[:, head_width:]), allowed)

    def total_step(step_index, carried):
        running_top, running_sum = carried
        key_heads, value_heads, allowed = key_piece(step_index)
        masked = jnp.where(allowed[None], scores_of(query_heads, key_heads), far_below)
        new_top = jnp.maximum(running_top, jnp.max(masked, axis=2))
        kept_exp = jnp.where(allowed[None], jnp.exp(masked - new_top[:, :, None]), 0.0)
        return (new_top, running_sum * jnp.exp(running_top - new_top) + jnp.sum(kept_exp, axis=2))

    start_top = jnp.full((head_count, row_count), far_below, jnp.float32)
    running_top, running_sum = lax.fori_loop(
        0, block_count, total_step, (start_top, jnp.zeros((head_count, row_count), jnp.float32))
    )
    log_total = running_top + jnp.log(running_sum)

    def mix_step(step_index, mixed):
        key_heads, value_heads, allowed = key_piece(step_index)
        weights = weights_of(scores_of(query_heads, key_heads), log_total, allowed).astype(
            jnp.bfloat16
        )
        return mixed + jnp.einsum(
            "hqk,khd->qhd", weights, value_heads, preferred_element_type=jnp.float32
        )

    attended = lax.fori_loop(
        0, block_count, mix_step, jnp.zeros((row_count, head_count, HEAD_DIM), jnp.float32)
    )
    attended_low = attended.reshape(row_count, head_width).astype(jnp.bfloat16)
    attn_part = jnp.dot(attended_low, out_full, preferred_element_type=jnp.float32)
    middle = inputs + (lax.psum(attn_part, "tensor") + out_bias)
    second_norm, second_normed, second_inverse = layer_norm(middle, second_gain, second_shift)
    second_low = second_norm.astype(jnp.bfloat16)
    pre_act = jnp.dot(second_low, up_full, preferred_element_type=jnp.float32) + up_bias
    hidden, gelu_back = jax.vjp(partial(jax.nn.gelu, approximate=False), pre_act)
    hidden_low = hidden.astype(jnp.bfloat16)
    mlp_part = jnp.dot(hidden_low, down_full, preferred_element_type=jnp.float32)
    result = (
        middle + (lax.psum(mlp_part.astype(jnp.bfloat16), "tensor").astype(jnp.float32) + down_bias)
    ).astype(jnp.bfloat16)
    top_grad = out_grad.astype(jnp.float32)
    grad_down_bias = jnp.sum(top_grad, axis=0)
    grad_down = jnp.einsum("rf,rd->fd", hidden_low, out_grad, preferred_element_type=jnp.float32)
    hidden_grad = jnp.einsum("rd,fd->rf", out_grad, down_full, preferred_element_type=jnp.float32)
    pre_grad = gelu_back(hidden_grad)[0].astype(jnp.bfloat16)
    grad_up_bias = jnp.sum(pre_grad.astype(jnp.float32), axis=0)
    grad_up = jnp.einsum("rd,rf->df", second_low, pre_grad, preferred_element_type=jnp.float32)
    second_part = jnp.einsum("rf,df->rd", pre_grad, up_full, preferred_element_type=jnp.float32)
    second_grad = lax.psum(second_part, "tensor")
    grad_second_gain = jnp.sum(second_grad * second_normed, axis=0)
    grad_second_shift = jnp.sum(second_grad, axis=0)
    middle_grad = top_grad + norm_back(second_grad, second_normed, second_inverse, second_gain)
    branch_grad = middle_grad.astype(jnp.bfloat16)
    grad_out_bias = jnp.sum(branch_grad.astype(jnp.float32), axis=0)
    grad_out = jnp.einsum(
        "re,rd->ed", attended_low, branch_grad, preferred_element_type=jnp.float32
    )
    attended_grad = jnp.einsum(
        "rd,ed->re", branch_grad, out_full, preferred_element_type=jnp.float32
    ).astype(jnp.bfloat16)
    grad_heads = head_view(attended_grad)

    def delta_step(step_index, row_delta):
        key_heads, value_heads, allowed = key_piece(step_index)
        weights = weights_of(scores_of(query_heads, key_heads), log_total, allowed)
        prob_grad = jnp.einsum(
            "qhd,khd->hqk", grad_heads, value_heads, preferred_element_type=jnp.float32
        )
        return row_delta + jnp.sum(weights * prob_grad, axis=2)

    row_delta = lax.fori_loop(
        0, block_count, delta_step, jnp.zeros((head_count, row_count), jnp.float32)
    )
    query_start = jnp.zeros((row_count, head_count, HEAD_DIM), jnp.float32)

    def back_step(step_index, carried):
        query_acc, key_acc = carried
        key_heads, value_heads, allowed = key_piece(step_index)
        score_low, weights_low = score_grads(
            query_heads, grad_heads, key_heads, value_heads, log_total, row_delta, allowed
        )
        query_acc = query_acc + jnp.einsum(
            "hqk,khd->qhd", score_low, key_heads, preferred_element_type=jnp.float32
        )
        key_part = jnp.einsum(
            "hqk,qhd->khd", score_low, query_heads, preferred_element_type=jnp.float32
        )
        value_part = jnp.einsum(
            "hqk,qhd->khd", weights_low, grad_heads, preferred_element_type=jnp.float32
        )
        joined = jnp.concatenate(
            [key_part.reshape(key_block, head_width), value_part.reshape(key_block, head_width)],
            axis=1,
        )
        return (
            query_acc,
            lax.dynamic_update_slice_in_dim(key_acc, joined, step_index * key_block, 0),
        )

    key_start = jnp.zeros((keys_all.shape[0], 2 * head_width), jnp.float32)
    query_acc, key_acc = lax.fori_loop(0, block_count, back_step, (query_start, key_start))
    key_value_grad = lax.psum_scatter(key_acc, "context", scatter_dimension=0, tiled=True)
    query_grad = (query_acc.reshape(row_count, head_width) * score_scale).astype(jnp.bfloat16)
    key_grad = (key_value_grad[:, :head_width] * score_scale).astype(jnp.bfloat16)
    value_grad = key_value_grad[:, head_width:].astype(jnp.bfloat16)
    stacked = jnp.stack([query_grad, key_grad, value_grad])
    grad_attn_bias = jnp.stack(
        [
            jnp.sum(query_grad.astype(jnp.float32), axis=0),
            jnp.sum(value_grad.astype(jnp.float32), axis=0),
        ]
    )
    grad_attn = jnp.einsum("rd,cre->cde", first_low, stacked, preferred_element_type=jnp.float32)
    first_grad = lax.psum(
        jnp.einsum("cre,cde->rd", stacked, attn_full, preferred_element_type=jnp.float32), "tensor"
    )
    grad_first_gain = jnp.sum(first_grad * first_normed, axis=0)
    grad_first_shift = jnp.sum(first_grad, axis=0)
    patch_grad = middle_grad + norm_back(first_grad, first_normed, first_inverse, first_gain)
    wide_attn, wide_out, wide_up, wide_down = (
        lax.psum_scatter(grad_attn, ("fsdp", "context"), scatter_dimension=1, tiled=True),
        lax.psum_scatter(grad_out, ("fsdp", "context"), scatter_dimension=1, tiled=True),
        lax.psum_scatter(grad_up, ("fsdp", "context"), scatter_dimension=0, tiled=True),
        lax.psum_scatter(grad_down, ("fsdp", "context"), scatter_dimension=1, tiled=True),
    )
    grad_attn, grad_out, grad_up, grad_down = (
        lax.all_gather(wide_attn, "context", axis=1, tiled=True),
        lax.all_gather(wide_out, "context", axis=1, tiled=True),
        lax.all_gather(wide_up, "context", axis=0, tiled=True),
        lax.all_gather(wide_down, "context", axis=1, tiled=True),
    )
    small_grads = lax.psum(
        (
            grad_first_gain,
            grad_first_shift,
            grad_attn_bias,
            grad_out_bias,
            grad_second_gain,
            grad_second_shift,
            grad_up_bias,
            grad_down_bias,
        ),
        ("fsdp", "context"),
    )
    return (
        result,
        patch_grad,
        small_grads[0],
        small_grads[1],
        grad_attn,
        small_grads[2],
        grad_out,
        small_grads[3],
        small_grads[4],
        small_grads[5],
        grad_up,
        small_grads[6],
        grad_down,
        small_grads[7],
    )


bf16 = jnp.bfloat16
f32 = jnp.float32
VMEM = pl.BlockSpec(memory_space=pltpu.VMEM)
SMEM = pl.BlockSpec(memory_space=pltpu.SMEM)
ANY = pl.BlockSpec(memory_space=pl.ANY)
MESH = pl.DeviceIdType.MESH
LIMIT = 60 * 1024 * 1024


def dot_nn(a, b):
    return lax.dot_general(a, b, (((1,), (0,)), ((), ())), preferred_element_type=f32)


def dot_nt(a, b):
    return lax.dot_general(a, b, (((1,), (1,)), ((), ())), preferred_element_type=f32)


def dot_tn(a, b):
    return lax.dot_general(a, b, (((0,), (0,)), ((), ())), preferred_element_type=f32)


class Here:
    def __init__(self, fsdp_count):
        self.f = lax.axis_index("fsdp")
        self.c = lax.axis_index("context")
        self.t = lax.axis_index("tensor")
        self.x = self.t // 2
        self.k = self.t % 2
        self.core = (self.f, self.c, 2 * self.x + 1 - self.k)
        self.xp = (self.f, self.c, 2 * (1 - self.x) + self.k)
        self.yp = (self.f, 1 - self.c, self.t)
        self.z = [((self.f + i) % fsdp_count, self.c, self.t) for i in range(1, fsdp_count)]
        self.back = [(self.f + fsdp_count - i) % fsdp_count for i in range(1, fsdp_count)]


def greet(devices):
    barrier = pltpu.get_barrier_semaphore()
    for device in devices:
        pl.semaphore_signal(barrier, inc=1, device_id=device, device_id_type=MESH)
    pl.semaphore_wait(barrier, len(devices))


class Post:
    def __init__(self, send_sem, recv_sem):
        self.send_sem, self.recv_sem = send_sem, recv_sem
        self.sent, self.open = [], []

    def send(self, src, dst, device):
        index = len(self.sent)
        copy = pltpu.make_async_remote_copy(
            src_ref=src,
            dst_ref=dst,
            send_sem=self.send_sem.at[index],
            recv_sem=self.recv_sem.at[index],
            device_id=device,
            device_id_type=MESH,
        )
        copy.start()
        self.sent.append(copy)
        self.open.append((copy, device))
        return copy

    def got(self, copy):
        copy.wait_recv()
        self.open = [entry for entry in self.open if entry[0] is not copy]

    def got_from(self, device):
        for copy, to in self.open:
            if to is device:
                self.got(copy)

    def close(self):
        for copy, _ in self.open:
            copy.wait_recv()
        for copy in self.sent:
            copy.wait_send()


def ds(start, size, step=16):
    return pl.ds(pl.multiple_of(start, step), size)


TRUNK = TRUNK_BLK * BLOCK
SUB = (1 + LEAVES) * BLOCK
KEYS = TRUNK + SUB
OWN = 2 * BLOCK + SUB
PIECES = (
    (2 * BLOCK, TRUNK, 2 * BLOCK),
    (3 * BLOCK, TRUNK + BLOCK, BLOCK),
    (4 * BLOCK, TRUNK + BLOCK, 2 * BLOCK),
)


def own_places(s):
    return [2 * s, 2 * s + 1, 12 + 2 * s, 8 + s, 13 + 2 * s]


def row_norm(values):
    center = values - jnp.mean(values, axis=1, keepdims=True)
    inverse = lax.rsqrt(jnp.mean(center * center, axis=1, keepdims=True) + epsilon)
    return center * inverse, inverse

HALF = OWN // 2
UNIT = 32


def wide(vector):
    return vector[...].reshape(1, -1)


def first_kernel(
    fsdp_count, order, patches, grads, attn_proj, out_proj, up, d_own, up_bias, attn_bias, gain1, shift1, gain2, shift2, out_bias, down_bias,
    q_out, k_out, v_out, kt_out, att_out, low_out, x_out, wh_out, g_up_out, g_down_out,
    lse, da, middle_grad, mlp_own, mlp_send, g_out_own, g_out_send, stats, up_stats,
    where, a_own, bias, rows_all, grads_all, wa, wh, wo_x, wu, wd, bias_all,
    low, low_own, x_own, g_own, q, k, v, kt, vt, attended, att_t, att_x, st, pt,
    middle, normed, inverse, low2, hidden, pre_grad, second, second_send, second_x, da_send, g_up, g_down,
    local, ss, rs,
):
    me = Here(fsdp_count)
    f, c, x, core, t = me.f, me.c, me.x, me.k, me.t
    s = 2 * c + core
    units = patches.shape[0]
    part = units // 4
    width = patches.shape[2]
    deep = up.shape[0]
    half = deep // 2
    head_width = attn_proj.shape[2]
    early = 640
    own_copies = []

    def keep(src, dst):
        copy = pltpu.make_async_copy(src, dst, local.at[len(own_copies)])
        copy.start()
        own_copies.append(copy)

    keep(patches, rows_all.at[pl.ds(units * c, units)])
    keep(grads, grads_all.at[pl.ds(units * c, units)])
    keep(up, wu.at[core, ds(deep * f, deep)])
    keep(d_own, wd.at[core, ds(deep * f, deep)])
    a_own[:, 0:128] = attn_proj[0, :, 0:128]
    a_own[:, 128:256] = attn_proj[1, :, 0:128]
    a_own[:, 256:384] = attn_proj[2, :, 0:128]
    out_t = out_proj[...].T
    a_own[:, 384:512] = jnp.concatenate([attn_proj[0, :, 128:head_width], attn_proj[1, :, 128:head_width]], axis=1)
    a_own[:, 512:640] = jnp.concatenate([attn_proj[2, :, 128:head_width], out_t[:, 128:head_width]], axis=1)
    a_own[:, 640:768] = out_t[:, 0:128]
    bias[...] = jnp.zeros_like(bias)
    bias[0:1, :] = wide(up_bias)
    bias[1:3, 0:head_width] = attn_bias[...]
    greet([me.core, me.xp, me.yp] + me.z)
    post = Post(ss, rs)
    there = units * (1 - c)
    strip, other_strip = half * c, half * (1 - c)

    def quarter(array, index, piece, count=2):
        size = part // count
        return array.at[pl.ds(there + part * index + size * piece, size)]

    def to_y(src, dst, piece, count=2):
        size = part // count
        return post.send(
            src.at[pl.ds(part * t + size * piece, size)],
            dst.at[pl.ds(units * c + part * t + size * piece, size)],
            me.yp,
        )

    def relay(piece, device):
        return post.send(piece, piece, device)

    a_dst = lambda shard, row, lanes: wa.at[shard, ds(row, half), lanes]
    lo, hi = pl.ds(0, early), pl.ds(early, width - early)
    patches_y = [to_y(patches, rows_all, i) for i in range(2)]
    a1_z = [
        post.send(a_own.at[ds(strip, half), lo], a_dst(core, deep * f + strip, lo), device) for device in me.z
    ]
    a_core = post.send(a_own, wa.at[core, ds(deep * f, deep)], me.core)
    bias_core = post.send(bias, bias_all.at[core], me.core)
    u_core = post.send(up, wu.at[core, ds(deep * f, deep)], me.core)
    slots = order.shape[1]

    def find(place, carried):
        slot = jnp.int32(0)
        for j in range(slots):
            slot = jnp.where(order[0, j] == place, j, slot)
        where[place] = slot * (BLOCK // UNIT)
        return carried

    lax.fori_loop(0, slots, find, 0)
    wa[core, ds(deep * f, deep), :] = a_own[...]
    bias_all[core] = bias[...]
    d_core = post.send(d_own, wd.at[core, ds(deep * f, deep)], me.core)
    patches_x = []
    for i in range(2):
        post.got(patches_y[i])
        patches_x.append(relay(quarter(rows_all, t, i), me.xp))
        relay(quarter(rows_all, t, i), me.core)
    a1_y = []
    for copy, source in zip(a1_z, me.back):
        post.got(copy)
        piece = a_dst(core, deep * source + strip, lo)
        a1_y.append(relay(piece, me.yp))
        relay(piece, me.core)
    a2_z = [
        post.send(a_own.at[ds(strip, half), hi], a_dst(core, deep * f + strip, hi), device) for device in me.z
    ]
    u_z = [
        post.send(up.at[ds(strip, half)], wu.at[core, ds(deep * f + strip, half)], device) for device in me.z
    ]
    over = (t + 2) % 4
    for i in range(2):
        post.got(patches_x[i])
        relay(quarter(rows_all, over, i), me.core)
    post.got_from(me.core)
    own_copies[0].wait()

    gain_row, shift_row = wide(gain1), wide(shift1)

    def block_of(array, place):
        return array[pl.ds(where[place], BLOCK // UNIT)].reshape(BLOCK, width)

    def norm_block(place, row):
        normed_rows, _ = row_norm(block_of(rows_all, place).astype(f32))
        low[ds(row, BLOCK), :] = (normed_rows * gain_row + shift_row).astype(bf16)

    def trunk_step(j, carried):
        norm_block(j, j * BLOCK)
        return carried

    lax.fori_loop(0, TRUNK_BLK, trunk_step, 0)
    places = own_places(s)
    for j in range(2, 5):
        norm_block(places[j], TRUNK + (j - 2) * BLOCK)
    for j, place in enumerate(places):
        x_own[pl.ds(j * BLOCK, BLOCK), :] = block_of(rows_all, place)
    low_own[0 : 2 * BLOCK, :] = low[ds(2 * BLOCK * s, 2 * BLOCK), :]
    low_own[2 * BLOCK :, :] = low[TRUNK:, :]
    for copy, source in zip(a1_y, me.back):
        post.got(copy)
        relay(a_dst(core, deep * source + other_strip, lo), me.core)
    grads_y = [to_y(grads, grads_all, i) for i in range(2)]
    post.got_from(me.core)

    def assemble(i):
        slab = (0, 1, 2, 5)[i]
        wh[i, :, 0:128] = wa[0, :, 128 * slab : 128 * slab + 128]
        wh[i, :, 128:256] = wa[1, :, 128 * slab : 128 * slab + 128]
        start = 384 + 64 * i
        wh[i, :, 256:384] = jnp.concatenate(
            [wa[0, :, start : start + 64], wa[1, :, start : start + 64]], axis=1
        )

    for i in range(3):
        assemble(i)

    def heads_row(row):
        a, b = bias_all[0, row : row + 1, :], bias_all[1, row : row + 1, :]
        return jnp.concatenate([a[:, 0:128], b[:, 0:128], a[:, 128:192], b[:, 128:192]], axis=1)

    q[...] = ((dot_nn(low_own[...], wh[0]) + heads_row(1)).astype(bf16) * HEAD_DIM ** (-0.5)).astype(bf16)
    value_bias = heads_row(2)

    def project(j, carried):
        rows = ds(j * (KEYS // 2), KEYS // 2)
        k[rows, :] = dot_nn(low[rows, :], wh[1]).astype(bf16)
        v[rows, :] = (dot_nn(low[rows, :], wh[2]) + value_bias).astype(bf16)
        return carried

    lax.fori_loop(0, 2, project, 0)
    kt[...] = k[...].T
    vt[...] = v[...].T
    for src, dst in ((q, q_out), (k, k_out), (v, v_out), (kt, kt_out), (low_own, low_out), (x_own, x_out)):
        keep(src, dst)
    lane = lax.broadcasted_iota(jnp.int32, (OWN, 128), 1) // HEAD_DIM

    def head(h, carried):
        slab, side = h // 2, h % 2
        lanes = pl.ds(pl.multiple_of(slab * 128, 128), 128)
        own_q = q[:, lanes]
        q_part = jnp.where(lane == side, own_q, jnp.zeros_like(own_q))
        st[0:TRUNK, :] = dot_nt(k[0:TRUNK, lanes], q_part)
        for q_row, k_row, count in PIECES:
            st[TRUNK : TRUNK + count, q_row : q_row + BLOCK] = dot_nt(
                k[k_row : k_row + count, lanes], q_part[q_row : q_row + BLOCK]
            )
        tops, sums = [], []
        for j in range(OWN // BLOCK):
            cols = slice(j * BLOCK, (j + 1) * BLOCK)
            count = TRUNK + (0 if j < 2 else PIECES[j - 2][2])
            top = jnp.full((8, BLOCK), far_below, f32)
            for r in range(0, count, BLOCK):
                piece = st[r : r + BLOCK, cols].reshape(BLOCK // 8, 8, BLOCK)
                top = jnp.maximum(top, jnp.max(piece, axis=0))
            top = jnp.max(top, axis=0, keepdims=True)
            total = jnp.zeros((8, BLOCK), f32)
            for r in range(0, count, BLOCK):
                weight = jnp.exp(st[r : r + BLOCK, cols] - top)
                total = total + jnp.sum(weight.reshape(BLOCK // 8, 8, BLOCK), axis=0)
                pt[r : r + BLOCK, cols] = weight.astype(bf16)
            tops.append(top)
            sums.append(jnp.sum(total, axis=0, keepdims=True))
        total = jnp.concatenate(sums, axis=1)
        head_rows = ds(h * HEAD_DIM, HEAD_DIM)
        att_t[head_rows, :] = dot_nn(vt[head_rows, 0:TRUNK], pt[0:TRUNK, :])
        for q_row, k_row, count in PIECES:
            cols = slice(q_row, q_row + BLOCK)
            att_t[head_rows, cols] += dot_nn(
                vt[head_rows, k_row : k_row + count], pt[TRUNK : TRUNK + count, cols]
            )
        att_t[head_rows, :] = att_t[head_rows, :] / total
        lse[pl.ds(h, 1), :] = jnp.concatenate(tops, axis=1) + jnp.log(total)
        return carried

    lax.fori_loop(0, 2, head, 0)
    a2_y, u_y, grads_x = [], [], []
    for copy, source in zip(a2_z, me.back):
        post.got(copy)
        piece = a_dst(core, deep * source + strip, hi)
        a2_y.append(relay(piece, me.yp))
        relay(piece, me.core)
    post.got(grads_y[0])
    grads_x.append(relay(quarter(grads_all, t, 0), me.xp))
    relay(quarter(grads_all, t, 0), me.core)
    for copy, source in zip(u_z, me.back):
        post.got(copy)
        piece = wu.at[core, ds(deep * source + strip, half)]
        u_y.append(relay(piece, me.yp))
        relay(piece, me.core)
    d_z = [
        post.send(d_own.at[ds(strip, half)], wd.at[core, ds(deep * f + strip, half)], device) for device in me.z
    ]
    lax.fori_loop(2, 4, head, 0)
    post.got(grads_y[1])
    grads_x.append(relay(quarter(grads_all, t, 1), me.xp))
    relay(quarter(grads_all, t, 1), me.core)
    for copy, source in zip(a2_y, me.back):
        post.got(copy)
        relay(a_dst(core, deep * source + other_strip, hi), me.core)
    lax.fori_loop(4, 6, head, 0)
    attended[...] = att_t[...].T.astype(bf16)
    mine, far = HALF * x, HALF * (1 - x)
    here_rows, far_rows = ds(mine, HALF), ds(far, HALF)
    att_copy = post.send(attended.at[far_rows], att_x, me.xp)
    keep(attended, att_out)
    post.got_from(me.core)
    assemble(3)
    keep(wh, wh_out)
    wo_rows = ds(width // 2 * core, width // 2)
    wo_copy = post.send(wh.at[3, wo_rows], wo_x.at[wo_rows], me.xp)
    middle[...] = (
        x_own[here_rows, :].astype(f32) + wide(out_bias) + dot_nt(attended[here_rows, :], wh[3])
    )
    d_y = []
    for copy, source in zip(d_z, me.back):
        post.got(copy)
        piece = wd.at[core, ds(deep * source + strip, half)]
        d_y.append(relay(piece, me.yp))
        relay(piece, me.core)
    post.got(wo_copy)
    relay(wo_x.at[wo_rows], me.core)
    for i in range(2):
        post.got(grads_x[i])
        relay(quarter(grads_all, over, i), me.core)
    post.got_from(me.core)
    post.got(att_copy)
    middle[...] += dot_nt(att_x[...], wo_x[...])
    n2, s2 = row_norm(middle[...])
    normed[...] = n2
    inverse[...] = s2
    low2[here_rows, :] = (n2 * wide(gain2) + wide(shift2)).astype(bf16)
    low_copy = post.send(low2.at[here_rows], low2.at[here_rows], me.xp)
    own_copies[1].wait()
    for j, place in enumerate(places):
        g_own[pl.ds(j * BLOCK, BLOCK), :] = block_of(grads_all, place)
    for copy, source in zip(u_y, me.back):
        post.got(copy)
        relay(wu.at[core, ds(deep * source + other_strip, half)], me.core)
    for copy, source in zip(d_y, me.back):
        post.got(copy)
        relay(wd.at[core, ds(deep * source + other_strip, half)], me.core)
    post.got_from(me.core)
    own_copies[2].wait()
    own_copies[3].wait()
    tile = 256

    def feed(rows):
        second[rows, :] = jnp.zeros((HALF, width), f32)

        def step(j, carried):
            shard, lanes = j // 3, pl.ds(pl.multiple_of(j % 3 * tile, 128), tile)
            out = pl.ds(pl.multiple_of(j * tile, 128), tile)
            pre = dot_nn(low2[rows, :], wu[shard, :, lanes]) + bias_all[shard, 0:1, lanes]
            below = 0.5 * (1.0 + lax.erf(pre * (2.0**-0.5)))
            density = jnp.exp(-0.5 * pre * pre) * (2.0 * jnp.pi) ** -0.5
            hidden[rows, out] = (pre * below).astype(bf16)
            back = dot_nn(g_own[rows, :], wd[shard, :, lanes])
            low_back = (back * (below + pre * density)).astype(bf16)
            pre_grad[rows, out] = low_back
            second[rows, :] += dot_nt(low_back, wu[shard, :, lanes])
            return carried

        lax.fori_loop(0, 6, step, 0)

    def mlp(rows):
        return dot_nt(hidden[rows, 0:width], wd[0]) + dot_nt(hidden[rows, width:], wd[1])

    feed(here_rows)
    post.got(low_copy)
    feed(far_rows)
    second_send[...] = second[far_rows, :].astype(bf16)
    second_copy = post.send(second_send, second_x, me.xp)

    def weight_step(j, carried):
        lanes = pl.ds(pl.multiple_of(j * tile, 128), tile)
        g_up[:, lanes] = dot_tn(low2[...], pre_grad[:, lanes]).astype(bf16)
        g_down[:, lanes] = dot_tn(g_own[...], hidden[:, lanes]).astype(bf16)
        return carried

    lax.fori_loop(0, 6, weight_step, 0)
    keep(g_up, g_up_out)
    keep(g_down, g_down_out)
    up_stats[0:1, :] = jnp.sum(pre_grad[:, 0:width].astype(f32), axis=0, keepdims=True)
    up_stats[1:2, :] = jnp.sum(pre_grad[:, width:].astype(f32), axis=0, keepdims=True)
    mlp_send[...] = mlp(far_rows).astype(bf16)
    mlp_own[...] = middle[...] + mlp(here_rows) + wide(down_bias)
    dy = g_own[here_rows, :].astype(f32)
    stats[2:3, :] = jnp.sum(dy, axis=0, keepdims=True)
    post.got(second_copy)
    second_grad = second[here_rows, :] + second_x[...].astype(f32)
    n2 = normed[...]
    stats[0:1, :] = jnp.sum(second_grad * n2, axis=0, keepdims=True)
    stats[1:2, :] = jnp.sum(second_grad, axis=0, keepdims=True)
    grad = dy + norm_back(second_grad, n2, inverse[...], wide(gain2))
    middle_grad[...] = grad
    branch = grad.astype(bf16)
    da_send[...] = dot_nn(branch, wo_x[...]).astype(bf16)
    post.send(da_send, da.at[here_rows], me.xp)
    stats[3:4, :] = jnp.sum(branch.astype(f32), axis=0, keepdims=True)
    da[here_rows, :] = dot_nn(branch, wh[3]).astype(bf16)
    g_out_send[...] = dot_tn(branch, att_x[...]).astype(bf16)
    g_out_own[...] = dot_tn(branch, attended[here_rows, :]).astype(bf16)
    post.close()
    for copy in own_copies[4:]:
        copy.wait()


def first_half(fsdp_count, order, patches, grads, attn_proj, out_proj, up, down_t, *vectors):
    width = patches.shape[1]
    shape = jax.ShapeDtypeStruct
    vmem = pltpu.VMEM
    units = 2 * up.shape[1]
    all_units = 2 * patches.shape[0] // UNIT
    deep = up.shape[0]
    fold = lambda a: a.reshape(-1, UNIT, width)
    return pl.pallas_call(
        partial(first_kernel, fsdp_count),
        out_shape=(
            shape((OWN, 384), bf16),
            shape((KEYS, 384), bf16),
            shape((KEYS, 384), bf16),
            shape((384, KEYS), bf16),
            shape((OWN, 384), bf16),
            shape((OWN, width), bf16),
            shape((OWN, width), bf16),
            shape((4, width, 384), bf16),
            shape((width, units), bf16),
            shape((width, units), bf16),
            shape((8, OWN), f32),
            shape((OWN, 384), bf16),
            shape((HALF, width), f32),
            shape((HALF, width), f32),
            shape((HALF, width), bf16),
            shape((width, 384), bf16),
            shape((width, 384), bf16),
            shape((4, width), f32),
            shape((2, width), f32),
        ),
        in_specs=[SMEM, ANY, ANY, VMEM, VMEM, ANY, ANY] + [VMEM] * 8,
        out_specs=(ANY,) * 10 + (VMEM,) * 9,
        scratch_shapes=[
            pltpu.SMEM(order.shape[1:], jnp.int32),
            vmem((deep, width), bf16),
            vmem((8, width), f32),
            vmem((all_units, UNIT, width), bf16),
            vmem((all_units, UNIT, width), bf16),
            vmem((2, width, width), bf16),
            vmem((4, width, 384), bf16),
            vmem((width, 384), bf16),
            vmem((2, width, up.shape[1]), bf16),
            vmem((2, width, up.shape[1]), bf16),
            vmem((2, 8, width), f32),
            vmem((KEYS, width), bf16),
            vmem((OWN, width), bf16),
            vmem((OWN, width), bf16),
            vmem((OWN, width), bf16),
            vmem((OWN, 384), bf16),
            vmem((KEYS, 384), bf16),
            vmem((KEYS, 384), bf16),
            vmem((384, KEYS), bf16),
            vmem((384, KEYS), bf16),
            vmem((OWN, 384), bf16),
            vmem((384, OWN), f32),
            vmem((HALF, 384), bf16),
            vmem((TRUNK + 2 * BLOCK, OWN), f32),
            vmem((TRUNK + 2 * BLOCK, OWN), bf16),
            vmem((HALF, width), f32),
            vmem((HALF, width), f32),
            vmem((HALF, 1), f32),
            vmem((OWN, width), bf16),
            vmem((OWN, units), bf16),
            vmem((OWN, units), bf16),
            vmem((OWN, width), f32),
            vmem((HALF, width), bf16),
            vmem((HALF, width), bf16),
            vmem((HALF, 384), bf16),
            vmem((width, units), bf16),
            vmem((width, units), bf16),
            pltpu.SemaphoreType.DMA((16,)),
            pltpu.SemaphoreType.DMA((80,)),
            pltpu.SemaphoreType.DMA((80,)),
        ],
        compiler_params=pltpu.CompilerParams(collective_id=0, has_side_effects=True, vmem_limit_bytes=LIMIT),
        name="first_half",
    )(order, fold(patches), fold(grads), attn_proj, out_proj, up, down_t, *vectors)


class StripSum:
    def __init__(self, me, post, fsdp_count, held, from_core, buffers):
        self.me, self.post, self.count = me, post, fsdp_count
        self.held, self.from_core = held, from_core
        self.from_y, self.from_z, self.done = buffers
        self.half = from_core.shape[0] // fsdp_count // 2

    def from_sibling(self, src):
        self.core_copy = self.post.send(src, self.from_core, self.me.core)

    def add_sibling(self):
        self.post.got(self.core_copy)
        half = self.half

        def step(j, carried):
            rows = ds(j * half, half)
            self.held[rows, :] = (self.held[rows, :].astype(f32) + self.from_core[rows, :].astype(f32)).astype(bf16)
            return carried

        lax.fori_loop(0, 2 * self.count, step, 0)

    def strip(self, g, side):
        return ds(self.half * (2 * g + side), self.half)

    def over_y(self):
        me = self.me
        self.y_copies = [
            self.post.send(self.held.at[self.strip(g, 1 - me.c)], self.from_y.at[g], me.yp)
            for g in range(self.count)
        ]

    def over_z(self):
        me = self.me
        for copy in self.y_copies:
            self.post.got(copy)

        def step(g, carried):
            rows = self.strip(g, me.c)
            self.held[rows, :] = (self.held[rows, :].astype(f32) + self.from_y[g].astype(f32)).astype(bf16)
            return carried

        lax.fori_loop(0, self.count, step, 0)
        self.z_copies = [
            self.post.send(self.held.at[self.strip((me.f + i + 1) % self.count, me.c)], self.from_z.at[i], device)
            for i, device in enumerate(me.z)
        ]

    def finish(self):
        me = self.me
        for copy in self.z_copies:
            self.post.got(copy)
        total = self.held[self.strip(me.f, me.c), :].astype(f32)
        for i in range(self.count - 1):
            total = total + self.from_z[i].astype(f32)
        self.done[me.c] = total.astype(bf16)
        self.last = self.post.send(self.done.at[me.c], self.done.at[me.c], me.yp)


def second_kernel(
    fsdp_count, q_in, k_in, v_in, kt_in, att_in, low_in, x_in, wh_in, g_up, g_down,
    lse, da, middle_grad, mlp_own, mlp_send, g_out_own, g_out_send, mid_stats, up_stats, gain1,
    rows_out, grads_out, all_total, part_total,
    q, k, v, kt, attended, low_own, x_own, wh, up_own, down_own,
    delta, st, dpt, pt, dst, dk_acc, dv_acc, dq_t, dq, trunk, trunk_own, trunk_far, trunk_send, trunk_y, dkv_own,
    mlp_x, first_send, first_x, rows_own, out_core, out_sum, out_x, packed,
    from_core, from_y, from_z, done, stat_buf, stat_in, stat_z, local, ss, rs,
):
    me = Here(fsdp_count)
    f, c, x, core = me.f, me.c, me.x, me.k
    s = 2 * c + core
    pair = 2 * BLOCK
    units = HALF // UNIT
    width = x_in.shape[1]
    shard = width
    mine, far = HALF * x, HALF * (1 - x)
    here_rows, far_rows = ds(mine, HALF), ds(far, HALF)
    loads = []
    own_lanes, sibling_lanes = pl.ds(pl.multiple_of(shard * core, 128), shard), pl.ds(
        pl.multiple_of(shard * (1 - core), 128), shard
    )
    for src, held in (
        (k_in, k), (q_in, q), (v_in, v), (att_in, attended), (kt_in, kt),
        (g_up.at[:, own_lanes], up_own), (g_down.at[:, own_lanes], down_own),
        (low_in, low_own), (x_in, x_own), (wh_in.at[pl.ds(0, 3)], wh),
    ):
        copy = pltpu.make_async_copy(src, held, local.at[len(loads)])
        copy.start()
        loads.append(copy)
    greet([me.core, me.xp, me.yp] + me.z)
    post = Post(ss, rs)
    mlp_copy = post.send(mlp_send, mlp_x, me.xp)
    sums = [
        StripSum(me, post, fsdp_count, held, from_core.at[i], (from_y.at[i], from_z.at[i], done.at[i]))
        for i, held in enumerate((up_own, down_own, packed.at[core]))
    ]
    sums[0].from_sibling(g_up.at[:, sibling_lanes])
    sums[1].from_sibling(g_down.at[:, sibling_lanes])
    slab_own = pl.ds(pl.multiple_of(128 * core, 128), 128)
    slab_sibling = pl.ds(pl.multiple_of(128 * (1 - core), 128), 128)
    slab_both = pl.ds(256, 128)
    out_copies = []
    for i, src in enumerate((g_out_own, g_out_send)):
        for j, lanes in enumerate((slab_sibling, slab_both)):
            out_copies.append(post.send(src.at[:, lanes], out_core.at[i, j], me.core))
    for copy in loads[:5]:
        copy.wait()
    product = (da[...].astype(f32) * attended[...].astype(f32)).T
    for h in range(6):
        delta[h : h + 1, :] = jnp.sum(product[h * HEAD_DIM : (h + 1) * HEAD_DIM], axis=0, keepdims=True)
    lane = lax.broadcasted_iota(jnp.int32, (OWN, 128), 1) // HEAD_DIM

    def head(h, carried):
        slab, part = h // 2, h % 2
        lanes = pl.ds(pl.multiple_of(slab * 128, 128), 128)
        q_slab, da_slab = q[:, lanes], da[:, lanes]
        q_part = jnp.where(lane == part, q_slab, jnp.zeros_like(q_slab))
        da_part = jnp.where(lane == part, da_slab, jnp.zeros_like(da_slab))
        st[0:TRUNK, :] = dot_nt(k[0:TRUNK, lanes], q_part)
        dpt[0:TRUNK, :] = dot_nt(v[0:TRUNK, lanes], da_part)
        for q_row, k_row, count in PIECES:
            cols, rows = slice(q_row, q_row + BLOCK), slice(TRUNK, TRUNK + count)
            st[rows, cols] = dot_nt(k[k_row : k_row + count, lanes], q_part[q_row : q_row + BLOCK])
            dpt[rows, cols] = dot_nt(v[k_row : k_row + count, lanes], da_part[q_row : q_row + BLOCK])
        log_total, row_delta = lse[pl.ds(h, 1), :], delta[pl.ds(h, 1), :]
        for j in range(OWN // BLOCK):
            cols = slice(j * BLOCK, (j + 1) * BLOCK)
            count = TRUNK + (0 if j < 2 else PIECES[j - 2][2])
            for r in range(0, count, BLOCK):
                weight = jnp.exp(st[r : r + BLOCK, cols] - log_total[:, cols])
                pt[r : r + BLOCK, cols] = weight.astype(bf16)
                dst[r : r + BLOCK, cols] = (
                    weight * (dpt[r : r + BLOCK, cols] - row_delta[:, cols])
                ).astype(bf16)
        dk_acc[0:TRUNK, :] += dot_nn(dst[0:TRUNK, :], q_part)
        dv_acc[0:TRUNK, :] += dot_nn(pt[0:TRUNK, :], da_part)
        head_rows = ds(h * HEAD_DIM, HEAD_DIM)
        dq_t[head_rows, :] = dot_nn(kt[head_rows, 0:TRUNK], dst[0:TRUNK, :])
        for q_row, k_row, count in PIECES:
            cols, rows = slice(q_row, q_row + BLOCK), slice(TRUNK, TRUNK + count)
            own = slice(k_row, k_row + count)
            dk_acc[own, :] += dot_nn(dst[rows, cols], q_part[q_row : q_row + BLOCK])
            dv_acc[own, :] += dot_nn(pt[rows, cols], da_part[q_row : q_row + BLOCK])
            dq_t[head_rows, cols] += dot_nn(kt[head_rows, own], dst[rows, cols])
        return carried

    chip_rows = lambda chip, side: ds(pair * (2 * chip + side), pair)
    trunk_copies, y_copies = [], []

    def slab_heads(slab):
        dk_acc[...] = jnp.zeros_like(dk_acc)
        dv_acc[...] = jnp.zeros_like(dv_acc)
        lax.fori_loop(2 * slab, 2 * slab + 2, head, 0)

    def trunk_out(slab):
        trunk[slab, 0] = dk_acc[0:TRUNK, :].astype(bf16)
        trunk[slab, 1] = dv_acc[0:TRUNK, :].astype(bf16)
        for i, total in enumerate((dk_acc, dv_acc)):
            lanes = slice(384 * i + 128 * slab, 384 * i + 128 * slab + 128)
            dkv_own[pair:, lanes] = total[TRUNK:, :].astype(bf16)
        trunk_copies.append(
            (
                post.send(trunk.at[slab, :, chip_rows(1 - c, 1 - core), :], trunk_far.at[slab], me.core),
                post.send(trunk.at[slab, :, chip_rows(c, 1 - core), :], trunk_own.at[slab], me.core),
            )
        )

    def trunk_over(slab):
        post.got(trunk_copies[slab][0])
        trunk_send[slab] = (
            trunk[slab, :, chip_rows(1 - c, core), :].astype(f32) + trunk_far[slab].astype(f32)
        ).astype(bf16)
        y_copies.append(post.send(trunk_send.at[slab], trunk_y.at[slab], me.yp))

    def trunk_in(slab):
        post.got(trunk_copies[slab][1])
        post.got(y_copies[slab])
        total = (
            trunk[slab, :, chip_rows(c, core), :].astype(f32)
            + trunk_own[slab].astype(f32)
            + trunk_y[slab].astype(f32)
        ).astype(bf16)
        for i in range(2):
            lanes = slice(384 * i + 128 * slab, 384 * i + 128 * slab + 128)
            dkv_own[0:pair, lanes] = total[i]

    slab_heads(0)
    trunk_out(0)
    for copy in loads[5:]:
        copy.wait()
    sums[0].add_sibling()
    sums[0].over_y()
    trunk_over(0)
    slab_heads(1)
    trunk_out(1)
    for copy in out_copies:
        post.got(copy)
    for i, src in enumerate((g_out_own, g_out_send)):
        for j, lanes in enumerate((slab_own, slab_both)):
            out_sum[i, j] = (src[:, lanes].astype(f32) + out_core[i, j].astype(f32)).astype(bf16)
    out_copy = post.send(out_sum.at[1], out_x, me.xp)
    trunk_over(1)
    sums[1].add_sibling()
    slab_heads(2)
    trunk_out(2)
    dq[...] = (dq_t[...].T * HEAD_DIM ** (-0.5)).astype(bf16)
    trunk_over(2)
    sums[0].over_z()
    for slab in range(3):
        trunk_in(slab)

    def first(rows):
        return (
            dot_nt(dq[rows, :], wh[0])
            + dot_nt(dkv_own[rows, 0:384], wh[1])
            + dot_nt(dkv_own[rows, 384:768], wh[2])
        )

    first_send[...] = first(far_rows).astype(bf16)
    first_copy = post.send(first_send, first_x, me.xp)
    sums[1].over_y()
    own_first = first(here_rows)
    post.got(mlp_copy)
    rows_own[0] = (mlp_own[...] + mlp_x[...].astype(f32)).astype(bf16).reshape(units, UNIT, width)
    post.got(out_copy)
    g_attn = [
        dot_tn(low_own[...], dq[...]),
        dot_tn(low_own[...], dkv_own[:, 0:384]),
        dot_tn(low_own[...], dkv_own[:, 384:768]),
    ]
    tails = []
    for j in (0, 1):
        for i in range(3):
            packed[j, :, 128 * i : 128 * i + 128] = g_attn[i][:, 128 * j : 128 * j + 128].astype(bf16)
        tail = [g[:, 256 + 64 * j : 320 + 64 * j] for g in g_attn]
        packed[j, :, 512:640] = jnp.concatenate(tail[0:2], axis=1).astype(bf16)
        packed[j, :, 640:768] = jnp.concatenate([tail[2], jnp.zeros_like(tail[2])], axis=1).astype(bf16)
    attn_stats = jnp.concatenate(
        [
            jnp.sum(dq[...].astype(f32), axis=0, keepdims=True),
            jnp.sum(dkv_own[:, 384:768].astype(f32), axis=0, keepdims=True),
        ],
        axis=1,
    )
    sums[2].from_sibling(packed.at[1 - core])
    sums[2].add_sibling()
    packed[core, :, 384:512] = (out_sum[0, 0].astype(f32) + out_x[0].astype(f32)).astype(bf16)
    last = out_sum[0, 1].astype(f32) + out_x[1].astype(f32)
    side = lax.broadcasted_iota(jnp.int32, last.shape, 1) // HEAD_DIM
    turned = jnp.concatenate([last[:, HEAD_DIM:], last[:, :HEAD_DIM]], axis=1)
    tail = jnp.where(core == 0, turned, last)
    packed[core, :, 640:768] = jnp.where(side == 0, packed[core, :, 640:768].astype(f32), tail).astype(bf16)
    post.got(first_copy)
    first_grad = own_first + first_x[...].astype(f32)
    n1, s1 = row_norm(x_own[here_rows, :].astype(f32))
    grad = middle_grad[...] + norm_back(first_grad, n1, s1, wide(gain1))
    rows_own[1] = grad.astype(bf16).reshape(units, UNIT, width)
    beside = 2 * s + 1 - x
    beyond = 2 * (2 * (1 - c) + core) + x
    corner = 2 * (2 * (1 - c) + core) + 1 - x
    near, over = {}, {}

    def piece(index, owner, start, count):
        return rows_out.at[index, pl.ds(units * owner + start, count)]

    def spread(index):
        own, there = rows_own.at[index], piece(index, 2 * s + x, 0, units)
        near[index] = (post.send(own, there, me.xp), post.send(own, there, me.yp))
        post.send(own, there, me.core)
        copy = pltpu.make_async_copy(own, there, local.at[len(loads)])
        copy.start()
        loads.append(copy)

    def pass_on(index):
        quarter = units // 2
        post.got(near[index][0])
        part = piece(index, beside, 0, quarter)
        diagonal = [post.send(part, part, me.yp)]
        whole = piece(index, beside, 0, units)
        post.send(whole, whole, me.core)
        post.got(near[index][1])
        part = piece(index, beyond, quarter, units - quarter)
        diagonal.append(post.send(part, part, me.xp))
        whole = piece(index, beyond, 0, units)
        post.send(whole, whole, me.core)
        over[index] = diagonal

    def corner_on(index):
        for copy in over[index]:
            post.got(copy)
        whole = piece(index, corner, 0, units)
        post.send(whole, whole, me.core)

    spread(1)
    rows_mid, rows_up = mid_stats.shape[0], up_stats.shape[0]
    stat_buf[0:1, :] = jnp.sum(first_grad * n1, axis=0, keepdims=True)
    stat_buf[1:2, :] = jnp.sum(first_grad, axis=0, keepdims=True)
    stat_buf[2 : 2 + rows_mid, :] = mid_stats[...]
    stat_buf[2 + rows_mid : 8, :] = jnp.zeros((6 - rows_mid, width), f32)
    stat_buf[8 : 8 + rows_up, :] = up_stats[...]
    stat_buf[8 + rows_up : 9 + rows_up, :] = attn_stats
    stat_buf[9 + rows_up : 16, :] = jnp.zeros((7 - rows_up, width), f32)
    level = lambda i: pl.ds(16 * i, 16)
    stat_copy = post.send(stat_buf.at[level(0)], stat_in.at[0], me.core)
    sums[2].over_y()
    post.got(stat_copy)
    stat_buf[level(1), :] = stat_buf[level(0), :] + stat_in[0]
    stat_copy = post.send(stat_buf.at[level(1)], stat_in.at[1], me.yp)
    sums[1].over_z()
    sums[0].finish()
    pass_on(1)
    spread(0)
    post.got(stat_copy)
    stat_buf[level(2), :] = stat_buf[level(1), :] + stat_in[1]
    stat_copy = post.send(stat_buf.at[level(2)], stat_in.at[2], me.xp)
    sums[2].over_z()
    corner_on(1)
    pass_on(0)
    post.got(stat_copy)
    stat_buf[48:56, :] = stat_buf[32:40, :] + stat_in[2, 0:8]
    stat_buf[56:64, :] = stat_buf[40:48, :]
    stat_z[f] = stat_buf[level(3), :]
    stat_copies = [post.send(stat_buf.at[level(3)], stat_z.at[f], device) for device in me.z]
    sums[1].finish()
    corner_on(0)
    sums[2].finish()
    for copy in stat_copies:
        post.got(copy)
    total = stat_z[0]
    for g in range(1, fsdp_count):
        total = total + stat_z[g]
    all_total[...] = total[0 : 2 + rows_mid]
    part_total[...] = total[8 : 9 + rows_up]
    for total in sums:
        post.got(total.last)
    grads_out[...] = done[...]
    post.close()
    for copy in loads[10:]:
        copy.wait()


def second_half(fsdp_count, row_count, *operands):
    shape = jax.ShapeDtypeStruct
    vmem = pltpu.VMEM
    width = operands[5].shape[1]
    rows = row_count
    tall = TRUNK + 2 * BLOCK
    pair = 2 * BLOCK
    deep = width // fsdp_count
    half = deep // 2
    return pl.pallas_call(
        partial(second_kernel, fsdp_count),
        out_shape=(
            shape((2, 2 * rows // UNIT, UNIT, width), bf16),
            shape((3, 2, half, width), bf16),
            shape((6, width), f32),
            shape((3, width), f32),
        ),
        in_specs=[ANY] * 10 + [VMEM] * 10,
        out_specs=(ANY,) + (VMEM,) * 3,
        scratch_shapes=[
            vmem((OWN, 384), bf16),
            vmem((KEYS, 384), bf16),
            vmem((KEYS, 384), bf16),
            vmem((384, KEYS), bf16),
            vmem((OWN, 384), bf16),
            vmem((OWN, width), bf16),
            vmem((OWN, width), bf16),
            vmem((3, width, 384), bf16),
            vmem((width, width), bf16),
            vmem((width, width), bf16),
            vmem((8, OWN), f32),
            vmem((tall, OWN), f32),
            vmem((tall, OWN), f32),
            vmem((tall, OWN), bf16),
            vmem((tall, OWN), bf16),
            vmem((KEYS, 128), f32),
            vmem((KEYS, 128), f32),
            vmem((384, OWN), f32),
            vmem((OWN, 384), bf16),
            vmem((3, 2, TRUNK, 128), bf16),
            vmem((3, 2, pair, 128), bf16),
            vmem((3, 2, pair, 128), bf16),
            vmem((3, 2, pair, 128), bf16),
            vmem((3, 2, pair, 128), bf16),
            vmem((OWN, 768), bf16),
            vmem((HALF, width), bf16),
            vmem((HALF, width), bf16),
            vmem((HALF, width), bf16),
            vmem((2, HALF // UNIT, UNIT, width), bf16),
            vmem((2, 2, width, 128), bf16),
            vmem((2, 2, width, 128), bf16),
            vmem((2, width, 128), bf16),
            vmem((2, width, width), bf16),
            vmem((3, width, width), bf16),
            vmem((3, fsdp_count, half, width), bf16),
            vmem((3, fsdp_count - 1, half, width), bf16),
            vmem((3, 2, half, width), bf16),
            vmem((64, width), f32),
            vmem((3, 16, width), f32),
            vmem((fsdp_count, 16, width), f32),
            pltpu.SemaphoreType.DMA((12,)),
            pltpu.SemaphoreType.DMA((80,)),
            pltpu.SemaphoreType.DMA((80,)),
        ],
        compiler_params=pltpu.CompilerParams(collective_id=1, has_side_effects=True, vmem_limit_bytes=LIMIT),
        name="second_half",
    )(*operands)


def place_kernel(
    order, rows_all, grads, all_total, part_total,
    result, patch_grad, gain1, shift1, grad_attn, attn_bias, grad_out, out_bias, gain2, shift2, grad_up, up_bias,
    grad_down_t, down_bias, patch_low, sems,
):
    own = result.shape[0] // BLOCK
    units = BLOCK // UNIT
    core = lax.axis_index("tensor") % 2
    copies = []
    for j in range(own):
        block = order[0, own * lax.axis_index("context") + j]
        branch, leaf = block - TRUNK_BLK, block - TRUNK_BLK - BRANCHES
        index = jnp.where(
            branch < 0,
            5 * (block // 2) + block % 2,
            jnp.where(leaf < 0, 5 * branch + 3, 5 * (leaf // 2) + 2 + 2 * (leaf % 2)),
        )
        to = pl.ds(j * units, units)
        for i, dest in enumerate((result, patch_low)):
            if i == 0:
                dest = result.reshape(own * units, UNIT, result.shape[1])
            copy = pltpu.make_async_copy(
                rows_all.at[i, pl.ds(index * units, units)], dest.at[to], sems.at[i, j]
            )
            copy.start()
            copies.append(copy)
    total = lambda i: all_total[i, :]
    gain1[...], shift1[...], gain2[...], shift2[...] = total(0), total(1), total(2), total(3)
    down_bias[...], out_bias[...] = total(4), total(5)
    up_bias[...] = part_total[core, :]
    for i in range(2):
        lanes = slice(384 * i, 384 * i + 384)
        row = part_total[2:3, lanes]
        first = jnp.where(core == 0, row[:, 0:128], row[:, 128:256])
        second = jnp.where(core == 0, row[:, 256:320], row[:, 320:384])
        attn_bias[i : i + 1, :] = jnp.concatenate([first, second], axis=1)
    side, half, width = grads.shape[1:]
    value = lambda i: grads[i].reshape(side * half, width).astype(f32)
    grad_up[...] = value(0)
    grad_down_t[...] = value(1)
    attn = value(2)
    tails = [attn[:, 512:576], attn[:, 576:640], attn[:, 640:704], attn[:, 704:768]]
    for i in range(3):
        grad_attn[i, :, 0:128] = attn[:, 128 * i : 128 * i + 128]
        grad_attn[i, :, 128:192] = tails[i]
    grad_out[...] = jnp.concatenate([attn[:, 384:512], tails[3]], axis=1).T
    for copy in copies:
        copy.wait()
    patch_grad[...] = patch_low[...].reshape(patch_grad.shape).astype(f32)


def place(order, row_count, rows_all, grads, all_total, part_total):
    shape = jax.ShapeDtypeStruct
    width = rows_all.shape[3]
    deep = grads.shape[1] * grads.shape[2]
    vector = shape((width,), f32)
    return pl.pallas_call(
        place_kernel,
        out_shape=(
            shape((row_count, width), bf16), shape((row_count, width), f32), vector, vector,
            shape((3, deep, 192), f32), shape((2, 192), f32), shape((192, deep), f32), vector, vector, vector,
            shape((deep, width), f32), vector, shape((deep, width), f32), vector,
        ),
        in_specs=[SMEM, ANY] + [VMEM] * 3,
        out_specs=(VMEM,) * 14,
        scratch_shapes=[
            pltpu.VMEM((row_count // UNIT, UNIT, width), bf16),
            pltpu.SemaphoreType.DMA((2, row_count // BLOCK)),
        ],
        compiler_params=pltpu.CompilerParams(vmem_limit_bytes=LIMIT),
        name="place",
    )(order, rows_all, grads, all_total, part_total)


def tree_shards(
    fsdp_count, patches, out_grad, block_order, first_gain, first_shift, attn_proj, attn_bias, out_proj, out_bias,
    second_gain, second_shift, up_proj, up_bias, down_proj, down_bias,
):
    middle = first_half(
        fsdp_count, block_order, patches, out_grad, attn_proj, out_proj, up_proj, down_proj.T, up_bias, attn_bias,
        first_gain, first_shift, second_gain, second_shift, out_bias, down_bias,
    )
    sums = second_half(fsdp_count, patches.shape[0], *middle, first_gain)
    outputs = list(place(block_order, patches.shape[0], *sums))
    outputs[12] = outputs[12].T
    return tuple(outputs)


def solution(mesh):
    fits = mesh.shape["context"] * 2 == BRANCHES and mesh.shape["tensor"] == 4 and mesh.shape["fsdp"] == 4
    body = partial(tree_shards, mesh.shape["fsdp"]) if fits else shards
    return jax.shard_map(
        body,
        mesh=mesh,
        in_specs=(
            P(("fsdp", "context"), None),
            P(("fsdp", "context"), None),
            P("fsdp", None),
            P(),
            P(),
            P(None, "fsdp", "tensor"),
            P(None, "tensor"),
            P("tensor", "fsdp"),
            P(),
            P(),
            P(),
            P("fsdp", "tensor"),
            P("tensor"),
            P("tensor", "fsdp"),
            P(),
        ),
        out_specs=(
            P(("fsdp", "context"), None),
            P(("fsdp", "context"), None),
            P(),
            P(),
            P(None, "fsdp", "tensor"),
            P(None, "tensor"),
            P("tensor", "fsdp"),
            P(),
            P(),
            P(),
            P("fsdp", "tensor"),
            P("tensor"),
            P("tensor", "fsdp"),
            P(),
        ),
        check_vma=False,
    )
```

```python
from functools import partial

import jax
import jax.numpy as jnp
from jax import lax
from jax.experimental import pallas as pl
from jax.experimental.pallas import tpu as pltpu
from jax.sharding import PartitionSpec as P

HEAD_DIM = 64
BLOCK = 128
TRUNK_BLK = 8
BRANCHES = 4
LEAVES = 2
TREE_BLK = 20


epsilon = 1e-05
far_below = -1e30


def layer_norm(values, norm_gain, norm_shift):
    center = values - jnp.mean(values, axis=1, keepdims=True)
    inverse = lax.rsqrt(jnp.mean(center * center, axis=1, keepdims=True) + epsilon)
    normed = center * inverse
    return (normed * norm_gain + norm_shift, normed, inverse)


def norm_back(gradient, normed, inverse, norm_gain):
    scaled = gradient * norm_gain
    return inverse * (
        scaled
        - jnp.mean(scaled, axis=1, keepdims=True)
        - normed * jnp.mean(scaled * normed, axis=1, keepdims=True)
    )


def slot_labels(order_row):
    position = order_row % TREE_BLK
    return (order_row // TREE_BLK, jnp.where(position < TRUNK_BLK, 0, position - TRUNK_BLK + 1))


def spread_rows(values):
    return jnp.broadcast_to(values[:, None], (values.shape[0], BLOCK)).reshape(-1)


def row_labels(labels, first_slot, slot_count):
    return tuple(
        (
            spread_rows(lax.dynamic_slice_in_dim(label_table, first_slot, slot_count))
            for label_table in labels
        )
    )


def visible(query_labels, key_labels):
    query_tree, query_seg = query_labels
    key_tree, key_seg = key_labels
    parent = jnp.where(query_seg > BRANCHES, 1 + (query_seg - BRANCHES - 1) // LEAVES, 0)
    reaches = (
        (key_seg[None, :] == 0)
        | (key_seg[None, :] == query_seg[:, None])
        | (key_seg[None, :] == parent[:, None])
    )
    return (query_tree[:, None] == key_tree[None, :]) & reaches


def head_view(matrix):
    return matrix.reshape(matrix.shape[0], matrix.shape[1] // HEAD_DIM, HEAD_DIM)


def scores_of(query_heads, key_heads):
    return jnp.einsum(
        "qhd,khd->hqk", query_heads, key_heads, preferred_element_type=jnp.float32
    ) * HEAD_DIM ** (-0.5)


def weights_of(scores, log_total, allowed):
    return jnp.where(allowed[None], jnp.exp(scores - log_total[:, :, None]), 0.0)


def score_grads(query_heads, grad_heads, key_heads, value_heads, log_total, row_delta, allowed):
    weights = weights_of(scores_of(query_heads, key_heads), log_total, allowed)
    prob_grad = jnp.einsum(
        "qhd,khd->hqk", grad_heads, value_heads, preferred_element_type=jnp.float32
    )
    return (
        (weights * (prob_grad - row_delta[:, :, None])).astype(jnp.bfloat16),
        weights.astype(jnp.bfloat16),
    )


def shards(
    patches,
    out_grad,
    block_order,
    first_gain,
    first_shift,
    attn_proj,
    attn_bias,
    out_proj,
    out_bias,
    second_gain,
    second_shift,
    up_proj,
    up_bias,
    down_proj,
    down_bias,
):
    attn_full, out_full, up_full, down_full = (
        lax.all_gather(attn_proj, "fsdp", axis=1, tiled=True),
        lax.all_gather(out_proj, "fsdp", axis=1, tiled=True),
        lax.all_gather(up_proj, "fsdp", axis=0, tiled=True),
        lax.all_gather(down_proj, "fsdp", axis=1, tiled=True),
    )
    labels = slot_labels(block_order[0])
    row_count = patches.shape[0]
    own_slots = row_count // BLOCK
    query_labels = row_labels(labels, lax.axis_index("context") * own_slots, own_slots)
    head_width = attn_full.shape[2]
    head_count = head_width // HEAD_DIM
    key_block = 4 * BLOCK
    block_slots = key_block // BLOCK
    score_scale = HEAD_DIM ** (-0.5)
    inputs = patches.astype(jnp.float32)
    first_norm, first_normed, first_inverse = layer_norm(inputs, first_gain, first_shift)
    first_low = first_norm.astype(jnp.bfloat16)
    projected = jnp.einsum("rd,cde->cre", first_low, attn_full, preferred_element_type=jnp.float32)
    queries = (projected[0] + attn_bias[0]).astype(jnp.bfloat16)
    keys_low = projected[1].astype(jnp.bfloat16)
    values_low = (projected[2] + attn_bias[1]).astype(jnp.bfloat16)
    keys_all = lax.all_gather(
        jnp.concatenate([keys_low, values_low], axis=1), "context", axis=0, tiled=True
    )
    block_count = keys_all.shape[0] // key_block
    query_heads = head_view(queries)

    def key_piece(step_index):
        key_slab = lax.dynamic_slice_in_dim(keys_all, step_index * key_block, key_block, 0)
        allowed = visible(query_labels, row_labels(labels, step_index * block_slots, block_slots))
        return (head_view(key_slab[:, :head_width]), head_view(key_slab[:, head_width:]), allowed)

    def total_step(step_index, carried):
        running_top, running_sum = carried
        key_heads, value_heads, allowed = key_piece(step_index)
        masked = jnp.where(allowed[None], scores_of(query_heads, key_heads), far_below)
        new_top = jnp.maximum(running_top, jnp.max(masked, axis=2))
        kept_exp = jnp.where(allowed[None], jnp.exp(masked - new_top[:, :, None]), 0.0)
        return (new_top, running_sum * jnp.exp(running_top - new_top) + jnp.sum(kept_exp, axis=2))

    start_top = jnp.full((head_count, row_count), far_below, jnp.float32)
    running_top, running_sum = lax.fori_loop(
        0, block_count, total_step, (start_top, jnp.zeros((head_count, row_count), jnp.float32))
    )
    log_total = running_top + jnp.log(running_sum)

    def mix_step(step_index, mixed):
        key_heads, value_heads, allowed = key_piece(step_index)
        weights = weights_of(scores_of(query_heads, key_heads), log_total, allowed).astype(
            jnp.bfloat16
        )
        return mixed + jnp.einsum(
            "hqk,khd->qhd", weights, value_heads, preferred_element_type=jnp.float32
        )

    attended = lax.fori_loop(
        0, block_count, mix_step, jnp.zeros((row_count, head_count, HEAD_DIM), jnp.float32)
    )
    attended_low = attended.reshape(row_count, head_width).astype(jnp.bfloat16)
    attn_part = jnp.dot(attended_low, out_full, preferred_element_type=jnp.float32)
    middle = inputs + (lax.psum(attn_part, "tensor") + out_bias)
    second_norm, second_normed, second_inverse = layer_norm(middle, second_gain, second_shift)
    second_low = second_norm.astype(jnp.bfloat16)
    pre_act = jnp.dot(second_low, up_full, preferred_element_type=jnp.float32) + up_bias
    hidden, gelu_back = jax.vjp(partial(jax.nn.gelu, approximate=False), pre_act)
    hidden_low = hidden.astype(jnp.bfloat16)
    mlp_part = jnp.dot(hidden_low, down_full, preferred_element_type=jnp.float32)
    result = (
        middle + (lax.psum(mlp_part.astype(jnp.bfloat16), "tensor").astype(jnp.float32) + down_bias)
    ).astype(jnp.bfloat16)
    top_grad = out_grad.astype(jnp.float32)
    grad_down_bias = jnp.sum(top_grad, axis=0)
    grad_down = jnp.einsum("rf,rd->fd", hidden_low, out_grad, preferred_element_type=jnp.float32)
    hidden_grad = jnp.einsum("rd,fd->rf", out_grad, down_full, preferred_element_type=jnp.float32)
    pre_grad = gelu_back(hidden_grad)[0].astype(jnp.bfloat16)
    grad_up_bias = jnp.sum(pre_grad.astype(jnp.float32), axis=0)
    grad_up = jnp.einsum("rd,rf->df", second_low, pre_grad, preferred_element_type=jnp.float32)
    second_part = jnp.einsum("rf,df->rd", pre_grad, up_full, preferred_element_type=jnp.float32)
    second_grad = lax.psum(second_part, "tensor")
    grad_second_gain = jnp.sum(second_grad * second_normed, axis=0)
    grad_second_shift = jnp.sum(second_grad, axis=0)
    middle_grad = top_grad + norm_back(second_grad, second_normed, second_inverse, second_gain)
    branch_grad = middle_grad.astype(jnp.bfloat16)
    grad_out_bias = jnp.sum(branch_grad.astype(jnp.float32), axis=0)
    grad_out = jnp.einsum(
        "re,rd->ed", attended_low, branch_grad, preferred_element_type=jnp.float32
    )
    attended_grad = jnp.einsum(
        "rd,ed->re", branch_grad, out_full, preferred_element_type=jnp.float32
    ).astype(jnp.bfloat16)
    grad_heads = head_view(attended_grad)

    def delta_step(step_index, row_delta):
        key_heads, value_heads, allowed = key_piece(step_index)
        weights = weights_of(scores_of(query_heads, key_heads), log_total, allowed)
        prob_grad = jnp.einsum(
            "qhd,khd->hqk", grad_heads, value_heads, preferred_element_type=jnp.float32
        )
        return row_delta + jnp.sum(weights * prob_grad, axis=2)

    row_delta = lax.fori_loop(
        0, block_count, delta_step, jnp.zeros((head_count, row_count), jnp.float32)
    )
    query_start = jnp.zeros((row_count, head_count, HEAD_DIM), jnp.float32)

    def back_step(step_index, carried):
        query_acc, key_acc = carried
        key_heads, value_heads, allowed = key_piece(step_index)
        score_low, weights_low = score_grads(
            query_heads, grad_heads, key_heads, value_heads, log_total, row_delta, allowed
        )
        query_acc = query_acc + jnp.einsum(
            "hqk,khd->qhd", score_low, key_heads, preferred_element_type=jnp.float32
        )
        key_part = jnp.einsum(
            "hqk,qhd->khd", score_low, query_heads, preferred_element_type=jnp.float32
        )
        value_part = jnp.einsum(
            "hqk,qhd->khd", weights_low, grad_heads, preferred_element_type=jnp.float32
        )
        joined = jnp.concatenate(
            [key_part.reshape(key_block, head_width), value_part.reshape(key_block, head_width)],
            axis=1,
        )
        return (
            query_acc,
            lax.dynamic_update_slice_in_dim(key_acc, joined, step_index * key_block, 0),
        )

    key_start = jnp.zeros((keys_all.shape[0], 2 * head_width), jnp.float32)
    query_acc, key_acc = lax.fori_loop(0, block_count, back_step, (query_start, key_start))
    key_value_grad = lax.psum_scatter(key_acc, "context", scatter_dimension=0, tiled=True)
    query_grad = (query_acc.reshape(row_count, head_width) * score_scale).astype(jnp.bfloat16)
    key_grad = (key_value_grad[:, :head_width] * score_scale).astype(jnp.bfloat16)
    value_grad = key_value_grad[:, head_width:].astype(jnp.bfloat16)
    stacked = jnp.stack([query_grad, key_grad, value_grad])
    grad_attn_bias = jnp.stack(
        [
            jnp.sum(query_grad.astype(jnp.float32), axis=0),
            jnp.sum(value_grad.astype(jnp.float32), axis=0),
        ]
    )
    grad_attn = jnp.einsum("rd,cre->cde", first_low, stacked, preferred_element_type=jnp.float32)
    first_grad = lax.psum(
        jnp.einsum("cre,cde->rd", stacked, attn_full, preferred_element_type=jnp.float32), "tensor"
    )
    grad_first_gain = jnp.sum(first_grad * first_normed, axis=0)
    grad_first_shift = jnp.sum(first_grad, axis=0)
    patch_grad = middle_grad + norm_back(first_grad, first_normed, first_inverse, first_gain)
    wide_attn, wide_out, wide_up, wide_down = (
        lax.psum_scatter(grad_attn, ("fsdp", "context"), scatter_dimension=1, tiled=True),
        lax.psum_scatter(grad_out, ("fsdp", "context"), scatter_dimension=1, tiled=True),
        lax.psum_scatter(grad_up, ("fsdp", "context"), scatter_dimension=0, tiled=True),
        lax.psum_scatter(grad_down, ("fsdp", "context"), scatter_dimension=1, tiled=True),
    )
    grad_attn, grad_out, grad_up, grad_down = (
        lax.all_gather(wide_attn, "context", axis=1, tiled=True),
        lax.all_gather(wide_out, "context", axis=1, tiled=True),
        lax.all_gather(wide_up, "context", axis=0, tiled=True),
        lax.all_gather(wide_down, "context", axis=1, tiled=True),
    )
    small_grads = lax.psum(
        (
            grad_first_gain,
            grad_first_shift,
            grad_attn_bias,
            grad_out_bias,
            grad_second_gain,
            grad_second_shift,
            grad_up_bias,
            grad_down_bias,
        ),
        ("fsdp", "context"),
    )
    return (
        result,
        patch_grad,
        small_grads[0],
        small_grads[1],
        grad_attn,
        small_grads[2],
        grad_out,
        small_grads[3],
        small_grads[4],
        small_grads[5],
        grad_up,
        small_grads[6],
        grad_down,
        small_grads[7],
    )


bf16 = jnp.bfloat16
f32 = jnp.float32
VMEM = pl.BlockSpec(memory_space=pltpu.VMEM)
SMEM = pl.BlockSpec(memory_space=pltpu.SMEM)
ANY = pl.BlockSpec(memory_space=pl.ANY)
MESH = pl.DeviceIdType.MESH
LIMIT = 61 * 1024 * 1024


def dot_nn(a, b):
    return lax.dot_general(a, b, (((1,), (0,)), ((), ())), preferred_element_type=f32)


def dot_nt(a, b):
    return lax.dot_general(a, b, (((1,), (1,)), ((), ())), preferred_element_type=f32)


def dot_tn(a, b):
    return lax.dot_general(a, b, (((0,), (0,)), ((), ())), preferred_element_type=f32)


class Here:
    def __init__(self, fsdp_count):
        self.f = lax.axis_index("fsdp")
        self.c = lax.axis_index("context")
        self.t = lax.axis_index("tensor")
        self.x = self.t // 2
        self.k = self.t % 2
        self.core = (self.f, self.c, 2 * self.x + 1 - self.k)
        self.xp = (self.f, self.c, 2 * (1 - self.x) + self.k)
        self.yp = (self.f, 1 - self.c, self.t)
        self.z = [((self.f + i) % fsdp_count, self.c, self.t) for i in range(1, fsdp_count)]
        self.back = [(self.f + fsdp_count - i) % fsdp_count for i in range(1, fsdp_count)]


def greet(devices):
    barrier = pltpu.get_barrier_semaphore()
    for device in devices:
        pl.semaphore_signal(barrier, inc=1, device_id=device, device_id_type=MESH)
    pl.semaphore_wait(barrier, len(devices))


class Post:
    def __init__(self, send_sem, recv_sem):
        self.send_sem, self.recv_sem = send_sem, recv_sem
        self.sent, self.open = [], []

    def send(self, src, dst, device):
        index = len(self.sent)
        copy = pltpu.make_async_remote_copy(
            src_ref=src,
            dst_ref=dst,
            send_sem=self.send_sem.at[index],
            recv_sem=self.recv_sem.at[index],
            device_id=device,
            device_id_type=MESH,
        )
        copy.start()
        self.sent.append(copy)
        self.open.append((copy, device))
        return copy

    def got(self, copy):
        copy.wait_recv()
        self.open = [entry for entry in self.open if entry[0] is not copy]

    def got_from(self, device):
        for copy, to in self.open:
            if to is device:
                self.got(copy)

    def close(self):
        for copy, _ in self.open:
            copy.wait_recv()
        for copy in self.sent:
            copy.wait_send()


def ds(start, size, step=16):
    return pl.ds(pl.multiple_of(start, step), size)


TRUNK = TRUNK_BLK * BLOCK
SUB = (1 + LEAVES) * BLOCK
KEYS = TRUNK + SUB
OWN = 2 * BLOCK + SUB
PIECES = (
    (2 * BLOCK, TRUNK, 2 * BLOCK),
    (3 * BLOCK, TRUNK + BLOCK, BLOCK),
    (4 * BLOCK, TRUNK + BLOCK, 2 * BLOCK),
)


def own_places(s):
    return [2 * s, 2 * s + 1, 12 + 2 * s, 8 + s, 13 + 2 * s]


def row_norm(values):
    center = values - jnp.mean(values, axis=1, keepdims=True)
    inverse = lax.rsqrt(jnp.mean(center * center, axis=1, keepdims=True) + epsilon)
    return center * inverse, inverse

HALF = OWN // 2
UNIT = 16


def wide(vector):
    return vector[...].reshape(1, -1)


def first_kernel(
    fsdp_count, order, patches, grads, attn_proj, out_proj, up, d_own, up_bias, attn_bias, gain1, shift1, gain2, shift2, out_bias, down_bias,
    q_out, k_out, v_out, att_out, low_out, x_out, wh_out, g_up_out, g_down_out,
    lse, da, middle_grad, mlp_own, mlp_send, g_out_own, g_out_send, stats, up_stats,
    where, a_own, bias, rows_all, grads_all, wa, wh, wo_x, wu, wd, bias_all,
    low_all, low, low_own, x_own, g_own, q, k, v, vt, attended, att_t, att_x, st, pt,
    middle, normed, inverse, low2, hidden, pre_grad, second, second_send, second_x, branch, da_send, g_up, g_down, g_sum,
    local, ss, rs,
):
    me = Here(fsdp_count)
    f, c, x, core, t = me.f, me.c, me.x, me.k, me.t
    s = 2 * c + core
    units = patches.shape[0]
    part = units // 4
    width = patches.shape[2]
    deep = up.shape[0]
    head_width = attn_proj.shape[2]
    own_copies = []

    def keep(src, dst):
        copy = pltpu.make_async_copy(src, dst, local.at[len(own_copies)])
        copy.start()
        own_copies.append(copy)

    keep(patches, rows_all.at[pl.ds(units * c, units)])
    keep(grads, grads_all.at[pl.ds(units * c, units)])
    keep(up, wu.at[core, ds(deep * f, deep)])
    keep(d_own, wd.at[core, ds(deep * f, deep)])
    a_own[:, 0:128] = attn_proj[0, :, 0:128]
    a_own[:, 128:256] = attn_proj[1, :, 0:128]
    a_own[:, 256:384] = attn_proj[2, :, 0:128]
    out_t = out_proj[...].T
    a_own[:, 384:512] = jnp.concatenate([attn_proj[0, :, 128:head_width], attn_proj[1, :, 128:head_width]], axis=1)
    a_own[:, 512:640] = jnp.concatenate([attn_proj[2, :, 128:head_width], out_t[:, 128:head_width]], axis=1)
    a_own[:, 640:768] = out_t[:, 0:128]
    bias[...] = jnp.zeros_like(bias)
    bias[0:1, :] = wide(up_bias)
    bias[1:3, 0:head_width] = attn_bias[...]
    greet([me.core, me.xp, me.yp] + me.z)
    post = Post(ss, rs)
    there = units * (1 - c)
    half = deep // 2
    strip, other_strip = half * c, half * (1 - c)

    def quarter(array, index, piece, count):
        size = part // count
        return array.at[pl.ds(there + part * index + size * piece, size)]

    def to_y(src, dst, piece, count):
        size = part // count
        return post.send(
            src.at[pl.ds(part * t + size * piece, size)],
            dst.at[pl.ds(units * c + part * t + size * piece, size)],
            me.yp,
        )

    def relay(piece, device):
        return post.send(piece, piece, device)

    part_rows = half // 2
    a_part = lambda source, row, count: wa.at[core, ds(deep * source + row, count)]
    pieces = 4
    patches_y = [to_y(patches, rows_all, i, pieces) for i in range(pieces)]
    a_z = [
        [
            post.send(
                a_own.at[ds(strip + part_rows * i, part_rows)], a_part(f, strip + part_rows * i, part_rows), device
            )
            for device in me.z
        ]
        for i in range(2)
    ]
    post.send(a_own, wa.at[core, ds(deep * f, deep)], me.core)
    post.send(bias, bias_all.at[core], me.core)
    gain_row, shift_row = wide(gain1), wide(shift1)

    def norm_units(start, count):
        values = rows_all[pl.ds(start, count)].reshape(count * UNIT, width).astype(f32)
        normed_rows, _ = row_norm(values)
        low_rows = (normed_rows * gain_row + shift_row).astype(bf16)
        low_all[pl.ds(start, count)] = low_rows.reshape(count, UNIT, width)

    block_units = BLOCK // UNIT
    own_blocks = units // block_units

    def norm_own(j, carried):
        norm_units(units * c + block_units * j, block_units)
        return carried

    slots = order.shape[1]

    def find(place, carried):
        slot = jnp.int32(0)
        for j in range(slots):
            slot = jnp.where(order[0, j] == place, j, slot)
        where[place] = slot * block_units
        return carried

    lax.fori_loop(0, slots, find, 0)
    wa[core, ds(deep * f, deep), :] = a_own[...]
    bias_all[core] = bias[...]
    own_copies[0].wait()
    lax.fori_loop(0, own_blocks - pieces, norm_own, 0)
    size = part // pieces
    over = (t + 2) % 4
    beside, across = t + 1 - 2 * core, over + 1 - 2 * core
    patches_x, patches_core = [], []
    for i in range(pieces):
        post.got(patches_y[i])
        patches_x.append(relay(quarter(rows_all, t, i, pieces), me.xp))
        patches_core.append(relay(quarter(rows_all, t, i, pieces), me.core))
        norm_units(there + part * t + size * i, size)
        norm_own(own_blocks - pieces + i, 0)
    a_y = []
    for i in range(2):
        for copy, source in zip(a_z[i], me.back):
            post.got(copy)
            piece = a_part(source, strip + part_rows * i, part_rows)
            a_y.append(relay(piece, me.yp))
            relay(piece, me.core)
    grads_y = [to_y(grads, grads_all, i, 2) for i in range(2)]
    u_z = [
        post.send(up.at[ds(strip, half)], wu.at[core, ds(deep * f + strip, half)], device) for device in me.z
    ]
    post.send(up, wu.at[core, ds(deep * f, deep)], me.core)
    post.send(d_own, wd.at[core, ds(deep * f, deep)], me.core)
    for i in range(pieces):
        post.got(patches_core[i])
        norm_units(there + part * beside + size * i, size)
    patches_core = []
    for i in range(pieces):
        post.got(patches_x[i])
        patches_core.append(relay(quarter(rows_all, over, i, pieces), me.core))
        norm_units(there + part * over + size * i, size)
    for index, copy in enumerate(a_y):
        post.got(copy)
        source, i = me.back[index % len(me.back)], index // len(me.back)
        relay(a_part(source, other_strip + part_rows * i, part_rows), me.core)
    for i in range(pieces):
        post.got(patches_core[i])
        norm_units(there + part * across + size * i, size)

    def block_of(array, place):
        return array[pl.ds(where[place], block_units)].reshape(BLOCK, width)

    def trunk_step(j, carried):
        low[ds(j * BLOCK, BLOCK), :] = block_of(low_all, j)
        return carried

    lax.fori_loop(0, TRUNK_BLK, trunk_step, 0)
    places = own_places(s)
    for j in range(2, 5):
        low[TRUNK + (j - 2) * BLOCK : TRUNK + (j - 1) * BLOCK, :] = block_of(low_all, places[j])
    for j, place in enumerate(places):
        x_own[pl.ds(j * BLOCK, BLOCK), :] = block_of(rows_all, place)
    low_own[0 : 2 * BLOCK, :] = low[ds(2 * BLOCK * s, 2 * BLOCK), :]
    low_own[2 * BLOCK :, :] = low[TRUNK:, :]
    post.got_from(me.core)

    def assemble(i):
        slab = (0, 1, 2, 5)[i]
        wh[i, :, 0:128] = wa[0, :, 128 * slab : 128 * slab + 128]
        wh[i, :, 128:256] = wa[1, :, 128 * slab : 128 * slab + 128]
        start = 384 + 64 * i
        wh[i, :, 256:384] = jnp.concatenate(
            [wa[0, :, start : start + 64], wa[1, :, start : start + 64]], axis=1
        )

    for i in range(4):
        assemble(i)
    wo_rows = ds(width // 2 * core, width // 2)
    wo_copy = post.send(wh.at[3, wo_rows], wo_x.at[wo_rows], me.xp)
    keep(wh, wh_out)

    def heads_row(row):
        a, b = bias_all[0, row : row + 1, :], bias_all[1, row : row + 1, :]
        return jnp.concatenate([a[:, 0:128], b[:, 0:128], a[:, 128:192], b[:, 128:192]], axis=1)

    q[...] = ((dot_nn(low_own[...], wh[0]) + heads_row(1)).astype(bf16) * HEAD_DIM ** (-0.5)).astype(bf16)
    value_bias = heads_row(2)

    def project(j, carried):
        rows = ds(j * (KEYS // 2), KEYS // 2)
        k[rows, :] = dot_nn(low[rows, :], wh[1]).astype(bf16)
        v[rows, :] = (dot_nn(low[rows, :], wh[2]) + value_bias).astype(bf16)
        return carried

    lax.fori_loop(0, 2, project, 0)
    vt[...] = v[...].T
    for src, dst in ((q, q_out), (k, k_out), (v, v_out), (low_own, low_out), (x_own, x_out)):
        keep(src, dst)
    lane = lax.broadcasted_iota(jnp.int32, (OWN, 128), 1) // HEAD_DIM

    def head(h, carried):
        slab, side = h // 2, h % 2
        lanes = pl.ds(pl.multiple_of(slab * 128, 128), 128)
        own_q = q[:, lanes]
        q_part = jnp.where(lane == side, own_q, jnp.zeros_like(own_q))
        st[0:TRUNK, :] = dot_nt(k[0:TRUNK, lanes], q_part)
        for q_row, k_row, count in PIECES:
            st[TRUNK : TRUNK + count, q_row : q_row + BLOCK] = dot_nt(
                k[k_row : k_row + count, lanes], q_part[q_row : q_row + BLOCK]
            )
        tops, sums = [], []
        for j in range(OWN // BLOCK):
            cols = slice(j * BLOCK, (j + 1) * BLOCK)
            count = TRUNK + (0 if j < 2 else PIECES[j - 2][2])
            top = jnp.full((8, BLOCK), far_below, f32)
            for r in range(0, count, BLOCK):
                piece = st[r : r + BLOCK, cols].reshape(BLOCK // 8, 8, BLOCK)
                top = jnp.maximum(top, jnp.max(piece, axis=0))
            top = jnp.max(top, axis=0, keepdims=True)
            total = jnp.zeros((8, BLOCK), f32)
            for r in range(0, count, BLOCK):
                weight = jnp.exp(st[r : r + BLOCK, cols] - top)
                total = total + jnp.sum(weight.reshape(BLOCK // 8, 8, BLOCK), axis=0)
                pt[r : r + BLOCK, cols] = weight.astype(bf16)
            tops.append(top)
            sums.append(jnp.sum(total, axis=0, keepdims=True))
        total = jnp.concatenate(sums, axis=1)
        head_rows, side_rows = ds(h * HEAD_DIM, HEAD_DIM), ds(side * HEAD_DIM, HEAD_DIM)
        att_t[side_rows, :] = dot_nn(vt[head_rows, 0:TRUNK], pt[0:TRUNK, :])
        for q_row, k_row, count in PIECES:
            cols = slice(q_row, q_row + BLOCK)
            att_t[side_rows, cols] += dot_nn(
                vt[head_rows, k_row : k_row + count], pt[TRUNK : TRUNK + count, cols]
            )
        att_t[side_rows, :] = att_t[side_rows, :] / total
        lse[pl.ds(h, 1), :] = jnp.concatenate(tops, axis=1) + jnp.log(total)
        return carried

    mine, far = HALF * x, HALF * (1 - x)
    here_rows, far_rows = ds(mine, HALF), ds(far, HALF)
    att_copies = []

    def slab_heads(slab):
        lax.fori_loop(2 * slab, 2 * slab + 2, head, 0)
        lanes = pl.ds(128 * slab, 128)
        attended[:, lanes] = att_t[...].T.astype(bf16)
        att_copies.append(post.send(attended.at[far_rows, lanes], att_x.at[:, lanes], me.xp))

    def grads_on(i):
        post.got(grads_y[i])
        relay(quarter(grads_all, t, i, 2), me.core)
        return relay(quarter(grads_all, t, i, 2), me.xp)

    def strips_on(copies, array):
        passed = []
        for copy, source in zip(copies, me.back):
            post.got(copy)
            piece = array.at[core, ds(deep * source + strip, half)]
            passed.append(relay(piece, me.yp))
            relay(piece, me.core)
        return passed

    def strips_in(copies, array):
        for copy, source in zip(copies, me.back):
            post.got(copy)
            relay(array.at[core, ds(deep * source + other_strip, half)], me.core)

    grads_x = [grads_on(0)]
    u_y = strips_on(u_z, wu)
    d_z = [
        post.send(d_own.at[ds(strip, half)], wd.at[core, ds(deep * f + strip, half)], device) for device in me.z
    ]
    slab_heads(0)
    grads_x.append(grads_on(1))
    slab_heads(1)
    post.got(wo_copy)
    relay(wo_x.at[wo_rows], me.core)
    slab_heads(2)
    keep(attended, att_out)
    middle[...] = (
        x_own[here_rows, :].astype(f32) + wide(out_bias) + dot_nt(attended[here_rows, :], wh[3])
    )
    for i in range(2):
        post.got(grads_x[i])
        relay(quarter(grads_all, over, i, 2), me.core)
    strips_in(u_y, wu)
    post.got_from(me.core)
    for copy in att_copies:
        post.got(copy)
    middle[...] += dot_nt(att_x[...], wo_x[...])
    n2, s2 = row_norm(middle[...])
    normed[...] = n2
    inverse[...] = s2
    low2[here_rows, :] = (n2 * wide(gain2) + wide(shift2)).astype(bf16)
    chunk = HALF // 2
    here_chunks = [ds(mine + chunk * i, chunk) for i in range(2)]
    far_chunks = [ds(far + chunk * i, chunk) for i in range(2)]
    low_copies = [post.send(low2.at[rows], low2.at[rows], me.xp) for rows in here_chunks]
    own_copies[1].wait()
    for j, place in enumerate(places):
        g_own[pl.ds(j * BLOCK, BLOCK), :] = block_of(grads_all, place)
    d_y = strips_on(d_z, wd)
    own_copies[2].wait()
    own_copies[3].wait()
    strips_in(d_y, wd)
    post.got_from(me.core)
    tile = 256

    def feed(rows, count):
        second[rows, :] = jnp.zeros((count, width), f32)

        def step(j, carried):
            shard, lanes = j // 3, pl.ds(pl.multiple_of(j % 3 * tile, 128), tile)
            out = pl.ds(pl.multiple_of(j * tile, 128), tile)
            pre = dot_nn(low2[rows, :], wu[shard, :, lanes]) + bias_all[shard, 0:1, lanes]
            below = 0.5 * (1.0 + lax.erf(pre * (2.0**-0.5)))
            density = jnp.exp(-0.5 * pre * pre) * (2.0 * jnp.pi) ** -0.5
            hidden[rows, out] = (pre * below).astype(bf16)
            back = dot_nn(g_own[rows, :], wd[shard, :, lanes])
            low_back = (back * (below + pre * density)).astype(bf16)
            pre_grad[rows, out] = low_back
            second[rows, :] += dot_nt(low_back, wu[shard, :, lanes])
            return carried

        lax.fori_loop(0, 6, step, 0)

    def mlp(rows):
        return dot_nt(hidden[rows, 0:width], wd[0]) + dot_nt(hidden[rows, width:], wd[1])

    second_copies = []
    for i in range(2):
        post.got(low_copies[i])
        feed(far_chunks[i], chunk)
        second_send[i] = second[far_chunks[i], :].astype(bf16)
        second_copies.append(post.send(second_send.at[i], second_x.at[i], me.xp))
    feed(here_rows, HALF)

    own_lanes, sibling_lanes = (
        pl.ds(pl.multiple_of(width * side, 128), width) for side in (core, 1 - core)
    )
    sibling_copies = []
    for index, (left, right, grad) in enumerate(((low2, pre_grad, g_up), (g_own, hidden, g_down))):

        def weight_step(j, carried):
            lanes = pl.ds(pl.multiple_of(j * tile, 128), tile)
            grad[:, lanes] = dot_tn(left[...], right[:, lanes]).astype(bf16)
            return carried

        lax.fori_loop(0, 6, weight_step, 0)
        sibling_copies.append(post.send(grad.at[:, sibling_lanes], g_sum.at[index], me.core))
    up_stats[0:1, :] = jnp.sum(pre_grad[:, 0:width].astype(f32), axis=0, keepdims=True)
    up_stats[1:2, :] = jnp.sum(pre_grad[:, width:].astype(f32), axis=0, keepdims=True)
    mlp_send[...] = mlp(far_rows).astype(bf16)
    mlp_own[...] = middle[...] + mlp(here_rows) + wide(down_bias)
    total = [jnp.zeros((1, width), f32)] * 4
    for i in range(2):
        rows = here_chunks[i]
        part_rows = slice(chunk * i, chunk * i + chunk)
        post.got(second_copies[i])
        second_grad = second[rows, :] + second_x[i].astype(f32)
        n2 = normed[part_rows, :]
        dy = g_own[rows, :].astype(f32)
        grad = dy + norm_back(second_grad, n2, inverse[part_rows, :], wide(gain2))
        middle_grad[part_rows, :] = grad
        low_grad = grad.astype(bf16)
        branch[part_rows, :] = low_grad
        da_send[part_rows, :] = dot_nn(low_grad, wo_x[...]).astype(bf16)
        post.send(da_send.at[pl.ds(chunk * i, chunk)], da.at[rows], me.xp)
        terms = (second_grad * n2, second_grad, dy, low_grad.astype(f32))
        total = [a + jnp.sum(b, axis=0, keepdims=True) for a, b in zip(total, terms)]
    for i in range(4):
        stats[i : i + 1, :] = total[i]
    da[here_rows, :] = dot_nn(branch[...], wh[3]).astype(bf16)
    g_out_send[...] = dot_tn(branch[...], att_x[...]).astype(bf16)
    g_out_own[...] = dot_tn(branch[...], attended[here_rows, :]).astype(bf16)
    for index, (grad, out) in enumerate(((g_up, g_up_out), (g_down, g_down_out))):
        post.got(sibling_copies[index])

        def add_sibling(j, carried):
            rows = ds(j * BLOCK, BLOCK)
            g_sum[index, rows, :] = (
                g_sum[index, rows, :].astype(f32) + grad[rows, own_lanes].astype(f32)
            ).astype(bf16)
            return carried

        lax.fori_loop(0, width // BLOCK, add_sibling, 0)
        keep(g_sum.at[index], out)
    post.close()
    for copy in own_copies[4:]:
        copy.wait()


def first_half(fsdp_count, order, patches, grads, attn_proj, out_proj, up, down_t, *vectors):
    width = patches.shape[1]
    shape = jax.ShapeDtypeStruct
    vmem = pltpu.VMEM
    units = 2 * up.shape[1]
    all_units = 2 * patches.shape[0] // UNIT
    deep = up.shape[0]
    fold = lambda a: a.reshape(-1, UNIT, width)
    return pl.pallas_call(
        partial(first_kernel, fsdp_count),
        out_shape=(
            shape((OWN, 384), bf16),
            shape((KEYS, 384), bf16),
            shape((KEYS, 384), bf16),
            shape((OWN, 384), bf16),
            shape((OWN, width), bf16),
            shape((OWN, width), bf16),
            shape((4, width, 384), bf16),
            shape((width, width), bf16),
            shape((width, width), bf16),
            shape((8, OWN), f32),
            shape((OWN, 384), bf16),
            shape((HALF, width), f32),
            shape((HALF, width), f32),
            shape((HALF, width), bf16),
            shape((width, 384), bf16),
            shape((width, 384), bf16),
            shape((4, width), f32),
            shape((2, width), f32),
        ),
        in_specs=[SMEM, ANY, ANY, VMEM, VMEM, ANY, ANY] + [VMEM] * 8,
        out_specs=(ANY,) * 9 + (VMEM,) * 9,
        scratch_shapes=[
            pltpu.SMEM(order.shape[1:], jnp.int32),
            vmem((deep, width), bf16),
            vmem((8, width), f32),
            vmem((all_units, UNIT, width), bf16),
            vmem((all_units, UNIT, width), bf16),
            vmem((2, width, width), bf16),
            vmem((4, width, 384), bf16),
            vmem((width, 384), bf16),
            vmem((2, width, up.shape[1]), bf16),
            vmem((2, width, up.shape[1]), bf16),
            vmem((2, 8, width), f32),
            vmem((all_units, UNIT, width), bf16),
            vmem((KEYS, width), bf16),
            vmem((OWN, width), bf16),
            vmem((OWN, width), bf16),
            vmem((OWN, width), bf16),
            vmem((OWN, 384), bf16),
            vmem((KEYS, 384), bf16),
            vmem((KEYS, 384), bf16),
            vmem((384, KEYS), bf16),
            vmem((OWN, 384), bf16),
            vmem((128, OWN), f32),
            vmem((HALF, 384), bf16),
            vmem((TRUNK + 2 * BLOCK, OWN), f32),
            vmem((TRUNK + 2 * BLOCK, OWN), bf16),
            vmem((HALF, width), f32),
            vmem((HALF, width), f32),
            vmem((HALF, 1), f32),
            vmem((OWN, width), bf16),
            vmem((OWN, units), bf16),
            vmem((OWN, units), bf16),
            vmem((OWN, width), f32),
            vmem((2, HALF // 2, width), bf16),
            vmem((2, HALF // 2, width), bf16),
            vmem((HALF, width), bf16),
            vmem((HALF, 384), bf16),
            vmem((width, units), bf16),
            vmem((width, units), bf16),
            vmem((2, width, width), bf16),
            pltpu.SemaphoreType.DMA((16,)),
            pltpu.SemaphoreType.DMA((112,)),
            pltpu.SemaphoreType.DMA((112,)),
        ],
        compiler_params=pltpu.CompilerParams(collective_id=0, has_side_effects=True, vmem_limit_bytes=LIMIT),
        name="first_half",
    )(order, fold(patches), fold(grads), attn_proj, out_proj, up, down_t, *vectors)


class StripSum:
    def __init__(self, me, post, fsdp_count, held, from_core, buffers):
        self.me, self.post, self.count = me, post, fsdp_count
        self.held, self.from_core = held, from_core
        self.from_y, self.from_z, self.done = buffers
        self.half = held.shape[0] // fsdp_count // 2

    def from_sibling(self, src):
        self.core_copy = self.post.send(src, self.from_core, self.me.core)

    def add_sibling(self):
        self.post.got(self.core_copy)
        half = self.half

        def step(j, carried):
            rows = ds(j * half, half)
            self.held[rows, :] = (self.held[rows, :].astype(f32) + self.from_core[rows, :].astype(f32)).astype(bf16)
            return carried

        lax.fori_loop(0, 2 * self.count, step, 0)

    def strip(self, g, side):
        return ds(self.half * (2 * g + side), self.half)

    def over_y(self):
        me = self.me
        self.y_copies = [
            self.post.send(self.held.at[self.strip(g, 1 - me.c)], self.from_y.at[g], me.yp)
            for g in range(self.count)
        ]

    def over_z(self):
        me = self.me
        for copy in self.y_copies:
            self.post.got(copy)

        def step(g, carried):
            rows = self.strip(g, me.c)
            self.held[rows, :] = (self.held[rows, :].astype(f32) + self.from_y[g].astype(f32)).astype(bf16)
            return carried

        lax.fori_loop(0, self.count, step, 0)
        self.z_copies = [
            self.post.send(self.held.at[self.strip((me.f + i + 1) % self.count, me.c)], self.from_z.at[i], device)
            for i, device in enumerate(me.z)
        ]

    def over_z_first(self):
        me, deep = self.me, 2 * self.half
        self.z_copies = [
            self.post.send(self.held.at[ds(deep * ((me.f + i + 1) % self.count), deep)], self.from_z.at[i], device)
            for i, device in enumerate(me.z)
        ]

    def finish_z_first(self):
        me, deep = self.me, 2 * self.half
        for copy in self.z_copies:
            self.post.got(copy)
        total = self.held[ds(deep * me.f, deep), :].astype(f32)
        for i in range(self.count - 1):
            total = total + self.from_z[i].astype(f32)
        self.done[0] = total.astype(bf16)
        self.last = self.post.send(self.done.at[0], self.done.at[1], me.yp)

    def finish(self):
        me = self.me
        for copy in self.z_copies:
            self.post.got(copy)
        total = self.held[self.strip(me.f, me.c), :].astype(f32)
        for i in range(self.count - 1):
            total = total + self.from_z[i].astype(f32)
        self.done[me.c] = total.astype(bf16)
        self.last = self.post.send(self.done.at[me.c], self.done.at[me.c], me.yp)


def second_kernel(
    fsdp_count, q_in, k_in, v_in, att_in, low_in, x_in, wh_in, g_up, g_down,
    lse, da, middle_grad, mlp_own, mlp_send, g_out_own, g_out_send, mid_stats, up_stats, gain1,
    rows_out, up_out, rest_out, all_total, part_total,
    q, k, v, kt, attended, low_own, x_own, wh, up_own, down_own,
    delta, st, dpt, pt, dst, dk_acc, dv_acc, dq_t, dq, own_first, trunk, trunk_own, trunk_far, trunk_send, trunk_y, dkv_own,
    mlp_x, first_send, first_x, rows_own, out_core, out_sum, out_x, packed,
    from_core, from_y, from_z, done, deep_z, deep_done, stat_buf, stat_in, stat_z, local, ss, rs,
):
    me = Here(fsdp_count)
    f, c, x, core = me.f, me.c, me.x, me.k
    s = 2 * c + core
    pair = 2 * BLOCK
    units = HALF // UNIT
    width = x_in.shape[1]
    mine, far = HALF * x, HALF * (1 - x)
    here_rows, far_rows = ds(mine, HALF), ds(far, HALF)
    loads = []
    for src, held in (
        (g_up, up_own), (g_down, down_own), (k_in, k), (q_in, q), (v_in, v), (att_in, attended),
        (low_in, low_own), (x_in, x_own), (wh_in.at[pl.ds(0, 3)], wh),
    ):
        copy = pltpu.make_async_copy(src, held, local.at[len(loads)])
        copy.start()
        loads.append(copy)
    greet([me.core, me.xp, me.yp] + me.z)
    post = Post(ss, rs)
    mlp_copy = post.send(mlp_send, mlp_x, me.xp)
    buffers = [(from_y, from_z, done)] + [(None, deep_z.at[i], deep_done.at[i]) for i in range(2)]
    sums = [
        StripSum(me, post, fsdp_count, held, from_core, buffer)
        for held, buffer in zip((up_own, down_own, packed.at[core]), buffers)
    ]
    slab_own = pl.ds(pl.multiple_of(128 * core, 128), 128)
    slab_sibling = pl.ds(pl.multiple_of(128 * (1 - core), 128), 128)
    slab_both = pl.ds(256, 128)
    out_copies = []
    for i, src in enumerate((g_out_own, g_out_send)):
        for j, lanes in enumerate((slab_sibling, slab_both)):
            out_copies.append(post.send(src.at[:, lanes], out_core.at[i, j], me.core))
    for copy in loads[:2]:
        copy.wait()
    sums[0].over_y()
    sums[1].over_z_first()
    for copy in loads[2:6]:
        copy.wait()
    kt[...] = k[...].T
    product = (da[...].astype(f32) * attended[...].astype(f32)).T
    for h in range(6):
        delta[h : h + 1, :] = jnp.sum(product[h * HEAD_DIM : (h + 1) * HEAD_DIM], axis=0, keepdims=True)
    lane = lax.broadcasted_iota(jnp.int32, (OWN, 128), 1) // HEAD_DIM

    def head(h, carried):
        slab, part = h // 2, h % 2
        lanes = pl.ds(pl.multiple_of(slab * 128, 128), 128)
        q_slab, da_slab = q[:, lanes], da[:, lanes]
        q_part = jnp.where(lane == part, q_slab, jnp.zeros_like(q_slab))
        da_part = jnp.where(lane == part, da_slab, jnp.zeros_like(da_slab))
        st[0:TRUNK, :] = dot_nt(k[0:TRUNK, lanes], q_part)
        dpt[0:TRUNK, :] = dot_nt(v[0:TRUNK, lanes], da_part)
        for q_row, k_row, count in PIECES:
            cols, rows = slice(q_row, q_row + BLOCK), slice(TRUNK, TRUNK + count)
            st[rows, cols] = dot_nt(k[k_row : k_row + count, lanes], q_part[q_row : q_row + BLOCK])
            dpt[rows, cols] = dot_nt(v[k_row : k_row + count, lanes], da_part[q_row : q_row + BLOCK])
        log_total, row_delta = lse[pl.ds(h, 1), :], delta[pl.ds(h, 1), :]
        for j in range(OWN // BLOCK):
            cols = slice(j * BLOCK, (j + 1) * BLOCK)
            count = TRUNK + (0 if j < 2 else PIECES[j - 2][2])
            for r in range(0, count, BLOCK):
                weight = jnp.exp(st[r : r + BLOCK, cols] - log_total[:, cols])
                pt[r : r + BLOCK, cols] = weight.astype(bf16)
                dst[r : r + BLOCK, cols] = (
                    weight * (dpt[r : r + BLOCK, cols] - row_delta[:, cols])
                ).astype(bf16)
        dk_acc[0:TRUNK, :] += dot_nn(dst[0:TRUNK, :], q_part)
        dv_acc[0:TRUNK, :] += dot_nn(pt[0:TRUNK, :], da_part)
        head_rows = ds(h * HEAD_DIM, HEAD_DIM)
        dq_t[head_rows, :] = dot_nn(kt[head_rows, 0:TRUNK], dst[0:TRUNK, :])
        for q_row, k_row, count in PIECES:
            cols, rows = slice(q_row, q_row + BLOCK), slice(TRUNK, TRUNK + count)
            own = slice(k_row, k_row + count)
            dk_acc[own, :] += dot_nn(dst[rows, cols], q_part[q_row : q_row + BLOCK])
            dv_acc[own, :] += dot_nn(pt[rows, cols], da_part[q_row : q_row + BLOCK])
            dq_t[head_rows, cols] += dot_nn(kt[head_rows, own], dst[rows, cols])
        return carried

    chip_rows = lambda chip, side: ds(pair * (2 * chip + side), pair)
    trunk_copies, y_copies = [], []

    def slab_heads(slab):
        dk_acc[...] = jnp.zeros_like(dk_acc)
        dv_acc[...] = jnp.zeros_like(dv_acc)
        lax.fori_loop(2 * slab, 2 * slab + 2, head, 0)

    def trunk_out(slab):
        trunk[slab, 0] = dk_acc[0:TRUNK, :].astype(bf16)
        trunk[slab, 1] = dv_acc[0:TRUNK, :].astype(bf16)
        for i, total in enumerate((dk_acc, dv_acc)):
            lanes = slice(384 * i + 128 * slab, 384 * i + 128 * slab + 128)
            dkv_own[pair:, lanes] = total[TRUNK:, :].astype(bf16)
        trunk_copies.append(
            (
                post.send(trunk.at[slab, :, chip_rows(1 - c, 1 - core), :], trunk_far.at[slab], me.core),
                post.send(trunk.at[slab, :, chip_rows(c, 1 - core), :], trunk_own.at[slab], me.core),
            )
        )

    def trunk_over(slab):
        post.got(trunk_copies[slab][0])
        trunk_send[slab] = (
            trunk[slab, :, chip_rows(1 - c, core), :].astype(f32) + trunk_far[slab].astype(f32)
        ).astype(bf16)
        y_copies.append(post.send(trunk_send.at[slab], trunk_y.at[slab], me.yp))

    def trunk_in(slab):
        post.got(trunk_copies[slab][1])
        post.got(y_copies[slab])
        total = (
            trunk[slab, :, chip_rows(c, core), :].astype(f32)
            + trunk_own[slab].astype(f32)
            + trunk_y[slab].astype(f32)
        ).astype(bf16)
        for i in range(2):
            lanes = slice(384 * i + 128 * slab, 384 * i + 128 * slab + 128)
            dkv_own[0:pair, lanes] = total[i]

    slab_heads(0)
    trunk_out(0)
    for copy in out_copies:
        post.got(copy)
    for i, src in enumerate((g_out_own, g_out_send)):
        for j, lanes in enumerate((slab_own, slab_both)):
            out_sum[i, j] = (src[:, lanes].astype(f32) + out_core[i, j].astype(f32)).astype(bf16)
    out_copy = post.send(out_sum.at[1], out_x, me.xp)
    for copy in loads[6:]:
        copy.wait()
    trunk_over(0)
    slab_heads(1)
    trunk_out(1)
    post.got(mlp_copy)
    rows_own[0] = (mlp_own[...] + mlp_x[...].astype(f32)).astype(bf16).reshape(units, UNIT, width)
    beside = 2 * s + 1 - x
    beyond = 2 * (2 * (1 - c) + core) + x
    corner = 2 * (2 * (1 - c) + core) + 1 - x
    part = units // 2
    over_x, over_y, diagonal = {}, {}, {}

    def piece(index, owner, half):
        return rows_out.at[index, pl.ds(units * owner + part * half, part)]

    def own_piece(index, half):
        return rows_own.at[index, pl.ds(part * half, part)], piece(index, 2 * s + x, half)

    def spread_x(index, half):
        own, there = own_piece(index, half)
        over_x[index, half] = post.send(own, there, me.xp)
        post.send(own, there, me.core)
        copy = pltpu.make_async_copy(own, there, local.at[len(loads)])
        copy.start()
        loads.append(copy)

    def spread_y(index, half):
        own, there = own_piece(index, half)
        over_y[index, half] = post.send(own, there, me.yp)

    def pass_on(index, half):
        for copies, owner, onward in ((over_x, beside, me.yp), (over_y, beyond, me.xp)):
            post.got(copies[index, half])
            got = piece(index, owner, half)
            if (half == 0) == (onward is me.yp):
                diagonal[index, half] = post.send(got, got, onward)
            post.send(got, got, me.core)

    def corner_on(index):
        for half in range(2):
            post.got(diagonal[index, half])
            got = piece(index, corner, half)
            post.send(got, got, me.core)

    for half in range(2):
        spread_x(0, half)
    trunk_over(1)
    sums[0].over_z()
    slab_heads(2)
    trunk_out(2)
    dq[...] = (dq_t[...].T * HEAD_DIM ** (-0.5)).astype(bf16)
    trunk_over(2)
    for half in range(2):
        spread_y(0, half)
    for slab in range(3):
        trunk_in(slab)

    def first(rows):
        return (
            dot_nt(dq[rows, :], wh[0])
            + dot_nt(dkv_own[rows, 0:384], wh[1])
            + dot_nt(dkv_own[rows, 384:768], wh[2])
        )

    chunk = HALF // 2
    first_copies = []
    for i in range(2):
        first_send[i] = first(ds(far + chunk * i, chunk)).astype(bf16)
        first_copies.append(post.send(first_send.at[i], first_x.at[i], me.xp))
    own_first[...] = first(here_rows)
    post.got(out_copy)
    g_attn = [
        dot_tn(low_own[...], dq[...]),
        dot_tn(low_own[...], dkv_own[:, 0:384]),
        dot_tn(low_own[...], dkv_own[:, 384:768]),
    ]
    tails = []
    for j in (0, 1):
        for i in range(3):
            packed[j, :, 128 * i : 128 * i + 128] = g_attn[i][:, 128 * j : 128 * j + 128].astype(bf16)
        tail = [g[:, 256 + 64 * j : 320 + 64 * j] for g in g_attn]
        packed[j, :, 512:640] = jnp.concatenate(tail[0:2], axis=1).astype(bf16)
        packed[j, :, 640:768] = jnp.concatenate([tail[2], jnp.zeros_like(tail[2])], axis=1).astype(bf16)
    attn_stats = jnp.concatenate(
        [
            jnp.sum(dq[...].astype(f32), axis=0, keepdims=True),
            jnp.sum(dkv_own[:, 384:768].astype(f32), axis=0, keepdims=True),
        ],
        axis=1,
    )
    sums[2].from_sibling(packed.at[1 - core])
    def put_out():
        packed[core, :, 384:512] = (out_sum[0, 0].astype(f32) + out_x[0].astype(f32)).astype(bf16)
        last = out_sum[0, 1].astype(f32) + out_x[1].astype(f32)
        side = lax.broadcasted_iota(jnp.int32, last.shape, 1) // HEAD_DIM
        turned = jnp.concatenate([last[:, HEAD_DIM:], last[:, :HEAD_DIM]], axis=1)
        tail = jnp.where(core == 0, turned, last)
        packed[core, :, 640:768] = jnp.where(side == 0, packed[core, :, 640:768].astype(f32), tail).astype(bf16)

    for half in range(2):
        pass_on(0, half)
    n1_all, s1_all = row_norm(x_own[here_rows, :].astype(f32))
    first_total = [jnp.zeros((1, width), f32)] * 2
    for i in range(2):
        post.got(first_copies[i])
        rows = slice(chunk * i, chunk * i + chunk)
        first_grad = own_first[rows, :] + first_x[i].astype(f32)
        n1, s1 = n1_all[rows], s1_all[rows]
        grad = middle_grad[rows, :] + norm_back(first_grad, n1, s1, wide(gain1))
        rows_own[1, part * i : part * i + part] = grad.astype(bf16).reshape(part, UNIT, width)
        spread_x(1, i)
        spread_y(1, i)
        first_total = [
            a + jnp.sum(b, axis=0, keepdims=True) for a, b in zip(first_total, (first_grad * n1, first_grad))
        ]
    sums[2].add_sibling()
    put_out()
    sums[2].over_z_first()
    rows_mid, rows_up = mid_stats.shape[0], up_stats.shape[0]
    stat_buf[0:1, :], stat_buf[1:2, :] = first_total
    stat_buf[2 : 2 + rows_mid, :] = mid_stats[...]
    stat_buf[2 + rows_mid : 8, :] = jnp.zeros((6 - rows_mid, width), f32)
    stat_buf[8 : 8 + rows_up, :] = up_stats[...]
    stat_buf[8 + rows_up : 9 + rows_up, :] = attn_stats
    stat_buf[9 + rows_up : 16, :] = jnp.zeros((7 - rows_up, width), f32)
    level = lambda i: pl.ds(16 * i, 16)
    stat_copy = post.send(stat_buf.at[level(0)], stat_in.at[0], me.core)
    sums[0].finish()
    post.got(stat_copy)
    stat_buf[level(1), :] = stat_buf[level(0), :] + stat_in[0]
    stat_copy = post.send(stat_buf.at[level(1)], stat_in.at[1], me.yp)
    sums[1].finish_z_first()
    corner_on(0)
    post.got(stat_copy)
    stat_buf[level(2), :] = stat_buf[level(1), :] + stat_in[1]
    stat_copy = post.send(stat_buf.at[level(2)], stat_in.at[2], me.xp)
    pass_on(1, 0)
    post.got(stat_copy)
    stat_buf[48:56, :] = stat_buf[32:40, :] + stat_in[2, 0:8]
    stat_buf[56:64, :] = stat_buf[40:48, :]
    stat_z[f] = stat_buf[level(3), :]
    stat_copies = [post.send(stat_buf.at[level(3)], stat_z.at[f], device) for device in me.z]
    pass_on(1, 1)
    sums[2].finish_z_first()
    corner_on(1)
    for copy in stat_copies:
        post.got(copy)
    total = stat_z[0]
    for g in range(1, fsdp_count):
        total = total + stat_z[g]
    all_total[...] = total[0 : 2 + rows_mid]
    part_total[...] = total[8 : 9 + rows_up]
    for total in sums:
        post.got(total.last)
    up_out[...] = done[...]
    rest_out[...] = deep_done[...]
    post.close()
    for copy in loads[9:]:
        copy.wait()


def second_half(fsdp_count, row_count, *operands):
    shape = jax.ShapeDtypeStruct
    vmem = pltpu.VMEM
    width = operands[4].shape[1]
    rows = row_count
    tall = TRUNK + 2 * BLOCK
    pair = 2 * BLOCK
    deep = width // fsdp_count
    half = deep // 2
    return pl.pallas_call(
        partial(second_kernel, fsdp_count),
        out_shape=(
            shape((2, 2 * rows // UNIT, UNIT, width), bf16),
            shape((2, half, width), bf16),
            shape((2, 2, deep, width), bf16),
            shape((6, width), f32),
            shape((3, width), f32),
        ),
        in_specs=[ANY] * 9 + [VMEM] * 10,
        out_specs=(ANY,) + (VMEM,) * 4,
        scratch_shapes=[
            vmem((OWN, 384), bf16),
            vmem((KEYS, 384), bf16),
            vmem((KEYS, 384), bf16),
            vmem((384, KEYS), bf16),
            vmem((OWN, 384), bf16),
            vmem((OWN, width), bf16),
            vmem((OWN, width), bf16),
            vmem((3, width, 384), bf16),
            vmem((width, width), bf16),
            vmem((width, width), bf16),
            vmem((8, OWN), f32),
            vmem((tall, OWN), f32),
            vmem((tall, OWN), f32),
            vmem((tall, OWN), bf16),
            vmem((tall, OWN), bf16),
            vmem((KEYS, 128), f32),
            vmem((KEYS, 128), f32),
            vmem((384, OWN), f32),
            vmem((OWN, 384), bf16),
            vmem((HALF, width), f32),
            vmem((3, 2, TRUNK, 128), bf16),
            vmem((3, 2, pair, 128), bf16),
            vmem((3, 2, pair, 128), bf16),
            vmem((3, 2, pair, 128), bf16),
            vmem((3, 2, pair, 128), bf16),
            vmem((OWN, 768), bf16),
            vmem((HALF, width), bf16),
            vmem((2, HALF // 2, width), bf16),
            vmem((2, HALF // 2, width), bf16),
            vmem((2, HALF // UNIT, UNIT, width), bf16),
            vmem((2, 2, width, 128), bf16),
            vmem((2, 2, width, 128), bf16),
            vmem((2, width, 128), bf16),
            vmem((2, width, width), bf16),
            vmem((width, width), bf16),
            vmem((fsdp_count, half, width), bf16),
            vmem((fsdp_count - 1, half, width), bf16),
            vmem((2, half, width), bf16),
            vmem((2, fsdp_count - 1, deep, width), bf16),
            vmem((2, 2, deep, width), bf16),
            vmem((64, width), f32),
            vmem((3, 16, width), f32),
            vmem((fsdp_count, 16, width), f32),
            pltpu.SemaphoreType.DMA((16,)),
            pltpu.SemaphoreType.DMA((80,)),
            pltpu.SemaphoreType.DMA((80,)),
        ],
        compiler_params=pltpu.CompilerParams(collective_id=1, has_side_effects=True, vmem_limit_bytes=LIMIT),
        name="second_half",
    )(*operands)


def place_kernel(
    order, rows_all, up_sum, rest, all_total, part_total,
    result, patch_grad, gain1, shift1, grad_attn, attn_bias, grad_out, out_bias, gain2, shift2, grad_up, up_bias,
    grad_down_t, down_bias, patch_low, sems,
):
    own = result.shape[0] // BLOCK
    units = BLOCK // UNIT
    core = lax.axis_index("tensor") % 2
    copies = []
    for j in range(own):
        block = order[0, own * lax.axis_index("context") + j]
        branch, leaf = block - TRUNK_BLK, block - TRUNK_BLK - BRANCHES
        index = jnp.where(
            branch < 0,
            5 * (block // 2) + block % 2,
            jnp.where(leaf < 0, 5 * branch + 3, 5 * (leaf // 2) + 2 + 2 * (leaf % 2)),
        )
        to = pl.ds(j * units, units)
        for i, dest in enumerate((result, patch_low)):
            if i == 0:
                dest = result.reshape(own * units, UNIT, result.shape[1])
            copy = pltpu.make_async_copy(
                rows_all.at[i, pl.ds(index * units, units)], dest.at[to], sems.at[i, j]
            )
            copy.start()
            copies.append(copy)
    total = lambda i: all_total[i, :]
    gain1[...], shift1[...], gain2[...], shift2[...] = total(0), total(1), total(2), total(3)
    down_bias[...], out_bias[...] = total(4), total(5)
    up_bias[...] = part_total[core, :]
    for i in range(2):
        lanes = slice(384 * i, 384 * i + 384)
        row = part_total[2:3, lanes]
        first = jnp.where(core == 0, row[:, 0:128], row[:, 128:256])
        second = jnp.where(core == 0, row[:, 256:320], row[:, 320:384])
        attn_bias[i : i + 1, :] = jnp.concatenate([first, second], axis=1)
    grad_up[...] = up_sum[...].reshape(grad_up.shape).astype(f32)
    grad_down_t[...] = rest[0, 0].astype(f32) + rest[0, 1].astype(f32)
    attn = rest[1, 0].astype(f32) + rest[1, 1].astype(f32)
    tails = [attn[:, 512:576], attn[:, 576:640], attn[:, 640:704], attn[:, 704:768]]
    for i in range(3):
        grad_attn[i, :, 0:128] = attn[:, 128 * i : 128 * i + 128]
        grad_attn[i, :, 128:192] = tails[i]
    grad_out[...] = jnp.concatenate([attn[:, 384:512], tails[3]], axis=1).T
    for copy in copies:
        copy.wait()
    patch_grad[...] = patch_low[...].reshape(patch_grad.shape).astype(f32)


def place(order, row_count, rows_all, up_sum, rest, all_total, part_total):
    shape = jax.ShapeDtypeStruct
    width = rows_all.shape[3]
    deep = rest.shape[2]
    vector = shape((width,), f32)
    return pl.pallas_call(
        place_kernel,
        out_shape=(
            shape((row_count, width), bf16), shape((row_count, width), f32), vector, vector,
            shape((3, deep, 192), f32), shape((2, 192), f32), shape((192, deep), f32), vector, vector, vector,
            shape((deep, width), f32), vector, shape((deep, width), f32), vector,
        ),
        in_specs=[SMEM, ANY] + [VMEM] * 4,
        out_specs=(VMEM,) * 14,
        scratch_shapes=[
            pltpu.VMEM((row_count // UNIT, UNIT, width), bf16),
            pltpu.SemaphoreType.DMA((2, row_count // BLOCK)),
        ],
        compiler_params=pltpu.CompilerParams(vmem_limit_bytes=LIMIT),
        name="place",
    )(order, rows_all, up_sum, rest, all_total, part_total)


def tree_shards(
    fsdp_count, patches, out_grad, block_order, first_gain, first_shift, attn_proj, attn_bias, out_proj, out_bias,
    second_gain, second_shift, up_proj, up_bias, down_proj, down_bias,
):
    middle = first_half(
        fsdp_count, block_order, patches, out_grad, attn_proj, out_proj, up_proj, down_proj.T, up_bias, attn_bias,
        first_gain, first_shift, second_gain, second_shift, out_bias, down_bias,
    )
    sums = second_half(fsdp_count, patches.shape[0], *middle, first_gain)
    outputs = list(place(block_order, patches.shape[0], *sums))
    outputs[12] = outputs[12].T
    return tuple(outputs)


def solution(mesh):
    fits = mesh.shape["context"] * 2 == BRANCHES and mesh.shape["tensor"] == 4 and mesh.shape["fsdp"] == 4
    body = partial(tree_shards, mesh.shape["fsdp"]) if fits else shards
    return jax.shard_map(
        body,
        mesh=mesh,
        in_specs=(
            P(("fsdp", "context"), None),
            P(("fsdp", "context"), None),
            P("fsdp", None),
            P(),
            P(),
            P(None, "fsdp", "tensor"),
            P(None, "tensor"),
            P("tensor", "fsdp"),
            P(),
            P(),
            P(),
            P("fsdp", "tensor"),
            P("tensor"),
            P("tensor", "fsdp"),
            P(),
        ),
        out_specs=(
            P(("fsdp", "context"), None),
            P(("fsdp", "context"), None),
            P(),
            P(),
            P(None, "fsdp", "tensor"),
            P(None, "tensor"),
            P("tensor", "fsdp"),
            P(),
            P(),
            P(),
            P("fsdp", "tensor"),
            P("tensor"),
            P("tensor", "fsdp"),
            P(),
        ),
        check_vma=False,
    )
```

```python
from functools import partial

import jax
import jax.numpy as jnp
from jax import lax
from jax.experimental import pallas as pl
from jax.experimental.pallas import tpu as pltpu
from jax.sharding import PartitionSpec as P

HEAD_DIM = 64
BLOCK = 128
TRUNK_BLK = 8
BRANCHES = 4
LEAVES = 2
TREE_BLK = 20


epsilon = 1e-05
far_below = -1e30


def layer_norm(values, norm_gain, norm_shift):
    center = values - jnp.mean(values, axis=1, keepdims=True)
    inverse = lax.rsqrt(jnp.mean(center * center, axis=1, keepdims=True) + epsilon)
    normed = center * inverse
    return (normed * norm_gain + norm_shift, normed, inverse)


def norm_back(gradient, normed, inverse, norm_gain):
    scaled = gradient * norm_gain
    return inverse * (
        scaled
        - jnp.mean(scaled, axis=1, keepdims=True)
        - normed * jnp.mean(scaled * normed, axis=1, keepdims=True)
    )


def slot_labels(order_row):
    position = order_row % TREE_BLK
    return (order_row // TREE_BLK, jnp.where(position < TRUNK_BLK, 0, position - TRUNK_BLK + 1))


def spread_rows(values):
    return jnp.broadcast_to(values[:, None], (values.shape[0], BLOCK)).reshape(-1)


def row_labels(labels, first_slot, slot_count):
    return tuple(
        (
            spread_rows(lax.dynamic_slice_in_dim(label_table, first_slot, slot_count))
            for label_table in labels
        )
    )


def visible(query_labels, key_labels):
    query_tree, query_seg = query_labels
    key_tree, key_seg = key_labels
    parent = jnp.where(query_seg > BRANCHES, 1 + (query_seg - BRANCHES - 1) // LEAVES, 0)
    reaches = (
        (key_seg[None, :] == 0)
        | (key_seg[None, :] == query_seg[:, None])
        | (key_seg[None, :] == parent[:, None])
    )
    return (query_tree[:, None] == key_tree[None, :]) & reaches


def head_view(matrix):
    return matrix.reshape(matrix.shape[0], matrix.shape[1] // HEAD_DIM, HEAD_DIM)


def scores_of(query_heads, key_heads):
    return jnp.einsum(
        "qhd,khd->hqk", query_heads, key_heads, preferred_element_type=jnp.float32
    ) * HEAD_DIM ** (-0.5)


def weights_of(scores, log_total, allowed):
    return jnp.where(allowed[None], jnp.exp(scores - log_total[:, :, None]), 0.0)


def score_grads(query_heads, grad_heads, key_heads, value_heads, log_total, row_delta, allowed):
    weights = weights_of(scores_of(query_heads, key_heads), log_total, allowed)
    prob_grad = jnp.einsum(
        "qhd,khd->hqk", grad_heads, value_heads, preferred_element_type=jnp.float32
    )
    return (
        (weights * (prob_grad - row_delta[:, :, None])).astype(jnp.bfloat16),
        weights.astype(jnp.bfloat16),
    )


def shards(
    patches,
    out_grad,
    block_order,
    first_gain,
    first_shift,
    attn_proj,
    attn_bias,
    out_proj,
    out_bias,
    second_gain,
    second_shift,
    up_proj,
    up_bias,
    down_proj,
    down_bias,
):
    attn_full, out_full, up_full, down_full = (
        lax.all_gather(attn_proj, "fsdp", axis=1, tiled=True),
        lax.all_gather(out_proj, "fsdp", axis=1, tiled=True),
        lax.all_gather(up_proj, "fsdp", axis=0, tiled=True),
        lax.all_gather(down_proj, "fsdp", axis=1, tiled=True),
    )
    labels = slot_labels(block_order[0])
    row_count = patches.shape[0]
    own_slots = row_count // BLOCK
    query_labels = row_labels(labels, lax.axis_index("context") * own_slots, own_slots)
    head_width = attn_full.shape[2]
    head_count = head_width // HEAD_DIM
    key_block = 4 * BLOCK
    block_slots = key_block // BLOCK
    score_scale = HEAD_DIM ** (-0.5)
    inputs = patches.astype(jnp.float32)
    first_norm, first_normed, first_inverse = layer_norm(inputs, first_gain, first_shift)
    first_low = first_norm.astype(jnp.bfloat16)
    projected = jnp.einsum("rd,cde->cre", first_low, attn_full, preferred_element_type=jnp.float32)
    queries = (projected[0] + attn_bias[0]).astype(jnp.bfloat16)
    keys_low = projected[1].astype(jnp.bfloat16)
    values_low = (projected[2] + attn_bias[1]).astype(jnp.bfloat16)
    keys_all = lax.all_gather(
        jnp.concatenate([keys_low, values_low], axis=1), "context", axis=0, tiled=True
    )
    block_count = keys_all.shape[0] // key_block
    query_heads = head_view(queries)

    def key_piece(step_index):
        key_slab = lax.dynamic_slice_in_dim(keys_all, step_index * key_block, key_block, 0)
        allowed = visible(query_labels, row_labels(labels, step_index * block_slots, block_slots))
        return (head_view(key_slab[:, :head_width]), head_view(key_slab[:, head_width:]), allowed)

    def total_step(step_index, carried):
        running_top, running_sum = carried
        key_heads, value_heads, allowed = key_piece(step_index)
        masked = jnp.where(allowed[None], scores_of(query_heads, key_heads), far_below)
        new_top = jnp.maximum(running_top, jnp.max(masked, axis=2))
        kept_exp = jnp.where(allowed[None], jnp.exp(masked - new_top[:, :, None]), 0.0)
        return (new_top, running_sum * jnp.exp(running_top - new_top) + jnp.sum(kept_exp, axis=2))

    start_top = jnp.full((head_count, row_count), far_below, jnp.float32)
    running_top, running_sum = lax.fori_loop(
        0, block_count, total_step, (start_top, jnp.zeros((head_count, row_count), jnp.float32))
    )
    log_total = running_top + jnp.log(running_sum)

    def mix_step(step_index, mixed):
        key_heads, value_heads, allowed = key_piece(step_index)
        weights = weights_of(scores_of(query_heads, key_heads), log_total, allowed).astype(
            jnp.bfloat16
        )
        return mixed + jnp.einsum(
            "hqk,khd->qhd", weights, value_heads, preferred_element_type=jnp.float32
        )

    attended = lax.fori_loop(
        0, block_count, mix_step, jnp.zeros((row_count, head_count, HEAD_DIM), jnp.float32)
    )
    attended_low = attended.reshape(row_count, head_width).astype(jnp.bfloat16)
    attn_part = jnp.dot(attended_low, out_full, preferred_element_type=jnp.float32)
    middle = inputs + (lax.psum(attn_part, "tensor") + out_bias)
    second_norm, second_normed, second_inverse = layer_norm(middle, second_gain, second_shift)
    second_low = second_norm.astype(jnp.bfloat16)
    pre_act = jnp.dot(second_low, up_full, preferred_element_type=jnp.float32) + up_bias
    hidden, gelu_back = jax.vjp(partial(jax.nn.gelu, approximate=False), pre_act)
    hidden_low = hidden.astype(jnp.bfloat16)
    mlp_part = jnp.dot(hidden_low, down_full, preferred_element_type=jnp.float32)
    result = (
        middle + (lax.psum(mlp_part.astype(jnp.bfloat16), "tensor").astype(jnp.float32) + down_bias)
    ).astype(jnp.bfloat16)
    top_grad = out_grad.astype(jnp.float32)
    grad_down_bias = jnp.sum(top_grad, axis=0)
    grad_down = jnp.einsum("rf,rd->fd", hidden_low, out_grad, preferred_element_type=jnp.float32)
    hidden_grad = jnp.einsum("rd,fd->rf", out_grad, down_full, preferred_element_type=jnp.float32)
    pre_grad = gelu_back(hidden_grad)[0].astype(jnp.bfloat16)
    grad_up_bias = jnp.sum(pre_grad.astype(jnp.float32), axis=0)
    grad_up = jnp.einsum("rd,rf->df", second_low, pre_grad, preferred_element_type=jnp.float32)
    second_part = jnp.einsum("rf,df->rd", pre_grad, up_full, preferred_element_type=jnp.float32)
    second_grad = lax.psum(second_part, "tensor")
    grad_second_gain = jnp.sum(second_grad * second_normed, axis=0)
    grad_second_shift = jnp.sum(second_grad, axis=0)
    middle_grad = top_grad + norm_back(second_grad, second_normed, second_inverse, second_gain)
    branch_grad = middle_grad.astype(jnp.bfloat16)
    grad_out_bias = jnp.sum(branch_grad.astype(jnp.float32), axis=0)
    grad_out = jnp.einsum(
        "re,rd->ed", attended_low, branch_grad, preferred_element_type=jnp.float32
    )
    attended_grad = jnp.einsum(
        "rd,ed->re", branch_grad, out_full, preferred_element_type=jnp.float32
    ).astype(jnp.bfloat16)
    grad_heads = head_view(attended_grad)

    def delta_step(step_index, row_delta):
        key_heads, value_heads, allowed = key_piece(step_index)
        weights = weights_of(scores_of(query_heads, key_heads), log_total, allowed)
        prob_grad = jnp.einsum(
            "qhd,khd->hqk", grad_heads, value_heads, preferred_element_type=jnp.float32
        )
        return row_delta + jnp.sum(weights * prob_grad, axis=2)

    row_delta = lax.fori_loop(
        0, block_count, delta_step, jnp.zeros((head_count, row_count), jnp.float32)
    )
    query_start = jnp.zeros((row_count, head_count, HEAD_DIM), jnp.float32)

    def back_step(step_index, carried):
        query_acc, key_acc = carried
        key_heads, value_heads, allowed = key_piece(step_index)
        score_low, weights_low = score_grads(
            query_heads, grad_heads, key_heads, value_heads, log_total, row_delta, allowed
        )
        query_acc = query_acc + jnp.einsum(
            "hqk,khd->qhd", score_low, key_heads, preferred_element_type=jnp.float32
        )
        key_part = jnp.einsum(
            "hqk,qhd->khd", score_low, query_heads, preferred_element_type=jnp.float32
        )
        value_part = jnp.einsum(
            "hqk,qhd->khd", weights_low, grad_heads, preferred_element_type=jnp.float32
        )
        joined = jnp.concatenate(
            [key_part.reshape(key_block, head_width), value_part.reshape(key_block, head_width)],
            axis=1,
        )
        return (
            query_acc,
            lax.dynamic_update_slice_in_dim(key_acc, joined, step_index * key_block, 0),
        )

    key_start = jnp.zeros((keys_all.shape[0], 2 * head_width), jnp.float32)
    query_acc, key_acc = lax.fori_loop(0, block_count, back_step, (query_start, key_start))
    key_value_grad = lax.psum_scatter(key_acc, "context", scatter_dimension=0, tiled=True)
    query_grad = (query_acc.reshape(row_count, head_width) * score_scale).astype(jnp.bfloat16)
    key_grad = (key_value_grad[:, :head_width] * score_scale).astype(jnp.bfloat16)
    value_grad = key_value_grad[:, head_width:].astype(jnp.bfloat16)
    stacked = jnp.stack([query_grad, key_grad, value_grad])
    grad_attn_bias = jnp.stack(
        [
            jnp.sum(query_grad.astype(jnp.float32), axis=0),
            jnp.sum(value_grad.astype(jnp.float32), axis=0),
        ]
    )
    grad_attn = jnp.einsum("rd,cre->cde", first_low, stacked, preferred_element_type=jnp.float32)
    first_grad = lax.psum(
        jnp.einsum("cre,cde->rd", stacked, attn_full, preferred_element_type=jnp.float32), "tensor"
    )
    grad_first_gain = jnp.sum(first_grad * first_normed, axis=0)
    grad_first_shift = jnp.sum(first_grad, axis=0)
    patch_grad = middle_grad + norm_back(first_grad, first_normed, first_inverse, first_gain)
    wide_attn, wide_out, wide_up, wide_down = (
        lax.psum_scatter(grad_attn, ("fsdp", "context"), scatter_dimension=1, tiled=True),
        lax.psum_scatter(grad_out, ("fsdp", "context"), scatter_dimension=1, tiled=True),
        lax.psum_scatter(grad_up, ("fsdp", "context"), scatter_dimension=0, tiled=True),
        lax.psum_scatter(grad_down, ("fsdp", "context"), scatter_dimension=1, tiled=True),
    )
    grad_attn, grad_out, grad_up, grad_down = (
        lax.all_gather(wide_attn, "context", axis=1, tiled=True),
        lax.all_gather(wide_out, "context", axis=1, tiled=True),
        lax.all_gather(wide_up, "context", axis=0, tiled=True),
        lax.all_gather(wide_down, "context", axis=1, tiled=True),
    )
    small_grads = lax.psum(
        (
            grad_first_gain,
            grad_first_shift,
            grad_attn_bias,
            grad_out_bias,
            grad_second_gain,
            grad_second_shift,
            grad_up_bias,
            grad_down_bias,
        ),
        ("fsdp", "context"),
    )
    return (
        result,
        patch_grad,
        small_grads[0],
        small_grads[1],
        grad_attn,
        small_grads[2],
        grad_out,
        small_grads[3],
        small_grads[4],
        small_grads[5],
        grad_up,
        small_grads[6],
        grad_down,
        small_grads[7],
    )


bf16 = jnp.bfloat16
f32 = jnp.float32
VMEM = pl.BlockSpec(memory_space=pltpu.VMEM)
SMEM = pl.BlockSpec(memory_space=pltpu.SMEM)
ANY = pl.BlockSpec(memory_space=pl.ANY)
MESH = pl.DeviceIdType.MESH
LIMIT = 61 * 1024 * 1024


def dot_nn(a, b):
    return lax.dot_general(a, b, (((1,), (0,)), ((), ())), preferred_element_type=f32)


def dot_nt(a, b):
    return lax.dot_general(a, b, (((1,), (1,)), ((), ())), preferred_element_type=f32)


def dot_tn(a, b):
    return lax.dot_general(a, b, (((0,), (0,)), ((), ())), preferred_element_type=f32)


class Here:
    def __init__(self, fsdp_count):
        self.f = lax.axis_index("fsdp")
        self.c = lax.axis_index("context")
        self.t = lax.axis_index("tensor")
        self.x = self.t // 2
        self.k = self.t % 2
        self.core = (self.f, self.c, 2 * self.x + 1 - self.k)
        self.xp = (self.f, self.c, 2 * (1 - self.x) + self.k)
        self.yp = (self.f, 1 - self.c, self.t)
        self.z = [((self.f + i) % fsdp_count, self.c, self.t) for i in range(1, fsdp_count)]
        self.back = [(self.f + fsdp_count - i) % fsdp_count for i in range(1, fsdp_count)]


def greet(devices):
    barrier = pltpu.get_barrier_semaphore()
    for device in devices:
        pl.semaphore_signal(barrier, inc=1, device_id=device, device_id_type=MESH)
    pl.semaphore_wait(barrier, len(devices))


class Post:
    def __init__(self, send_sem, recv_sem):
        self.send_sem, self.recv_sem = send_sem, recv_sem
        self.sent, self.open = [], []

    def send(self, src, dst, device):
        index = len(self.sent)
        copy = pltpu.make_async_remote_copy(
            src_ref=src,
            dst_ref=dst,
            send_sem=self.send_sem.at[index],
            recv_sem=self.recv_sem.at[index],
            device_id=device,
            device_id_type=MESH,
        )
        copy.start()
        self.sent.append(copy)
        self.open.append((copy, device))
        return copy

    def got(self, copy):
        left = [entry for entry in self.open if entry[0] is not copy]
        if len(left) < len(self.open):
            copy.wait_recv()
        self.open = left

    def got_from(self, device):
        for copy, to in self.open:
            if to is device:
                self.got(copy)

    def close(self):
        for copy, _ in self.open:
            copy.wait_recv()
        for copy in self.sent:
            copy.wait_send()


def ds(start, size, step=16):
    return pl.ds(pl.multiple_of(start, step), size)


TRUNK = TRUNK_BLK * BLOCK
SUB = (1 + LEAVES) * BLOCK
KEYS = TRUNK + SUB
OWN = 2 * BLOCK + SUB
PIECES = (
    (2 * BLOCK, TRUNK, 2 * BLOCK),
    (3 * BLOCK, TRUNK + BLOCK, BLOCK),
    (4 * BLOCK, TRUNK + BLOCK, 2 * BLOCK),
)


def own_places(s):
    return [2 * s, 2 * s + 1, 12 + 2 * s, 8 + s, 13 + 2 * s]


def row_norm(values):
    center = values - jnp.mean(values, axis=1, keepdims=True)
    inverse = lax.rsqrt(jnp.mean(center * center, axis=1, keepdims=True) + epsilon)
    return center * inverse, inverse

HALF = OWN // 2
UNIT = 16


def wide(vector):
    return vector[...].reshape(1, -1)


def first_kernel(
    fsdp_count, order, patches, grads, attn_proj, out_proj, up, d_own, up_bias, attn_bias, gain1, shift1, gain2, shift2, out_bias, down_bias,
    q_out, k_out, v_out, att_out, low_out, x_out, wh_out, g_up_out, g_down_out,
    middle_grad_out, mlp_own_out, mlp_send_out, g_out_own_out, g_out_send_out,
    lse, da, stats, up_stats,
    middle_grad, mlp_own, mlp_send, g_out_own, g_out_send,
    where, a_own, bias, rows_all, grads_all, wa, wh, wo_x, wu, wd, bias_all,
    low_all, low, low_own, x_own, g_own, q, k, v, vt, attended, att_t, att_x, st, pt,
    middle, normed, inverse, low2, hidden, pre_grad, second, second_send, second_x, branch, da_send, g_up, g_down, g_sum,
    local, ss, rs,
):
    me = Here(fsdp_count)
    f, c, x, core, t = me.f, me.c, me.x, me.k, me.t
    s = 2 * c + core
    units = patches.shape[0]
    part = units // 4
    width = patches.shape[2]
    deep = up.shape[0]
    head_width = attn_proj.shape[2]
    own_copies = []

    def keep(src, dst):
        copy = pltpu.make_async_copy(src, dst, local.at[len(own_copies)])
        copy.start()
        own_copies.append(copy)

    keep(patches, rows_all.at[pl.ds(units * c, units)])
    keep(grads, grads_all.at[pl.ds(units * c, units)])
    keep(up, wu.at[core, ds(deep * f, deep)])
    keep(d_own, wd.at[core, ds(deep * f, deep)])
    greet([me.core, me.xp, me.yp] + me.z)
    post = Post(ss, rs)
    there = units * (1 - c)
    half = deep // 2
    strip, other_strip = half * c, half * (1 - c)

    def quarter(array, index, piece, count):
        size = part // count
        return array.at[pl.ds(there + part * index + size * piece, size)]

    def to_y(src, dst, piece, count):
        size = part // count
        return post.send(
            src.at[pl.ds(part * t + size * piece, size)],
            dst.at[pl.ds(units * c + part * t + size * piece, size)],
            me.yp,
        )

    def relay(piece, device):
        return post.send(piece, piece, device)

    third = deep // 3
    lone, other_lone = 2 * third * c, 2 * third * (1 - c)
    a_part = lambda source, row, count: wa.at[core, ds(deep * source + row, count)]
    pieces = 4
    patches_y = [to_y(patches, rows_all, i, pieces) for i in range(pieces)]
    a_own[:, 0:128] = attn_proj[0, :, 0:128]
    a_own[:, 128:256] = attn_proj[1, :, 0:128]
    a_own[:, 256:384] = attn_proj[2, :, 0:128]
    out_t = out_proj[...].T
    a_own[:, 384:512] = jnp.concatenate([attn_proj[0, :, 128:head_width], attn_proj[1, :, 128:head_width]], axis=1)
    a_own[:, 512:640] = jnp.concatenate([attn_proj[2, :, 128:head_width], out_t[:, 128:head_width]], axis=1)
    a_own[:, 640:768] = out_t[:, 0:128]
    bias[...] = jnp.zeros_like(bias)
    bias[0:1, :] = wide(up_bias)
    bias[1:3, 0:head_width] = attn_bias[...]
    a_z = [post.send(a_own.at[ds(lone, third)], a_part(f, lone, third), device) for device in me.z]
    post.send(a_own, wa.at[core, ds(deep * f, deep)], me.core)
    post.send(bias, bias_all.at[core], me.core)
    gain_row, shift_row = wide(gain1), wide(shift1)

    def norm_units(start, count):
        values = rows_all[pl.ds(start, count)].reshape(count * UNIT, width).astype(f32)
        normed_rows, _ = row_norm(values)
        low_rows = (normed_rows * gain_row + shift_row).astype(bf16)
        low_all[pl.ds(start, count)] = low_rows.reshape(count, UNIT, width)

    block_units = BLOCK // UNIT
    own_blocks = units // block_units

    def norm_own(j, carried):
        norm_units(units * c + block_units * j, block_units)
        return carried

    slots = order.shape[1]

    def find(place, carried):
        slot = jnp.int32(0)
        for j in range(slots):
            slot = jnp.where(order[0, j] == place, j, slot)
        where[place] = slot * block_units
        return carried

    lax.fori_loop(0, slots, find, 0)
    wa[core, ds(deep * f, deep), :] = a_own[...]
    bias_all[core] = bias[...]
    own_copies[0].wait()
    lax.fori_loop(0, own_blocks - pieces, norm_own, 0)
    size = part // pieces
    over = (t + 2) % 4
    beside, across = t + 1 - 2 * core, over + 1 - 2 * core
    patches_x, patches_core = [], []
    for i in range(pieces):
        post.got(patches_y[i])
        patches_x.append(relay(quarter(rows_all, t, i, pieces), me.xp))
        patches_core.append(relay(quarter(rows_all, t, i, pieces), me.core))
        norm_units(there + part * t + size * i, size)
        if i == 2:
            a_y = []
            for copy, source in zip(a_z, me.back):
                post.got(copy)
                a_y.append(relay(a_part(source, lone, third), me.yp))
                relay(a_part(source, lone, third), me.core)
            a_shared = [
                post.send(a_own.at[ds(third, third)], a_part(f, third, third), device) for device in me.z
            ]
        norm_own(own_blocks - pieces + i, 0)
    post.send(up, wu.at[core, ds(deep * f, deep)], me.core)
    post.send(d_own, wd.at[core, ds(deep * f, deep)], me.core)
    for i in range(pieces):
        post.got(patches_core[i])
        norm_units(there + part * beside + size * i, size)
    patches_core = []
    for i in range(pieces):
        post.got(patches_x[i])
        patches_core.append(relay(quarter(rows_all, over, i, pieces), me.core))
        norm_units(there + part * over + size * i, size)
    for copy, source in zip(a_shared, me.back):
        post.got(copy)
        relay(a_part(source, third, third), me.core)
    u_z = [
        post.send(up.at[ds(strip, half)], wu.at[core, ds(deep * f + strip, half)], device) for device in me.z
    ]
    for copy, source in zip(a_y, me.back):
        post.got(copy)
        relay(a_part(source, other_lone, third), me.core)
    grads_y = [to_y(grads, grads_all, i, 2) for i in range(2)]
    for i in range(pieces):
        post.got(patches_core[i])
        norm_units(there + part * across + size * i, size)

    def block_of(array, place):
        return array[pl.ds(where[place], block_units)].reshape(BLOCK, width)

    def trunk_step(j, carried):
        low[ds(j * BLOCK, BLOCK), :] = block_of(low_all, j)
        return carried

    lax.fori_loop(0, TRUNK_BLK, trunk_step, 0)
    places = own_places(s)
    for j in range(2, 5):
        low[TRUNK + (j - 2) * BLOCK : TRUNK + (j - 1) * BLOCK, :] = block_of(low_all, places[j])
    for j, place in enumerate(places):
        x_own[pl.ds(j * BLOCK, BLOCK), :] = block_of(rows_all, place)
    low_own[0 : 2 * BLOCK, :] = low[ds(2 * BLOCK * s, 2 * BLOCK), :]
    low_own[2 * BLOCK :, :] = low[TRUNK:, :]
    post.got_from(me.core)

    def assemble(i):
        slab = (0, 1, 2, 5)[i]
        wh[i, :, 0:128] = wa[0, :, 128 * slab : 128 * slab + 128]
        wh[i, :, 128:256] = wa[1, :, 128 * slab : 128 * slab + 128]
        start = 384 + 64 * i
        wh[i, :, 256:384] = jnp.concatenate(
            [wa[0, :, start : start + 64], wa[1, :, start : start + 64]], axis=1
        )

    for i in range(4):
        assemble(i)
    wo_quarter = width // 4
    wo_rows = ds(wo_quarter * (2 * c + core), wo_quarter)
    wo_copy = post.send(wh.at[3, wo_rows], wo_x.at[wo_rows], me.xp)
    keep(wh, wh_out)

    def heads_row(row):
        a, b = bias_all[0, row : row + 1, :], bias_all[1, row : row + 1, :]
        return jnp.concatenate([a[:, 0:128], b[:, 0:128], a[:, 128:192], b[:, 128:192]], axis=1)

    q[...] = ((dot_nn(low_own[...], wh[0]) + heads_row(1)).astype(bf16) * HEAD_DIM ** (-0.5)).astype(bf16)
    value_bias = heads_row(2)

    def project(j, carried):
        rows = ds(j * (KEYS // 2), KEYS // 2)
        k[rows, :] = dot_nn(low[rows, :], wh[1]).astype(bf16)
        v[rows, :] = (dot_nn(low[rows, :], wh[2]) + value_bias).astype(bf16)
        return carried

    lax.fori_loop(0, 2, project, 0)
    vt[...] = v[...].T
    for src, dst in ((q, q_out), (k, k_out), (v, v_out), (low_own, low_out), (x_own, x_out)):
        keep(src, dst)
    lane = lax.broadcasted_iota(jnp.int32, (OWN, 128), 1) // HEAD_DIM

    def head(h, carried):
        slab, side = h // 2, h % 2
        lanes = pl.ds(pl.multiple_of(slab * 128, 128), 128)
        own_q = q[:, lanes]
        q_part = jnp.where(lane == side, own_q, jnp.zeros_like(own_q))
        st[0:TRUNK, :] = dot_nt(k[0:TRUNK, lanes], q_part)
        for q_row, k_row, count in PIECES:
            st[TRUNK : TRUNK + count, q_row : q_row + BLOCK] = dot_nt(
                k[k_row : k_row + count, lanes], q_part[q_row : q_row + BLOCK]
            )
        tops, sums = [], []
        for j in range(OWN // BLOCK):
            cols = slice(j * BLOCK, (j + 1) * BLOCK)
            count = TRUNK + (0 if j < 2 else PIECES[j - 2][2])
            top = jnp.full((8, BLOCK), far_below, f32)
            for r in range(0, count, BLOCK):
                piece = st[r : r + BLOCK, cols].reshape(BLOCK // 8, 8, BLOCK)
                top = jnp.maximum(top, jnp.max(piece, axis=0))
            top = jnp.max(top, axis=0, keepdims=True)
            total = jnp.zeros((8, BLOCK), f32)
            for r in range(0, count, BLOCK):
                weight = jnp.exp(st[r : r + BLOCK, cols] - top)
                total = total + jnp.sum(weight.reshape(BLOCK // 8, 8, BLOCK), axis=0)
                pt[r : r + BLOCK, cols] = weight.astype(bf16)
            tops.append(top)
            sums.append(jnp.sum(total, axis=0, keepdims=True))
        total = jnp.concatenate(sums, axis=1)
        head_rows, side_rows = ds(h * HEAD_DIM, HEAD_DIM), ds(side * HEAD_DIM, HEAD_DIM)
        att_t[side_rows, :] = dot_nn(vt[head_rows, 0:TRUNK], pt[0:TRUNK, :])
        for q_row, k_row, count in PIECES:
            cols = slice(q_row, q_row + BLOCK)
            att_t[side_rows, cols] += dot_nn(
                vt[head_rows, k_row : k_row + count], pt[TRUNK : TRUNK + count, cols]
            )
        att_t[side_rows, :] = att_t[side_rows, :] / total
        lse[pl.ds(h, 1), :] = jnp.concatenate(tops, axis=1) + jnp.log(total)
        return carried

    mine, far = HALF * x, HALF * (1 - x)
    here_rows, far_rows = ds(mine, HALF), ds(far, HALF)
    att_copies = []

    def slab_heads(slab):
        lax.fori_loop(2 * slab, 2 * slab + 2, head, 0)
        lanes = pl.ds(128 * slab, 128)
        attended[:, lanes] = att_t[...].T.astype(bf16)
        att_copies.append(post.send(attended.at[far_rows, lanes], att_x.at[:, lanes], me.xp))

    def grads_on(i):
        post.got(grads_y[i])
        relay(quarter(grads_all, t, i, 2), me.core)
        return relay(quarter(grads_all, t, i, 2), me.xp)

    def strips_on(copies, array):
        passed = []
        for copy, source in zip(copies, me.back):
            post.got(copy)
            piece = array.at[core, ds(deep * source + strip, half)]
            passed.append(relay(piece, me.yp))
            relay(piece, me.core)
        return passed

    def strips_in(copies, array):
        for copy, source in zip(copies, me.back):
            post.got(copy)
            relay(array.at[core, ds(deep * source + other_strip, half)], me.core)

    d_part = lambda source, row: wd.at[core, ds(deep * source + row, third)]
    post.got(wo_copy)
    wo_y = relay(wo_x.at[wo_rows], me.yp)
    wo_core = [relay(wo_x.at[wo_rows], me.core)]
    grads_x = [grads_on(0)]
    slab_heads(0)
    grads_x.append(grads_on(1))
    slab_heads(1)
    u_y = strips_on(u_z, wu)
    d_lone = [post.send(d_own.at[ds(lone, third)], d_part(f, lone), device) for device in me.z]
    post.got(wo_y)
    wo_core.append(relay(wo_x.at[ds(wo_quarter * (2 * (1 - c) + core), wo_quarter)], me.core))
    slab_heads(2)
    keep(attended, att_out)
    middle[...] = (
        x_own[here_rows, :].astype(f32) + wide(out_bias) + dot_nt(attended[here_rows, :], wh[3])
    )
    d_y = []
    for copy, source in zip(d_lone, me.back):
        post.got(copy)
        d_y.append(relay(d_part(source, lone), me.yp))
        relay(d_part(source, lone), me.core)
    d_shared = [post.send(d_own.at[ds(third, third)], d_part(f, third), device) for device in me.z]
    for copy in wo_core + att_copies:
        post.got(copy)
    middle[...] += dot_nt(att_x[...], wo_x[...])
    n2, s2 = row_norm(middle[...])
    normed[...] = n2
    inverse[...] = s2
    low2[here_rows, :] = (n2 * wide(gain2) + wide(shift2)).astype(bf16)
    chunk = HALF // 2
    here_chunks = [ds(mine + chunk * i, chunk) for i in range(2)]
    far_chunks = [ds(far + chunk * i, chunk) for i in range(2)]
    low_copies = [post.send(low2.at[rows], low2.at[rows], me.xp) for rows in here_chunks]
    for i in range(2):
        post.got(grads_x[i])
        relay(quarter(grads_all, over, i, 2), me.core)
    strips_in(u_y, wu)
    for copy in own_copies[1:4]:
        copy.wait()
    post.got_from(me.core)
    for j, place in enumerate(places):
        g_own[pl.ds(j * BLOCK, BLOCK), :] = block_of(grads_all, place)
    tile = 256

    def tiles(step):
        def tile_step(j, carried):
            shard, lanes = j // 3, pl.ds(pl.multiple_of(j % 3 * tile, 128), tile)
            step(shard, lanes, pl.ds(pl.multiple_of(j * tile, 128), tile))
            return carried

        lax.fori_loop(0, 6, tile_step, 0)

    def forward(rows):
        def step(shard, lanes, out):
            pre = dot_nn(low2[rows, :], wu[shard, :, lanes]) + bias_all[shard, 0:1, lanes]
            below = 0.5 * (1.0 + lax.erf(pre * (2.0**-0.5)))
            density = jnp.exp(-0.5 * pre * pre) * (2.0 * jnp.pi) ** -0.5
            hidden[rows, out] = (pre * below).astype(bf16)
            pre_grad[rows, out] = (below + pre * density).astype(bf16)

        tiles(step)

    def backward(rows, count):
        second[rows, :] = jnp.zeros((count, width), f32)

        def step(shard, lanes, out):
            back = dot_nn(g_own[rows, :], wd[shard, :, lanes])
            low_back = (back * pre_grad[rows, out].astype(f32)).astype(bf16)
            pre_grad[rows, out] = low_back
            second[rows, :] += dot_nt(low_back, wu[shard, :, lanes])

        tiles(step)

    def mlp(rows):
        return dot_nt(hidden[rows, 0:width], wd[0]) + dot_nt(hidden[rows, width:], wd[1])

    own_lanes, sibling_lanes = (
        pl.ds(pl.multiple_of(width * side, 128), width) for side in (core, 1 - core)
    )
    sibling_copies = {}

    def weight_grad(index, left, right, grad):
        def step(shard, lanes, out):
            grad[:, out] = dot_tn(left[...], right[:, out]).astype(bf16)

        tiles(step)
        sibling_copies[index] = post.send(grad.at[:, sibling_lanes], g_sum.at[index], me.core)

    forward(here_rows)
    for i in range(2):
        post.got(low_copies[i])
        forward(far_chunks[i])
    weight_grad(1, g_own, hidden, g_down)
    for copies, row in ((d_shared, third), (d_y, other_lone)):
        for copy, source in zip(copies, me.back):
            post.got(copy)
            relay(d_part(source, row), me.core)
    post.got_from(me.core)
    second_copies = []
    for i in range(2):
        backward(far_chunks[i], chunk)
        second_send[i] = second[far_chunks[i], :].astype(bf16)
        second_copies.append(post.send(second_send.at[i], second_x.at[i], me.xp))
    backward(here_rows, HALF)

    weight_grad(0, low2, pre_grad, g_up)
    total = [jnp.zeros((1, width), f32)] * 4
    for i in range(2):
        rows = here_chunks[i]
        part_rows = slice(chunk * i, chunk * i + chunk)
        post.got(second_copies[i])
        second_grad = second[rows, :] + second_x[i].astype(f32)
        n2 = normed[part_rows, :]
        dy = g_own[rows, :].astype(f32)
        grad = dy + norm_back(second_grad, n2, inverse[part_rows, :], wide(gain2))
        middle_grad[part_rows, :] = grad
        low_grad = grad.astype(bf16)
        branch[part_rows, :] = low_grad
        da_send[part_rows, :] = dot_nn(low_grad, wo_x[...]).astype(bf16)
        post.send(da_send.at[pl.ds(chunk * i, chunk)], da.at[rows], me.xp)
        terms = (second_grad * n2, second_grad, dy, low_grad.astype(f32))
        total = [a + jnp.sum(b, axis=0, keepdims=True) for a, b in zip(total, terms)]
    for i in range(4):
        stats[i : i + 1, :] = total[i]
    up_stats[0:1, :] = jnp.sum(pre_grad[:, 0:width].astype(f32), axis=0, keepdims=True)
    up_stats[1:2, :] = jnp.sum(pre_grad[:, width:].astype(f32), axis=0, keepdims=True)
    mlp_send[...] = mlp(far_rows).astype(bf16)
    mlp_own[...] = middle[...] + mlp(here_rows) + wide(down_bias)
    for src, out in ((middle_grad, middle_grad_out), (mlp_own, mlp_own_out), (mlp_send, mlp_send_out)):
        keep(src, out)
    da[here_rows, :] = dot_nn(branch[...], wh[3]).astype(bf16)
    g_out_send[...] = dot_tn(branch[...], att_x[...]).astype(bf16)
    g_out_own[...] = dot_tn(branch[...], attended[here_rows, :]).astype(bf16)
    keep(g_out_send, g_out_send_out)
    keep(g_out_own, g_out_own_out)
    for index, (grad, out) in enumerate(((g_up, g_up_out), (g_down, g_down_out))):
        post.got(sibling_copies[index])

        def add_sibling(j, carried):
            rows = ds(j * BLOCK, BLOCK)
            g_sum[index, rows, :] = (
                g_sum[index, rows, :].astype(f32) + grad[rows, own_lanes].astype(f32)
            ).astype(bf16)
            return carried

        lax.fori_loop(0, width // BLOCK, add_sibling, 0)
        keep(g_sum.at[index], out)
    post.close()
    for copy in own_copies[4:]:
        copy.wait()


def first_half(fsdp_count, order, patches, grads, attn_proj, out_proj, up, down_t, *vectors):
    width = patches.shape[1]
    shape = jax.ShapeDtypeStruct
    vmem = pltpu.VMEM
    units = 2 * up.shape[1]
    all_units = 2 * patches.shape[0] // UNIT
    deep = up.shape[0]
    fold = lambda a: a.reshape(-1, UNIT, width)
    return pl.pallas_call(
        partial(first_kernel, fsdp_count),
        out_shape=(
            shape((OWN, 384), bf16),
            shape((KEYS, 384), bf16),
            shape((KEYS, 384), bf16),
            shape((OWN, 384), bf16),
            shape((OWN, width), bf16),
            shape((OWN, width), bf16),
            shape((4, width, 384), bf16),
            shape((width, width), bf16),
            shape((width, width), bf16),
            shape((HALF, width), f32),
            shape((HALF, width), f32),
            shape((HALF, width), bf16),
            shape((width, 384), bf16),
            shape((width, 384), bf16),
            shape((8, OWN), f32),
            shape((OWN, 384), bf16),
            shape((4, width), f32),
            shape((2, width), f32),
        ),
        in_specs=[SMEM, ANY, ANY, VMEM, VMEM, ANY, ANY] + [VMEM] * 8,
        out_specs=(ANY,) * 14 + (VMEM,) * 4,
        scratch_shapes=[
            vmem((HALF, width), f32),
            vmem((HALF, width), f32),
            vmem((HALF, width), bf16),
            vmem((width, 384), bf16),
            vmem((width, 384), bf16),
            pltpu.SMEM(order.shape[1:], jnp.int32),
            vmem((deep, width), bf16),
            vmem((8, width), f32),
            vmem((all_units, UNIT, width), bf16),
            vmem((all_units, UNIT, width), bf16),
            vmem((2, width, width), bf16),
            vmem((4, width, 384), bf16),
            vmem((width, 384), bf16),
            vmem((2, width, up.shape[1]), bf16),
            vmem((2, width, up.shape[1]), bf16),
            vmem((2, 8, width), f32),
            vmem((all_units, UNIT, width), bf16),
            vmem((KEYS, width), bf16),
            vmem((OWN, width), bf16),
            vmem((OWN, width), bf16),
            vmem((OWN, width), bf16),
            vmem((OWN, 384), bf16),
            vmem((KEYS, 384), bf16),
            vmem((KEYS, 384), bf16),
            vmem((384, KEYS), bf16),
            vmem((OWN, 384), bf16),
            vmem((128, OWN), f32),
            vmem((HALF, 384), bf16),
            vmem((TRUNK + 2 * BLOCK, OWN), f32),
            vmem((TRUNK + 2 * BLOCK, OWN), bf16),
            vmem((HALF, width), f32),
            vmem((HALF, width), f32),
            vmem((HALF, 1), f32),
            vmem((OWN, width), bf16),
            vmem((OWN, units), bf16),
            vmem((OWN, units), bf16),
            vmem((OWN, width), f32),
            vmem((2, HALF // 2, width), bf16),
            vmem((2, HALF // 2, width), bf16),
            vmem((HALF, width), bf16),
            vmem((HALF, 384), bf16),
            vmem((width, units), bf16),
            vmem((width, units), bf16),
            vmem((2, width, width), bf16),
            pltpu.SemaphoreType.DMA((24,)),
            pltpu.SemaphoreType.DMA((112,)),
            pltpu.SemaphoreType.DMA((112,)),
        ],
        compiler_params=pltpu.CompilerParams(collective_id=0, has_side_effects=True, vmem_limit_bytes=LIMIT),
        name="first_half",
    )(order, fold(patches), fold(grads), attn_proj, out_proj, up, down_t, *vectors)


class StripSum:
    def __init__(self, me, post, fsdp_count, held, from_core, buffers):
        self.me, self.post, self.count = me, post, fsdp_count
        self.held, self.from_core = held, from_core
        self.from_y, self.from_z, self.done = buffers
        self.half = held.shape[0] // fsdp_count // 2

    def from_sibling(self, src):
        self.core_copy = self.post.send(src, self.from_core, self.me.core)

    def add_sibling(self):
        self.post.got(self.core_copy)
        half = self.half

        def step(j, carried):
            rows = ds(j * half, half)
            self.held[rows, :] = (self.held[rows, :].astype(f32) + self.from_core[rows, :].astype(f32)).astype(bf16)
            return carried

        lax.fori_loop(0, 2 * self.count, step, 0)

    def strip(self, g, side):
        return ds(self.half * (2 * g + side), self.half)

    def over_y(self):
        me = self.me
        self.y_copies = [
            self.post.send(self.held.at[self.strip(g, 1 - me.c)], self.from_y.at[g], me.yp)
            for g in range(self.count)
        ]

    def over_z(self):
        me = self.me
        for copy in self.y_copies:
            self.post.got(copy)

        def step(g, carried):
            rows = self.strip(g, me.c)
            self.held[rows, :] = (self.held[rows, :].astype(f32) + self.from_y[g].astype(f32)).astype(bf16)
            return carried

        lax.fori_loop(0, self.count, step, 0)
        self.z_copies = [
            self.post.send(self.held.at[self.strip((me.f + i + 1) % self.count, me.c)], self.from_z.at[i], device)
            for i, device in enumerate(me.z)
        ]

    def over_z_first(self):
        me, deep = self.me, 2 * self.half
        self.z_copies = [
            self.post.send(self.held.at[ds(deep * ((me.f + i + 1) % self.count), deep)], self.from_z.at[i], device)
            for i, device in enumerate(me.z)
        ]

    def finish_z_first(self):
        me, deep = self.me, 2 * self.half
        for copy in self.z_copies:
            self.post.got(copy)
        total = self.held[ds(deep * me.f, deep), :].astype(f32)
        for i in range(self.count - 1):
            total = total + self.from_z[i].astype(f32)
        self.done[0] = total.astype(bf16)
        self.last = self.post.send(self.done.at[0], self.done.at[1], me.yp)

    def finish(self):
        me = self.me
        for copy in self.z_copies:
            self.post.got(copy)
        total = self.held[self.strip(me.f, me.c), :].astype(f32)
        for i in range(self.count - 1):
            total = total + self.from_z[i].astype(f32)
        self.done[me.c] = total.astype(bf16)
        self.last = self.post.send(self.done.at[me.c], self.done.at[me.c], me.yp)


def second_kernel(
    fsdp_count, q_in, k_in, v_in, att_in, low_in, x_in, wh_in, g_up, g_down,
    middle_grad_in, mlp_own_in, mlp_send, g_out_own_in, g_out_send_in, lse, da, mid_stats, up_stats, gain1,
    rows_out, up_out, rest_out, all_total, part_total,
    middle_grad, mlp_own, g_out_own, g_out_send, q, k, v, kt, attended, low_own, x_own, wh, up_own, down_own,
    delta, st, dpt, pt, dst, dk_acc, dv_acc, dq_t, dq, own_first, trunk, trunk_own, trunk_far, trunk_send, trunk_y, dkv_own,
    mlp_x, first_send, first_x, rows_own, out_core, out_sum, out_x, packed,
    from_core, from_y, from_z, done, deep_z, deep_done, stat_buf, stat_in, stat_z, local, ss, rs,
):
    me = Here(fsdp_count)
    f, c, x, core = me.f, me.c, me.x, me.k
    s = 2 * c + core
    pair = 2 * BLOCK
    units = HALF // UNIT
    width = x_in.shape[1]
    mine, far = HALF * x, HALF * (1 - x)
    here_rows, far_rows = ds(mine, HALF), ds(far, HALF)
    loads = []
    for src, held in (
        (g_up, up_own), (g_down, down_own), (k_in, k), (q_in, q), (v_in, v), (att_in, attended),
        (g_out_own_in, g_out_own), (g_out_send_in, g_out_send), (mlp_own_in, mlp_own),
        (low_in, low_own), (x_in, x_own), (middle_grad_in, middle_grad), (wh_in.at[pl.ds(0, 3)], wh),
    ):
        copy = pltpu.make_async_copy(src, held, local.at[len(loads)])
        copy.start()
        loads.append(copy)
    greet([me.core, me.xp, me.yp] + me.z)
    post = Post(ss, rs)
    mlp_copy = post.send(mlp_send, mlp_x, me.xp)
    buffers = [(from_y, from_z, done)] + [(None, deep_z.at[i], deep_done.at[i]) for i in range(2)]
    sums = [
        StripSum(me, post, fsdp_count, held, from_core, buffer)
        for held, buffer in zip((up_own, down_own, packed.at[core]), buffers)
    ]
    slab_own = pl.ds(pl.multiple_of(128 * core, 128), 128)
    slab_sibling = pl.ds(pl.multiple_of(128 * (1 - core), 128), 128)
    slab_both = pl.ds(256, 128)
    out_copies = []
    for i, src in enumerate((g_out_own_in, g_out_send_in)):
        for j, lanes in enumerate((slab_sibling, slab_both)):
            out_copies.append(post.send(src.at[:, lanes], out_core.at[i, j], me.core))
    for copy in loads[:2]:
        copy.wait()
    sums[0].over_y()
    sums[1].over_z_first()
    for copy in loads[2:6]:
        copy.wait()
    kt[...] = k[...].T
    product = (da[...].astype(f32) * attended[...].astype(f32)).T
    for h in range(6):
        delta[h : h + 1, :] = jnp.sum(product[h * HEAD_DIM : (h + 1) * HEAD_DIM], axis=0, keepdims=True)
    lane = lax.broadcasted_iota(jnp.int32, (OWN, 128), 1) // HEAD_DIM

    def head(h, carried):
        slab, part = h // 2, h % 2
        lanes = pl.ds(pl.multiple_of(slab * 128, 128), 128)
        q_slab, da_slab = q[:, lanes], da[:, lanes]
        q_part = jnp.where(lane == part, q_slab, jnp.zeros_like(q_slab))
        da_part = jnp.where(lane == part, da_slab, jnp.zeros_like(da_slab))
        st[0:TRUNK, :] = dot_nt(k[0:TRUNK, lanes], q_part)
        dpt[0:TRUNK, :] = dot_nt(v[0:TRUNK, lanes], da_part)
        for q_row, k_row, count in PIECES:
            cols, rows = slice(q_row, q_row + BLOCK), slice(TRUNK, TRUNK + count)
            st[rows, cols] = dot_nt(k[k_row : k_row + count, lanes], q_part[q_row : q_row + BLOCK])
            dpt[rows, cols] = dot_nt(v[k_row : k_row + count, lanes], da_part[q_row : q_row + BLOCK])
        log_total, row_delta = lse[pl.ds(h, 1), :], delta[pl.ds(h, 1), :]
        for j in range(OWN // BLOCK):
            cols = slice(j * BLOCK, (j + 1) * BLOCK)
            count = TRUNK + (0 if j < 2 else PIECES[j - 2][2])
            for r in range(0, count, BLOCK):
                weight = jnp.exp(st[r : r + BLOCK, cols] - log_total[:, cols])
                pt[r : r + BLOCK, cols] = weight.astype(bf16)
                dst[r : r + BLOCK, cols] = (
                    weight * (dpt[r : r + BLOCK, cols] - row_delta[:, cols])
                ).astype(bf16)
        dk_acc[0:TRUNK, :] += dot_nn(dst[0:TRUNK, :], q_part)
        dv_acc[0:TRUNK, :] += dot_nn(pt[0:TRUNK, :], da_part)
        head_rows = ds(h * HEAD_DIM, HEAD_DIM)
        dq_t[head_rows, :] = dot_nn(kt[head_rows, 0:TRUNK], dst[0:TRUNK, :])
        for q_row, k_row, count in PIECES:
            cols, rows = slice(q_row, q_row + BLOCK), slice(TRUNK, TRUNK + count)
            own = slice(k_row, k_row + count)
            dk_acc[own, :] += dot_nn(dst[rows, cols], q_part[q_row : q_row + BLOCK])
            dv_acc[own, :] += dot_nn(pt[rows, cols], da_part[q_row : q_row + BLOCK])
            dq_t[head_rows, cols] += dot_nn(kt[head_rows, own], dst[rows, cols])
        return carried

    chip_rows = lambda chip, side: ds(pair * (2 * chip + side), pair)
    trunk_copies, y_copies = [], []

    def slab_heads(slab):
        dk_acc[...] = jnp.zeros_like(dk_acc)
        dv_acc[...] = jnp.zeros_like(dv_acc)
        lax.fori_loop(2 * slab, 2 * slab + 2, head, 0)

    def trunk_out(slab):
        trunk[slab, 0] = dk_acc[0:TRUNK, :].astype(bf16)
        trunk[slab, 1] = dv_acc[0:TRUNK, :].astype(bf16)
        for i, total in enumerate((dk_acc, dv_acc)):
            lanes = slice(384 * i + 128 * slab, 384 * i + 128 * slab + 128)
            dkv_own[pair:, lanes] = total[TRUNK:, :].astype(bf16)
        trunk_copies.append(
            (
                post.send(trunk.at[slab, :, chip_rows(1 - c, 1 - core), :], trunk_far.at[slab], me.core),
                post.send(trunk.at[slab, :, chip_rows(c, 1 - core), :], trunk_own.at[slab], me.core),
            )
        )

    def trunk_over(slab):
        post.got(trunk_copies[slab][0])
        trunk_send[slab] = (
            trunk[slab, :, chip_rows(1 - c, core), :].astype(f32) + trunk_far[slab].astype(f32)
        ).astype(bf16)
        y_copies.append(post.send(trunk_send.at[slab], trunk_y.at[slab], me.yp))

    def trunk_in(slab):
        post.got(trunk_copies[slab][1])
        post.got(y_copies[slab])
        total = (
            trunk[slab, :, chip_rows(c, core), :].astype(f32)
            + trunk_own[slab].astype(f32)
            + trunk_y[slab].astype(f32)
        ).astype(bf16)
        for i in range(2):
            lanes = slice(384 * i + 128 * slab, 384 * i + 128 * slab + 128)
            dkv_own[0:pair, lanes] = total[i]

    slab_heads(0)
    trunk_out(0)
    for copy in loads[6:13]:
        copy.wait()
    for copy in out_copies:
        post.got(copy)
    for i, src in enumerate((g_out_own, g_out_send)):
        for j, lanes in enumerate((slab_own, slab_both)):
            out_sum[i, j] = (src[:, lanes].astype(f32) + out_core[i, j].astype(f32)).astype(bf16)
    out_copy = post.send(out_sum.at[1], out_x, me.xp)
    trunk_over(0)
    slab_heads(1)
    trunk_out(1)
    post.got(mlp_copy)
    rows_own[0] = (mlp_own[...] + mlp_x[...].astype(f32)).astype(bf16).reshape(units, UNIT, width)
    beside = 2 * s + 1 - x
    beyond = 2 * (2 * (1 - c) + core) + x
    corner = 2 * (2 * (1 - c) + core) + 1 - x
    part = units // 2
    over_x, over_y, diagonal = {}, {}, {}

    def piece(index, owner, half):
        return rows_out.at[index, pl.ds(units * owner + part * half, part)]

    def own_piece(index, half):
        return rows_own.at[index, pl.ds(part * half, part)], piece(index, 2 * s + x, half)

    def spread_x(index, half):
        own, there = own_piece(index, half)
        over_x[index, half] = post.send(own, there, me.xp)
        post.send(own, there, me.core)
        copy = pltpu.make_async_copy(own, there, local.at[len(loads)])
        copy.start()
        loads.append(copy)

    def spread_y(index, half):
        own, there = own_piece(index, half)
        over_y[index, half] = post.send(own, there, me.yp)

    def pass_on(index, half):
        for copies, owner, onward in ((over_x, beside, me.yp), (over_y, beyond, me.xp)):
            post.got(copies[index, half])
            got = piece(index, owner, half)
            if (half == 0) == (onward is me.yp):
                diagonal[index, half] = post.send(got, got, onward)
            post.send(got, got, me.core)

    def corner_on(index):
        for half in range(2):
            post.got(diagonal[index, half])
            got = piece(index, corner, half)
            post.send(got, got, me.core)

    for half in range(2):
        spread_x(0, half)
    trunk_over(1)
    sums[0].over_z()
    slab_heads(2)
    trunk_out(2)
    dq[...] = (dq_t[...].T * HEAD_DIM ** (-0.5)).astype(bf16)
    trunk_over(2)
    for half in range(2):
        spread_y(0, half)
    for slab in range(3):
        trunk_in(slab)

    def first(rows):
        return (
            dot_nt(dq[rows, :], wh[0])
            + dot_nt(dkv_own[rows, 0:384], wh[1])
            + dot_nt(dkv_own[rows, 384:768], wh[2])
        )

    chunk = HALF // 2
    first_copies = []
    for i in range(2):
        first_send[i] = first(ds(far + chunk * i, chunk)).astype(bf16)
        first_copies.append(post.send(first_send.at[i], first_x.at[i], me.xp))
    g_attn = [
        dot_tn(low_own[...], dq[...]),
        dot_tn(low_own[...], dkv_own[:, 0:384]),
        dot_tn(low_own[...], dkv_own[:, 384:768]),
    ]
    tails = []
    for j in (0, 1):
        for i in range(3):
            packed[j, :, 128 * i : 128 * i + 128] = g_attn[i][:, 128 * j : 128 * j + 128].astype(bf16)
        tail = [g[:, 256 + 64 * j : 320 + 64 * j] for g in g_attn]
        packed[j, :, 512:640] = jnp.concatenate(tail[0:2], axis=1).astype(bf16)
        packed[j, :, 640:768] = jnp.concatenate([tail[2], jnp.zeros_like(tail[2])], axis=1).astype(bf16)
    attn_stats = jnp.concatenate(
        [
            jnp.sum(dq[...].astype(f32), axis=0, keepdims=True),
            jnp.sum(dkv_own[:, 384:768].astype(f32), axis=0, keepdims=True),
        ],
        axis=1,
    )
    sums[2].from_sibling(packed.at[1 - core])
    def put_out():
        post.got(out_copy)
        packed[core, :, 384:512] = (out_sum[0, 0].astype(f32) + out_x[0].astype(f32)).astype(bf16)
        last = out_sum[0, 1].astype(f32) + out_x[1].astype(f32)
        side = lax.broadcasted_iota(jnp.int32, last.shape, 1) // HEAD_DIM
        turned = jnp.concatenate([last[:, HEAD_DIM:], last[:, :HEAD_DIM]], axis=1)
        tail = jnp.where(core == 0, turned, last)
        packed[core, :, 640:768] = jnp.where(side == 0, packed[core, :, 640:768].astype(f32), tail).astype(bf16)

    sums[2].add_sibling()
    put_out()
    sums[2].over_z_first()
    own_first[...] = first(here_rows)
    for half in range(2):
        pass_on(0, half)
    n1_all, s1_all = row_norm(x_own[here_rows, :].astype(f32))
    first_total = [jnp.zeros((1, width), f32)] * 2
    for i in range(2):
        post.got(first_copies[i])
        rows = slice(chunk * i, chunk * i + chunk)
        first_grad = own_first[rows, :] + first_x[i].astype(f32)
        n1, s1 = n1_all[rows], s1_all[rows]
        grad = middle_grad[rows, :] + norm_back(first_grad, n1, s1, wide(gain1))
        rows_own[1, part * i : part * i + part] = grad.astype(bf16).reshape(part, UNIT, width)
        spread_x(1, i)
        spread_y(1, i)
        first_total = [
            a + jnp.sum(b, axis=0, keepdims=True) for a, b in zip(first_total, (first_grad * n1, first_grad))
        ]
    rows_mid, rows_up = mid_stats.shape[0], up_stats.shape[0]
    stat_buf[0:1, :], stat_buf[1:2, :] = first_total
    stat_buf[2 : 2 + rows_mid, :] = mid_stats[...]
    stat_buf[2 + rows_mid : 8, :] = jnp.zeros((6 - rows_mid, width), f32)
    stat_buf[8 : 8 + rows_up, :] = up_stats[...]
    stat_buf[8 + rows_up : 9 + rows_up, :] = attn_stats
    stat_buf[9 + rows_up : 16, :] = jnp.zeros((7 - rows_up, width), f32)
    level = lambda i: pl.ds(16 * i, 16)
    stat_copy = post.send(stat_buf.at[level(0)], stat_in.at[0], me.core)
    sums[0].finish()
    post.got(stat_copy)
    stat_buf[level(1), :] = stat_buf[level(0), :] + stat_in[0]
    stat_copy = post.send(stat_buf.at[level(1)], stat_in.at[1], me.yp)
    sums[1].finish_z_first()
    corner_on(0)
    post.got(stat_copy)
    stat_buf[level(2), :] = stat_buf[level(1), :] + stat_in[1]
    stat_copy = post.send(stat_buf.at[level(2)], stat_in.at[2], me.xp)
    pass_on(1, 0)
    post.got(stat_copy)
    stat_buf[48:56, :] = stat_buf[32:40, :] + stat_in[2, 0:8]
    stat_buf[56:64, :] = stat_buf[40:48, :]
    stat_z[f] = stat_buf[level(3), :]
    stat_copies = [post.send(stat_buf.at[level(3)], stat_z.at[f], device) for device in me.z]
    pass_on(1, 1)
    sums[2].finish_z_first()
    corner_on(1)
    for copy in stat_copies:
        post.got(copy)
    total = stat_z[0]
    for g in range(1, fsdp_count):
        total = total + stat_z[g]
    all_total[...] = total[0 : 2 + rows_mid]
    part_total[...] = total[8 : 9 + rows_up]
    for total in sums:
        post.got(total.last)
    up_out[...] = done[...]
    rest_out[...] = deep_done[...]
    post.close()
    for copy in loads[13:]:
        copy.wait()


def second_half(fsdp_count, row_count, *operands):
    shape = jax.ShapeDtypeStruct
    vmem = pltpu.VMEM
    width = operands[4].shape[1]
    rows = row_count
    tall = TRUNK + 2 * BLOCK
    pair = 2 * BLOCK
    deep = width // fsdp_count
    half = deep // 2
    return pl.pallas_call(
        partial(second_kernel, fsdp_count),
        out_shape=(
            shape((2, 2 * rows // UNIT, UNIT, width), bf16),
            shape((2, half, width), bf16),
            shape((2, 2, deep, width), bf16),
            shape((6, width), f32),
            shape((3, width), f32),
        ),
        in_specs=[ANY] * 14 + [VMEM] * 5,
        out_specs=(ANY,) + (VMEM,) * 4,
        scratch_shapes=[
            vmem((HALF, width), f32),
            vmem((HALF, width), f32),
            vmem((width, 384), bf16),
            vmem((width, 384), bf16),
            vmem((OWN, 384), bf16),
            vmem((KEYS, 384), bf16),
            vmem((KEYS, 384), bf16),
            vmem((384, KEYS), bf16),
            vmem((OWN, 384), bf16),
            vmem((OWN, width), bf16),
            vmem((OWN, width), bf16),
            vmem((3, width, 384), bf16),
            vmem((width, width), bf16),
            vmem((width, width), bf16),
            vmem((8, OWN), f32),
            vmem((tall, OWN), f32),
            vmem((tall, OWN), f32),
            vmem((tall, OWN), bf16),
            vmem((tall, OWN), bf16),
            vmem((KEYS, 128), f32),
            vmem((KEYS, 128), f32),
            vmem((384, OWN), f32),
            vmem((OWN, 384), bf16),
            vmem((HALF, width), f32),
            vmem((3, 2, TRUNK, 128), bf16),
            vmem((3, 2, pair, 128), bf16),
            vmem((3, 2, pair, 128), bf16),
            vmem((3, 2, pair, 128), bf16),
            vmem((3, 2, pair, 128), bf16),
            vmem((OWN, 768), bf16),
            vmem((HALF, width), bf16),
            vmem((2, HALF // 2, width), bf16),
            vmem((2, HALF // 2, width), bf16),
            vmem((2, HALF // UNIT, UNIT, width), bf16),
            vmem((2, 2, width, 128), bf16),
            vmem((2, 2, width, 128), bf16),
            vmem((2, width, 128), bf16),
            vmem((2, width, width), bf16),
            vmem((width, width), bf16),
            vmem((fsdp_count, half, width), bf16),
            vmem((fsdp_count - 1, half, width), bf16),
            vmem((2, half, width), bf16),
            vmem((2, fsdp_count - 1, deep, width), bf16),
            vmem((2, 2, deep, width), bf16),
            vmem((64, width), f32),
            vmem((3, 16, width), f32),
            vmem((fsdp_count, 16, width), f32),
            pltpu.SemaphoreType.DMA((20,)),
            pltpu.SemaphoreType.DMA((80,)),
            pltpu.SemaphoreType.DMA((80,)),
        ],
        compiler_params=pltpu.CompilerParams(collective_id=1, has_side_effects=True, vmem_limit_bytes=LIMIT),
        name="second_half",
    )(*operands)


def place_kernel(
    order, rows_all, up_sum, rest, all_total, part_total,
    result, patch_grad, gain1, shift1, grad_attn, attn_bias, grad_out, out_bias, gain2, shift2, grad_up, up_bias,
    grad_down_t, down_bias, result_low, patch_low, patch_wide, sems, out_sems,
):
    units = BLOCK // UNIT
    own = result.shape[0] // units
    core = lax.axis_index("tensor") % 2
    copies = []
    for j in range(own):
        block = order[0, own * lax.axis_index("context") + j]
        branch, leaf = block - TRUNK_BLK, block - TRUNK_BLK - BRANCHES
        index = jnp.where(
            branch < 0,
            5 * (block // 2) + block % 2,
            jnp.where(leaf < 0, 5 * branch + 3, 5 * (leaf // 2) + 2 + 2 * (leaf % 2)),
        )
        to = pl.ds(j * units, units)
        for i, dest in enumerate((result_low, patch_low)):
            copy = pltpu.make_async_copy(
                rows_all.at[i, pl.ds(index * units, units)], dest.at[to], sems.at[i, j]
            )
            copy.start()
            copies.append(copy)
    total = lambda i: all_total[i, :]
    gain1[...], shift1[...], gain2[...], shift2[...] = total(0), total(1), total(2), total(3)
    down_bias[...], out_bias[...] = total(4), total(5)
    up_bias[...] = part_total[core, :]
    for i in range(2):
        lanes = slice(384 * i, 384 * i + 384)
        row = part_total[2:3, lanes]
        first = jnp.where(core == 0, row[:, 0:128], row[:, 128:256])
        second = jnp.where(core == 0, row[:, 256:320], row[:, 320:384])
        attn_bias[i : i + 1, :] = jnp.concatenate([first, second], axis=1)
    grad_up[...] = up_sum[...].reshape(grad_up.shape).astype(f32)
    grad_down_t[...] = rest[0, 0].astype(f32) + rest[0, 1].astype(f32)
    attn = rest[1, 0].astype(f32) + rest[1, 1].astype(f32)
    tails = [attn[:, 512:576], attn[:, 576:640], attn[:, 640:704], attn[:, 704:768]]
    for i in range(3):
        grad_attn[i, :, 0:128] = attn[:, 128 * i : 128 * i + 128]
        grad_attn[i, :, 128:192] = tails[i]
    grad_out[...] = jnp.concatenate([attn[:, 384:512], tails[3]], axis=1).T
    out = []
    for j in range(own):
        block = pl.ds(j * units, units)
        copies[2 * j].wait()
        copies[2 * j + 1].wait()
        patch_wide[block] = patch_low[block].astype(f32)
        for i, (src, dest) in enumerate(((result_low, result), (patch_wide, patch_grad))):
            copy = pltpu.make_async_copy(src.at[block], dest.at[block], out_sems.at[i, j])
            copy.start()
            out.append(copy)
    for copy in out:
        copy.wait()


def place(order, row_count, rows_all, up_sum, rest, all_total, part_total):
    shape = jax.ShapeDtypeStruct
    width = rows_all.shape[3]
    deep = rest.shape[2]
    vector = shape((width,), f32)
    return pl.pallas_call(
        place_kernel,
        out_shape=(
            shape((row_count // UNIT, UNIT, width), bf16), shape((row_count // UNIT, UNIT, width), f32), vector, vector,
            shape((3, deep, 192), f32), shape((2, 192), f32), shape((192, deep), f32), vector, vector, vector,
            shape((deep, width), f32), vector, shape((deep, width), f32), vector,
        ),
        in_specs=[SMEM, ANY] + [VMEM] * 4,
        out_specs=(ANY,) * 2 + (VMEM,) * 12,
        scratch_shapes=[
            pltpu.VMEM((row_count // UNIT, UNIT, width), bf16),
            pltpu.VMEM((row_count // UNIT, UNIT, width), bf16),
            pltpu.VMEM((row_count // UNIT, UNIT, width), f32),
            pltpu.SemaphoreType.DMA((2, row_count // BLOCK)),
            pltpu.SemaphoreType.DMA((2, row_count // BLOCK)),
        ],
        compiler_params=pltpu.CompilerParams(vmem_limit_bytes=LIMIT),
        name="place",
    )(order, rows_all, up_sum, rest, all_total, part_total)


def tree_shards(
    fsdp_count, patches, out_grad, block_order, first_gain, first_shift, attn_proj, attn_bias, out_proj, out_bias,
    second_gain, second_shift, up_proj, up_bias, down_proj, down_bias,
):
    middle = first_half(
        fsdp_count, block_order, patches, out_grad, attn_proj, out_proj, up_proj, down_proj.T, up_bias, attn_bias,
        first_gain, first_shift, second_gain, second_shift, out_bias, down_bias,
    )
    sums = second_half(fsdp_count, patches.shape[0], *middle, first_gain)
    outputs = list(place(block_order, patches.shape[0], *sums))
    outputs[0], outputs[1] = (rows.reshape(patches.shape) for rows in outputs[:2])
    outputs[12] = outputs[12].T
    return tuple(outputs)


def solution(mesh):
    fits = mesh.shape["context"] * 2 == BRANCHES and mesh.shape["tensor"] == 4 and mesh.shape["fsdp"] == 4
    body = partial(tree_shards, mesh.shape["fsdp"]) if fits else shards
    return jax.shard_map(
        body,
        mesh=mesh,
        in_specs=(
            P(("fsdp", "context"), None),
            P(("fsdp", "context"), None),
            P("fsdp", None),
            P(),
            P(),
            P(None, "fsdp", "tensor"),
            P(None, "tensor"),
            P("tensor", "fsdp"),
            P(),
            P(),
            P(),
            P("fsdp", "tensor"),
            P("tensor"),
            P("tensor", "fsdp"),
            P(),
        ),
        out_specs=(
            P(("fsdp", "context"), None),
            P(("fsdp", "context"), None),
            P(),
            P(),
            P(None, "fsdp", "tensor"),
            P(None, "tensor"),
            P("tensor", "fsdp"),
            P(),
            P(),
            P(),
            P("fsdp", "tensor"),
            P("tensor"),
            P("tensor", "fsdp"),
            P(),
        ),
        check_vma=False,
    )
```

```python
from functools import partial

import jax
import jax.numpy as jnp
from jax import lax
from jax.experimental import pallas as pl
from jax.experimental.pallas import tpu as pltpu
from jax.sharding import PartitionSpec as P

HEAD_DIM = 64
BLOCK = 128
TRUNK_BLK = 8
BRANCHES = 4
LEAVES = 2
TREE_BLK = 20


epsilon = 1e-05
far_below = -1e30


def layer_norm(values, norm_gain, norm_shift):
    center = values - jnp.mean(values, axis=1, keepdims=True)
    inverse = lax.rsqrt(jnp.mean(center * center, axis=1, keepdims=True) + epsilon)
    normed = center * inverse
    return (normed * norm_gain + norm_shift, normed, inverse)


def norm_back(gradient, normed, inverse, norm_gain):
    scaled = gradient * norm_gain
    return inverse * (
        scaled
        - jnp.mean(scaled, axis=1, keepdims=True)
        - normed * jnp.mean(scaled * normed, axis=1, keepdims=True)
    )


def slot_labels(order_row):
    position = order_row % TREE_BLK
    return (order_row // TREE_BLK, jnp.where(position < TRUNK_BLK, 0, position - TRUNK_BLK + 1))


def spread_rows(values):
    return jnp.broadcast_to(values[:, None], (values.shape[0], BLOCK)).reshape(-1)


def row_labels(labels, first_slot, slot_count):
    return tuple(
        (
            spread_rows(lax.dynamic_slice_in_dim(label_table, first_slot, slot_count))
            for label_table in labels
        )
    )


def visible(query_labels, key_labels):
    query_tree, query_seg = query_labels
    key_tree, key_seg = key_labels
    parent = jnp.where(query_seg > BRANCHES, 1 + (query_seg - BRANCHES - 1) // LEAVES, 0)
    reaches = (
        (key_seg[None, :] == 0)
        | (key_seg[None, :] == query_seg[:, None])
        | (key_seg[None, :] == parent[:, None])
    )
    return (query_tree[:, None] == key_tree[None, :]) & reaches


def head_view(matrix):
    return matrix.reshape(matrix.shape[0], matrix.shape[1] // HEAD_DIM, HEAD_DIM)


def scores_of(query_heads, key_heads):
    return jnp.einsum(
        "qhd,khd->hqk", query_heads, key_heads, preferred_element_type=jnp.float32
    ) * HEAD_DIM ** (-0.5)


def weights_of(scores, log_total, allowed):
    return jnp.where(allowed[None], jnp.exp(scores - log_total[:, :, None]), 0.0)


def score_grads(query_heads, grad_heads, key_heads, value_heads, log_total, row_delta, allowed):
    weights = weights_of(scores_of(query_heads, key_heads), log_total, allowed)
    prob_grad = jnp.einsum(
        "qhd,khd->hqk", grad_heads, value_heads, preferred_element_type=jnp.float32
    )
    return (
        (weights * (prob_grad - row_delta[:, :, None])).astype(jnp.bfloat16),
        weights.astype(jnp.bfloat16),
    )


def shards(
    patches,
    out_grad,
    block_order,
    first_gain,
    first_shift,
    attn_proj,
    attn_bias,
    out_proj,
    out_bias,
    second_gain,
    second_shift,
    up_proj,
    up_bias,
    down_proj,
    down_bias,
):
    attn_full, out_full, up_full, down_full = (
        lax.all_gather(attn_proj, "fsdp", axis=1, tiled=True),
        lax.all_gather(out_proj, "fsdp", axis=1, tiled=True),
        lax.all_gather(up_proj, "fsdp", axis=0, tiled=True),
        lax.all_gather(down_proj, "fsdp", axis=1, tiled=True),
    )
    labels = slot_labels(block_order[0])
    row_count = patches.shape[0]
    own_slots = row_count // BLOCK
    query_labels = row_labels(labels, lax.axis_index("context") * own_slots, own_slots)
    head_width = attn_full.shape[2]
    head_count = head_width // HEAD_DIM
    key_block = 4 * BLOCK
    block_slots = key_block // BLOCK
    score_scale = HEAD_DIM ** (-0.5)
    inputs = patches.astype(jnp.float32)
    first_norm, first_normed, first_inverse = layer_norm(inputs, first_gain, first_shift)
    first_low = first_norm.astype(jnp.bfloat16)
    projected = jnp.einsum("rd,cde->cre", first_low, attn_full, preferred_element_type=jnp.float32)
    queries = (projected[0] + attn_bias[0]).astype(jnp.bfloat16)
    keys_low = projected[1].astype(jnp.bfloat16)
    values_low = (projected[2] + attn_bias[1]).astype(jnp.bfloat16)
    keys_all = lax.all_gather(
        jnp.concatenate([keys_low, values_low], axis=1), "context", axis=0, tiled=True
    )
    block_count = keys_all.shape[0] // key_block
    query_heads = head_view(queries)

    def key_piece(step_index):
        key_slab = lax.dynamic_slice_in_dim(keys_all, step_index * key_block, key_block, 0)
        allowed = visible(query_labels, row_labels(labels, step_index * block_slots, block_slots))
        return (head_view(key_slab[:, :head_width]), head_view(key_slab[:, head_width:]), allowed)

    def total_step(step_index, carried):
        running_top, running_sum = carried
        key_heads, value_heads, allowed = key_piece(step_index)
        masked = jnp.where(allowed[None], scores_of(query_heads, key_heads), far_below)
        new_top = jnp.maximum(running_top, jnp.max(masked, axis=2))
        kept_exp = jnp.where(allowed[None], jnp.exp(masked - new_top[:, :, None]), 0.0)
        return (new_top, running_sum * jnp.exp(running_top - new_top) + jnp.sum(kept_exp, axis=2))

    start_top = jnp.full((head_count, row_count), far_below, jnp.float32)
    running_top, running_sum = lax.fori_loop(
        0, block_count, total_step, (start_top, jnp.zeros((head_count, row_count), jnp.float32))
    )
    log_total = running_top + jnp.log(running_sum)

    def mix_step(step_index, mixed):
        key_heads, value_heads, allowed = key_piece(step_index)
        weights = weights_of(scores_of(query_heads, key_heads), log_total, allowed).astype(
            jnp.bfloat16
        )
        return mixed + jnp.einsum(
            "hqk,khd->qhd", weights, value_heads, preferred_element_type=jnp.float32
        )

    attended = lax.fori_loop(
        0, block_count, mix_step, jnp.zeros((row_count, head_count, HEAD_DIM), jnp.float32)
    )
    attended_low = attended.reshape(row_count, head_width).astype(jnp.bfloat16)
    attn_part = jnp.dot(attended_low, out_full, preferred_element_type=jnp.float32)
    middle = inputs + (lax.psum(attn_part, "tensor") + out_bias)
    second_norm, second_normed, second_inverse = layer_norm(middle, second_gain, second_shift)
    second_low = second_norm.astype(jnp.bfloat16)
    pre_act = jnp.dot(second_low, up_full, preferred_element_type=jnp.float32) + up_bias
    hidden, gelu_back = jax.vjp(partial(jax.nn.gelu, approximate=False), pre_act)
    hidden_low = hidden.astype(jnp.bfloat16)
    mlp_part = jnp.dot(hidden_low, down_full, preferred_element_type=jnp.float32)
    result = (
        middle + (lax.psum(mlp_part.astype(jnp.bfloat16), "tensor").astype(jnp.float32) + down_bias)
    ).astype(jnp.bfloat16)
    top_grad = out_grad.astype(jnp.float32)
    grad_down_bias = jnp.sum(top_grad, axis=0)
    grad_down = jnp.einsum("rf,rd->fd", hidden_low, out_grad, preferred_element_type=jnp.float32)
    hidden_grad = jnp.einsum("rd,fd->rf", out_grad, down_full, preferred_element_type=jnp.float32)
    pre_grad = gelu_back(hidden_grad)[0].astype(jnp.bfloat16)
    grad_up_bias = jnp.sum(pre_grad.astype(jnp.float32), axis=0)
    grad_up = jnp.einsum("rd,rf->df", second_low, pre_grad, preferred_element_type=jnp.float32)
    second_part = jnp.einsum("rf,df->rd", pre_grad, up_full, preferred_element_type=jnp.float32)
    second_grad = lax.psum(second_part, "tensor")
    grad_second_gain = jnp.sum(second_grad * second_normed, axis=0)
    grad_second_shift = jnp.sum(second_grad, axis=0)
    middle_grad = top_grad + norm_back(second_grad, second_normed, second_inverse, second_gain)
    branch_grad = middle_grad.astype(jnp.bfloat16)
    grad_out_bias = jnp.sum(branch_grad.astype(jnp.float32), axis=0)
    grad_out = jnp.einsum(
        "re,rd->ed", attended_low, branch_grad, preferred_element_type=jnp.float32
    )
    attended_grad = jnp.einsum(
        "rd,ed->re", branch_grad, out_full, preferred_element_type=jnp.float32
    ).astype(jnp.bfloat16)
    grad_heads = head_view(attended_grad)

    def delta_step(step_index, row_delta):
        key_heads, value_heads, allowed = key_piece(step_index)
        weights = weights_of(scores_of(query_heads, key_heads), log_total, allowed)
        prob_grad = jnp.einsum(
            "qhd,khd->hqk", grad_heads, value_heads, preferred_element_type=jnp.float32
        )
        return row_delta + jnp.sum(weights * prob_grad, axis=2)

    row_delta = lax.fori_loop(
        0, block_count, delta_step, jnp.zeros((head_count, row_count), jnp.float32)
    )
    query_start = jnp.zeros((row_count, head_count, HEAD_DIM), jnp.float32)

    def back_step(step_index, carried):
        query_acc, key_acc = carried
        key_heads, value_heads, allowed = key_piece(step_index)
        score_low, weights_low = score_grads(
            query_heads, grad_heads, key_heads, value_heads, log_total, row_delta, allowed
        )
        query_acc = query_acc + jnp.einsum(
            "hqk,khd->qhd", score_low, key_heads, preferred_element_type=jnp.float32
        )
        key_part = jnp.einsum(
            "hqk,qhd->khd", score_low, query_heads, preferred_element_type=jnp.float32
        )
        value_part = jnp.einsum(
            "hqk,qhd->khd", weights_low, grad_heads, preferred_element_type=jnp.float32
        )
        joined = jnp.concatenate(
            [key_part.reshape(key_block, head_width), value_part.reshape(key_block, head_width)],
            axis=1,
        )
        return (
            query_acc,
            lax.dynamic_update_slice_in_dim(key_acc, joined, step_index * key_block, 0),
        )

    key_start = jnp.zeros((keys_all.shape[0], 2 * head_width), jnp.float32)
    query_acc, key_acc = lax.fori_loop(0, block_count, back_step, (query_start, key_start))
    key_value_grad = lax.psum_scatter(key_acc, "context", scatter_dimension=0, tiled=True)
    query_grad = (query_acc.reshape(row_count, head_width) * score_scale).astype(jnp.bfloat16)
    key_grad = (key_value_grad[:, :head_width] * score_scale).astype(jnp.bfloat16)
    value_grad = key_value_grad[:, head_width:].astype(jnp.bfloat16)
    stacked = jnp.stack([query_grad, key_grad, value_grad])
    grad_attn_bias = jnp.stack(
        [
            jnp.sum(query_grad.astype(jnp.float32), axis=0),
            jnp.sum(value_grad.astype(jnp.float32), axis=0),
        ]
    )
    grad_attn = jnp.einsum("rd,cre->cde", first_low, stacked, preferred_element_type=jnp.float32)
    first_grad = lax.psum(
        jnp.einsum("cre,cde->rd", stacked, attn_full, preferred_element_type=jnp.float32), "tensor"
    )
    grad_first_gain = jnp.sum(first_grad * first_normed, axis=0)
    grad_first_shift = jnp.sum(first_grad, axis=0)
    patch_grad = middle_grad + norm_back(first_grad, first_normed, first_inverse, first_gain)
    wide_attn, wide_out, wide_up, wide_down = (
        lax.psum_scatter(grad_attn, ("fsdp", "context"), scatter_dimension=1, tiled=True),
        lax.psum_scatter(grad_out, ("fsdp", "context"), scatter_dimension=1, tiled=True),
        lax.psum_scatter(grad_up, ("fsdp", "context"), scatter_dimension=0, tiled=True),
        lax.psum_scatter(grad_down, ("fsdp", "context"), scatter_dimension=1, tiled=True),
    )
    grad_attn, grad_out, grad_up, grad_down = (
        lax.all_gather(wide_attn, "context", axis=1, tiled=True),
        lax.all_gather(wide_out, "context", axis=1, tiled=True),
        lax.all_gather(wide_up, "context", axis=0, tiled=True),
        lax.all_gather(wide_down, "context", axis=1, tiled=True),
    )
    small_grads = lax.psum(
        (
            grad_first_gain,
            grad_first_shift,
            grad_attn_bias,
            grad_out_bias,
            grad_second_gain,
            grad_second_shift,
            grad_up_bias,
            grad_down_bias,
        ),
        ("fsdp", "context"),
    )
    return (
        result,
        patch_grad,
        small_grads[0],
        small_grads[1],
        grad_attn,
        small_grads[2],
        grad_out,
        small_grads[3],
        small_grads[4],
        small_grads[5],
        grad_up,
        small_grads[6],
        grad_down,
        small_grads[7],
    )


bf16 = jnp.bfloat16
f32 = jnp.float32
VMEM = pl.BlockSpec(memory_space=pltpu.VMEM)
SMEM = pl.BlockSpec(memory_space=pltpu.SMEM)
ANY = pl.BlockSpec(memory_space=pl.ANY)
MESH = pl.DeviceIdType.MESH
LIMIT = 61 * 1024 * 1024


def dot_nn(a, b):
    return lax.dot_general(a, b, (((1,), (0,)), ((), ())), preferred_element_type=f32)


def dot_nt(a, b):
    return lax.dot_general(a, b, (((1,), (1,)), ((), ())), preferred_element_type=f32)


def dot_tn(a, b):
    return lax.dot_general(a, b, (((0,), (0,)), ((), ())), preferred_element_type=f32)


class Here:
    def __init__(self, fsdp_count):
        self.f = lax.axis_index("fsdp")
        self.c = lax.axis_index("context")
        self.t = lax.axis_index("tensor")
        self.x = self.t // 2
        self.k = self.t % 2
        self.core = (self.f, self.c, 2 * self.x + 1 - self.k)
        self.xp = (self.f, self.c, 2 * (1 - self.x) + self.k)
        self.yp = (self.f, 1 - self.c, self.t)
        self.z = [((self.f + i) % fsdp_count, self.c, self.t) for i in range(1, fsdp_count)]
        self.back = [(self.f + fsdp_count - i) % fsdp_count for i in range(1, fsdp_count)]


def greet(devices):
    barrier = pltpu.get_barrier_semaphore()
    for device in devices:
        pl.semaphore_signal(barrier, inc=1, device_id=device, device_id_type=MESH)
    pl.semaphore_wait(barrier, len(devices))


class Post:
    def __init__(self, send_sem, recv_sem):
        self.send_sem, self.recv_sem = send_sem, recv_sem
        self.sent, self.open = [], []

    def send(self, src, dst, device):
        index = len(self.sent)
        copy = pltpu.make_async_remote_copy(
            src_ref=src,
            dst_ref=dst,
            send_sem=self.send_sem.at[index],
            recv_sem=self.recv_sem.at[index],
            device_id=device,
            device_id_type=MESH,
        )
        copy.start()
        self.sent.append(copy)
        self.open.append((copy, device))
        return copy

    def got(self, copy):
        left = [entry for entry in self.open if entry[0] is not copy]
        if len(left) < len(self.open):
            copy.wait_recv()
        self.open = left

    def got_from(self, device):
        for copy, to in self.open:
            if to is device:
                self.got(copy)

    def close(self):
        for copy, _ in self.open:
            copy.wait_recv()
        for copy in self.sent:
            copy.wait_send()


def ds(start, size, step=16):
    return pl.ds(pl.multiple_of(start, step), size)


TRUNK = TRUNK_BLK * BLOCK
SUB = (1 + LEAVES) * BLOCK
KEYS = TRUNK + SUB
OWN = 2 * BLOCK + SUB
PIECES = (
    (2 * BLOCK, TRUNK, 2 * BLOCK),
    (3 * BLOCK, TRUNK + BLOCK, BLOCK),
    (4 * BLOCK, TRUNK + BLOCK, 2 * BLOCK),
)


def own_places(s):
    return [2 * s, 2 * s + 1, 12 + 2 * s, 8 + s, 13 + 2 * s]


def row_norm(values):
    center = values - jnp.mean(values, axis=1, keepdims=True)
    inverse = lax.rsqrt(jnp.mean(center * center, axis=1, keepdims=True) + epsilon)
    return center * inverse, inverse

HALF = OWN // 2
UNIT = 16


def wide(vector):
    return vector[...].reshape(1, -1)


def first_kernel(
    fsdp_count, order, patches, grads, attn_proj, out_proj, up, d_own, up_bias, attn_bias, gain1, shift1, gain2, shift2, out_bias, down_bias,
    q_out, k_out, v_out, att_out, low_out, x_out, wh_out, g_up_out, g_down_out,
    middle_grad_out, mlp_own_out, mlp_send_out, g_out_own_out, g_out_send_out,
    lse, da, stats, up_stats,
    middle_grad, mlp_own, mlp_send, g_out_own, g_out_send,
    where, a_own, bias, rows_all, grads_all, wa, wh, wo_x, wu, wd, bias_all,
    low_all, low, low_own, x_own, g_own, q, k, v, vt, attended, att_t, att_x, st, pt,
    middle, normed, inverse, low2, hidden, pre_grad, second, second_send, second_x, branch, da_send, g_up, g_down, g_sum,
    local, ss, rs,
):
    me = Here(fsdp_count)
    f, c, x, core, t = me.f, me.c, me.x, me.k, me.t
    s = 2 * c + core
    units = patches.shape[0]
    part = units // 4
    width = patches.shape[2]
    deep = up.shape[0]
    head_width = attn_proj.shape[2]
    own_copies = []

    def keep(src, dst):
        copy = pltpu.make_async_copy(src, dst, local.at[len(own_copies)])
        copy.start()
        own_copies.append(copy)

    keep(patches, rows_all.at[pl.ds(units * c, units)])
    keep(grads, grads_all.at[pl.ds(units * c, units)])
    keep(up, wu.at[core, ds(deep * f, deep)])
    keep(d_own, wd.at[core, ds(deep * f, deep)])
    greet([me.core, me.xp, me.yp] + me.z)
    post = Post(ss, rs)
    there = units * (1 - c)
    half = deep // 2
    strip, other_strip = half * c, half * (1 - c)

    def quarter(array, index, piece, count):
        size = part // count
        return array.at[pl.ds(there + part * index + size * piece, size)]

    def to_y(src, dst, piece, count):
        size = part // count
        return post.send(
            src.at[pl.ds(part * t + size * piece, size)],
            dst.at[pl.ds(units * c + part * t + size * piece, size)],
            me.yp,
        )

    def relay(piece, device):
        return post.send(piece, piece, device)

    third = deep // 3
    lone, other_lone = 2 * third * c, 2 * third * (1 - c)
    a_part = lambda source, row, count: wa.at[core, ds(deep * source + row, count)]
    pieces = 4
    patches_y = [to_y(patches, rows_all, i, pieces) for i in range(pieces)]
    a_own[:, 0:128] = attn_proj[0, :, 0:128]
    a_own[:, 128:256] = attn_proj[1, :, 0:128]
    a_own[:, 256:384] = attn_proj[2, :, 0:128]
    out_t = out_proj[...].T
    a_own[:, 384:512] = jnp.concatenate([attn_proj[0, :, 128:head_width], attn_proj[1, :, 128:head_width]], axis=1)
    a_own[:, 512:640] = jnp.concatenate([attn_proj[2, :, 128:head_width], out_t[:, 128:head_width]], axis=1)
    a_own[:, 640:768] = out_t[:, 0:128]
    bias[...] = jnp.zeros_like(bias)
    bias[0:1, :] = wide(up_bias)
    bias[1:3, 0:head_width] = attn_bias[...]
    a_z = [post.send(a_own.at[ds(lone, third)], a_part(f, lone, third), device) for device in me.z]
    post.send(a_own, wa.at[core, ds(deep * f, deep)], me.core)
    post.send(bias, bias_all.at[core], me.core)
    gain_row, shift_row = wide(gain1), wide(shift1)

    def norm_units(start, count):
        values = rows_all[pl.ds(start, count)].reshape(count * UNIT, width).astype(f32)
        normed_rows, _ = row_norm(values)
        low_rows = (normed_rows * gain_row + shift_row).astype(bf16)
        low_all[pl.ds(start, count)] = low_rows.reshape(count, UNIT, width)

    block_units = BLOCK // UNIT
    own_blocks = units // block_units

    def norm_own(j, carried):
        norm_units(units * c + block_units * j, block_units)
        return carried

    slots = order.shape[1]

    def find(place, carried):
        slot = jnp.int32(0)
        for j in range(slots):
            slot = jnp.where(order[0, j] == place, j, slot)
        where[place] = slot * block_units
        return carried

    lax.fori_loop(0, slots, find, 0)
    wa[core, ds(deep * f, deep), :] = a_own[...]
    bias_all[core] = bias[...]
    own_copies[0].wait()
    lax.fori_loop(0, own_blocks - pieces, norm_own, 0)
    size = part // pieces
    over = (t + 2) % 4
    beside, across = t + 1 - 2 * core, over + 1 - 2 * core
    patches_x, patches_core = [], []
    for i in range(pieces):
        post.got(patches_y[i])
        patches_x.append(relay(quarter(rows_all, t, i, pieces), me.xp))
        patches_core.append(relay(quarter(rows_all, t, i, pieces), me.core))
        norm_units(there + part * t + size * i, size)
        if i == 2:
            a_y = []
            for copy, source in zip(a_z, me.back):
                post.got(copy)
                a_y.append(relay(a_part(source, lone, third), me.yp))
                relay(a_part(source, lone, third), me.core)
            a_shared = [
                post.send(a_own.at[ds(third, third)], a_part(f, third, third), device) for device in me.z
            ]
        norm_own(own_blocks - pieces + i, 0)
    post.send(up, wu.at[core, ds(deep * f, deep)], me.core)
    post.send(d_own, wd.at[core, ds(deep * f, deep)], me.core)
    for i in range(pieces):
        post.got(patches_core[i])
        norm_units(there + part * beside + size * i, size)
    patches_core = []
    for i in range(pieces):
        post.got(patches_x[i])
        patches_core.append(relay(quarter(rows_all, over, i, pieces), me.core))
        norm_units(there + part * over + size * i, size)
    for copy, source in zip(a_shared, me.back):
        post.got(copy)
        relay(a_part(source, third, third), me.core)
    u_z = [
        post.send(up.at[ds(strip, half)], wu.at[core, ds(deep * f + strip, half)], device) for device in me.z
    ]
    for copy, source in zip(a_y, me.back):
        post.got(copy)
        relay(a_part(source, other_lone, third), me.core)
    grads_y = [to_y(grads, grads_all, i, 2) for i in range(2)]
    for i in range(pieces):
        post.got(patches_core[i])
        norm_units(there + part * across + size * i, size)

    def block_of(array, place):
        return array[pl.ds(where[place], block_units)].reshape(BLOCK, width)

    def trunk_step(j, carried):
        low[ds(j * BLOCK, BLOCK), :] = block_of(low_all, j)
        return carried

    lax.fori_loop(0, TRUNK_BLK, trunk_step, 0)
    places = own_places(s)
    for j in range(2, 5):
        low[TRUNK + (j - 2) * BLOCK : TRUNK + (j - 1) * BLOCK, :] = block_of(low_all, places[j])
    for j, place in enumerate(places):
        x_own[pl.ds(j * BLOCK, BLOCK), :] = block_of(rows_all, place)
    low_own[0 : 2 * BLOCK, :] = low[ds(2 * BLOCK * s, 2 * BLOCK), :]
    low_own[2 * BLOCK :, :] = low[TRUNK:, :]
    post.got_from(me.core)

    def assemble(i):
        slab = (0, 1, 2, 5)[i]
        wh[i, :, 0:128] = wa[0, :, 128 * slab : 128 * slab + 128]
        wh[i, :, 128:256] = wa[1, :, 128 * slab : 128 * slab + 128]
        start = 384 + 64 * i
        wh[i, :, 256:384] = jnp.concatenate(
            [wa[0, :, start : start + 64], wa[1, :, start : start + 64]], axis=1
        )

    for i in range(4):
        assemble(i)
    wo_quarter = width // 4
    wo_rows = ds(wo_quarter * (2 * c + core), wo_quarter)
    wo_copy = post.send(wh.at[3, wo_rows], wo_x.at[wo_rows], me.xp)
    keep(wh, wh_out)

    def heads_row(row):
        a, b = bias_all[0, row : row + 1, :], bias_all[1, row : row + 1, :]
        return jnp.concatenate([a[:, 0:128], b[:, 0:128], a[:, 128:192], b[:, 128:192]], axis=1)

    q[...] = ((dot_nn(low_own[...], wh[0]) + heads_row(1)).astype(bf16) * HEAD_DIM ** (-0.5)).astype(bf16)
    value_bias = heads_row(2)

    def project(j, carried):
        rows = ds(j * (KEYS // 2), KEYS // 2)
        k[rows, :] = dot_nn(low[rows, :], wh[1]).astype(bf16)
        v[rows, :] = (dot_nn(low[rows, :], wh[2]) + value_bias).astype(bf16)
        return carried

    lax.fori_loop(0, 2, project, 0)
    vt[...] = v[...].T
    for src, dst in ((q, q_out), (k, k_out), (v, v_out), (low_own, low_out), (x_own, x_out)):
        keep(src, dst)
    lane = lax.broadcasted_iota(jnp.int32, (OWN, 128), 1) // HEAD_DIM

    def head(h, carried):
        slab, side = h // 2, h % 2
        lanes = pl.ds(pl.multiple_of(slab * 128, 128), 128)
        own_q = q[:, lanes]
        q_part = jnp.where(lane == side, own_q, jnp.zeros_like(own_q))
        st[0:TRUNK, :] = dot_nt(k[0:TRUNK, lanes], q_part)
        for q_row, k_row, count in PIECES:
            st[TRUNK : TRUNK + count, q_row : q_row + BLOCK] = dot_nt(
                k[k_row : k_row + count, lanes], q_part[q_row : q_row + BLOCK]
            )
        tops, sums = [], []
        for j in range(OWN // BLOCK):
            cols = slice(j * BLOCK, (j + 1) * BLOCK)
            count = TRUNK + (0 if j < 2 else PIECES[j - 2][2])
            top = jnp.full((8, BLOCK), far_below, f32)
            for r in range(0, count, BLOCK):
                piece = st[r : r + BLOCK, cols].reshape(BLOCK // 8, 8, BLOCK)
                top = jnp.maximum(top, jnp.max(piece, axis=0))
            top = jnp.max(top, axis=0, keepdims=True)
            total = jnp.zeros((8, BLOCK), f32)
            for r in range(0, count, BLOCK):
                weight = jnp.exp(st[r : r + BLOCK, cols] - top)
                total = total + jnp.sum(weight.reshape(BLOCK // 8, 8, BLOCK), axis=0)
                pt[r : r + BLOCK, cols] = weight.astype(bf16)
            tops.append(top)
            sums.append(jnp.sum(total, axis=0, keepdims=True))
        total = jnp.concatenate(sums, axis=1)
        head_rows, side_rows = ds(h * HEAD_DIM, HEAD_DIM), ds(side * HEAD_DIM, HEAD_DIM)
        att_t[side_rows, :] = dot_nn(vt[head_rows, 0:TRUNK], pt[0:TRUNK, :])
        for q_row, k_row, count in PIECES:
            cols = slice(q_row, q_row + BLOCK)
            att_t[side_rows, cols] += dot_nn(
                vt[head_rows, k_row : k_row + count], pt[TRUNK : TRUNK + count, cols]
            )
        att_t[side_rows, :] = att_t[side_rows, :] / total
        lse[pl.ds(h, 1), :] = jnp.concatenate(tops, axis=1) + jnp.log(total)
        return carried

    mine, far = HALF * x, HALF * (1 - x)
    here_rows, far_rows = ds(mine, HALF), ds(far, HALF)
    att_copies = []

    def slab_heads(slab):
        lax.fori_loop(2 * slab, 2 * slab + 2, head, 0)
        lanes = pl.ds(128 * slab, 128)
        attended[:, lanes] = att_t[...].T.astype(bf16)
        att_copies.append(post.send(attended.at[far_rows, lanes], att_x.at[:, lanes], me.xp))

    def grads_on(i):
        post.got(grads_y[i])
        relay(quarter(grads_all, t, i, 2), me.core)
        return relay(quarter(grads_all, t, i, 2), me.xp)

    def strips_on(copies, array):
        passed = []
        for copy, source in zip(copies, me.back):
            post.got(copy)
            piece = array.at[core, ds(deep * source + strip, half)]
            passed.append(relay(piece, me.yp))
            relay(piece, me.core)
        return passed

    def strips_in(copies, array):
        for copy, source in zip(copies, me.back):
            post.got(copy)
            relay(array.at[core, ds(deep * source + other_strip, half)], me.core)

    d_part = lambda source, row: wd.at[core, ds(deep * source + row, third)]
    post.got(wo_copy)
    wo_y = relay(wo_x.at[wo_rows], me.yp)
    wo_core = [relay(wo_x.at[wo_rows], me.core)]
    grads_x = [grads_on(0)]
    slab_heads(0)
    grads_x.append(grads_on(1))
    slab_heads(1)
    u_y = strips_on(u_z, wu)
    d_lone = [post.send(d_own.at[ds(lone, third)], d_part(f, lone), device) for device in me.z]
    post.got(wo_y)
    wo_core.append(relay(wo_x.at[ds(wo_quarter * (2 * (1 - c) + core), wo_quarter)], me.core))
    slab_heads(2)
    keep(attended, att_out)
    middle[...] = (
        x_own[here_rows, :].astype(f32) + wide(out_bias) + dot_nt(attended[here_rows, :], wh[3])
    )
    d_y = []
    for copy, source in zip(d_lone, me.back):
        post.got(copy)
        d_y.append(relay(d_part(source, lone), me.yp))
        relay(d_part(source, lone), me.core)
    d_shared = [post.send(d_own.at[ds(third, third)], d_part(f, third), device) for device in me.z]
    for copy in wo_core + att_copies:
        post.got(copy)
    middle[...] += dot_nt(att_x[...], wo_x[...])
    n2, s2 = row_norm(middle[...])
    normed[...] = n2
    inverse[...] = s2
    low2[here_rows, :] = (n2 * wide(gain2) + wide(shift2)).astype(bf16)
    chunk = HALF // 2
    here_chunks = [ds(mine + chunk * i, chunk) for i in range(2)]
    far_chunks = [ds(far + chunk * i, chunk) for i in range(2)]
    low_copies = [post.send(low2.at[rows], low2.at[rows], me.xp) for rows in here_chunks]
    for i in range(2):
        post.got(grads_x[i])
        relay(quarter(grads_all, over, i, 2), me.core)
    strips_in(u_y, wu)
    for copy in own_copies[1:4]:
        copy.wait()
    post.got_from(me.core)
    for j, place in enumerate(places):
        g_own[pl.ds(j * BLOCK, BLOCK), :] = block_of(grads_all, place)
    tile = 256

    def tiles(step):
        def tile_step(j, carried):
            shard, lanes = j // 3, pl.ds(pl.multiple_of(j % 3 * tile, 128), tile)
            step(shard, lanes, pl.ds(pl.multiple_of(j * tile, 128), tile))
            return carried

        lax.fori_loop(0, 6, tile_step, 0)

    def forward(rows):
        def step(shard, lanes, out):
            pre = dot_nn(low2[rows, :], wu[shard, :, lanes]) + bias_all[shard, 0:1, lanes]
            below = 0.5 * (1.0 + lax.erf(pre * (2.0**-0.5)))
            density = jnp.exp(-0.5 * pre * pre) * (2.0 * jnp.pi) ** -0.5
            hidden[rows, out] = (pre * below).astype(bf16)
            pre_grad[rows, out] = (below + pre * density).astype(bf16)

        tiles(step)

    def backward(rows, count):
        second[rows, :] = jnp.zeros((count, width), f32)

        def step(shard, lanes, out):
            back = dot_nn(g_own[rows, :], wd[shard, :, lanes])
            low_back = (back * pre_grad[rows, out].astype(f32)).astype(bf16)
            pre_grad[rows, out] = low_back
            second[rows, :] += dot_nt(low_back, wu[shard, :, lanes])

        tiles(step)

    def mlp(rows):
        return dot_nt(hidden[rows, 0:width], wd[0]) + dot_nt(hidden[rows, width:], wd[1])

    own_lanes, sibling_lanes = (
        pl.ds(pl.multiple_of(width * side, 128), width) for side in (core, 1 - core)
    )
    sibling_copies = {}

    def weight_grad(index, left, right, grad):
        def step(shard, lanes, out):
            grad[:, out] = dot_tn(left[...], right[:, out]).astype(bf16)

        tiles(step)
        sibling_copies[index] = post.send(grad.at[:, sibling_lanes], g_sum.at[index], me.core)

    forward(here_rows)
    for i in range(2):
        post.got(low_copies[i])
        forward(far_chunks[i])
    weight_grad(1, g_own, hidden, g_down)
    for copies, row in ((d_shared, third), (d_y, other_lone)):
        for copy, source in zip(copies, me.back):
            post.got(copy)
            relay(d_part(source, row), me.core)
    post.got_from(me.core)
    second_copies = []
    for i in range(2):
        backward(far_chunks[i], chunk)
        second_send[i] = second[far_chunks[i], :].astype(bf16)
        second_copies.append(post.send(second_send.at[i], second_x.at[i], me.xp))
    backward(here_rows, HALF)

    weight_grad(0, low2, pre_grad, g_up)
    total = [jnp.zeros((1, width), f32)] * 4
    for i in range(2):
        rows = here_chunks[i]
        part_rows = slice(chunk * i, chunk * i + chunk)
        post.got(second_copies[i])
        second_grad = second[rows, :] + second_x[i].astype(f32)
        n2 = normed[part_rows, :]
        dy = g_own[rows, :].astype(f32)
        grad = dy + norm_back(second_grad, n2, inverse[part_rows, :], wide(gain2))
        middle_grad[part_rows, :] = grad
        low_grad = grad.astype(bf16)
        branch[part_rows, :] = low_grad
        da_send[part_rows, :] = dot_nn(low_grad, wo_x[...]).astype(bf16)
        post.send(da_send.at[pl.ds(chunk * i, chunk)], da.at[rows], me.xp)
        terms = (second_grad * n2, second_grad, dy, low_grad.astype(f32))
        total = [a + jnp.sum(b, axis=0, keepdims=True) for a, b in zip(total, terms)]
    for i in range(4):
        stats[i : i + 1, :] = total[i]
    up_stats[0:1, :] = jnp.sum(pre_grad[:, 0:width].astype(f32), axis=0, keepdims=True)
    up_stats[1:2, :] = jnp.sum(pre_grad[:, width:].astype(f32), axis=0, keepdims=True)
    mlp_send[...] = mlp(far_rows).astype(bf16)
    mlp_own[...] = middle[...] + mlp(here_rows) + wide(down_bias)
    for src, out in ((middle_grad, middle_grad_out), (mlp_own, mlp_own_out), (mlp_send, mlp_send_out)):
        keep(src, out)
    da[here_rows, :] = dot_nn(branch[...], wh[3]).astype(bf16)
    g_out_send[...] = dot_tn(branch[...], att_x[...]).astype(bf16)
    g_out_own[...] = dot_tn(branch[...], attended[here_rows, :]).astype(bf16)
    keep(g_out_send, g_out_send_out)
    keep(g_out_own, g_out_own_out)
    for index, (grad, out) in enumerate(((g_up, g_up_out), (g_down, g_down_out))):
        post.got(sibling_copies[index])

        def add_sibling(j, carried):
            rows = ds(j * BLOCK, BLOCK)
            g_sum[index, rows, :] = (
                g_sum[index, rows, :].astype(f32) + grad[rows, own_lanes].astype(f32)
            ).astype(bf16)
            return carried

        lax.fori_loop(0, width // BLOCK, add_sibling, 0)
        keep(g_sum.at[index], out)
    post.close()
    for copy in own_copies[4:]:
        copy.wait()


def first_half(fsdp_count, order, patches, grads, attn_proj, out_proj, up, down_t, *vectors):
    width = patches.shape[1]
    shape = jax.ShapeDtypeStruct
    vmem = pltpu.VMEM
    units = 2 * up.shape[1]
    all_units = 2 * patches.shape[0] // UNIT
    deep = up.shape[0]
    fold = lambda a: a.reshape(-1, UNIT, width)
    return pl.pallas_call(
        partial(first_kernel, fsdp_count),
        out_shape=(
            shape((OWN, 384), bf16),
            shape((KEYS, 384), bf16),
            shape((KEYS, 384), bf16),
            shape((OWN, 384), bf16),
            shape((OWN, width), bf16),
            shape((OWN, width), bf16),
            shape((4, width, 384), bf16),
            shape((width, width), bf16),
            shape((width, width), bf16),
            shape((HALF, width), f32),
            shape((HALF, width), f32),
            shape((HALF, width), bf16),
            shape((width, 384), bf16),
            shape((width, 384), bf16),
            shape((8, OWN), f32),
            shape((OWN, 384), bf16),
            shape((4, width), f32),
            shape((2, width), f32),
        ),
        in_specs=[SMEM, ANY, ANY, VMEM, VMEM, ANY, ANY] + [VMEM] * 8,
        out_specs=(ANY,) * 14 + (VMEM,) * 4,
        scratch_shapes=[
            vmem((HALF, width), f32),
            vmem((HALF, width), f32),
            vmem((HALF, width), bf16),
            vmem((width, 384), bf16),
            vmem((width, 384), bf16),
            pltpu.SMEM(order.shape[1:], jnp.int32),
            vmem((deep, width), bf16),
            vmem((8, width), f32),
            vmem((all_units, UNIT, width), bf16),
            vmem((all_units, UNIT, width), bf16),
            vmem((2, width, width), bf16),
            vmem((4, width, 384), bf16),
            vmem((width, 384), bf16),
            vmem((2, width, up.shape[1]), bf16),
            vmem((2, width, up.shape[1]), bf16),
            vmem((2, 8, width), f32),
            vmem((all_units, UNIT, width), bf16),
            vmem((KEYS, width), bf16),
            vmem((OWN, width), bf16),
            vmem((OWN, width), bf16),
            vmem((OWN, width), bf16),
            vmem((OWN, 384), bf16),
            vmem((KEYS, 384), bf16),
            vmem((KEYS, 384), bf16),
            vmem((384, KEYS), bf16),
            vmem((OWN, 384), bf16),
            vmem((128, OWN), f32),
            vmem((HALF, 384), bf16),
            vmem((TRUNK + 2 * BLOCK, OWN), f32),
            vmem((TRUNK + 2 * BLOCK, OWN), bf16),
            vmem((HALF, width), f32),
            vmem((HALF, width), f32),
            vmem((HALF, 1), f32),
            vmem((OWN, width), bf16),
            vmem((OWN, units), bf16),
            vmem((OWN, units), bf16),
            vmem((OWN, width), f32),
            vmem((2, HALF // 2, width), bf16),
            vmem((2, HALF // 2, width), bf16),
            vmem((HALF, width), bf16),
            vmem((HALF, 384), bf16),
            vmem((width, units), bf16),
            vmem((width, units), bf16),
            vmem((2, width, width), bf16),
            pltpu.SemaphoreType.DMA((24,)),
            pltpu.SemaphoreType.DMA((112,)),
            pltpu.SemaphoreType.DMA((112,)),
        ],
        compiler_params=pltpu.CompilerParams(collective_id=0, has_side_effects=True, vmem_limit_bytes=LIMIT),
        name="first_half",
    )(order, fold(patches), fold(grads), attn_proj, out_proj, up, down_t, *vectors)


class StripSum:
    def __init__(self, me, post, fsdp_count, held, from_core, buffers):
        self.me, self.post, self.count = me, post, fsdp_count
        self.held, self.from_core = held, from_core
        self.from_y, self.from_z, self.done = buffers
        self.half = held.shape[0] // fsdp_count // 2

    def from_sibling(self, src):
        self.core_copy = self.post.send(src, self.from_core, self.me.core)

    def add_sibling(self):
        self.post.got(self.core_copy)
        half = self.half

        def step(j, carried):
            rows = ds(j * half, half)
            self.held[rows, :] = (self.held[rows, :].astype(f32) + self.from_core[rows, :].astype(f32)).astype(bf16)
            return carried

        lax.fori_loop(0, 2 * self.count, step, 0)

    def strip(self, g, side):
        return ds(self.half * (2 * g + side), self.half)

    def over_y(self):
        me = self.me
        self.y_copies = [
            self.post.send(self.held.at[self.strip(g, 1 - me.c)], self.from_y.at[g], me.yp)
            for g in range(self.count)
        ]

    def over_z(self):
        me = self.me
        for copy in self.y_copies:
            self.post.got(copy)

        def step(g, carried):
            rows = self.strip(g, me.c)
            self.held[rows, :] = (self.held[rows, :].astype(f32) + self.from_y[g].astype(f32)).astype(bf16)
            return carried

        lax.fori_loop(0, self.count, step, 0)
        self.z_copies = [
            self.post.send(self.held.at[self.strip((me.f + i + 1) % self.count, me.c)], self.from_z.at[i], device)
            for i, device in enumerate(me.z)
        ]

    def over_z_first(self):
        me, deep = self.me, 2 * self.half
        self.z_copies = [
            self.post.send(self.held.at[ds(deep * ((me.f + i + 1) % self.count), deep)], self.from_z.at[i], device)
            for i, device in enumerate(me.z)
        ]

    def finish_z_first(self):
        me, deep = self.me, 2 * self.half
        for copy in self.z_copies:
            self.post.got(copy)
        total = self.held[ds(deep * me.f, deep), :].astype(f32)
        for i in range(self.count - 1):
            total = total + self.from_z[i].astype(f32)
        self.done[0] = total.astype(bf16)
        self.last = self.post.send(self.done.at[0], self.done.at[1], me.yp)

    def finish(self):
        me = self.me
        for copy in self.z_copies:
            self.post.got(copy)
        total = self.held[self.strip(me.f, me.c), :].astype(f32)
        for i in range(self.count - 1):
            total = total + self.from_z[i].astype(f32)
        self.done[me.c] = total.astype(bf16)
        self.last = self.post.send(self.done.at[me.c], self.done.at[me.c], me.yp)


TALL, WIDE = 256, 256


def second_kernel(
    fsdp_count, q_in, k_in, v_in, att_in, low_in, x_in, wh_in, g_up, g_down,
    middle_grad_in, mlp_own_in, mlp_send, g_out_own_in, g_out_send_in, lse, da, mid_stats, up_stats, gain1,
    rows_out, up_out, rest_out, all_total, part_total,
    middle_grad, mlp_own, g_out_own, g_out_send, q, k, v, kt, attended, low_own, x_own, wh, up_own, down_own,
    delta, pt, dst, dk_acc, dv_acc, dq_t, dq, own_first, trunk, trunk_own, trunk_far, trunk_send, trunk_y, dkv_own,
    mlp_x, first_send, first_x, rows_own, out_core, out_sum, out_x, packed,
    from_core, from_y, from_z, done, deep_z, deep_done, stat_buf, stat_in, stat_z, local, ss, rs,
):
    me = Here(fsdp_count)
    f, c, x, core = me.f, me.c, me.x, me.k
    s = 2 * c + core
    pair = 2 * BLOCK
    units = HALF // UNIT
    width = x_in.shape[1]
    mine, far = HALF * x, HALF * (1 - x)
    here_rows, far_rows = ds(mine, HALF), ds(far, HALF)
    loads = []
    for src, held in (
        (g_up, up_own), (g_down, down_own), (k_in, k), (q_in, q), (v_in, v), (att_in, attended),
        (g_out_own_in, g_out_own), (g_out_send_in, g_out_send), (mlp_own_in, mlp_own),
        (low_in, low_own), (x_in, x_own), (middle_grad_in, middle_grad), (wh_in.at[pl.ds(0, 3)], wh),
    ):
        copy = pltpu.make_async_copy(src, held, local.at[len(loads)])
        copy.start()
        loads.append(copy)
    greet([me.core, me.xp, me.yp] + me.z)
    post = Post(ss, rs)
    mlp_copy = post.send(mlp_send, mlp_x, me.xp)
    buffers = [(from_y, from_z, done)] + [(None, deep_z.at[i], deep_done.at[i]) for i in range(2)]
    sums = [
        StripSum(me, post, fsdp_count, held, from_core, buffer)
        for held, buffer in zip((up_own, down_own, packed.at[core]), buffers)
    ]
    slab_own = pl.ds(pl.multiple_of(128 * core, 128), 128)
    slab_sibling = pl.ds(pl.multiple_of(128 * (1 - core), 128), 128)
    slab_both = pl.ds(256, 128)
    out_copies = []
    for i, src in enumerate((g_out_own_in, g_out_send_in)):
        for j, lanes in enumerate((slab_sibling, slab_both)):
            out_copies.append(post.send(src.at[:, lanes], out_core.at[i, j], me.core))
    for copy in loads[:2]:
        copy.wait()
    sums[0].over_y()
    sums[1].over_z_first()
    for copy in loads[2:6]:
        copy.wait()
    kt[...] = k[...].T
    product = (da[...].astype(f32) * attended[...].astype(f32)).T
    for h in range(6):
        delta[h : h + 1, :] = jnp.sum(product[h * HEAD_DIM : (h + 1) * HEAD_DIM], axis=0, keepdims=True)
    lane = lax.broadcasted_iota(jnp.int32, (OWN, 128), 1) // HEAD_DIM

    def head(h, carried):
        slab, part = h // 2, h % 2
        lanes = pl.ds(pl.multiple_of(slab * 128, 128), 128)
        q_slab, da_slab = q[:, lanes], da[:, lanes]
        q_part = jnp.where(lane == part, q_slab, jnp.zeros_like(q_slab))
        da_part = jnp.where(lane == part, da_slab, jnp.zeros_like(da_slab))
        log_total, row_delta = lse[pl.ds(h, 1), :], delta[pl.ds(h, 1), :]

        def tile(keys, rows, cols):
            scores = dot_nt(k[keys, lanes], q_part[cols])
            prob_grad = dot_nt(v[keys, lanes], da_part[cols])
            weight = jnp.exp(scores - log_total[:, cols])
            pt[rows, cols] = weight.astype(bf16)
            dst[rows, cols] = (weight * (prob_grad - row_delta[:, cols])).astype(bf16)

        for col in range(0, OWN, WIDE):
            cols = slice(col, min(col + WIDE, OWN))
            for row in range(0, TRUNK, TALL):
                tile(slice(row, row + TALL), slice(row, row + TALL), cols)
        for q_row, k_row, count in PIECES:
            tile(slice(k_row, k_row + count), slice(TRUNK, TRUNK + count), slice(q_row, q_row + BLOCK))
        dk_acc[0:TRUNK, :] += dot_nn(dst[0:TRUNK, :], q_part)
        dv_acc[0:TRUNK, :] += dot_nn(pt[0:TRUNK, :], da_part)
        head_rows = ds(h * HEAD_DIM, HEAD_DIM)
        dq_t[head_rows, :] = dot_nn(kt[head_rows, 0:TRUNK], dst[0:TRUNK, :])
        for q_row, k_row, count in PIECES:
            cols, rows = slice(q_row, q_row + BLOCK), slice(TRUNK, TRUNK + count)
            own = slice(k_row, k_row + count)
            dk_acc[own, :] += dot_nn(dst[rows, cols], q_part[q_row : q_row + BLOCK])
            dv_acc[own, :] += dot_nn(pt[rows, cols], da_part[q_row : q_row + BLOCK])
            dq_t[head_rows, cols] += dot_nn(kt[head_rows, own], dst[rows, cols])
        return carried

    chip_rows = lambda chip, side: ds(pair * (2 * chip + side), pair)
    trunk_copies, y_copies = [], []

    def slab_heads(slab):
        dk_acc[...] = jnp.zeros_like(dk_acc)
        dv_acc[...] = jnp.zeros_like(dv_acc)
        lax.fori_loop(2 * slab, 2 * slab + 2, head, 0)

    def trunk_out(slab):
        trunk[slab, 0] = dk_acc[0:TRUNK, :].astype(bf16)
        trunk[slab, 1] = dv_acc[0:TRUNK, :].astype(bf16)
        for i, total in enumerate((dk_acc, dv_acc)):
            lanes = slice(384 * i + 128 * slab, 384 * i + 128 * slab + 128)
            dkv_own[pair:, lanes] = total[TRUNK:, :].astype(bf16)
        trunk_copies.append(
            (
                post.send(trunk.at[slab, :, chip_rows(1 - c, 1 - core), :], trunk_far.at[slab], me.core),
                post.send(trunk.at[slab, :, chip_rows(c, 1 - core), :], trunk_own.at[slab], me.core),
            )
        )

    def trunk_over(slab):
        post.got(trunk_copies[slab][0])
        trunk_send[slab] = (
            trunk[slab, :, chip_rows(1 - c, core), :].astype(f32) + trunk_far[slab].astype(f32)
        ).astype(bf16)
        y_copies.append(post.send(trunk_send.at[slab], trunk_y.at[slab], me.yp))

    def trunk_in(slab):
        post.got(trunk_copies[slab][1])
        post.got(y_copies[slab])
        total = (
            trunk[slab, :, chip_rows(c, core), :].astype(f32)
            + trunk_own[slab].astype(f32)
            + trunk_y[slab].astype(f32)
        ).astype(bf16)
        for i in range(2):
            lanes = slice(384 * i + 128 * slab, 384 * i + 128 * slab + 128)
            dkv_own[0:pair, lanes] = total[i]

    slab_heads(0)
    trunk_out(0)
    for copy in loads[6:13]:
        copy.wait()
    for copy in out_copies:
        post.got(copy)
    for i, src in enumerate((g_out_own, g_out_send)):
        for j, lanes in enumerate((slab_own, slab_both)):
            out_sum[i, j] = (src[:, lanes].astype(f32) + out_core[i, j].astype(f32)).astype(bf16)
    out_copy = post.send(out_sum.at[1], out_x, me.xp)
    trunk_over(0)
    slab_heads(1)
    trunk_out(1)
    post.got(mlp_copy)
    rows_own[0] = (mlp_own[...] + mlp_x[...].astype(f32)).astype(bf16).reshape(units, UNIT, width)
    beside = 2 * s + 1 - x
    beyond = 2 * (2 * (1 - c) + core) + x
    corner = 2 * (2 * (1 - c) + core) + 1 - x
    part = units // 2
    over_x, over_y, diagonal = {}, {}, {}

    def piece(index, owner, half):
        return rows_out.at[index, pl.ds(units * owner + part * half, part)]

    def own_piece(index, half):
        return rows_own.at[index, pl.ds(part * half, part)], piece(index, 2 * s + x, half)

    def spread_x(index, half):
        own, there = own_piece(index, half)
        over_x[index, half] = post.send(own, there, me.xp)
        post.send(own, there, me.core)
        copy = pltpu.make_async_copy(own, there, local.at[len(loads)])
        copy.start()
        loads.append(copy)

    def spread_y(index, half):
        own, there = own_piece(index, half)
        over_y[index, half] = post.send(own, there, me.yp)

    def pass_on(index, half):
        for copies, owner, onward in ((over_x, beside, me.yp), (over_y, beyond, me.xp)):
            post.got(copies[index, half])
            got = piece(index, owner, half)
            if (half == 0) == (onward is me.yp):
                diagonal[index, half] = post.send(got, got, onward)
            post.send(got, got, me.core)

    def corner_on(index):
        for half in range(2):
            post.got(diagonal[index, half])
            got = piece(index, corner, half)
            post.send(got, got, me.core)

    for half in range(2):
        spread_x(0, half)
    trunk_over(1)
    sums[0].over_z()
    slab_heads(2)
    trunk_out(2)
    dq[...] = (dq_t[...].T * HEAD_DIM ** (-0.5)).astype(bf16)
    trunk_over(2)
    for half in range(2):
        spread_y(0, half)
    for slab in range(3):
        trunk_in(slab)

    def first(rows):
        return (
            dot_nt(dq[rows, :], wh[0])
            + dot_nt(dkv_own[rows, 0:384], wh[1])
            + dot_nt(dkv_own[rows, 384:768], wh[2])
        )

    chunk = HALF // 2
    first_copies = []
    for i in range(2):
        first_send[i] = first(ds(far + chunk * i, chunk)).astype(bf16)
        first_copies.append(post.send(first_send.at[i], first_x.at[i], me.xp))
    g_attn = [
        dot_tn(low_own[...], dq[...]),
        dot_tn(low_own[...], dkv_own[:, 0:384]),
        dot_tn(low_own[...], dkv_own[:, 384:768]),
    ]
    tails = []
    for j in (0, 1):
        for i in range(3):
            packed[j, :, 128 * i : 128 * i + 128] = g_attn[i][:, 128 * j : 128 * j + 128].astype(bf16)
        tail = [g[:, 256 + 64 * j : 320 + 64 * j] for g in g_attn]
        packed[j, :, 512:640] = jnp.concatenate(tail[0:2], axis=1).astype(bf16)
        packed[j, :, 640:768] = jnp.concatenate([tail[2], jnp.zeros_like(tail[2])], axis=1).astype(bf16)
    attn_stats = jnp.concatenate(
        [
            jnp.sum(dq[...].astype(f32), axis=0, keepdims=True),
            jnp.sum(dkv_own[:, 384:768].astype(f32), axis=0, keepdims=True),
        ],
        axis=1,
    )
    sums[2].from_sibling(packed.at[1 - core])
    def put_out():
        post.got(out_copy)
        packed[core, :, 384:512] = (out_sum[0, 0].astype(f32) + out_x[0].astype(f32)).astype(bf16)
        last = out_sum[0, 1].astype(f32) + out_x[1].astype(f32)
        side = lax.broadcasted_iota(jnp.int32, last.shape, 1) // HEAD_DIM
        turned = jnp.concatenate([last[:, HEAD_DIM:], last[:, :HEAD_DIM]], axis=1)
        tail = jnp.where(core == 0, turned, last)
        packed[core, :, 640:768] = jnp.where(side == 0, packed[core, :, 640:768].astype(f32), tail).astype(bf16)

    sums[2].add_sibling()
    put_out()
    sums[2].over_z_first()
    own_first[...] = first(here_rows)
    for half in range(2):
        pass_on(0, half)
    n1_all, s1_all = row_norm(x_own[here_rows, :].astype(f32))
    first_total = [jnp.zeros((1, width), f32)] * 2
    for i in range(2):
        post.got(first_copies[i])
        rows = slice(chunk * i, chunk * i + chunk)
        first_grad = own_first[rows, :] + first_x[i].astype(f32)
        n1, s1 = n1_all[rows], s1_all[rows]
        grad = middle_grad[rows, :] + norm_back(first_grad, n1, s1, wide(gain1))
        rows_own[1, part * i : part * i + part] = grad.astype(bf16).reshape(part, UNIT, width)
        spread_x(1, i)
        spread_y(1, i)
        first_total = [
            a + jnp.sum(b, axis=0, keepdims=True) for a, b in zip(first_total, (first_grad * n1, first_grad))
        ]
    rows_mid, rows_up = mid_stats.shape[0], up_stats.shape[0]
    stat_buf[0:1, :], stat_buf[1:2, :] = first_total
    stat_buf[2 : 2 + rows_mid, :] = mid_stats[...]
    stat_buf[2 + rows_mid : 8, :] = jnp.zeros((6 - rows_mid, width), f32)
    stat_buf[8 : 8 + rows_up, :] = up_stats[...]
    stat_buf[8 + rows_up : 9 + rows_up, :] = attn_stats
    stat_buf[9 + rows_up : 16, :] = jnp.zeros((7 - rows_up, width), f32)
    level = lambda i: pl.ds(16 * i, 16)
    stat_copy = post.send(stat_buf.at[level(0)], stat_in.at[0], me.core)
    sums[0].finish()
    post.got(stat_copy)
    stat_buf[level(1), :] = stat_buf[level(0), :] + stat_in[0]
    stat_copy = post.send(stat_buf.at[level(1)], stat_in.at[1], me.yp)
    sums[1].finish_z_first()
    corner_on(0)
    post.got(stat_copy)
    stat_buf[level(2), :] = stat_buf[level(1), :] + stat_in[1]
    stat_copy = post.send(stat_buf.at[level(2)], stat_in.at[2], me.xp)
    pass_on(1, 0)
    post.got(stat_copy)
    stat_buf[48:56, :] = stat_buf[32:40, :] + stat_in[2, 0:8]
    stat_buf[56:64, :] = stat_buf[40:48, :]
    stat_z[f] = stat_buf[level(3), :]
    stat_copies = [post.send(stat_buf.at[level(3)], stat_z.at[f], device) for device in me.z]
    pass_on(1, 1)
    sums[2].finish_z_first()
    corner_on(1)
    for copy in stat_copies:
        post.got(copy)
    total = stat_z[0]
    for g in range(1, fsdp_count):
        total = total + stat_z[g]
    all_total[...] = total[0 : 2 + rows_mid]
    part_total[...] = total[8 : 9 + rows_up]
    for total in sums:
        post.got(total.last)
    up_out[...] = done[...]
    rest_out[...] = deep_done[...]
    post.close()
    for copy in loads[13:]:
        copy.wait()


def second_half(fsdp_count, row_count, *operands):
    shape = jax.ShapeDtypeStruct
    vmem = pltpu.VMEM
    width = operands[4].shape[1]
    rows = row_count
    tall = TRUNK + 2 * BLOCK
    pair = 2 * BLOCK
    deep = width // fsdp_count
    half = deep // 2
    return pl.pallas_call(
        partial(second_kernel, fsdp_count),
        out_shape=(
            shape((2, 2 * rows // UNIT, UNIT, width), bf16),
            shape((2, half, width), bf16),
            shape((2, 2, deep, width), bf16),
            shape((6, width), f32),
            shape((3, width), f32),
        ),
        in_specs=[ANY] * 14 + [VMEM] * 5,
        out_specs=(ANY,) + (VMEM,) * 4,
        scratch_shapes=[
            vmem((HALF, width), f32),
            vmem((HALF, width), f32),
            vmem((width, 384), bf16),
            vmem((width, 384), bf16),
            vmem((OWN, 384), bf16),
            vmem((KEYS, 384), bf16),
            vmem((KEYS, 384), bf16),
            vmem((384, KEYS), bf16),
            vmem((OWN, 384), bf16),
            vmem((OWN, width), bf16),
            vmem((OWN, width), bf16),
            vmem((3, width, 384), bf16),
            vmem((width, width), bf16),
            vmem((width, width), bf16),
            vmem((8, OWN), f32),
            vmem((tall, OWN), bf16),
            vmem((tall, OWN), bf16),
            vmem((KEYS, 128), f32),
            vmem((KEYS, 128), f32),
            vmem((384, OWN), f32),
            vmem((OWN, 384), bf16),
            vmem((HALF, width), f32),
            vmem((3, 2, TRUNK, 128), bf16),
            vmem((3, 2, pair, 128), bf16),
            vmem((3, 2, pair, 128), bf16),
            vmem((3, 2, pair, 128), bf16),
            vmem((3, 2, pair, 128), bf16),
            vmem((OWN, 768), bf16),
            vmem((HALF, width), bf16),
            vmem((2, HALF // 2, width), bf16),
            vmem((2, HALF // 2, width), bf16),
            vmem((2, HALF // UNIT, UNIT, width), bf16),
            vmem((2, 2, width, 128), bf16),
            vmem((2, 2, width, 128), bf16),
            vmem((2, width, 128), bf16),
            vmem((2, width, width), bf16),
            vmem((width, width), bf16),
            vmem((fsdp_count, half, width), bf16),
            vmem((fsdp_count - 1, half, width), bf16),
            vmem((2, half, width), bf16),
            vmem((2, fsdp_count - 1, deep, width), bf16),
            vmem((2, 2, deep, width), bf16),
            vmem((64, width), f32),
            vmem((3, 16, width), f32),
            vmem((fsdp_count, 16, width), f32),
            pltpu.SemaphoreType.DMA((20,)),
            pltpu.SemaphoreType.DMA((80,)),
            pltpu.SemaphoreType.DMA((80,)),
        ],
        compiler_params=pltpu.CompilerParams(collective_id=1, has_side_effects=True, vmem_limit_bytes=LIMIT),
        name="second_half",
    )(*operands)


def place_kernel(
    order, rows_all, up_sum, rest, all_total, part_total,
    result, patch_grad, gain1, shift1, grad_attn, attn_bias, grad_out, out_bias, gain2, shift2, grad_up, up_bias,
    grad_down_t, down_bias, result_low, patch_low, patch_wide, sems, out_sems,
):
    units = BLOCK // UNIT
    own = result.shape[0] // units
    core = lax.axis_index("tensor") % 2
    copies = []
    for j in range(own):
        block = order[0, own * lax.axis_index("context") + j]
        branch, leaf = block - TRUNK_BLK, block - TRUNK_BLK - BRANCHES
        index = jnp.where(
            branch < 0,
            5 * (block // 2) + block % 2,
            jnp.where(leaf < 0, 5 * branch + 3, 5 * (leaf // 2) + 2 + 2 * (leaf % 2)),
        )
        to = pl.ds(j * units, units)
        for i, dest in enumerate((result_low, patch_low)):
            copy = pltpu.make_async_copy(
                rows_all.at[i, pl.ds(index * units, units)], dest.at[to], sems.at[i, j]
            )
            copy.start()
            copies.append(copy)
    total = lambda i: all_total[i, :]
    gain1[...], shift1[...], gain2[...], shift2[...] = total(0), total(1), total(2), total(3)
    down_bias[...], out_bias[...] = total(4), total(5)
    up_bias[...] = part_total[core, :]
    for i in range(2):
        lanes = slice(384 * i, 384 * i + 384)
        row = part_total[2:3, lanes]
        first = jnp.where(core == 0, row[:, 0:128], row[:, 128:256])
        second = jnp.where(core == 0, row[:, 256:320], row[:, 320:384])
        attn_bias[i : i + 1, :] = jnp.concatenate([first, second], axis=1)
    grad_up[...] = up_sum[...].reshape(grad_up.shape).astype(f32)
    grad_down_t[...] = rest[0, 0].astype(f32) + rest[0, 1].astype(f32)
    attn = rest[1, 0].astype(f32) + rest[1, 1].astype(f32)
    tails = [attn[:, 512:576], attn[:, 576:640], attn[:, 640:704], attn[:, 704:768]]
    for i in range(3):
        grad_attn[i, :, 0:128] = attn[:, 128 * i : 128 * i + 128]
        grad_attn[i, :, 128:192] = tails[i]
    grad_out[...] = jnp.concatenate([attn[:, 384:512], tails[3]], axis=1).T
    out = []
    for j in range(own):
        block = pl.ds(j * units, units)
        copies[2 * j].wait()
        copies[2 * j + 1].wait()
        patch_wide[block] = patch_low[block].astype(f32)
        for i, (src, dest) in enumerate(((result_low, result), (patch_wide, patch_grad))):
            copy = pltpu.make_async_copy(src.at[block], dest.at[block], out_sems.at[i, j])
            copy.start()
            out.append(copy)
    for copy in out:
        copy.wait()


def place(order, row_count, rows_all, up_sum, rest, all_total, part_total):
    shape = jax.ShapeDtypeStruct
    width = rows_all.shape[3]
    deep = rest.shape[2]
    vector = shape((width,), f32)
    return pl.pallas_call(
        place_kernel,
        out_shape=(
            shape((row_count // UNIT, UNIT, width), bf16), shape((row_count // UNIT, UNIT, width), f32), vector, vector,
            shape((3, deep, 192), f32), shape((2, 192), f32), shape((192, deep), f32), vector, vector, vector,
            shape((deep, width), f32), vector, shape((deep, width), f32), vector,
        ),
        in_specs=[SMEM, ANY] + [VMEM] * 4,
        out_specs=(ANY,) * 2 + (VMEM,) * 12,
        scratch_shapes=[
            pltpu.VMEM((row_count // UNIT, UNIT, width), bf16),
            pltpu.VMEM((row_count // UNIT, UNIT, width), bf16),
            pltpu.VMEM((row_count // UNIT, UNIT, width), f32),
            pltpu.SemaphoreType.DMA((2, row_count // BLOCK)),
            pltpu.SemaphoreType.DMA((2, row_count // BLOCK)),
        ],
        compiler_params=pltpu.CompilerParams(vmem_limit_bytes=LIMIT),
        name="place",
    )(order, rows_all, up_sum, rest, all_total, part_total)


def tree_shards(
    fsdp_count, patches, out_grad, block_order, first_gain, first_shift, attn_proj, attn_bias, out_proj, out_bias,
    second_gain, second_shift, up_proj, up_bias, down_proj, down_bias,
):
    middle = first_half(
        fsdp_count, block_order, patches, out_grad, attn_proj, out_proj, up_proj, down_proj.T, up_bias, attn_bias,
        first_gain, first_shift, second_gain, second_shift, out_bias, down_bias,
    )
    sums = second_half(fsdp_count, patches.shape[0], *middle, first_gain)
    outputs = list(place(block_order, patches.shape[0], *sums))
    outputs[0], outputs[1] = (rows.reshape(patches.shape) for rows in outputs[:2])
    outputs[12] = outputs[12].T
    return tuple(outputs)


def solution(mesh):
    fits = mesh.shape["context"] * 2 == BRANCHES and mesh.shape["tensor"] == 4 and mesh.shape["fsdp"] == 4
    body = partial(tree_shards, mesh.shape["fsdp"]) if fits else shards
    return jax.shard_map(
        body,
        mesh=mesh,
        in_specs=(
            P(("fsdp", "context"), None),
            P(("fsdp", "context"), None),
            P("fsdp", None),
            P(),
            P(),
            P(None, "fsdp", "tensor"),
            P(None, "tensor"),
            P("tensor", "fsdp"),
            P(),
            P(),
            P(),
            P("fsdp", "tensor"),
            P("tensor"),
            P("tensor", "fsdp"),
            P(),
        ),
        out_specs=(
            P(("fsdp", "context"), None),
            P(("fsdp", "context"), None),
            P(),
            P(),
            P(None, "fsdp", "tensor"),
            P(None, "tensor"),
            P("tensor", "fsdp"),
            P(),
            P(),
            P(),
            P("fsdp", "tensor"),
            P("tensor"),
            P("tensor", "fsdp"),
            P(),
        ),
        check_vma=False,
    )
```

```python
from functools import partial

import jax
import jax.numpy as jnp
from jax import lax
from jax.experimental import pallas as pl
from jax.experimental.pallas import tpu as pltpu
from jax.sharding import PartitionSpec as P

HEAD_DIM = 64
BLOCK = 128
TRUNK_BLK = 8
BRANCHES = 4
LEAVES = 2
TREE_BLK = 20


epsilon = 1e-05
far_below = -1e30


def layer_norm(values, norm_gain, norm_shift):
    center = values - jnp.mean(values, axis=1, keepdims=True)
    inverse = lax.rsqrt(jnp.mean(center * center, axis=1, keepdims=True) + epsilon)
    normed = center * inverse
    return (normed * norm_gain + norm_shift, normed, inverse)


def norm_back(gradient, normed, inverse, norm_gain):
    scaled = gradient * norm_gain
    return inverse * (
        scaled
        - jnp.mean(scaled, axis=1, keepdims=True)
        - normed * jnp.mean(scaled * normed, axis=1, keepdims=True)
    )


def slot_labels(order_row):
    position = order_row % TREE_BLK
    return (order_row // TREE_BLK, jnp.where(position < TRUNK_BLK, 0, position - TRUNK_BLK + 1))


def spread_rows(values):
    return jnp.broadcast_to(values[:, None], (values.shape[0], BLOCK)).reshape(-1)


def row_labels(labels, first_slot, slot_count):
    return tuple(
        (
            spread_rows(lax.dynamic_slice_in_dim(label_table, first_slot, slot_count))
            for label_table in labels
        )
    )


def visible(query_labels, key_labels):
    query_tree, query_seg = query_labels
    key_tree, key_seg = key_labels
    parent = jnp.where(query_seg > BRANCHES, 1 + (query_seg - BRANCHES - 1) // LEAVES, 0)
    reaches = (
        (key_seg[None, :] == 0)
        | (key_seg[None, :] == query_seg[:, None])
        | (key_seg[None, :] == parent[:, None])
    )
    return (query_tree[:, None] == key_tree[None, :]) & reaches


def head_view(matrix):
    return matrix.reshape(matrix.shape[0], matrix.shape[1] // HEAD_DIM, HEAD_DIM)


def scores_of(query_heads, key_heads):
    return jnp.einsum(
        "qhd,khd->hqk", query_heads, key_heads, preferred_element_type=jnp.float32
    ) * HEAD_DIM ** (-0.5)


def weights_of(scores, log_total, allowed):
    return jnp.where(allowed[None], jnp.exp(scores - log_total[:, :, None]), 0.0)


def score_grads(query_heads, grad_heads, key_heads, value_heads, log_total, row_delta, allowed):
    weights = weights_of(scores_of(query_heads, key_heads), log_total, allowed)
    prob_grad = jnp.einsum(
        "qhd,khd->hqk", grad_heads, value_heads, preferred_element_type=jnp.float32
    )
    return (
        (weights * (prob_grad - row_delta[:, :, None])).astype(jnp.bfloat16),
        weights.astype(jnp.bfloat16),
    )


def shards(
    patches,
    out_grad,
    block_order,
    first_gain,
    first_shift,
    attn_proj,
    attn_bias,
    out_proj,
    out_bias,
    second_gain,
    second_shift,
    up_proj,
    up_bias,
    down_proj,
    down_bias,
):
    attn_full, out_full, up_full, down_full = (
        lax.all_gather(attn_proj, "fsdp", axis=1, tiled=True),
        lax.all_gather(out_proj, "fsdp", axis=1, tiled=True),
        lax.all_gather(up_proj, "fsdp", axis=0, tiled=True),
        lax.all_gather(down_proj, "fsdp", axis=1, tiled=True),
    )
    labels = slot_labels(block_order[0])
    row_count = patches.shape[0]
    own_slots = row_count // BLOCK
    query_labels = row_labels(labels, lax.axis_index("context") * own_slots, own_slots)
    head_width = attn_full.shape[2]
    head_count = head_width // HEAD_DIM
    key_block = 4 * BLOCK
    block_slots = key_block // BLOCK
    score_scale = HEAD_DIM ** (-0.5)
    inputs = patches.astype(jnp.float32)
    first_norm, first_normed, first_inverse = layer_norm(inputs, first_gain, first_shift)
    first_low = first_norm.astype(jnp.bfloat16)
    projected = jnp.einsum("rd,cde->cre", first_low, attn_full, preferred_element_type=jnp.float32)
    queries = (projected[0] + attn_bias[0]).astype(jnp.bfloat16)
    keys_low = projected[1].astype(jnp.bfloat16)
    values_low = (projected[2] + attn_bias[1]).astype(jnp.bfloat16)
    keys_all = lax.all_gather(
        jnp.concatenate([keys_low, values_low], axis=1), "context", axis=0, tiled=True
    )
    block_count = keys_all.shape[0] // key_block
    query_heads = head_view(queries)

    def key_piece(step_index):
        key_slab = lax.dynamic_slice_in_dim(keys_all, step_index * key_block, key_block, 0)
        allowed = visible(query_labels, row_labels(labels, step_index * block_slots, block_slots))
        return (head_view(key_slab[:, :head_width]), head_view(key_slab[:, head_width:]), allowed)

    def total_step(step_index, carried):
        running_top, running_sum = carried
        key_heads, value_heads, allowed = key_piece(step_index)
        masked = jnp.where(allowed[None], scores_of(query_heads, key_heads), far_below)
        new_top = jnp.maximum(running_top, jnp.max(masked, axis=2))
        kept_exp = jnp.where(allowed[None], jnp.exp(masked - new_top[:, :, None]), 0.0)
        return (new_top, running_sum * jnp.exp(running_top - new_top) + jnp.sum(kept_exp, axis=2))

    start_top = jnp.full((head_count, row_count), far_below, jnp.float32)
    running_top, running_sum = lax.fori_loop(
        0, block_count, total_step, (start_top, jnp.zeros((head_count, row_count), jnp.float32))
    )
    log_total = running_top + jnp.log(running_sum)

    def mix_step(step_index, mixed):
        key_heads, value_heads, allowed = key_piece(step_index)
        weights = weights_of(scores_of(query_heads, key_heads), log_total, allowed).astype(
            jnp.bfloat16
        )
        return mixed + jnp.einsum(
            "hqk,khd->qhd", weights, value_heads, preferred_element_type=jnp.float32
        )

    attended = lax.fori_loop(
        0, block_count, mix_step, jnp.zeros((row_count, head_count, HEAD_DIM), jnp.float32)
    )
    attended_low = attended.reshape(row_count, head_width).astype(jnp.bfloat16)
    attn_part = jnp.dot(attended_low, out_full, preferred_element_type=jnp.float32)
    middle = inputs + (lax.psum(attn_part, "tensor") + out_bias)
    second_norm, second_normed, second_inverse = layer_norm(middle, second_gain, second_shift)
    second_low = second_norm.astype(jnp.bfloat16)
    pre_act = jnp.dot(second_low, up_full, preferred_element_type=jnp.float32) + up_bias
    hidden, gelu_back = jax.vjp(partial(jax.nn.gelu, approximate=False), pre_act)
    hidden_low = hidden.astype(jnp.bfloat16)
    mlp_part = jnp.dot(hidden_low, down_full, preferred_element_type=jnp.float32)
    result = (
        middle + (lax.psum(mlp_part.astype(jnp.bfloat16), "tensor").astype(jnp.float32) + down_bias)
    ).astype(jnp.bfloat16)
    top_grad = out_grad.astype(jnp.float32)
    grad_down_bias = jnp.sum(top_grad, axis=0)
    grad_down = jnp.einsum("rf,rd->fd", hidden_low, out_grad, preferred_element_type=jnp.float32)
    hidden_grad = jnp.einsum("rd,fd->rf", out_grad, down_full, preferred_element_type=jnp.float32)
    pre_grad = gelu_back(hidden_grad)[0].astype(jnp.bfloat16)
    grad_up_bias = jnp.sum(pre_grad.astype(jnp.float32), axis=0)
    grad_up = jnp.einsum("rd,rf->df", second_low, pre_grad, preferred_element_type=jnp.float32)
    second_part = jnp.einsum("rf,df->rd", pre_grad, up_full, preferred_element_type=jnp.float32)
    second_grad = lax.psum(second_part, "tensor")
    grad_second_gain = jnp.sum(second_grad * second_normed, axis=0)
    grad_second_shift = jnp.sum(second_grad, axis=0)
    middle_grad = top_grad + norm_back(second_grad, second_normed, second_inverse, second_gain)
    branch_grad = middle_grad.astype(jnp.bfloat16)
    grad_out_bias = jnp.sum(branch_grad.astype(jnp.float32), axis=0)
    grad_out = jnp.einsum(
        "re,rd->ed", attended_low, branch_grad, preferred_element_type=jnp.float32
    )
    attended_grad = jnp.einsum(
        "rd,ed->re", branch_grad, out_full, preferred_element_type=jnp.float32
    ).astype(jnp.bfloat16)
    grad_heads = head_view(attended_grad)

    def delta_step(step_index, row_delta):
        key_heads, value_heads, allowed = key_piece(step_index)
        weights = weights_of(scores_of(query_heads, key_heads), log_total, allowed)
        prob_grad = jnp.einsum(
            "qhd,khd->hqk", grad_heads, value_heads, preferred_element_type=jnp.float32
        )
        return row_delta + jnp.sum(weights * prob_grad, axis=2)

    row_delta = lax.fori_loop(
        0, block_count, delta_step, jnp.zeros((head_count, row_count), jnp.float32)
    )
    query_start = jnp.zeros((row_count, head_count, HEAD_DIM), jnp.float32)

    def back_step(step_index, carried):
        query_acc, key_acc = carried
        key_heads, value_heads, allowed = key_piece(step_index)
        score_low, weights_low = score_grads(
            query_heads, grad_heads, key_heads, value_heads, log_total, row_delta, allowed
        )
        query_acc = query_acc + jnp.einsum(
            "hqk,khd->qhd", score_low, key_heads, preferred_element_type=jnp.float32
        )
        key_part = jnp.einsum(
            "hqk,qhd->khd", score_low, query_heads, preferred_element_type=jnp.float32
        )
        value_part = jnp.einsum(
            "hqk,qhd->khd", weights_low, grad_heads, preferred_element_type=jnp.float32
        )
        joined = jnp.concatenate(
            [key_part.reshape(key_block, head_width), value_part.reshape(key_block, head_width)],
            axis=1,
        )
        return (
            query_acc,
            lax.dynamic_update_slice_in_dim(key_acc, joined, step_index * key_block, 0),
        )

    key_start = jnp.zeros((keys_all.shape[0], 2 * head_width), jnp.float32)
    query_acc, key_acc = lax.fori_loop(0, block_count, back_step, (query_start, key_start))
    key_value_grad = lax.psum_scatter(key_acc, "context", scatter_dimension=0, tiled=True)
    query_grad = (query_acc.reshape(row_count, head_width) * score_scale).astype(jnp.bfloat16)
    key_grad = (key_value_grad[:, :head_width] * score_scale).astype(jnp.bfloat16)
    value_grad = key_value_grad[:, head_width:].astype(jnp.bfloat16)
    stacked = jnp.stack([query_grad, key_grad, value_grad])
    grad_attn_bias = jnp.stack(
        [
            jnp.sum(query_grad.astype(jnp.float32), axis=0),
            jnp.sum(value_grad.astype(jnp.float32), axis=0),
        ]
    )
    grad_attn = jnp.einsum("rd,cre->cde", first_low, stacked, preferred_element_type=jnp.float32)
    first_grad = lax.psum(
        jnp.einsum("cre,cde->rd", stacked, attn_full, preferred_element_type=jnp.float32), "tensor"
    )
    grad_first_gain = jnp.sum(first_grad * first_normed, axis=0)
    grad_first_shift = jnp.sum(first_grad, axis=0)
    patch_grad = middle_grad + norm_back(first_grad, first_normed, first_inverse, first_gain)
    wide_attn, wide_out, wide_up, wide_down = (
        lax.psum_scatter(grad_attn, ("fsdp", "context"), scatter_dimension=1, tiled=True),
        lax.psum_scatter(grad_out, ("fsdp", "context"), scatter_dimension=1, tiled=True),
        lax.psum_scatter(grad_up, ("fsdp", "context"), scatter_dimension=0, tiled=True),
        lax.psum_scatter(grad_down, ("fsdp", "context"), scatter_dimension=1, tiled=True),
    )
    grad_attn, grad_out, grad_up, grad_down = (
        lax.all_gather(wide_attn, "context", axis=1, tiled=True),
        lax.all_gather(wide_out, "context", axis=1, tiled=True),
        lax.all_gather(wide_up, "context", axis=0, tiled=True),
        lax.all_gather(wide_down, "context", axis=1, tiled=True),
    )
    small_grads = lax.psum(
        (
            grad_first_gain,
            grad_first_shift,
            grad_attn_bias,
            grad_out_bias,
            grad_second_gain,
            grad_second_shift,
            grad_up_bias,
            grad_down_bias,
        ),
        ("fsdp", "context"),
    )
    return (
        result,
        patch_grad,
        small_grads[0],
        small_grads[1],
        grad_attn,
        small_grads[2],
        grad_out,
        small_grads[3],
        small_grads[4],
        small_grads[5],
        grad_up,
        small_grads[6],
        grad_down,
        small_grads[7],
    )


bf16 = jnp.bfloat16
f32 = jnp.float32
VMEM = pl.BlockSpec(memory_space=pltpu.VMEM)
SMEM = pl.BlockSpec(memory_space=pltpu.SMEM)
ANY = pl.BlockSpec(memory_space=pl.ANY)
MESH = pl.DeviceIdType.MESH
LIMIT = 61 * 1024 * 1024


def dot_nn(a, b):
    return lax.dot_general(a, b, (((1,), (0,)), ((), ())), preferred_element_type=f32)


def dot_nt(a, b):
    return lax.dot_general(a, b, (((1,), (1,)), ((), ())), preferred_element_type=f32)


def dot_tn(a, b):
    return lax.dot_general(a, b, (((0,), (0,)), ((), ())), preferred_element_type=f32)


class Here:
    def __init__(self, fsdp_count):
        self.f = lax.axis_index("fsdp")
        self.c = lax.axis_index("context")
        self.t = lax.axis_index("tensor")
        self.x = self.t // 2
        self.k = self.t % 2
        self.core = (self.f, self.c, 2 * self.x + 1 - self.k)
        self.xp = (self.f, self.c, 2 * (1 - self.x) + self.k)
        self.yp = (self.f, 1 - self.c, self.t)
        self.z = [((self.f + i) % fsdp_count, self.c, self.t) for i in range(1, fsdp_count)]
        self.back = [(self.f + fsdp_count - i) % fsdp_count for i in range(1, fsdp_count)]


def greet(devices):
    barrier = pltpu.get_barrier_semaphore()
    for device in devices:
        pl.semaphore_signal(barrier, inc=1, device_id=device, device_id_type=MESH)
    pl.semaphore_wait(barrier, len(devices))


class Post:
    def __init__(self, send_sem, recv_sem):
        self.send_sem, self.recv_sem = send_sem, recv_sem
        self.sent, self.open = [], []

    def send(self, src, dst, device):
        index = len(self.sent)
        copy = pltpu.make_async_remote_copy(
            src_ref=src,
            dst_ref=dst,
            send_sem=self.send_sem.at[index],
            recv_sem=self.recv_sem.at[index],
            device_id=device,
            device_id_type=MESH,
        )
        copy.start()
        self.sent.append(copy)
        self.open.append((copy, device))
        return copy

    def got(self, copy):
        left = [entry for entry in self.open if entry[0] is not copy]
        if len(left) < len(self.open):
            copy.wait_recv()
        self.open = left

    def got_from(self, device):
        for copy, to in self.open:
            if to is device:
                self.got(copy)

    def close(self):
        for copy, _ in self.open:
            copy.wait_recv()
        for copy in self.sent:
            copy.wait_send()


def ds(start, size, step=16):
    return pl.ds(pl.multiple_of(start, step), size)


TRUNK = TRUNK_BLK * BLOCK
SUB = (1 + LEAVES) * BLOCK
KEYS = TRUNK + SUB
OWN = 2 * BLOCK + SUB
PIECES = (
    (2 * BLOCK, TRUNK, 2 * BLOCK),
    (3 * BLOCK, TRUNK + BLOCK, BLOCK),
    (4 * BLOCK, TRUNK + BLOCK, 2 * BLOCK),
)


def own_places(s):
    return [2 * s, 2 * s + 1, 12 + 2 * s, 8 + s, 13 + 2 * s]


def row_norm(values):
    center = values - jnp.mean(values, axis=1, keepdims=True)
    inverse = lax.rsqrt(jnp.mean(center * center, axis=1, keepdims=True) + epsilon)
    return center * inverse, inverse

HALF = OWN // 2
UNIT = 16


def wide(vector):
    return vector[...].reshape(1, -1)


def first_kernel(
    fsdp_count, order, patches, grads, attn_proj, out_proj, up, d_own, up_bias, attn_bias, gain1, shift1, gain2, shift2, out_bias, down_bias,
    q_out, k_out, v_out, att_out, low_out, x_out, wh_out, g_up_out, g_down_out,
    middle_grad_out, mlp_own_out, mlp_send_out, g_out_own_out, g_out_send_out,
    lse, da, stats, up_stats,
    middle_grad, mlp_own, mlp_send, g_out_own, g_out_send,
    where, a_own, bias, rows_all, grads_all, wa, wh, wo_x, wu, wd, bias_all,
    low_all, low, low_own, x_own, g_own, q, k, v, vt, attended, att_t, att_x, st, pt,
    middle, normed, inverse, low2, hidden, pre_grad, second, second_send, second_x, branch, da_send, g_up, g_down, g_sum,
    local, ss, rs,
):
    me = Here(fsdp_count)
    f, c, x, core, t = me.f, me.c, me.x, me.k, me.t
    s = 2 * c + core
    units = patches.shape[0]
    part = units // 4
    width = patches.shape[2]
    deep = up.shape[0]
    head_width = attn_proj.shape[2]
    own_copies = []

    def keep(src, dst):
        copy = pltpu.make_async_copy(src, dst, local.at[len(own_copies)])
        copy.start()
        own_copies.append(copy)

    keep(patches, rows_all.at[pl.ds(units * c, units)])
    keep(grads, grads_all.at[pl.ds(units * c, units)])
    keep(up, wu.at[core, ds(deep * f, deep)])
    keep(d_own, wd.at[core, ds(deep * f, deep)])
    greet([me.core, me.xp, me.yp] + me.z)
    post = Post(ss, rs)
    there = units * (1 - c)
    half = deep // 2
    strip, other_strip = half * c, half * (1 - c)

    def quarter(array, index, piece, count):
        size = part // count
        return array.at[pl.ds(there + part * index + size * piece, size)]

    def to_y(src, dst, piece, count):
        size = part // count
        return post.send(
            src.at[pl.ds(part * t + size * piece, size)],
            dst.at[pl.ds(units * c + part * t + size * piece, size)],
            me.yp,
        )

    def relay(piece, device):
        return post.send(piece, piece, device)

    third = deep // 3
    lone, other_lone = 2 * third * c, 2 * third * (1 - c)
    a_part = lambda source, row, count: wa.at[core, ds(deep * source + row, count)]
    pieces = 4
    patches_y = [to_y(patches, rows_all, i, pieces) for i in range(pieces)]
    a_own[:, 0:128] = attn_proj[0, :, 0:128]
    a_own[:, 128:256] = attn_proj[1, :, 0:128]
    a_own[:, 256:384] = attn_proj[2, :, 0:128]
    out_t = out_proj[...].T
    a_own[:, 384:512] = jnp.concatenate([attn_proj[0, :, 128:head_width], attn_proj[1, :, 128:head_width]], axis=1)
    a_own[:, 512:640] = jnp.concatenate([attn_proj[2, :, 128:head_width], out_t[:, 128:head_width]], axis=1)
    a_own[:, 640:768] = out_t[:, 0:128]
    bias[...] = jnp.zeros_like(bias)
    bias[0:1, :] = wide(up_bias)
    bias[1:3, 0:head_width] = attn_bias[...]
    a_z = [post.send(a_own.at[ds(lone, third)], a_part(f, lone, third), device) for device in me.z]
    post.send(a_own, wa.at[core, ds(deep * f, deep)], me.core)
    post.send(bias, bias_all.at[core], me.core)
    gain_row, shift_row = wide(gain1), wide(shift1)

    def norm_units(start, count):
        values = rows_all[pl.ds(start, count)].reshape(count * UNIT, width).astype(f32)
        normed_rows, _ = row_norm(values)
        low_rows = (normed_rows * gain_row + shift_row).astype(bf16)
        low_all[pl.ds(start, count)] = low_rows.reshape(count, UNIT, width)

    block_units = BLOCK // UNIT
    own_blocks = units // block_units

    def norm_own(j, carried):
        norm_units(units * c + block_units * j, block_units)
        return carried

    slots = order.shape[1]

    def find(place, carried):
        slot = jnp.int32(0)
        for j in range(slots):
            slot = jnp.where(order[0, j] == place, j, slot)
        where[place] = slot * block_units
        return carried

    lax.fori_loop(0, slots, find, 0)
    wa[core, ds(deep * f, deep), :] = a_own[...]
    bias_all[core] = bias[...]
    own_copies[0].wait()
    lax.fori_loop(0, own_blocks - pieces, norm_own, 0)
    size = part // pieces
    over = (t + 2) % 4
    beside, across = t + 1 - 2 * core, over + 1 - 2 * core
    patches_x, patches_core = [], []
    for i in range(pieces):
        post.got(patches_y[i])
        patches_x.append(relay(quarter(rows_all, t, i, pieces), me.xp))
        patches_core.append(relay(quarter(rows_all, t, i, pieces), me.core))
        norm_units(there + part * t + size * i, size)
        if i == 2:
            a_y = []
            for copy, source in zip(a_z, me.back):
                post.got(copy)
                a_y.append(relay(a_part(source, lone, third), me.yp))
                relay(a_part(source, lone, third), me.core)
            a_shared = [
                post.send(a_own.at[ds(third, third)], a_part(f, third, third), device) for device in me.z
            ]
        norm_own(own_blocks - pieces + i, 0)
    post.send(up, wu.at[core, ds(deep * f, deep)], me.core)
    post.send(d_own, wd.at[core, ds(deep * f, deep)], me.core)
    for i in range(pieces):
        post.got(patches_core[i])
        norm_units(there + part * beside + size * i, size)
    patches_core = []
    for i in range(pieces):
        post.got(patches_x[i])
        patches_core.append(relay(quarter(rows_all, over, i, pieces), me.core))
        norm_units(there + part * over + size * i, size)
    for copy, source in zip(a_shared, me.back):
        post.got(copy)
        relay(a_part(source, third, third), me.core)
    u_z = [
        post.send(up.at[ds(strip, half)], wu.at[core, ds(deep * f + strip, half)], device) for device in me.z
    ]
    for copy, source in zip(a_y, me.back):
        post.got(copy)
        relay(a_part(source, other_lone, third), me.core)
    grads_y = [to_y(grads, grads_all, i, 2) for i in range(2)]
    for i in range(pieces):
        post.got(patches_core[i])
        norm_units(there + part * across + size * i, size)

    def block_of(array, place):
        return array[pl.ds(where[place], block_units)].reshape(BLOCK, width)

    def trunk_step(j, carried):
        low[ds(j * BLOCK, BLOCK), :] = block_of(low_all, j)
        return carried

    lax.fori_loop(0, TRUNK_BLK, trunk_step, 0)
    places = own_places(s)
    for j in range(2, 5):
        low[TRUNK + (j - 2) * BLOCK : TRUNK + (j - 1) * BLOCK, :] = block_of(low_all, places[j])
    for j, place in enumerate(places):
        x_own[pl.ds(j * BLOCK, BLOCK), :] = block_of(rows_all, place)
    low_own[0 : 2 * BLOCK, :] = low[ds(2 * BLOCK * s, 2 * BLOCK), :]
    low_own[2 * BLOCK :, :] = low[TRUNK:, :]
    post.got_from(me.core)

    def assemble(i):
        slab = (0, 1, 2, 5)[i]
        wh[i, :, 0:128] = wa[0, :, 128 * slab : 128 * slab + 128]
        wh[i, :, 128:256] = wa[1, :, 128 * slab : 128 * slab + 128]
        start = 384 + 64 * i
        wh[i, :, 256:384] = jnp.concatenate(
            [wa[0, :, start : start + 64], wa[1, :, start : start + 64]], axis=1
        )

    for i in range(4):
        assemble(i)
    wo_quarter = width // 4
    wo_rows = ds(wo_quarter * (2 * c + core), wo_quarter)
    wo_copy = post.send(wh.at[3, wo_rows], wo_x.at[wo_rows], me.xp)
    keep(wh, wh_out)

    def heads_row(row):
        a, b = bias_all[0, row : row + 1, :], bias_all[1, row : row + 1, :]
        return jnp.concatenate([a[:, 0:128], b[:, 0:128], a[:, 128:192], b[:, 128:192]], axis=1)

    q[...] = ((dot_nn(low_own[...], wh[0]) + heads_row(1)).astype(bf16) * HEAD_DIM ** (-0.5)).astype(bf16)
    value_bias = heads_row(2)

    def project(j, carried):
        rows = ds(j * (KEYS // 2), KEYS // 2)
        k[rows, :] = dot_nn(low[rows, :], wh[1]).astype(bf16)
        v[rows, :] = (dot_nn(low[rows, :], wh[2]) + value_bias).astype(bf16)
        return carried

    lax.fori_loop(0, 2, project, 0)
    vt[...] = v[...].T
    for src, dst in ((q, q_out), (k, k_out), (v, v_out), (low_own, low_out), (x_own, x_out)):
        keep(src, dst)
    lane = lax.broadcasted_iota(jnp.int32, (OWN, 128), 1) // HEAD_DIM

    def head(h, carried):
        slab, side = h // 2, h % 2
        lanes = pl.ds(pl.multiple_of(slab * 128, 128), 128)
        own_q = q[:, lanes]
        q_part = jnp.where(lane == side, own_q, jnp.zeros_like(own_q))
        st[0:TRUNK, :] = dot_nt(k[0:TRUNK, lanes], q_part)
        for q_row, k_row, count in PIECES:
            st[TRUNK : TRUNK + count, q_row : q_row + BLOCK] = dot_nt(
                k[k_row : k_row + count, lanes], q_part[q_row : q_row + BLOCK]
            )
        tops, sums = [], []
        for j in range(OWN // BLOCK):
            cols = slice(j * BLOCK, (j + 1) * BLOCK)
            count = TRUNK + (0 if j < 2 else PIECES[j - 2][2])
            top = jnp.full((8, BLOCK), far_below, f32)
            for r in range(0, count, BLOCK):
                piece = st[r : r + BLOCK, cols].reshape(BLOCK // 8, 8, BLOCK)
                top = jnp.maximum(top, jnp.max(piece, axis=0))
            top = jnp.max(top, axis=0, keepdims=True)
            total = jnp.zeros((8, BLOCK), f32)
            for r in range(0, count, BLOCK):
                weight = jnp.exp(st[r : r + BLOCK, cols] - top)
                total = total + jnp.sum(weight.reshape(BLOCK // 8, 8, BLOCK), axis=0)
                pt[r : r + BLOCK, cols] = weight.astype(bf16)
            tops.append(top)
            sums.append(jnp.sum(total, axis=0, keepdims=True))
        total = jnp.concatenate(sums, axis=1)
        head_rows, side_rows = ds(h * HEAD_DIM, HEAD_DIM), ds(side * HEAD_DIM, HEAD_DIM)
        att_t[side_rows, :] = dot_nn(vt[head_rows, 0:TRUNK], pt[0:TRUNK, :])
        for q_row, k_row, count in PIECES:
            cols = slice(q_row, q_row + BLOCK)
            att_t[side_rows, cols] += dot_nn(
                vt[head_rows, k_row : k_row + count], pt[TRUNK : TRUNK + count, cols]
            )
        att_t[side_rows, :] = att_t[side_rows, :] / total
        lse[pl.ds(h, 1), :] = jnp.concatenate(tops, axis=1) + jnp.log(total)
        return carried

    mine, far = HALF * x, HALF * (1 - x)
    here_rows, far_rows = ds(mine, HALF), ds(far, HALF)
    att_copies = []

    def slab_heads(slab):
        lax.fori_loop(2 * slab, 2 * slab + 2, head, 0)
        lanes = pl.ds(128 * slab, 128)
        attended[:, lanes] = att_t[...].T.astype(bf16)
        att_copies.append(post.send(attended.at[far_rows, lanes], att_x.at[:, lanes], me.xp))

    def grads_on(i):
        post.got(grads_y[i])
        relay(quarter(grads_all, t, i, 2), me.core)
        return relay(quarter(grads_all, t, i, 2), me.xp)

    def strips_on(copies, array):
        passed = []
        for copy, source in zip(copies, me.back):
            post.got(copy)
            piece = array.at[core, ds(deep * source + strip, half)]
            passed.append(relay(piece, me.yp))
            relay(piece, me.core)
        return passed

    def strips_in(copies, array):
        for copy, source in zip(copies, me.back):
            post.got(copy)
            relay(array.at[core, ds(deep * source + other_strip, half)], me.core)

    d_part = lambda source, row: wd.at[core, ds(deep * source + row, third)]
    post.got(wo_copy)
    wo_y = relay(wo_x.at[wo_rows], me.yp)
    wo_core = [relay(wo_x.at[wo_rows], me.core)]
    grads_x = [grads_on(0)]
    slab_heads(0)
    grads_x.append(grads_on(1))
    slab_heads(1)
    u_y = strips_on(u_z, wu)
    d_lone = [post.send(d_own.at[ds(lone, third)], d_part(f, lone), device) for device in me.z]
    post.got(wo_y)
    wo_core.append(relay(wo_x.at[ds(wo_quarter * (2 * (1 - c) + core), wo_quarter)], me.core))
    slab_heads(2)
    keep(attended, att_out)
    middle[...] = (
        x_own[here_rows, :].astype(f32) + wide(out_bias) + dot_nt(attended[here_rows, :], wh[3])
    )
    d_y = []
    for copy, source in zip(d_lone, me.back):
        post.got(copy)
        d_y.append(relay(d_part(source, lone), me.yp))
        relay(d_part(source, lone), me.core)
    d_shared = [post.send(d_own.at[ds(third, third)], d_part(f, third), device) for device in me.z]
    for copy in wo_core + att_copies:
        post.got(copy)
    middle[...] += dot_nt(att_x[...], wo_x[...])
    n2, s2 = row_norm(middle[...])
    normed[...] = n2
    inverse[...] = s2
    low2[here_rows, :] = (n2 * wide(gain2) + wide(shift2)).astype(bf16)
    chunk = HALF // 2
    here_chunks = [ds(mine + chunk * i, chunk) for i in range(2)]
    far_chunks = [ds(far + chunk * i, chunk) for i in range(2)]
    low_copies = [post.send(low2.at[rows], low2.at[rows], me.xp) for rows in here_chunks]
    for i in range(2):
        post.got(grads_x[i])
        relay(quarter(grads_all, over, i, 2), me.core)
    strips_in(u_y, wu)
    for copy in own_copies[1:4]:
        copy.wait()
    post.got_from(me.core)
    for j, place in enumerate(places):
        g_own[pl.ds(j * BLOCK, BLOCK), :] = block_of(grads_all, place)
    tile = 256

    def tiles(step):
        def tile_step(j, carried):
            shard, lanes = j // 3, pl.ds(pl.multiple_of(j % 3 * tile, 128), tile)
            step(shard, lanes, pl.ds(pl.multiple_of(j * tile, 128), tile))
            return carried

        lax.fori_loop(0, 6, tile_step, 0)

    def forward(rows):
        def step(shard, lanes, out):
            pre = dot_nn(low2[rows, :], wu[shard, :, lanes]) + bias_all[shard, 0:1, lanes]
            below = 0.5 * (1.0 + lax.erf(pre * (2.0**-0.5)))
            density = jnp.exp(-0.5 * pre * pre) * (2.0 * jnp.pi) ** -0.5
            hidden[rows, out] = (pre * below).astype(bf16)
            pre_grad[rows, out] = (below + pre * density).astype(bf16)

        tiles(step)

    def backward(rows, count):
        second[rows, :] = jnp.zeros((count, width), f32)

        def step(shard, lanes, out):
            back = dot_nn(g_own[rows, :], wd[shard, :, lanes])
            low_back = (back * pre_grad[rows, out].astype(f32)).astype(bf16)
            pre_grad[rows, out] = low_back
            second[rows, :] += dot_nt(low_back, wu[shard, :, lanes])

        tiles(step)

    def mlp(rows):
        return dot_nt(hidden[rows, 0:width], wd[0]) + dot_nt(hidden[rows, width:], wd[1])

    own_lanes, sibling_lanes = (
        pl.ds(pl.multiple_of(width * side, 128), width) for side in (core, 1 - core)
    )
    sibling_copies = {}

    def weight_grad(index, left, right, grad):
        def step(shard, lanes, out):
            grad[:, out] = dot_tn(left[...], right[:, out]).astype(bf16)

        tiles(step)
        sibling_copies[index] = post.send(grad.at[:, sibling_lanes], g_sum.at[index], me.core)

    forward(here_rows)
    for i in range(2):
        post.got(low_copies[i])
        forward(far_chunks[i])
    weight_grad(1, g_own, hidden, g_down)
    for copies, row in ((d_shared, third), (d_y, other_lone)):
        for copy, source in zip(copies, me.back):
            post.got(copy)
            relay(d_part(source, row), me.core)
    post.got_from(me.core)
    second_copies = []
    for i in range(2):
        backward(far_chunks[i], chunk)
        second_send[i] = second[far_chunks[i], :].astype(bf16)
        second_copies.append(post.send(second_send.at[i], second_x.at[i], me.xp))
    backward(here_rows, HALF)

    weight_grad(0, low2, pre_grad, g_up)
    total = [jnp.zeros((1, width), f32)] * 4
    for i in range(2):
        rows = here_chunks[i]
        part_rows = slice(chunk * i, chunk * i + chunk)
        post.got(second_copies[i])
        second_grad = second[rows, :] + second_x[i].astype(f32)
        n2 = normed[part_rows, :]
        dy = g_own[rows, :].astype(f32)
        grad = dy + norm_back(second_grad, n2, inverse[part_rows, :], wide(gain2))
        middle_grad[part_rows, :] = grad
        low_grad = grad.astype(bf16)
        branch[part_rows, :] = low_grad
        da_send[part_rows, :] = dot_nn(low_grad, wo_x[...]).astype(bf16)
        post.send(da_send.at[pl.ds(chunk * i, chunk)], da.at[rows], me.xp)
        terms = (second_grad * n2, second_grad, dy, low_grad.astype(f32))
        total = [a + jnp.sum(b, axis=0, keepdims=True) for a, b in zip(total, terms)]
    for i in range(4):
        stats[i : i + 1, :] = total[i]
    up_stats[0:1, :] = jnp.sum(pre_grad[:, 0:width].astype(f32), axis=0, keepdims=True)
    up_stats[1:2, :] = jnp.sum(pre_grad[:, width:].astype(f32), axis=0, keepdims=True)
    mlp_send[...] = mlp(far_rows).astype(bf16)
    mlp_own[...] = middle[...] + mlp(here_rows) + wide(down_bias)
    for src, out in ((middle_grad, middle_grad_out), (mlp_own, mlp_own_out), (mlp_send, mlp_send_out)):
        keep(src, out)
    da[here_rows, :] = dot_nn(branch[...], wh[3]).astype(bf16)
    g_out_send[...] = dot_tn(branch[...], att_x[...]).astype(bf16)
    g_out_own[...] = dot_tn(branch[...], attended[here_rows, :]).astype(bf16)
    keep(g_out_send, g_out_send_out)
    keep(g_out_own, g_out_own_out)
    for index, (grad, out) in enumerate(((g_up, g_up_out), (g_down, g_down_out))):
        post.got(sibling_copies[index])

        def add_sibling(j, carried):
            rows = ds(j * BLOCK, BLOCK)
            g_sum[index, rows, :] = (
                g_sum[index, rows, :].astype(f32) + grad[rows, own_lanes].astype(f32)
            ).astype(bf16)
            return carried

        lax.fori_loop(0, width // BLOCK, add_sibling, 0)
        keep(g_sum.at[index], out)
    post.close()
    for copy in own_copies[4:]:
        copy.wait()


def first_half(fsdp_count, order, patches, grads, attn_proj, out_proj, up, down_t, *vectors):
    width = patches.shape[1]
    shape = jax.ShapeDtypeStruct
    vmem = pltpu.VMEM
    units = 2 * up.shape[1]
    all_units = 2 * patches.shape[0] // UNIT
    deep = up.shape[0]
    fold = lambda a: a.reshape(-1, UNIT, width)
    return pl.pallas_call(
        partial(first_kernel, fsdp_count),
        out_shape=(
            shape((OWN, 384), bf16),
            shape((KEYS, 384), bf16),
            shape((KEYS, 384), bf16),
            shape((OWN, 384), bf16),
            shape((OWN, width), bf16),
            shape((OWN, width), bf16),
            shape((4, width, 384), bf16),
            shape((width, width), bf16),
            shape((width, width), bf16),
            shape((HALF, width), f32),
            shape((HALF, width), f32),
            shape((HALF, width), bf16),
            shape((width, 384), bf16),
            shape((width, 384), bf16),
            shape((8, OWN), f32),
            shape((OWN, 384), bf16),
            shape((4, width), f32),
            shape((2, width), f32),
        ),
        in_specs=[SMEM, ANY, ANY, VMEM, VMEM, ANY, ANY] + [VMEM] * 8,
        out_specs=(ANY,) * 14 + (VMEM,) * 4,
        scratch_shapes=[
            vmem((HALF, width), f32),
            vmem((HALF, width), f32),
            vmem((HALF, width), bf16),
            vmem((width, 384), bf16),
            vmem((width, 384), bf16),
            pltpu.SMEM(order.shape[1:], jnp.int32),
            vmem((deep, width), bf16),
            vmem((8, width), f32),
            vmem((all_units, UNIT, width), bf16),
            vmem((all_units, UNIT, width), bf16),
            vmem((2, width, width), bf16),
            vmem((4, width, 384), bf16),
            vmem((width, 384), bf16),
            vmem((2, width, up.shape[1]), bf16),
            vmem((2, width, up.shape[1]), bf16),
            vmem((2, 8, width), f32),
            vmem((all_units, UNIT, width), bf16),
            vmem((KEYS, width), bf16),
            vmem((OWN, width), bf16),
            vmem((OWN, width), bf16),
            vmem((OWN, width), bf16),
            vmem((OWN, 384), bf16),
            vmem((KEYS, 384), bf16),
            vmem((KEYS, 384), bf16),
            vmem((384, KEYS), bf16),
            vmem((OWN, 384), bf16),
            vmem((128, OWN), f32),
            vmem((HALF, 384), bf16),
            vmem((TRUNK + 2 * BLOCK, OWN), f32),
            vmem((TRUNK + 2 * BLOCK, OWN), bf16),
            vmem((HALF, width), f32),
            vmem((HALF, width), f32),
            vmem((HALF, 1), f32),
            vmem((OWN, width), bf16),
            vmem((OWN, units), bf16),
            vmem((OWN, units), bf16),
            vmem((OWN, width), f32),
            vmem((2, HALF // 2, width), bf16),
            vmem((2, HALF // 2, width), bf16),
            vmem((HALF, width), bf16),
            vmem((HALF, 384), bf16),
            vmem((width, units), bf16),
            vmem((width, units), bf16),
            vmem((2, width, width), bf16),
            pltpu.SemaphoreType.DMA((24,)),
            pltpu.SemaphoreType.DMA((112,)),
            pltpu.SemaphoreType.DMA((112,)),
        ],
        compiler_params=pltpu.CompilerParams(collective_id=0, has_side_effects=True, vmem_limit_bytes=LIMIT),
        name="first_half",
    )(order, fold(patches), fold(grads), attn_proj, out_proj, up, down_t, *vectors)


class StripSum:
    def __init__(self, me, post, fsdp_count, held, from_core, buffers):
        self.me, self.post, self.count = me, post, fsdp_count
        self.held, self.from_core = held, from_core
        self.from_y, self.from_z, self.done = buffers
        self.half = held.shape[0] // fsdp_count // 2

    def from_sibling(self, src):
        self.core_copy = self.post.send(src, self.from_core, self.me.core)

    def add_sibling(self):
        self.post.got(self.core_copy)
        half = self.half

        def step(j, carried):
            rows = ds(j * half, half)
            self.held[rows, :] = (self.held[rows, :].astype(f32) + self.from_core[rows, :].astype(f32)).astype(bf16)
            return carried

        lax.fori_loop(0, 2 * self.count, step, 0)

    def strip(self, g, side):
        return ds(self.half * (2 * g + side), self.half)

    def over_y(self):
        me = self.me
        self.y_copies = [
            self.post.send(self.held.at[self.strip(g, 1 - me.c)], self.from_y.at[g], me.yp)
            for g in range(self.count)
        ]

    def over_z(self):
        me = self.me
        for copy in self.y_copies:
            self.post.got(copy)

        def step(g, carried):
            rows = self.strip(g, me.c)
            self.held[rows, :] = (self.held[rows, :].astype(f32) + self.from_y[g].astype(f32)).astype(bf16)
            return carried

        lax.fori_loop(0, self.count, step, 0)
        self.z_copies = [
            self.post.send(self.held.at[self.strip((me.f + i + 1) % self.count, me.c)], self.from_z.at[i], device)
            for i, device in enumerate(me.z)
        ]

    def over_z_first(self):
        me, deep = self.me, 2 * self.half
        self.z_copies = [
            self.post.send(self.held.at[ds(deep * ((me.f + i + 1) % self.count), deep)], self.from_z.at[i], device)
            for i, device in enumerate(me.z)
        ]

    def finish_z_first(self):
        me, deep = self.me, 2 * self.half
        for copy in self.z_copies:
            self.post.got(copy)
        total = self.held[ds(deep * me.f, deep), :].astype(f32)
        for i in range(self.count - 1):
            total = total + self.from_z[i].astype(f32)
        self.done[0] = total.astype(bf16)
        self.last = self.post.send(self.done.at[0], self.done.at[1], me.yp)

    def finish(self):
        me = self.me
        for copy in self.z_copies:
            self.post.got(copy)
        total = self.held[self.strip(me.f, me.c), :].astype(f32)
        for i in range(self.count - 1):
            total = total + self.from_z[i].astype(f32)
        self.done[me.c] = total.astype(bf16)
        self.last = self.post.send(self.done.at[me.c], self.done.at[me.c], me.yp)


TALL, WIDE = 256, 256


def second_kernel(
    fsdp_count, q_in, k_in, v_in, att_in, low_in, x_in, wh_in, g_up, g_down,
    middle_grad_in, mlp_own_in, mlp_send, g_out_own_in, g_out_send_in, lse, da, mid_stats, up_stats, gain1,
    rows_out, up_out, rest_out, all_total, part_total,
    middle_grad, mlp_own, g_out_own, g_out_send, q, k, v, kt, attended, low_own, x_own, wh, up_own, down_own,
    delta, pt, dst, dk_acc, dv_acc, dq_t, dq, own_first, trunk, trunk_own, trunk_far, trunk_send, trunk_y, dkv_own,
    mlp_x, first_send, first_x, rows_own, out_core, out_sum, out_x, packed,
    from_core, from_y, from_z, done, deep_z, deep_done, stat_buf, stat_in, stat_z, local, ss, rs,
):
    me = Here(fsdp_count)
    f, c, x, core = me.f, me.c, me.x, me.k
    s = 2 * c + core
    pair = 2 * BLOCK
    units = HALF // UNIT
    width = x_in.shape[1]
    mine, far = HALF * x, HALF * (1 - x)
    here_rows, far_rows = ds(mine, HALF), ds(far, HALF)
    loads = []
    for src, held in (
        (g_up, up_own), (g_down, down_own), (k_in, k), (q_in, q), (v_in, v), (att_in, attended),
        (g_out_own_in, g_out_own), (g_out_send_in, g_out_send), (mlp_own_in, mlp_own),
        (low_in, low_own), (x_in, x_own), (middle_grad_in, middle_grad), (wh_in.at[pl.ds(0, 3)], wh),
    ):
        copy = pltpu.make_async_copy(src, held, local.at[len(loads)])
        copy.start()
        loads.append(copy)
    greet([me.core, me.xp, me.yp] + me.z)
    post = Post(ss, rs)
    mlp_copy = post.send(mlp_send, mlp_x, me.xp)
    buffers = [(from_y, from_z, done)] + [(None, deep_z.at[i], deep_done.at[i]) for i in range(2)]
    sums = [
        StripSum(me, post, fsdp_count, held, from_core, buffer)
        for held, buffer in zip((up_own, down_own, packed.at[core]), buffers)
    ]
    slab_own = pl.ds(pl.multiple_of(128 * core, 128), 128)
    slab_sibling = pl.ds(pl.multiple_of(128 * (1 - core), 128), 128)
    slab_both = pl.ds(256, 128)
    out_copies = []
    for i, src in enumerate((g_out_own_in, g_out_send_in)):
        for j, lanes in enumerate((slab_sibling, slab_both)):
            out_copies.append(post.send(src.at[:, lanes], out_core.at[i, j], me.core))
    for copy in loads[:2]:
        copy.wait()
    sums[0].over_y()
    sums[1].over_z_first()
    for copy in loads[2:6]:
        copy.wait()
    kt[...] = k[...].T
    product = (da[...].astype(f32) * attended[...].astype(f32)).T
    for h in range(6):
        delta[h : h + 1, :] = jnp.sum(product[h * HEAD_DIM : (h + 1) * HEAD_DIM], axis=0, keepdims=True)
    lane = lax.broadcasted_iota(jnp.int32, (OWN, 128), 1) // HEAD_DIM

    def head(h, carried):
        slab, part = h // 2, h % 2
        lanes = pl.ds(pl.multiple_of(slab * 128, 128), 128)
        q_slab, da_slab = q[:, lanes], da[:, lanes]
        q_part = jnp.where(lane == part, q_slab, jnp.zeros_like(q_slab))
        da_part = jnp.where(lane == part, da_slab, jnp.zeros_like(da_slab))
        log_total, row_delta = lse[pl.ds(h, 1), :], delta[pl.ds(h, 1), :]

        def tile(keys, rows, cols):
            scores = dot_nt(k[keys, lanes], q_part[cols])
            prob_grad = dot_nt(v[keys, lanes], da_part[cols])
            weight = jnp.exp(scores - log_total[:, cols])
            pt[rows, cols] = weight.astype(bf16)
            dst[rows, cols] = (weight * (prob_grad - row_delta[:, cols])).astype(bf16)

        for col in range(0, OWN, WIDE):
            cols = slice(col, min(col + WIDE, OWN))
            for row in range(0, TRUNK, TALL):
                tile(slice(row, row + TALL), slice(row, row + TALL), cols)
        for q_row, k_row, count in PIECES:
            tile(slice(k_row, k_row + count), slice(TRUNK, TRUNK + count), slice(q_row, q_row + BLOCK))
        dk_acc[0:TRUNK, :] += dot_nn(dst[0:TRUNK, :], q_part)
        dv_acc[0:TRUNK, :] += dot_nn(pt[0:TRUNK, :], da_part)
        head_rows = ds(h * HEAD_DIM, HEAD_DIM)
        dq_t[head_rows, :] = dot_nn(kt[head_rows, 0:TRUNK], dst[0:TRUNK, :])
        for q_row, k_row, count in PIECES:
            cols, rows = slice(q_row, q_row + BLOCK), slice(TRUNK, TRUNK + count)
            own = slice(k_row, k_row + count)
            dk_acc[own, :] += dot_nn(dst[rows, cols], q_part[q_row : q_row + BLOCK])
            dv_acc[own, :] += dot_nn(pt[rows, cols], da_part[q_row : q_row + BLOCK])
            dq_t[head_rows, cols] += dot_nn(kt[head_rows, own], dst[rows, cols])
        return carried

    chip_rows = lambda chip, side: ds(pair * (2 * chip + side), pair)
    trunk_copies, y_copies = [], []

    def slab_heads(slab):
        dk_acc[...] = jnp.zeros_like(dk_acc)
        dv_acc[...] = jnp.zeros_like(dv_acc)
        lax.fori_loop(2 * slab, 2 * slab + 2, head, 0)

    def trunk_out(slab):
        trunk[slab, 0] = dk_acc[0:TRUNK, :].astype(bf16)
        trunk[slab, 1] = dv_acc[0:TRUNK, :].astype(bf16)
        for i, total in enumerate((dk_acc, dv_acc)):
            lanes = slice(384 * i + 128 * slab, 384 * i + 128 * slab + 128)
            dkv_own[pair:, lanes] = total[TRUNK:, :].astype(bf16)
        trunk_copies.append(
            (
                post.send(trunk.at[slab, :, chip_rows(1 - c, 1 - core), :], trunk_far.at[slab], me.core),
                post.send(trunk.at[slab, :, chip_rows(c, 1 - core), :], trunk_own.at[slab], me.core),
            )
        )

    def trunk_over(slab):
        post.got(trunk_copies[slab][0])
        trunk_send[slab] = (
            trunk[slab, :, chip_rows(1 - c, core), :].astype(f32) + trunk_far[slab].astype(f32)
        ).astype(bf16)
        y_copies.append(post.send(trunk_send.at[slab], trunk_y.at[slab], me.yp))

    def trunk_in(slab):
        post.got(trunk_copies[slab][1])
        post.got(y_copies[slab])
        total = (
            trunk[slab, :, chip_rows(c, core), :].astype(f32)
            + trunk_own[slab].astype(f32)
            + trunk_y[slab].astype(f32)
        ).astype(bf16)
        for i in range(2):
            lanes = slice(384 * i + 128 * slab, 384 * i + 128 * slab + 128)
            dkv_own[0:pair, lanes] = total[i]

    slab_heads(0)
    trunk_out(0)
    for copy in loads[6:13]:
        copy.wait()
    for copy in out_copies:
        post.got(copy)
    for i, src in enumerate((g_out_own, g_out_send)):
        for j, lanes in enumerate((slab_own, slab_both)):
            out_sum[i, j] = (src[:, lanes].astype(f32) + out_core[i, j].astype(f32)).astype(bf16)
    out_copy = post.send(out_sum.at[1], out_x, me.xp)
    trunk_over(0)
    slab_heads(1)
    trunk_out(1)
    post.got(mlp_copy)
    rows_own[0] = (mlp_own[...] + mlp_x[...].astype(f32)).astype(bf16).reshape(units, UNIT, width)
    beside = 2 * s + 1 - x
    beyond = 2 * (2 * (1 - c) + core) + x
    corner = 2 * (2 * (1 - c) + core) + 1 - x
    part = units // 2
    over_x, over_y, diagonal = {}, {}, {}

    def piece(index, owner, half):
        return rows_out.at[index, pl.ds(units * owner + part * half, part)]

    def own_piece(index, half):
        return rows_own.at[index, pl.ds(part * half, part)], piece(index, 2 * s + x, half)

    def spread_x(index, half):
        own, there = own_piece(index, half)
        over_x[index, half] = post.send(own, there, me.xp)
        post.send(own, there, me.core)
        copy = pltpu.make_async_copy(own, there, local.at[len(loads)])
        copy.start()
        loads.append(copy)

    def spread_y(index, half):
        own, there = own_piece(index, half)
        over_y[index, half] = post.send(own, there, me.yp)

    def pass_on(index, half):
        for copies, owner, onward in ((over_x, beside, me.yp), (over_y, beyond, me.xp)):
            post.got(copies[index, half])
            got = piece(index, owner, half)
            if (index == 1 and half == 0) == (onward is me.yp):
                diagonal[index, half] = post.send(got, got, onward)
            post.send(got, got, me.core)

    def corner_on(index):
        for half in range(2):
            post.got(diagonal[index, half])
            got = piece(index, corner, half)
            post.send(got, got, me.core)

    for half in range(2):
        spread_x(0, half)
    trunk_over(1)
    sums[0].over_z()
    slab_heads(2)
    trunk_out(2)
    dq[...] = (dq_t[...].T * HEAD_DIM ** (-0.5)).astype(bf16)
    trunk_over(2)
    for half in range(2):
        spread_y(0, half)
    for slab in range(3):
        trunk_in(slab)

    def first(rows):
        return (
            dot_nt(dq[rows, :], wh[0])
            + dot_nt(dkv_own[rows, 0:384], wh[1])
            + dot_nt(dkv_own[rows, 384:768], wh[2])
        )

    chunk = HALF // 2
    first_copies = []
    for i in range(2):
        first_send[i] = first(ds(far + chunk * i, chunk)).astype(bf16)
        first_copies.append(post.send(first_send.at[i], first_x.at[i], me.xp))
    g_attn = [
        dot_tn(low_own[...], dq[...]),
        dot_tn(low_own[...], dkv_own[:, 0:384]),
        dot_tn(low_own[...], dkv_own[:, 384:768]),
    ]
    tails = []
    for j in (0, 1):
        for i in range(3):
            packed[j, :, 128 * i : 128 * i + 128] = g_attn[i][:, 128 * j : 128 * j + 128].astype(bf16)
        tail = [g[:, 256 + 64 * j : 320 + 64 * j] for g in g_attn]
        packed[j, :, 512:640] = jnp.concatenate(tail[0:2], axis=1).astype(bf16)
        packed[j, :, 640:768] = jnp.concatenate([tail[2], jnp.zeros_like(tail[2])], axis=1).astype(bf16)
    attn_stats = jnp.concatenate(
        [
            jnp.sum(dq[...].astype(f32), axis=0, keepdims=True),
            jnp.sum(dkv_own[:, 384:768].astype(f32), axis=0, keepdims=True),
        ],
        axis=1,
    )
    sums[2].from_sibling(packed.at[1 - core])
    def put_out():
        post.got(out_copy)
        packed[core, :, 384:512] = (out_sum[0, 0].astype(f32) + out_x[0].astype(f32)).astype(bf16)
        last = out_sum[0, 1].astype(f32) + out_x[1].astype(f32)
        side = lax.broadcasted_iota(jnp.int32, last.shape, 1) // HEAD_DIM
        turned = jnp.concatenate([last[:, HEAD_DIM:], last[:, :HEAD_DIM]], axis=1)
        tail = jnp.where(core == 0, turned, last)
        packed[core, :, 640:768] = jnp.where(side == 0, packed[core, :, 640:768].astype(f32), tail).astype(bf16)

    sums[2].add_sibling()
    put_out()
    sums[2].over_z_first()
    own_first[...] = first(here_rows)
    for half in range(2):
        pass_on(0, half)
    n1_all, s1_all = row_norm(x_own[here_rows, :].astype(f32))
    first_total = [jnp.zeros((1, width), f32)] * 2
    for i in range(2):
        post.got(first_copies[i])
        rows = slice(chunk * i, chunk * i + chunk)
        first_grad = own_first[rows, :] + first_x[i].astype(f32)
        n1, s1 = n1_all[rows], s1_all[rows]
        grad = middle_grad[rows, :] + norm_back(first_grad, n1, s1, wide(gain1))
        rows_own[1, part * i : part * i + part] = grad.astype(bf16).reshape(part, UNIT, width)
        spread_x(1, i)
        spread_y(1, i)
        first_total = [
            a + jnp.sum(b, axis=0, keepdims=True) for a, b in zip(first_total, (first_grad * n1, first_grad))
        ]
    rows_mid, rows_up = mid_stats.shape[0], up_stats.shape[0]
    stat_buf[0:1, :], stat_buf[1:2, :] = first_total
    stat_buf[2 : 2 + rows_mid, :] = mid_stats[...]
    stat_buf[2 + rows_mid : 8, :] = jnp.zeros((6 - rows_mid, width), f32)
    stat_buf[8 : 8 + rows_up, :] = up_stats[...]
    stat_buf[8 + rows_up : 9 + rows_up, :] = attn_stats
    stat_buf[9 + rows_up : 16, :] = jnp.zeros((7 - rows_up, width), f32)
    level = lambda i: pl.ds(16 * i, 16)
    stat_copy = post.send(stat_buf.at[level(0)], stat_in.at[0], me.core)
    sums[0].finish()
    post.got(stat_copy)
    stat_buf[level(1), :] = stat_buf[level(0), :] + stat_in[0]
    stat_copy = post.send(stat_buf.at[level(1)], stat_in.at[1], me.yp)
    sums[1].finish_z_first()
    corner_on(0)
    post.got(stat_copy)
    stat_buf[level(2), :] = stat_buf[level(1), :] + stat_in[1]
    stat_copy = post.send(stat_buf.at[level(2)], stat_in.at[2], me.xp)
    pass_on(1, 0)
    post.got(stat_copy)
    stat_buf[48:56, :] = stat_buf[32:40, :] + stat_in[2, 0:8]
    stat_buf[56:64, :] = stat_buf[40:48, :]
    stat_z[f] = stat_buf[level(3), :]
    stat_copies = [post.send(stat_buf.at[level(3)], stat_z.at[f], device) for device in me.z]
    pass_on(1, 1)
    sums[2].finish_z_first()
    corner_on(1)
    for copy in stat_copies:
        post.got(copy)
    total = stat_z[0]
    for g in range(1, fsdp_count):
        total = total + stat_z[g]
    all_total[...] = total[0 : 2 + rows_mid]
    part_total[...] = total[8 : 9 + rows_up]
    for total in sums:
        post.got(total.last)
    up_out[...] = done[...]
    rest_out[...] = deep_done[...]
    post.close()
    for copy in loads[13:]:
        copy.wait()


def second_half(fsdp_count, row_count, *operands):
    shape = jax.ShapeDtypeStruct
    vmem = pltpu.VMEM
    width = operands[4].shape[1]
    rows = row_count
    tall = TRUNK + 2 * BLOCK
    pair = 2 * BLOCK
    deep = width // fsdp_count
    half = deep // 2
    return pl.pallas_call(
        partial(second_kernel, fsdp_count),
        out_shape=(
            shape((2, 2 * rows // UNIT, UNIT, width), bf16),
            shape((2, half, width), bf16),
            shape((2, 2, deep, width), bf16),
            shape((6, width), f32),
            shape((3, width), f32),
        ),
        in_specs=[ANY] * 14 + [VMEM] * 5,
        out_specs=(ANY,) + (VMEM,) * 4,
        scratch_shapes=[
            vmem((HALF, width), f32),
            vmem((HALF, width), f32),
            vmem((width, 384), bf16),
            vmem((width, 384), bf16),
            vmem((OWN, 384), bf16),
            vmem((KEYS, 384), bf16),
            vmem((KEYS, 384), bf16),
            vmem((384, KEYS), bf16),
            vmem((OWN, 384), bf16),
            vmem((OWN, width), bf16),
            vmem((OWN, width), bf16),
            vmem((3, width, 384), bf16),
            vmem((width, width), bf16),
            vmem((width, width), bf16),
            vmem((8, OWN), f32),
            vmem((tall, OWN), bf16),
            vmem((tall, OWN), bf16),
            vmem((KEYS, 128), f32),
            vmem((KEYS, 128), f32),
            vmem((384, OWN), f32),
            vmem((OWN, 384), bf16),
            vmem((HALF, width), f32),
            vmem((3, 2, TRUNK, 128), bf16),
            vmem((3, 2, pair, 128), bf16),
            vmem((3, 2, pair, 128), bf16),
            vmem((3, 2, pair, 128), bf16),
            vmem((3, 2, pair, 128), bf16),
            vmem((OWN, 768), bf16),
            vmem((HALF, width), bf16),
            vmem((2, HALF // 2, width), bf16),
            vmem((2, HALF // 2, width), bf16),
            vmem((2, HALF // UNIT, UNIT, width), bf16),
            vmem((2, 2, width, 128), bf16),
            vmem((2, 2, width, 128), bf16),
            vmem((2, width, 128), bf16),
            vmem((2, width, width), bf16),
            vmem((width, width), bf16),
            vmem((fsdp_count, half, width), bf16),
            vmem((fsdp_count - 1, half, width), bf16),
            vmem((2, half, width), bf16),
            vmem((2, fsdp_count - 1, deep, width), bf16),
            vmem((2, 2, deep, width), bf16),
            vmem((64, width), f32),
            vmem((3, 16, width), f32),
            vmem((fsdp_count, 16, width), f32),
            pltpu.SemaphoreType.DMA((20,)),
            pltpu.SemaphoreType.DMA((80,)),
            pltpu.SemaphoreType.DMA((80,)),
        ],
        compiler_params=pltpu.CompilerParams(collective_id=1, has_side_effects=True, vmem_limit_bytes=LIMIT),
        name="second_half",
    )(*operands)


def place_kernel(
    order, rows_all, up_sum, rest, all_total, part_total,
    result, patch_grad, gain1, shift1, grad_attn, attn_bias, grad_out, out_bias, gain2, shift2, grad_up, up_bias,
    grad_down_t, down_bias, result_low, patch_low, patch_wide, sems, out_sems,
):
    units = BLOCK // UNIT
    own = result.shape[0] // units
    core = lax.axis_index("tensor") % 2
    copies = []
    for j in range(own):
        block = order[0, own * lax.axis_index("context") + j]
        branch, leaf = block - TRUNK_BLK, block - TRUNK_BLK - BRANCHES
        index = jnp.where(
            branch < 0,
            5 * (block // 2) + block % 2,
            jnp.where(leaf < 0, 5 * branch + 3, 5 * (leaf // 2) + 2 + 2 * (leaf % 2)),
        )
        to = pl.ds(j * units, units)
        for i, dest in enumerate((result_low, patch_low)):
            copy = pltpu.make_async_copy(
                rows_all.at[i, pl.ds(index * units, units)], dest.at[to], sems.at[i, j]
            )
            copy.start()
            copies.append(copy)
    total = lambda i: all_total[i, :]
    gain1[...], shift1[...], gain2[...], shift2[...] = total(0), total(1), total(2), total(3)
    down_bias[...], out_bias[...] = total(4), total(5)
    up_bias[...] = part_total[core, :]
    for i in range(2):
        lanes = slice(384 * i, 384 * i + 384)
        row = part_total[2:3, lanes]
        first = jnp.where(core == 0, row[:, 0:128], row[:, 128:256])
        second = jnp.where(core == 0, row[:, 256:320], row[:, 320:384])
        attn_bias[i : i + 1, :] = jnp.concatenate([first, second], axis=1)
    grad_up[...] = up_sum[...].reshape(grad_up.shape).astype(f32)
    grad_down_t[...] = rest[0, 0].astype(f32) + rest[0, 1].astype(f32)
    attn = rest[1, 0].astype(f32) + rest[1, 1].astype(f32)
    tails = [attn[:, 512:576], attn[:, 576:640], attn[:, 640:704], attn[:, 704:768]]
    for i in range(3):
        grad_attn[i, :, 0:128] = attn[:, 128 * i : 128 * i + 128]
        grad_attn[i, :, 128:192] = tails[i]
    grad_out[...] = jnp.concatenate([attn[:, 384:512], tails[3]], axis=1).T
    out = []
    for j in range(own):
        block = pl.ds(j * units, units)
        copies[2 * j].wait()
        copies[2 * j + 1].wait()
        patch_wide[block] = patch_low[block].astype(f32)
        for i, (src, dest) in enumerate(((result_low, result), (patch_wide, patch_grad))):
            copy = pltpu.make_async_copy(src.at[block], dest.at[block], out_sems.at[i, j])
            copy.start()
            out.append(copy)
    for copy in out:
        copy.wait()


def place(order, row_count, rows_all, up_sum, rest, all_total, part_total):
    shape = jax.ShapeDtypeStruct
    width = rows_all.shape[3]
    deep = rest.shape[2]
    vector = shape((width,), f32)
    return pl.pallas_call(
        place_kernel,
        out_shape=(
            shape((row_count // UNIT, UNIT, width), bf16), shape((row_count // UNIT, UNIT, width), f32), vector, vector,
            shape((3, deep, 192), f32), shape((2, 192), f32), shape((192, deep), f32), vector, vector, vector,
            shape((deep, width), f32), vector, shape((deep, width), f32), vector,
        ),
        in_specs=[SMEM, ANY] + [VMEM] * 4,
        out_specs=(ANY,) * 2 + (VMEM,) * 12,
        scratch_shapes=[
            pltpu.VMEM((row_count // UNIT, UNIT, width), bf16),
            pltpu.VMEM((row_count // UNIT, UNIT, width), bf16),
            pltpu.VMEM((row_count // UNIT, UNIT, width), f32),
            pltpu.SemaphoreType.DMA((2, row_count // BLOCK)),
            pltpu.SemaphoreType.DMA((2, row_count // BLOCK)),
        ],
        compiler_params=pltpu.CompilerParams(vmem_limit_bytes=LIMIT),
        name="place",
    )(order, rows_all, up_sum, rest, all_total, part_total)


def tree_shards(
    fsdp_count, patches, out_grad, block_order, first_gain, first_shift, attn_proj, attn_bias, out_proj, out_bias,
    second_gain, second_shift, up_proj, up_bias, down_proj, down_bias,
):
    middle = first_half(
        fsdp_count, block_order, patches, out_grad, attn_proj, out_proj, up_proj, down_proj.T, up_bias, attn_bias,
        first_gain, first_shift, second_gain, second_shift, out_bias, down_bias,
    )
    sums = second_half(fsdp_count, patches.shape[0], *middle, first_gain)
    outputs = list(place(block_order, patches.shape[0], *sums))
    outputs[0], outputs[1] = (rows.reshape(patches.shape) for rows in outputs[:2])
    outputs[12] = outputs[12].T
    return tuple(outputs)


def solution(mesh):
    fits = mesh.shape["context"] * 2 == BRANCHES and mesh.shape["tensor"] == 4 and mesh.shape["fsdp"] == 4
    body = partial(tree_shards, mesh.shape["fsdp"]) if fits else shards
    return jax.shard_map(
        body,
        mesh=mesh,
        in_specs=(
            P(("fsdp", "context"), None),
            P(("fsdp", "context"), None),
            P("fsdp", None),
            P(),
            P(),
            P(None, "fsdp", "tensor"),
            P(None, "tensor"),
            P("tensor", "fsdp"),
            P(),
            P(),
            P(),
            P("fsdp", "tensor"),
            P("tensor"),
            P("tensor", "fsdp"),
            P(),
        ),
        out_specs=(
            P(("fsdp", "context"), None),
            P(("fsdp", "context"), None),
            P(),
            P(),
            P(None, "fsdp", "tensor"),
            P(None, "tensor"),
            P("tensor", "fsdp"),
            P(),
            P(),
            P(),
            P("fsdp", "tensor"),
            P("tensor"),
            P("tensor", "fsdp"),
            P(),
        ),
        check_vma=False,
    )
```

```python
from functools import partial

import jax
import jax.numpy as jnp
from jax import lax
from jax.experimental import pallas as pl
from jax.experimental.pallas import tpu as pltpu
from jax.sharding import PartitionSpec as P

HEAD_DIM = 64
BLOCK = 128
TRUNK_BLK = 8
BRANCHES = 4
LEAVES = 2
TREE_BLK = 20


epsilon = 1e-05
far_below = -1e30


def layer_norm(values, norm_gain, norm_shift):
    center = values - jnp.mean(values, axis=1, keepdims=True)
    inverse = lax.rsqrt(jnp.mean(center * center, axis=1, keepdims=True) + epsilon)
    normed = center * inverse
    return (normed * norm_gain + norm_shift, normed, inverse)


def norm_back(gradient, normed, inverse, norm_gain):
    scaled = gradient * norm_gain
    return inverse * (
        scaled
        - jnp.mean(scaled, axis=1, keepdims=True)
        - normed * jnp.mean(scaled * normed, axis=1, keepdims=True)
    )


def slot_labels(order_row):
    position = order_row % TREE_BLK
    return (order_row // TREE_BLK, jnp.where(position < TRUNK_BLK, 0, position - TRUNK_BLK + 1))


def spread_rows(values):
    return jnp.broadcast_to(values[:, None], (values.shape[0], BLOCK)).reshape(-1)


def row_labels(labels, first_slot, slot_count):
    return tuple(
        (
            spread_rows(lax.dynamic_slice_in_dim(label_table, first_slot, slot_count))
            for label_table in labels
        )
    )


def visible(query_labels, key_labels):
    query_tree, query_seg = query_labels
    key_tree, key_seg = key_labels
    parent = jnp.where(query_seg > BRANCHES, 1 + (query_seg - BRANCHES - 1) // LEAVES, 0)
    reaches = (
        (key_seg[None, :] == 0)
        | (key_seg[None, :] == query_seg[:, None])
        | (key_seg[None, :] == parent[:, None])
    )
    return (query_tree[:, None] == key_tree[None, :]) & reaches


def head_view(matrix):
    return matrix.reshape(matrix.shape[0], matrix.shape[1] // HEAD_DIM, HEAD_DIM)


def scores_of(query_heads, key_heads):
    return jnp.einsum(
        "qhd,khd->hqk", query_heads, key_heads, preferred_element_type=jnp.float32
    ) * HEAD_DIM ** (-0.5)


def weights_of(scores, log_total, allowed):
    return jnp.where(allowed[None], jnp.exp(scores - log_total[:, :, None]), 0.0)


def score_grads(query_heads, grad_heads, key_heads, value_heads, log_total, row_delta, allowed):
    weights = weights_of(scores_of(query_heads, key_heads), log_total, allowed)
    prob_grad = jnp.einsum(
        "qhd,khd->hqk", grad_heads, value_heads, preferred_element_type=jnp.float32
    )
    return (
        (weights * (prob_grad - row_delta[:, :, None])).astype(jnp.bfloat16),
        weights.astype(jnp.bfloat16),
    )


def shards(
    patches,
    out_grad,
    block_order,
    first_gain,
    first_shift,
    attn_proj,
    attn_bias,
    out_proj,
    out_bias,
    second_gain,
    second_shift,
    up_proj,
    up_bias,
    down_proj,
    down_bias,
):
    attn_full, out_full, up_full, down_full = (
        lax.all_gather(attn_proj, "fsdp", axis=1, tiled=True),
        lax.all_gather(out_proj, "fsdp", axis=1, tiled=True),
        lax.all_gather(up_proj, "fsdp", axis=0, tiled=True),
        lax.all_gather(down_proj, "fsdp", axis=1, tiled=True),
    )
    labels = slot_labels(block_order[0])
    row_count = patches.shape[0]
    own_slots = row_count // BLOCK
    query_labels = row_labels(labels, lax.axis_index("context") * own_slots, own_slots)
    head_width = attn_full.shape[2]
    head_count = head_width // HEAD_DIM
    key_block = 4 * BLOCK
    block_slots = key_block // BLOCK
    score_scale = HEAD_DIM ** (-0.5)
    inputs = patches.astype(jnp.float32)
    first_norm, first_normed, first_inverse = layer_norm(inputs, first_gain, first_shift)
    first_low = first_norm.astype(jnp.bfloat16)
    projected = jnp.einsum("rd,cde->cre", first_low, attn_full, preferred_element_type=jnp.float32)
    queries = (projected[0] + attn_bias[0]).astype(jnp.bfloat16)
    keys_low = projected[1].astype(jnp.bfloat16)
    values_low = (projected[2] + attn_bias[1]).astype(jnp.bfloat16)
    keys_all = lax.all_gather(
        jnp.concatenate([keys_low, values_low], axis=1), "context", axis=0, tiled=True
    )
    block_count = keys_all.shape[0] // key_block
    query_heads = head_view(queries)

    def key_piece(step_index):
        key_slab = lax.dynamic_slice_in_dim(keys_all, step_index * key_block, key_block, 0)
        allowed = visible(query_labels, row_labels(labels, step_index * block_slots, block_slots))
        return (head_view(key_slab[:, :head_width]), head_view(key_slab[:, head_width:]), allowed)

    def total_step(step_index, carried):
        running_top, running_sum = carried
        key_heads, value_heads, allowed = key_piece(step_index)
        masked = jnp.where(allowed[None], scores_of(query_heads, key_heads), far_below)
        new_top = jnp.maximum(running_top, jnp.max(masked, axis=2))
        kept_exp = jnp.where(allowed[None], jnp.exp(masked - new_top[:, :, None]), 0.0)
        return (new_top, running_sum * jnp.exp(running_top - new_top) + jnp.sum(kept_exp, axis=2))

    start_top = jnp.full((head_count, row_count), far_below, jnp.float32)
    running_top, running_sum = lax.fori_loop(
        0, block_count, total_step, (start_top, jnp.zeros((head_count, row_count), jnp.float32))
    )
    log_total = running_top + jnp.log(running_sum)

    def mix_step(step_index, mixed):
        key_heads, value_heads, allowed = key_piece(step_index)
        weights = weights_of(scores_of(query_heads, key_heads), log_total, allowed).astype(
            jnp.bfloat16
        )
        return mixed + jnp.einsum(
            "hqk,khd->qhd", weights, value_heads, preferred_element_type=jnp.float32
        )

    attended = lax.fori_loop(
        0, block_count, mix_step, jnp.zeros((row_count, head_count, HEAD_DIM), jnp.float32)
    )
    attended_low = attended.reshape(row_count, head_width).astype(jnp.bfloat16)
    attn_part = jnp.dot(attended_low, out_full, preferred_element_type=jnp.float32)
    middle = inputs + (lax.psum(attn_part, "tensor") + out_bias)
    second_norm, second_normed, second_inverse = layer_norm(middle, second_gain, second_shift)
    second_low = second_norm.astype(jnp.bfloat16)
    pre_act = jnp.dot(second_low, up_full, preferred_element_type=jnp.float32) + up_bias
    hidden, gelu_back = jax.vjp(partial(jax.nn.gelu, approximate=False), pre_act)
    hidden_low = hidden.astype(jnp.bfloat16)
    mlp_part = jnp.dot(hidden_low, down_full, preferred_element_type=jnp.float32)
    result = (
        middle + (lax.psum(mlp_part.astype(jnp.bfloat16), "tensor").astype(jnp.float32) + down_bias)
    ).astype(jnp.bfloat16)
    top_grad = out_grad.astype(jnp.float32)
    grad_down_bias = jnp.sum(top_grad, axis=0)
    grad_down = jnp.einsum("rf,rd->fd", hidden_low, out_grad, preferred_element_type=jnp.float32)
    hidden_grad = jnp.einsum("rd,fd->rf", out_grad, down_full, preferred_element_type=jnp.float32)
    pre_grad = gelu_back(hidden_grad)[0].astype(jnp.bfloat16)
    grad_up_bias = jnp.sum(pre_grad.astype(jnp.float32), axis=0)
    grad_up = jnp.einsum("rd,rf->df", second_low, pre_grad, preferred_element_type=jnp.float32)
    second_part = jnp.einsum("rf,df->rd", pre_grad, up_full, preferred_element_type=jnp.float32)
    second_grad = lax.psum(second_part, "tensor")
    grad_second_gain = jnp.sum(second_grad * second_normed, axis=0)
    grad_second_shift = jnp.sum(second_grad, axis=0)
    middle_grad = top_grad + norm_back(second_grad, second_normed, second_inverse, second_gain)
    branch_grad = middle_grad.astype(jnp.bfloat16)
    grad_out_bias = jnp.sum(branch_grad.astype(jnp.float32), axis=0)
    grad_out = jnp.einsum(
        "re,rd->ed", attended_low, branch_grad, preferred_element_type=jnp.float32
    )
    attended_grad = jnp.einsum(
        "rd,ed->re", branch_grad, out_full, preferred_element_type=jnp.float32
    ).astype(jnp.bfloat16)
    grad_heads = head_view(attended_grad)

    def delta_step(step_index, row_delta):
        key_heads, value_heads, allowed = key_piece(step_index)
        weights = weights_of(scores_of(query_heads, key_heads), log_total, allowed)
        prob_grad = jnp.einsum(
            "qhd,khd->hqk", grad_heads, value_heads, preferred_element_type=jnp.float32
        )
        return row_delta + jnp.sum(weights * prob_grad, axis=2)

    row_delta = lax.fori_loop(
        0, block_count, delta_step, jnp.zeros((head_count, row_count), jnp.float32)
    )
    query_start = jnp.zeros((row_count, head_count, HEAD_DIM), jnp.float32)

    def back_step(step_index, carried):
        query_acc, key_acc = carried
        key_heads, value_heads, allowed = key_piece(step_index)
        score_low, weights_low = score_grads(
            query_heads, grad_heads, key_heads, value_heads, log_total, row_delta, allowed
        )
        query_acc = query_acc + jnp.einsum(
            "hqk,khd->qhd", score_low, key_heads, preferred_element_type=jnp.float32
        )
        key_part = jnp.einsum(
            "hqk,qhd->khd", score_low, query_heads, preferred_element_type=jnp.float32
        )
        value_part = jnp.einsum(
            "hqk,qhd->khd", weights_low, grad_heads, preferred_element_type=jnp.float32
        )
        joined = jnp.concatenate(
            [key_part.reshape(key_block, head_width), value_part.reshape(key_block, head_width)],
            axis=1,
        )
        return (
            query_acc,
            lax.dynamic_update_slice_in_dim(key_acc, joined, step_index * key_block, 0),
        )

    key_start = jnp.zeros((keys_all.shape[0], 2 * head_width), jnp.float32)
    query_acc, key_acc = lax.fori_loop(0, block_count, back_step, (query_start, key_start))
    key_value_grad = lax.psum_scatter(key_acc, "context", scatter_dimension=0, tiled=True)
    query_grad = (query_acc.reshape(row_count, head_width) * score_scale).astype(jnp.bfloat16)
    key_grad = (key_value_grad[:, :head_width] * score_scale).astype(jnp.bfloat16)
    value_grad = key_value_grad[:, head_width:].astype(jnp.bfloat16)
    stacked = jnp.stack([query_grad, key_grad, value_grad])
    grad_attn_bias = jnp.stack(
        [
            jnp.sum(query_grad.astype(jnp.float32), axis=0),
            jnp.sum(value_grad.astype(jnp.float32), axis=0),
        ]
    )
    grad_attn = jnp.einsum("rd,cre->cde", first_low, stacked, preferred_element_type=jnp.float32)
    first_grad = lax.psum(
        jnp.einsum("cre,cde->rd", stacked, attn_full, preferred_element_type=jnp.float32), "tensor"
    )
    grad_first_gain = jnp.sum(first_grad * first_normed, axis=0)
    grad_first_shift = jnp.sum(first_grad, axis=0)
    patch_grad = middle_grad + norm_back(first_grad, first_normed, first_inverse, first_gain)
    wide_attn, wide_out, wide_up, wide_down = (
        lax.psum_scatter(grad_attn, ("fsdp", "context"), scatter_dimension=1, tiled=True),
        lax.psum_scatter(grad_out, ("fsdp", "context"), scatter_dimension=1, tiled=True),
        lax.psum_scatter(grad_up, ("fsdp", "context"), scatter_dimension=0, tiled=True),
        lax.psum_scatter(grad_down, ("fsdp", "context"), scatter_dimension=1, tiled=True),
    )
    grad_attn, grad_out, grad_up, grad_down = (
        lax.all_gather(wide_attn, "context", axis=1, tiled=True),
        lax.all_gather(wide_out, "context", axis=1, tiled=True),
        lax.all_gather(wide_up, "context", axis=0, tiled=True),
        lax.all_gather(wide_down, "context", axis=1, tiled=True),
    )
    small_grads = lax.psum(
        (
            grad_first_gain,
            grad_first_shift,
            grad_attn_bias,
            grad_out_bias,
            grad_second_gain,
            grad_second_shift,
            grad_up_bias,
            grad_down_bias,
        ),
        ("fsdp", "context"),
    )
    return (
        result,
        patch_grad,
        small_grads[0],
        small_grads[1],
        grad_attn,
        small_grads[2],
        grad_out,
        small_grads[3],
        small_grads[4],
        small_grads[5],
        grad_up,
        small_grads[6],
        grad_down,
        small_grads[7],
    )


bf16 = jnp.bfloat16
f32 = jnp.float32
VMEM = pl.BlockSpec(memory_space=pltpu.VMEM)
SMEM = pl.BlockSpec(memory_space=pltpu.SMEM)
ANY = pl.BlockSpec(memory_space=pl.ANY)
MESH = pl.DeviceIdType.MESH
LIMIT = 61 * 1024 * 1024


def dot_nn(a, b):
    return lax.dot_general(a, b, (((1,), (0,)), ((), ())), preferred_element_type=f32)


def dot_nt(a, b):
    return lax.dot_general(a, b, (((1,), (1,)), ((), ())), preferred_element_type=f32)


def dot_tn(a, b):
    return lax.dot_general(a, b, (((0,), (0,)), ((), ())), preferred_element_type=f32)


class Here:
    def __init__(self, fsdp_count):
        self.f = lax.axis_index("fsdp")
        self.c = lax.axis_index("context")
        self.t = lax.axis_index("tensor")
        self.x = self.t // 2
        self.k = self.t % 2
        self.core = (self.f, self.c, 2 * self.x + 1 - self.k)
        self.xp = (self.f, self.c, 2 * (1 - self.x) + self.k)
        self.yp = (self.f, 1 - self.c, self.t)
        self.z = [((self.f + i) % fsdp_count, self.c, self.t) for i in range(1, fsdp_count)]
        self.back = [(self.f + fsdp_count - i) % fsdp_count for i in range(1, fsdp_count)]


def greet(devices):
    barrier = pltpu.get_barrier_semaphore()
    for device in devices:
        pl.semaphore_signal(barrier, inc=1, device_id=device, device_id_type=MESH)
    pl.semaphore_wait(barrier, len(devices))


class Post:
    def __init__(self, send_sem, recv_sem):
        self.send_sem, self.recv_sem = send_sem, recv_sem
        self.sent, self.open = [], []

    def send(self, src, dst, device):
        index = len(self.sent)
        copy = pltpu.make_async_remote_copy(
            src_ref=src,
            dst_ref=dst,
            send_sem=self.send_sem.at[index],
            recv_sem=self.recv_sem.at[index],
            device_id=device,
            device_id_type=MESH,
        )
        copy.start()
        self.sent.append(copy)
        self.open.append((copy, device))
        return copy

    def got(self, copy):
        left = [entry for entry in self.open if entry[0] is not copy]
        if len(left) < len(self.open):
            copy.wait_recv()
        self.open = left

    def got_from(self, device):
        for copy, to in self.open:
            if to is device:
                self.got(copy)

    def close(self):
        for copy, _ in self.open:
            copy.wait_recv()
        for copy in self.sent:
            copy.wait_send()


def ds(start, size, step=16):
    return pl.ds(pl.multiple_of(start, step), size)


TRUNK = TRUNK_BLK * BLOCK
SUB = (1 + LEAVES) * BLOCK
KEYS = TRUNK + SUB
OWN = 2 * BLOCK + SUB
PIECES = (
    (2 * BLOCK, TRUNK, 2 * BLOCK),
    (3 * BLOCK, TRUNK + BLOCK, BLOCK),
    (4 * BLOCK, TRUNK + BLOCK, 2 * BLOCK),
)


def own_places(s):
    return [2 * s, 2 * s + 1, 12 + 2 * s, 8 + s, 13 + 2 * s]


def row_norm(values):
    center = values - jnp.mean(values, axis=1, keepdims=True)
    inverse = lax.rsqrt(jnp.mean(center * center, axis=1, keepdims=True) + epsilon)
    return center * inverse, inverse

HALF = OWN // 2
UNIT = 16


def wide(vector):
    return vector[...].reshape(1, -1)


def first_kernel(
    fsdp_count, order, patches, grads, attn_proj, out_proj, up, d_own, up_bias, attn_bias, gain1, shift1, gain2, shift2, out_bias, down_bias,
    q_out, k_out, v_out, att_out, low_out, x_out, wh_out, g_up_out, g_down_out,
    middle_grad_out, mlp_own_out, mlp_send_out, g_out_own_out, g_out_send_out,
    lse, da, stats, up_stats,
    middle_grad, mlp_own, mlp_send, g_out_own, g_out_send,
    where, a_own, bias, rows_all, grads_all, wa, wh, wo_x, wu, wd, bias_all,
    low_all, low, low_own, x_own, g_own, q, k, v, vt, attended, att_t, att_x, st, pt,
    middle, normed, inverse, low2, hidden, pre_grad, second, second_send, second_x, branch, da_send, g_up, g_down, g_sum,
    local, ss, rs,
):
    me = Here(fsdp_count)
    f, c, x, core, t = me.f, me.c, me.x, me.k, me.t
    s = 2 * c + core
    units = patches.shape[0]
    part = units // 4
    width = patches.shape[2]
    deep = up.shape[0]
    head_width = attn_proj.shape[2]
    own_copies = []

    def keep(src, dst):
        copy = pltpu.make_async_copy(src, dst, local.at[len(own_copies)])
        copy.start()
        own_copies.append(copy)

    keep(patches, rows_all.at[pl.ds(units * c, units)])
    keep(grads, grads_all.at[pl.ds(units * c, units)])
    keep(up, wu.at[core, ds(deep * f, deep)])
    keep(d_own, wd.at[core, ds(deep * f, deep)])
    greet([me.core, me.xp, me.yp] + me.z)
    post = Post(ss, rs)
    there = units * (1 - c)
    half = deep // 2
    strip, other_strip = half * c, half * (1 - c)

    def quarter(array, index, piece, count):
        size = part // count
        return array.at[pl.ds(there + part * index + size * piece, size)]

    def to_y(src, dst, piece, count):
        size = part // count
        return post.send(
            src.at[pl.ds(part * t + size * piece, size)],
            dst.at[pl.ds(units * c + part * t + size * piece, size)],
            me.yp,
        )

    def relay(piece, device):
        return post.send(piece, piece, device)

    third = deep // 3
    lone, other_lone = 2 * third * c, 2 * third * (1 - c)
    a_part = lambda source, row, count: wa.at[core, ds(deep * source + row, count)]
    pieces = 4
    patches_y = [to_y(patches, rows_all, i, pieces) for i in range(pieces)]
    a_own[:, 0:128] = attn_proj[0, :, 0:128]
    a_own[:, 128:256] = attn_proj[1, :, 0:128]
    a_own[:, 256:384] = attn_proj[2, :, 0:128]
    out_t = out_proj[...].T
    a_own[:, 384:512] = jnp.concatenate([attn_proj[0, :, 128:head_width], attn_proj[1, :, 128:head_width]], axis=1)
    a_own[:, 512:640] = jnp.concatenate([attn_proj[2, :, 128:head_width], out_t[:, 128:head_width]], axis=1)
    a_own[:, 640:768] = out_t[:, 0:128]
    bias[...] = jnp.zeros_like(bias)
    bias[0:1, :] = wide(up_bias)
    bias[1:3, 0:head_width] = attn_bias[...]
    a_z = [post.send(a_own.at[ds(lone, third)], a_part(f, lone, third), device) for device in me.z]
    post.send(a_own, wa.at[core, ds(deep * f, deep)], me.core)
    post.send(bias, bias_all.at[core], me.core)
    gain_row, shift_row = wide(gain1), wide(shift1)

    def norm_units(start, count):
        values = rows_all[pl.ds(start, count)].reshape(count * UNIT, width).astype(f32)
        normed_rows, _ = row_norm(values)
        low_rows = (normed_rows * gain_row + shift_row).astype(bf16)
        low_all[pl.ds(start, count)] = low_rows.reshape(count, UNIT, width)

    block_units = BLOCK // UNIT
    own_blocks = units // block_units

    def norm_own(j, carried):
        norm_units(units * c + block_units * j, block_units)
        return carried

    slots = order.shape[1]

    def find(place, carried):
        slot = jnp.int32(0)
        for j in range(slots):
            slot = jnp.where(order[0, j] == place, j, slot)
        where[place] = slot * block_units
        return carried

    lax.fori_loop(0, slots, find, 0)
    wa[core, ds(deep * f, deep), :] = a_own[...]
    bias_all[core] = bias[...]
    own_copies[0].wait()
    lax.fori_loop(0, own_blocks - pieces, norm_own, 0)
    size = part // pieces
    over = (t + 2) % 4
    beside, across = t + 1 - 2 * core, over + 1 - 2 * core
    patches_x, patches_core = [], []
    for i in range(pieces):
        post.got(patches_y[i])
        patches_x.append(relay(quarter(rows_all, t, i, pieces), me.xp))
        patches_core.append(relay(quarter(rows_all, t, i, pieces), me.core))
        norm_units(there + part * t + size * i, size)
        if i == 2:
            a_y = []
            for copy, source in zip(a_z, me.back):
                post.got(copy)
                a_y.append(relay(a_part(source, lone, third), me.yp))
                relay(a_part(source, lone, third), me.core)
            a_shared = [
                post.send(a_own.at[ds(third, third)], a_part(f, third, third), device) for device in me.z
            ]
        norm_own(own_blocks - pieces + i, 0)
    post.send(up, wu.at[core, ds(deep * f, deep)], me.core)
    post.send(d_own, wd.at[core, ds(deep * f, deep)], me.core)
    for i in range(pieces):
        post.got(patches_core[i])
        norm_units(there + part * beside + size * i, size)
    patches_core = []
    for i in range(pieces):
        post.got(patches_x[i])
        patches_core.append(relay(quarter(rows_all, over, i, pieces), me.core))
        norm_units(there + part * over + size * i, size)
    for copy, source in zip(a_shared, me.back):
        post.got(copy)
        relay(a_part(source, third, third), me.core)
    u_z = [
        post.send(up.at[ds(strip, half)], wu.at[core, ds(deep * f + strip, half)], device) for device in me.z
    ]
    for copy, source in zip(a_y, me.back):
        post.got(copy)
        relay(a_part(source, other_lone, third), me.core)
    grads_y = [to_y(grads, grads_all, i, 2) for i in range(2)]
    for i in range(pieces):
        post.got(patches_core[i])
        norm_units(there + part * across + size * i, size)

    def block_of(array, place):
        return array[pl.ds(where[place], block_units)].reshape(BLOCK, width)

    def trunk_step(j, carried):
        low[ds(j * BLOCK, BLOCK), :] = block_of(low_all, j)
        return carried

    lax.fori_loop(0, TRUNK_BLK, trunk_step, 0)
    places = own_places(s)
    for j in range(2, 5):
        low[TRUNK + (j - 2) * BLOCK : TRUNK + (j - 1) * BLOCK, :] = block_of(low_all, places[j])
    for j, place in enumerate(places):
        x_own[pl.ds(j * BLOCK, BLOCK), :] = block_of(rows_all, place)
    low_own[0 : 2 * BLOCK, :] = low[ds(2 * BLOCK * s, 2 * BLOCK), :]
    low_own[2 * BLOCK :, :] = low[TRUNK:, :]
    post.got_from(me.core)

    def assemble(i):
        slab = (0, 1, 2, 5)[i]
        wh[i, :, 0:128] = wa[0, :, 128 * slab : 128 * slab + 128]
        wh[i, :, 128:256] = wa[1, :, 128 * slab : 128 * slab + 128]
        start = 384 + 64 * i
        wh[i, :, 256:384] = jnp.concatenate(
            [wa[0, :, start : start + 64], wa[1, :, start : start + 64]], axis=1
        )

    for i in range(4):
        assemble(i)
    wo_quarter = width // 4
    wo_rows = ds(wo_quarter * (2 * c + core), wo_quarter)
    wo_copy = post.send(wh.at[3, wo_rows], wo_x.at[wo_rows], me.xp)
    keep(wh, wh_out)

    def heads_row(row):
        a, b = bias_all[0, row : row + 1, :], bias_all[1, row : row + 1, :]
        return jnp.concatenate([a[:, 0:128], b[:, 0:128], a[:, 128:192], b[:, 128:192]], axis=1)

    q[...] = ((dot_nn(low_own[...], wh[0]) + heads_row(1)).astype(bf16) * HEAD_DIM ** (-0.5)).astype(bf16)
    value_bias = heads_row(2)

    def project(j, carried):
        rows = ds(j * (KEYS // 2), KEYS // 2)
        k[rows, :] = dot_nn(low[rows, :], wh[1]).astype(bf16)
        v[rows, :] = (dot_nn(low[rows, :], wh[2]) + value_bias).astype(bf16)
        return carried

    lax.fori_loop(0, 2, project, 0)
    vt[...] = v[...].T
    for src, dst in ((q, q_out), (k, k_out), (v, v_out), (low_own, low_out), (x_own, x_out)):
        keep(src, dst)
    lane = lax.broadcasted_iota(jnp.int32, (OWN, 128), 1) // HEAD_DIM

    def head(h, carried):
        slab, side = h // 2, h % 2
        lanes = pl.ds(pl.multiple_of(slab * 128, 128), 128)
        own_q = q[:, lanes]
        q_part = jnp.where(lane == side, own_q, jnp.zeros_like(own_q))
        st[0:TRUNK, :] = dot_nt(k[0:TRUNK, lanes], q_part)
        for q_row, k_row, count in PIECES:
            st[TRUNK : TRUNK + count, q_row : q_row + BLOCK] = dot_nt(
                k[k_row : k_row + count, lanes], q_part[q_row : q_row + BLOCK]
            )
        tops, sums = [], []
        for j in range(OWN // BLOCK):
            cols = slice(j * BLOCK, (j + 1) * BLOCK)
            count = TRUNK + (0 if j < 2 else PIECES[j - 2][2])
            top = jnp.full((8, BLOCK), far_below, f32)
            for r in range(0, count, BLOCK):
                piece = st[r : r + BLOCK, cols].reshape(BLOCK // 8, 8, BLOCK)
                top = jnp.maximum(top, jnp.max(piece, axis=0))
            top = jnp.max(top, axis=0, keepdims=True)
            total = jnp.zeros((8, BLOCK), f32)
            for r in range(0, count, BLOCK):
                weight = jnp.exp(st[r : r + BLOCK, cols] - top)
                total = total + jnp.sum(weight.reshape(BLOCK // 8, 8, BLOCK), axis=0)
                pt[r : r + BLOCK, cols] = weight.astype(bf16)
            tops.append(top)
            sums.append(jnp.sum(total, axis=0, keepdims=True))
        total = jnp.concatenate(sums, axis=1)
        head_rows, side_rows = ds(h * HEAD_DIM, HEAD_DIM), ds(side * HEAD_DIM, HEAD_DIM)
        att_t[side_rows, :] = dot_nn(vt[head_rows, 0:TRUNK], pt[0:TRUNK, :])
        for q_row, k_row, count in PIECES:
            cols = slice(q_row, q_row + BLOCK)
            att_t[side_rows, cols] += dot_nn(
                vt[head_rows, k_row : k_row + count], pt[TRUNK : TRUNK + count, cols]
            )
        att_t[side_rows, :] = att_t[side_rows, :] / total
        lse[pl.ds(h, 1), :] = jnp.concatenate(tops, axis=1) + jnp.log(total)
        return carried

    mine, far = HALF * x, HALF * (1 - x)
    here_rows, far_rows = ds(mine, HALF), ds(far, HALF)
    att_copies = []

    def slab_heads(slab):
        lax.fori_loop(2 * slab, 2 * slab + 2, head, 0)
        lanes = pl.ds(128 * slab, 128)
        attended[:, lanes] = att_t[...].T.astype(bf16)
        att_copies.append(post.send(attended.at[far_rows, lanes], att_x.at[:, lanes], me.xp))

    def grads_on(i):
        post.got(grads_y[i])
        relay(quarter(grads_all, t, i, 2), me.core)
        return relay(quarter(grads_all, t, i, 2), me.xp)

    def strips_on(copies, array):
        passed = []
        for copy, source in zip(copies, me.back):
            post.got(copy)
            piece = array.at[core, ds(deep * source + strip, half)]
            passed.append(relay(piece, me.yp))
            relay(piece, me.core)
        return passed

    def strips_in(copies, array):
        for copy, source in zip(copies, me.back):
            post.got(copy)
            relay(array.at[core, ds(deep * source + other_strip, half)], me.core)

    d_part = lambda source, row: wd.at[core, ds(deep * source + row, third)]
    post.got(wo_copy)
    wo_y = relay(wo_x.at[wo_rows], me.yp)
    wo_core = [relay(wo_x.at[wo_rows], me.core)]
    grads_x = [grads_on(0)]
    slab_heads(0)
    grads_x.append(grads_on(1))
    slab_heads(1)
    u_y = strips_on(u_z, wu)
    d_lone = [post.send(d_own.at[ds(lone, third)], d_part(f, lone), device) for device in me.z]
    post.got(wo_y)
    wo_core.append(relay(wo_x.at[ds(wo_quarter * (2 * (1 - c) + core), wo_quarter)], me.core))
    slab_heads(2)
    keep(attended, att_out)
    middle[...] = (
        x_own[here_rows, :].astype(f32) + wide(out_bias) + dot_nt(attended[here_rows, :], wh[3])
    )
    d_y = []
    for copy, source in zip(d_lone, me.back):
        post.got(copy)
        d_y.append(relay(d_part(source, lone), me.yp))
        relay(d_part(source, lone), me.core)
    d_shared = [post.send(d_own.at[ds(third, third)], d_part(f, third), device) for device in me.z]
    for copy in wo_core + att_copies:
        post.got(copy)
    middle[...] += dot_nt(att_x[...], wo_x[...])
    n2, s2 = row_norm(middle[...])
    normed[...] = n2
    inverse[...] = s2
    low2[here_rows, :] = (n2 * wide(gain2) + wide(shift2)).astype(bf16)
    chunk = HALF // 2
    here_chunks = [ds(mine + chunk * i, chunk) for i in range(2)]
    far_chunks = [ds(far + chunk * i, chunk) for i in range(2)]
    low_copies = [post.send(low2.at[rows], low2.at[rows], me.xp) for rows in here_chunks]
    for i in range(2):
        post.got(grads_x[i])
        relay(quarter(grads_all, over, i, 2), me.core)
    strips_in(u_y, wu)
    for copy in own_copies[1:4]:
        copy.wait()
    post.got_from(me.core)
    for j, place in enumerate(places):
        g_own[pl.ds(j * BLOCK, BLOCK), :] = block_of(grads_all, place)
    tile = 256

    def tiles(step):
        def tile_step(j, carried):
            shard, lanes = j // 3, pl.ds(pl.multiple_of(j % 3 * tile, 128), tile)
            step(shard, lanes, pl.ds(pl.multiple_of(j * tile, 128), tile))
            return carried

        lax.fori_loop(0, 6, tile_step, 0)

    def forward(rows):
        def step(shard, lanes, out):
            pre = dot_nn(low2[rows, :], wu[shard, :, lanes]) + bias_all[shard, 0:1, lanes]
            below = 0.5 * (1.0 + lax.erf(pre * (2.0**-0.5)))
            density = jnp.exp(-0.5 * pre * pre) * (2.0 * jnp.pi) ** -0.5
            hidden[rows, out] = (pre * below).astype(bf16)
            pre_grad[rows, out] = (below + pre * density).astype(bf16)

        tiles(step)

    def backward(rows, count):
        second[rows, :] = jnp.zeros((count, width), f32)

        def step(shard, lanes, out):
            back = dot_nn(g_own[rows, :], wd[shard, :, lanes])
            low_back = (back * pre_grad[rows, out].astype(f32)).astype(bf16)
            pre_grad[rows, out] = low_back
            second[rows, :] += dot_nt(low_back, wu[shard, :, lanes])

        tiles(step)

    def mlp(rows):
        return dot_nt(hidden[rows, 0:width], wd[0]) + dot_nt(hidden[rows, width:], wd[1])

    own_lanes, sibling_lanes = (
        pl.ds(pl.multiple_of(width * side, 128), width) for side in (core, 1 - core)
    )
    sibling_copies = {}

    def weight_grad(index, left, right, grad):
        def step(shard, lanes, out):
            grad[:, out] = dot_tn(left[...], right[:, out]).astype(bf16)

        tiles(step)
        sibling_copies[index] = post.send(grad.at[:, sibling_lanes], g_sum.at[index], me.core)

    forward(here_rows)
    for i in range(2):
        post.got(low_copies[i])
        forward(far_chunks[i])
    weight_grad(1, g_own, hidden, g_down)
    for copies, row in ((d_shared, third), (d_y, other_lone)):
        for copy, source in zip(copies, me.back):
            post.got(copy)
            relay(d_part(source, row), me.core)
    post.got_from(me.core)
    second_copies = []
    for i in range(2):
        backward(far_chunks[i], chunk)
        second_send[i] = second[far_chunks[i], :].astype(bf16)
        second_copies.append(post.send(second_send.at[i], second_x.at[i], me.xp))
    backward(here_rows, HALF)

    weight_grad(0, low2, pre_grad, g_up)
    total = [jnp.zeros((1, width), f32)] * 4
    for i in range(2):
        rows = here_chunks[i]
        part_rows = slice(chunk * i, chunk * i + chunk)
        post.got(second_copies[i])
        second_grad = second[rows, :] + second_x[i].astype(f32)
        n2 = normed[part_rows, :]
        dy = g_own[rows, :].astype(f32)
        grad = dy + norm_back(second_grad, n2, inverse[part_rows, :], wide(gain2))
        middle_grad[part_rows, :] = grad
        low_grad = grad.astype(bf16)
        branch[part_rows, :] = low_grad
        da_send[part_rows, :] = dot_nn(low_grad, wo_x[...]).astype(bf16)
        post.send(da_send.at[pl.ds(chunk * i, chunk)], da.at[rows], me.xp)
        terms = (second_grad * n2, second_grad, dy, low_grad.astype(f32))
        total = [a + jnp.sum(b, axis=0, keepdims=True) for a, b in zip(total, terms)]
    for i in range(4):
        stats[i : i + 1, :] = total[i]
    up_stats[0:1, :] = jnp.sum(pre_grad[:, 0:width].astype(f32), axis=0, keepdims=True)
    up_stats[1:2, :] = jnp.sum(pre_grad[:, width:].astype(f32), axis=0, keepdims=True)
    mlp_send[...] = mlp(far_rows).astype(bf16)
    mlp_own[...] = middle[...] + mlp(here_rows) + wide(down_bias)
    for src, out in ((middle_grad, middle_grad_out), (mlp_own, mlp_own_out), (mlp_send, mlp_send_out)):
        keep(src, out)
    da[here_rows, :] = dot_nn(branch[...], wh[3]).astype(bf16)
    g_out_send[...] = dot_tn(branch[...], att_x[...]).astype(bf16)
    g_out_own[...] = dot_tn(branch[...], attended[here_rows, :]).astype(bf16)
    keep(g_out_send, g_out_send_out)
    keep(g_out_own, g_out_own_out)
    for index, (grad, out) in enumerate(((g_up, g_up_out), (g_down, g_down_out))):
        post.got(sibling_copies[index])

        def add_sibling(j, carried):
            rows = ds(j * BLOCK, BLOCK)
            g_sum[index, rows, :] = (
                g_sum[index, rows, :].astype(f32) + grad[rows, own_lanes].astype(f32)
            ).astype(bf16)
            return carried

        lax.fori_loop(0, width // BLOCK, add_sibling, 0)
        keep(g_sum.at[index], out)
    post.close()
    for copy in own_copies[4:]:
        copy.wait()


def first_half(fsdp_count, order, patches, grads, attn_proj, out_proj, up, down_t, *vectors):
    width = patches.shape[1]
    shape = jax.ShapeDtypeStruct
    vmem = pltpu.VMEM
    units = 2 * up.shape[1]
    all_units = 2 * patches.shape[0] // UNIT
    deep = up.shape[0]
    fold = lambda a: a.reshape(-1, UNIT, width)
    return pl.pallas_call(
        partial(first_kernel, fsdp_count),
        out_shape=(
            shape((OWN, 384), bf16),
            shape((KEYS, 384), bf16),
            shape((KEYS, 384), bf16),
            shape((OWN, 384), bf16),
            shape((OWN, width), bf16),
            shape((OWN, width), bf16),
            shape((4, width, 384), bf16),
            shape((width, width), bf16),
            shape((width, width), bf16),
            shape((HALF, width), f32),
            shape((HALF, width), f32),
            shape((HALF, width), bf16),
            shape((width, 384), bf16),
            shape((width, 384), bf16),
            shape((8, OWN), f32),
            shape((OWN, 384), bf16),
            shape((4, width), f32),
            shape((2, width), f32),
        ),
        in_specs=[SMEM, ANY, ANY, VMEM, VMEM, ANY, ANY] + [VMEM] * 8,
        out_specs=(ANY,) * 14 + (VMEM,) * 4,
        scratch_shapes=[
            vmem((HALF, width), f32),
            vmem((HALF, width), f32),
            vmem((HALF, width), bf16),
            vmem((width, 384), bf16),
            vmem((width, 384), bf16),
            pltpu.SMEM(order.shape[1:], jnp.int32),
            vmem((deep, width), bf16),
            vmem((8, width), f32),
            vmem((all_units, UNIT, width), bf16),
            vmem((all_units, UNIT, width), bf16),
            vmem((2, width, width), bf16),
            vmem((4, width, 384), bf16),
            vmem((width, 384), bf16),
            vmem((2, width, up.shape[1]), bf16),
            vmem((2, width, up.shape[1]), bf16),
            vmem((2, 8, width), f32),
            vmem((all_units, UNIT, width), bf16),
            vmem((KEYS, width), bf16),
            vmem((OWN, width), bf16),
            vmem((OWN, width), bf16),
            vmem((OWN, width), bf16),
            vmem((OWN, 384), bf16),
            vmem((KEYS, 384), bf16),
            vmem((KEYS, 384), bf16),
            vmem((384, KEYS), bf16),
            vmem((OWN, 384), bf16),
            vmem((128, OWN), f32),
            vmem((HALF, 384), bf16),
            vmem((TRUNK + 2 * BLOCK, OWN), f32),
            vmem((TRUNK + 2 * BLOCK, OWN), bf16),
            vmem((HALF, width), f32),
            vmem((HALF, width), f32),
            vmem((HALF, 1), f32),
            vmem((OWN, width), bf16),
            vmem((OWN, units), bf16),
            vmem((OWN, units), bf16),
            vmem((OWN, width), f32),
            vmem((2, HALF // 2, width), bf16),
            vmem((2, HALF // 2, width), bf16),
            vmem((HALF, width), bf16),
            vmem((HALF, 384), bf16),
            vmem((width, units), bf16),
            vmem((width, units), bf16),
            vmem((2, width, width), bf16),
            pltpu.SemaphoreType.DMA((24,)),
            pltpu.SemaphoreType.DMA((112,)),
            pltpu.SemaphoreType.DMA((112,)),
        ],
        compiler_params=pltpu.CompilerParams(collective_id=0, has_side_effects=True, vmem_limit_bytes=LIMIT),
        name="first_half",
    )(order, fold(patches), fold(grads), attn_proj, out_proj, up, down_t, *vectors)


class StripSum:
    def __init__(self, me, post, fsdp_count, held, from_core, buffers):
        self.me, self.post, self.count = me, post, fsdp_count
        self.held, self.from_core = held, from_core
        self.from_y, self.from_z, self.done = buffers
        self.half = held.shape[0] // fsdp_count // 2

    def from_sibling(self, src):
        self.core_copy = self.post.send(src, self.from_core, self.me.core)

    def add_sibling(self):
        self.post.got(self.core_copy)
        half = self.half

        def step(j, carried):
            rows = ds(j * half, half)
            self.held[rows, :] = (self.held[rows, :].astype(f32) + self.from_core[rows, :].astype(f32)).astype(bf16)
            return carried

        lax.fori_loop(0, 2 * self.count, step, 0)

    def strip(self, g, side):
        return ds(self.half * (2 * g + side), self.half)

    def over_y(self):
        me = self.me
        self.y_copies = [
            self.post.send(self.held.at[self.strip(g, 1 - me.c)], self.from_y.at[g], me.yp)
            for g in range(self.count)
        ]

    def over_z(self):
        me = self.me
        for copy in self.y_copies:
            self.post.got(copy)

        def step(g, carried):
            rows = self.strip(g, me.c)
            self.held[rows, :] = (self.held[rows, :].astype(f32) + self.from_y[g].astype(f32)).astype(bf16)
            return carried

        lax.fori_loop(0, self.count, step, 0)
        self.z_copies = [
            self.post.send(self.held.at[self.strip((me.f + i + 1) % self.count, me.c)], self.from_z.at[i], device)
            for i, device in enumerate(me.z)
        ]

    def over_z_first(self):
        me, deep = self.me, 2 * self.half
        self.z_copies = [
            self.post.send(self.held.at[ds(deep * ((me.f + i + 1) % self.count), deep)], self.from_z.at[i], device)
            for i, device in enumerate(me.z)
        ]

    def finish_z_first(self):
        me, deep = self.me, 2 * self.half
        for copy in self.z_copies:
            self.post.got(copy)
        total = self.held[ds(deep * me.f, deep), :].astype(f32)
        for i in range(self.count - 1):
            total = total + self.from_z[i].astype(f32)
        self.done[0] = total.astype(bf16)
        self.last = self.post.send(self.done.at[0], self.done.at[1], me.yp)

    def finish(self):
        me = self.me
        for copy in self.z_copies:
            self.post.got(copy)
        total = self.held[self.strip(me.f, me.c), :].astype(f32)
        for i in range(self.count - 1):
            total = total + self.from_z[i].astype(f32)
        self.done[me.c] = total.astype(bf16)
        self.last = self.post.send(self.done.at[me.c], self.done.at[me.c], me.yp)


TALL, WIDE = 256, 256


def second_kernel(
    fsdp_count, q_in, k_in, v_in, att_in, low_in, x_in, wh_in, g_up, g_down,
    middle_grad_in, mlp_own_in, mlp_send, g_out_own_in, g_out_send_in, lse, da, mid_stats, up_stats, gain1,
    rows_out, up_out, rest_out, all_total, part_total,
    middle_grad, mlp_own, g_out_own, g_out_send, q, k, v, kt, attended, low_own, x_own, wh, up_own, down_own,
    delta, pt, dst, dk_acc, dv_acc, dq_t, dq, own_first, trunk, trunk_own, trunk_far, trunk_send, trunk_y, dkv_own,
    mlp_x, first_send, first_x, rows_own, out_core, out_sum, out_x, packed,
    from_core, from_y, from_z, done, deep_z, deep_done, stat_buf, stat_in, stat_z, local, ss, rs,
):
    me = Here(fsdp_count)
    f, c, x, core = me.f, me.c, me.x, me.k
    s = 2 * c + core
    pair = 2 * BLOCK
    units = HALF // UNIT
    width = x_in.shape[1]
    mine, far = HALF * x, HALF * (1 - x)
    here_rows, far_rows = ds(mine, HALF), ds(far, HALF)
    loads = []
    for src, held in (
        (g_up, up_own), (g_down, down_own), (k_in, k), (q_in, q), (v_in, v), (att_in, attended),
        (g_out_own_in, g_out_own), (g_out_send_in, g_out_send), (mlp_own_in, mlp_own),
        (low_in, low_own), (x_in, x_own), (middle_grad_in, middle_grad), (wh_in.at[pl.ds(0, 3)], wh),
    ):
        copy = pltpu.make_async_copy(src, held, local.at[len(loads)])
        copy.start()
        loads.append(copy)
    greet([me.core, me.xp, me.yp] + me.z)
    post = Post(ss, rs)
    mlp_copy = post.send(mlp_send, mlp_x, me.xp)
    buffers = [(from_y, from_z, done)] + [(None, deep_z.at[i], deep_done.at[i]) for i in range(2)]
    sums = [
        StripSum(me, post, fsdp_count, held, from_core, buffer)
        for held, buffer in zip((up_own, down_own, packed.at[core]), buffers)
    ]
    slab_own = pl.ds(pl.multiple_of(128 * core, 128), 128)
    slab_sibling = pl.ds(pl.multiple_of(128 * (1 - core), 128), 128)
    slab_both = pl.ds(256, 128)
    out_copies = []
    for i, src in enumerate((g_out_own_in, g_out_send_in)):
        for j, lanes in enumerate((slab_sibling, slab_both)):
            out_copies.append(post.send(src.at[:, lanes], out_core.at[i, j], me.core))
    for copy in loads[:2]:
        copy.wait()
    sums[0].over_y()
    sums[1].over_z_first()
    for copy in loads[2:6]:
        copy.wait()
    kt[...] = k[...].T
    product = (da[...].astype(f32) * attended[...].astype(f32)).T
    for h in range(6):
        delta[h : h + 1, :] = jnp.sum(product[h * HEAD_DIM : (h + 1) * HEAD_DIM], axis=0, keepdims=True)
    lane = lax.broadcasted_iota(jnp.int32, (OWN, 128), 1) // HEAD_DIM

    def head(h, carried):
        slab, part = h // 2, h % 2
        lanes = pl.ds(pl.multiple_of(slab * 128, 128), 128)
        q_slab, da_slab = q[:, lanes], da[:, lanes]
        q_part = jnp.where(lane == part, q_slab, jnp.zeros_like(q_slab))
        da_part = jnp.where(lane == part, da_slab, jnp.zeros_like(da_slab))
        log_total, row_delta = lse[pl.ds(h, 1), :], delta[pl.ds(h, 1), :]

        def tile(keys, rows, cols):
            scores = dot_nt(k[keys, lanes], q_part[cols])
            prob_grad = dot_nt(v[keys, lanes], da_part[cols])
            weight = jnp.exp(scores - log_total[:, cols])
            pt[rows, cols] = weight.astype(bf16)
            dst[rows, cols] = (weight * (prob_grad - row_delta[:, cols])).astype(bf16)

        for col in range(0, OWN, WIDE):
            cols = slice(col, min(col + WIDE, OWN))
            for row in range(0, TRUNK, TALL):
                tile(slice(row, row + TALL), slice(row, row + TALL), cols)
        for q_row, k_row, count in PIECES:
            tile(slice(k_row, k_row + count), slice(TRUNK, TRUNK + count), slice(q_row, q_row + BLOCK))
        dk_acc[0:TRUNK, :] += dot_nn(dst[0:TRUNK, :], q_part)
        dv_acc[0:TRUNK, :] += dot_nn(pt[0:TRUNK, :], da_part)
        head_rows = ds(h * HEAD_DIM, HEAD_DIM)
        dq_t[head_rows, :] = dot_nn(kt[head_rows, 0:TRUNK], dst[0:TRUNK, :])
        for q_row, k_row, count in PIECES:
            cols, rows = slice(q_row, q_row + BLOCK), slice(TRUNK, TRUNK + count)
            own = slice(k_row, k_row + count)
            dk_acc[own, :] += dot_nn(dst[rows, cols], q_part[q_row : q_row + BLOCK])
            dv_acc[own, :] += dot_nn(pt[rows, cols], da_part[q_row : q_row + BLOCK])
            dq_t[head_rows, cols] += dot_nn(kt[head_rows, own], dst[rows, cols])
        return carried

    chip_rows = lambda chip, side: ds(pair * (2 * chip + side), pair)
    trunk_copies, y_copies = [], []

    def slab_heads(slab):
        dk_acc[...] = jnp.zeros_like(dk_acc)
        dv_acc[...] = jnp.zeros_like(dv_acc)
        lax.fori_loop(2 * slab, 2 * slab + 2, head, 0)

    def trunk_out(slab):
        trunk[slab, 0] = dk_acc[0:TRUNK, :].astype(bf16)
        trunk[slab, 1] = dv_acc[0:TRUNK, :].astype(bf16)
        for i, total in enumerate((dk_acc, dv_acc)):
            lanes = slice(384 * i + 128 * slab, 384 * i + 128 * slab + 128)
            dkv_own[pair:, lanes] = total[TRUNK:, :].astype(bf16)
        trunk_copies.append(
            (
                post.send(trunk.at[slab, :, chip_rows(1 - c, 1 - core), :], trunk_far.at[slab], me.core),
                post.send(trunk.at[slab, :, chip_rows(c, 1 - core), :], trunk_own.at[slab], me.core),
            )
        )

    def trunk_over(slab):
        post.got(trunk_copies[slab][0])
        trunk_send[slab] = (
            trunk[slab, :, chip_rows(1 - c, core), :].astype(f32) + trunk_far[slab].astype(f32)
        ).astype(bf16)
        y_copies.append(post.send(trunk_send.at[slab], trunk_y.at[slab], me.yp))

    def trunk_in(slab):
        post.got(trunk_copies[slab][1])
        post.got(y_copies[slab])
        total = (
            trunk[slab, :, chip_rows(c, core), :].astype(f32)
            + trunk_own[slab].astype(f32)
            + trunk_y[slab].astype(f32)
        ).astype(bf16)
        for i in range(2):
            lanes = slice(384 * i + 128 * slab, 384 * i + 128 * slab + 128)
            dkv_own[0:pair, lanes] = total[i]

    slab_heads(0)
    trunk_out(0)
    for copy in loads[6:13]:
        copy.wait()
    for copy in out_copies:
        post.got(copy)
    for i, src in enumerate((g_out_own, g_out_send)):
        for j, lanes in enumerate((slab_own, slab_both)):
            out_sum[i, j] = (src[:, lanes].astype(f32) + out_core[i, j].astype(f32)).astype(bf16)
    out_copy = post.send(out_sum.at[1], out_x, me.xp)
    trunk_over(0)
    slab_heads(1)
    trunk_out(1)
    post.got(mlp_copy)
    rows_own[0] = (mlp_own[...] + mlp_x[...].astype(f32)).astype(bf16).reshape(units, UNIT, width)
    beside = 2 * s + 1 - x
    beyond = 2 * (2 * (1 - c) + core) + x
    corner = 2 * (2 * (1 - c) + core) + 1 - x
    part = units // 2
    over_x, over_y, diagonal = {}, {}, {}

    def piece(index, owner, half):
        return rows_out.at[index, pl.ds(units * owner + part * half, part)]

    def own_piece(index, half):
        return rows_own.at[index, pl.ds(part * half, part)], piece(index, 2 * s + x, half)

    def spread_x(index, half):
        own, there = own_piece(index, half)
        over_x[index, half] = post.send(own, there, me.xp)
        post.send(own, there, me.core)
        copy = pltpu.make_async_copy(own, there, local.at[len(loads)])
        copy.start()
        loads.append(copy)

    def spread_y(index, half):
        own, there = own_piece(index, half)
        over_y[index, half] = post.send(own, there, me.yp)

    def pass_on(index, half):
        for copies, owner, onward in ((over_x, beside, me.yp), (over_y, beyond, me.xp)):
            post.got(copies[index, half])
            got = piece(index, owner, half)
            if (index == 1 and half == 0) == (onward is me.yp):
                diagonal[index, half] = post.send(got, got, onward)
            post.send(got, got, me.core)

    def corner_on(index):
        for half in range(2):
            post.got(diagonal[index, half])
            got = piece(index, corner, half)
            post.send(got, got, me.core)

    for half in range(2):
        spread_x(0, half)
    trunk_over(1)
    sums[0].over_z()
    slab_heads(2)
    trunk_out(2)
    dq[...] = (dq_t[...].T * HEAD_DIM ** (-0.5)).astype(bf16)
    trunk_over(2)
    for slab in range(3):
        trunk_in(slab)
    for half in range(2):
        spread_y(0, half)

    def first(rows):
        return (
            dot_nt(dq[rows, :], wh[0])
            + dot_nt(dkv_own[rows, 0:384], wh[1])
            + dot_nt(dkv_own[rows, 384:768], wh[2])
        )

    chunk = HALF // 2
    first_copies = []
    for i in range(2):
        first_send[i] = first(ds(far + chunk * i, chunk)).astype(bf16)
        first_copies.append(post.send(first_send.at[i], first_x.at[i], me.xp))
    g_attn = [
        dot_tn(low_own[...], dq[...]),
        dot_tn(low_own[...], dkv_own[:, 0:384]),
        dot_tn(low_own[...], dkv_own[:, 384:768]),
    ]
    tails = []
    for j in (0, 1):
        for i in range(3):
            packed[j, :, 128 * i : 128 * i + 128] = g_attn[i][:, 128 * j : 128 * j + 128].astype(bf16)
        tail = [g[:, 256 + 64 * j : 320 + 64 * j] for g in g_attn]
        packed[j, :, 512:640] = jnp.concatenate(tail[0:2], axis=1).astype(bf16)
        packed[j, :, 640:768] = jnp.concatenate([tail[2], jnp.zeros_like(tail[2])], axis=1).astype(bf16)
    attn_stats = jnp.concatenate(
        [
            jnp.sum(dq[...].astype(f32), axis=0, keepdims=True),
            jnp.sum(dkv_own[:, 384:768].astype(f32), axis=0, keepdims=True),
        ],
        axis=1,
    )
    sums[2].from_sibling(packed.at[1 - core])
    def put_out():
        post.got(out_copy)
        packed[core, :, 384:512] = (out_sum[0, 0].astype(f32) + out_x[0].astype(f32)).astype(bf16)
        last = out_sum[0, 1].astype(f32) + out_x[1].astype(f32)
        side = lax.broadcasted_iota(jnp.int32, last.shape, 1) // HEAD_DIM
        turned = jnp.concatenate([last[:, HEAD_DIM:], last[:, :HEAD_DIM]], axis=1)
        tail = jnp.where(core == 0, turned, last)
        packed[core, :, 640:768] = jnp.where(side == 0, packed[core, :, 640:768].astype(f32), tail).astype(bf16)

    sums[2].add_sibling()
    put_out()
    sums[2].over_z_first()
    own_first[...] = first(here_rows)
    for half in range(2):
        pass_on(0, half)
    n1_all, s1_all = row_norm(x_own[here_rows, :].astype(f32))
    first_total = [jnp.zeros((1, width), f32)] * 2
    for i in range(2):
        post.got(first_copies[i])
        rows = slice(chunk * i, chunk * i + chunk)
        first_grad = own_first[rows, :] + first_x[i].astype(f32)
        n1, s1 = n1_all[rows], s1_all[rows]
        grad = middle_grad[rows, :] + norm_back(first_grad, n1, s1, wide(gain1))
        rows_own[1, part * i : part * i + part] = grad.astype(bf16).reshape(part, UNIT, width)
        spread_x(1, i)
        spread_y(1, i)
        first_total = [
            a + jnp.sum(b, axis=0, keepdims=True) for a, b in zip(first_total, (first_grad * n1, first_grad))
        ]
    rows_mid, rows_up = mid_stats.shape[0], up_stats.shape[0]
    stat_buf[0:1, :], stat_buf[1:2, :] = first_total
    stat_buf[2 : 2 + rows_mid, :] = mid_stats[...]
    stat_buf[2 + rows_mid : 8, :] = jnp.zeros((6 - rows_mid, width), f32)
    stat_buf[8 : 8 + rows_up, :] = up_stats[...]
    stat_buf[8 + rows_up : 9 + rows_up, :] = attn_stats
    stat_buf[9 + rows_up : 16, :] = jnp.zeros((7 - rows_up, width), f32)
    level = lambda i: pl.ds(16 * i, 16)
    stat_copy = post.send(stat_buf.at[level(0)], stat_in.at[0], me.core)
    sums[0].finish()
    post.got(stat_copy)
    stat_buf[level(1), :] = stat_buf[level(0), :] + stat_in[0]
    stat_copy = post.send(stat_buf.at[level(1)], stat_in.at[1], me.yp)
    sums[1].finish_z_first()
    corner_on(0)
    post.got(stat_copy)
    stat_buf[level(2), :] = stat_buf[level(1), :] + stat_in[1]
    stat_copy = post.send(stat_buf.at[level(2)], stat_in.at[2], me.xp)
    pass_on(1, 0)
    post.got(stat_copy)
    stat_buf[48:56, :] = stat_buf[32:40, :] + stat_in[2, 0:8]
    stat_buf[56:64, :] = stat_buf[40:48, :]
    stat_z[f] = stat_buf[level(3), :]
    stat_copies = [post.send(stat_buf.at[level(3)], stat_z.at[f], device) for device in me.z]
    pass_on(1, 1)
    sums[2].finish_z_first()
    corner_on(1)
    for copy in stat_copies:
        post.got(copy)
    total = stat_z[0]
    for g in range(1, fsdp_count):
        total = total + stat_z[g]
    all_total[...] = total[0 : 2 + rows_mid]
    part_total[...] = total[8 : 9 + rows_up]
    for total in sums:
        post.got(total.last)
    up_out[...] = done[...]
    rest_out[...] = deep_done[...]
    post.close()
    for copy in loads[13:]:
        copy.wait()


def second_half(fsdp_count, row_count, *operands):
    shape = jax.ShapeDtypeStruct
    vmem = pltpu.VMEM
    width = operands[4].shape[1]
    rows = row_count
    tall = TRUNK + 2 * BLOCK
    pair = 2 * BLOCK
    deep = width // fsdp_count
    half = deep // 2
    return pl.pallas_call(
        partial(second_kernel, fsdp_count),
        out_shape=(
            shape((2, 2 * rows // UNIT, UNIT, width), bf16),
            shape((2, half, width), bf16),
            shape((2, 2, deep, width), bf16),
            shape((6, width), f32),
            shape((3, width), f32),
        ),
        in_specs=[ANY] * 14 + [VMEM] * 5,
        out_specs=(ANY,) + (VMEM,) * 4,
        scratch_shapes=[
            vmem((HALF, width), f32),
            vmem((HALF, width), f32),
            vmem((width, 384), bf16),
            vmem((width, 384), bf16),
            vmem((OWN, 384), bf16),
            vmem((KEYS, 384), bf16),
            vmem((KEYS, 384), bf16),
            vmem((384, KEYS), bf16),
            vmem((OWN, 384), bf16),
            vmem((OWN, width), bf16),
            vmem((OWN, width), bf16),
            vmem((3, width, 384), bf16),
            vmem((width, width), bf16),
            vmem((width, width), bf16),
            vmem((8, OWN), f32),
            vmem((tall, OWN), bf16),
            vmem((tall, OWN), bf16),
            vmem((KEYS, 128), f32),
            vmem((KEYS, 128), f32),
            vmem((384, OWN), f32),
            vmem((OWN, 384), bf16),
            vmem((HALF, width), f32),
            vmem((3, 2, TRUNK, 128), bf16),
            vmem((3, 2, pair, 128), bf16),
            vmem((3, 2, pair, 128), bf16),
            vmem((3, 2, pair, 128), bf16),
            vmem((3, 2, pair, 128), bf16),
            vmem((OWN, 768), bf16),
            vmem((HALF, width), bf16),
            vmem((2, HALF // 2, width), bf16),
            vmem((2, HALF // 2, width), bf16),
            vmem((2, HALF // UNIT, UNIT, width), bf16),
            vmem((2, 2, width, 128), bf16),
            vmem((2, 2, width, 128), bf16),
            vmem((2, width, 128), bf16),
            vmem((2, width, width), bf16),
            vmem((width, width), bf16),
            vmem((fsdp_count, half, width), bf16),
            vmem((fsdp_count - 1, half, width), bf16),
            vmem((2, half, width), bf16),
            vmem((2, fsdp_count - 1, deep, width), bf16),
            vmem((2, 2, deep, width), bf16),
            vmem((64, width), f32),
            vmem((3, 16, width), f32),
            vmem((fsdp_count, 16, width), f32),
            pltpu.SemaphoreType.DMA((20,)),
            pltpu.SemaphoreType.DMA((80,)),
            pltpu.SemaphoreType.DMA((80,)),
        ],
        compiler_params=pltpu.CompilerParams(collective_id=1, has_side_effects=True, vmem_limit_bytes=LIMIT),
        name="second_half",
    )(*operands)


def place_kernel(
    order, rows_all, up_sum, rest, all_total, part_total,
    result, patch_grad, gain1, shift1, grad_attn, attn_bias, grad_out, out_bias, gain2, shift2, grad_up, up_bias,
    grad_down_t, down_bias, result_low, patch_low, patch_wide, sems, out_sems,
):
    units = BLOCK // UNIT
    own = result.shape[0] // units
    core = lax.axis_index("tensor") % 2
    copies = []
    for j in range(own):
        block = order[0, own * lax.axis_index("context") + j]
        branch, leaf = block - TRUNK_BLK, block - TRUNK_BLK - BRANCHES
        index = jnp.where(
            branch < 0,
            5 * (block // 2) + block % 2,
            jnp.where(leaf < 0, 5 * branch + 3, 5 * (leaf // 2) + 2 + 2 * (leaf % 2)),
        )
        to = pl.ds(j * units, units)
        for i, dest in enumerate((result_low, patch_low)):
            copy = pltpu.make_async_copy(
                rows_all.at[i, pl.ds(index * units, units)], dest.at[to], sems.at[i, j]
            )
            copy.start()
            copies.append(copy)
    total = lambda i: all_total[i, :]
    gain1[...], shift1[...], gain2[...], shift2[...] = total(0), total(1), total(2), total(3)
    down_bias[...], out_bias[...] = total(4), total(5)
    up_bias[...] = part_total[core, :]
    for i in range(2):
        lanes = slice(384 * i, 384 * i + 384)
        row = part_total[2:3, lanes]
        first = jnp.where(core == 0, row[:, 0:128], row[:, 128:256])
        second = jnp.where(core == 0, row[:, 256:320], row[:, 320:384])
        attn_bias[i : i + 1, :] = jnp.concatenate([first, second], axis=1)
    grad_up[...] = up_sum[...].reshape(grad_up.shape).astype(f32)
    grad_down_t[...] = rest[0, 0].astype(f32) + rest[0, 1].astype(f32)
    attn = rest[1, 0].astype(f32) + rest[1, 1].astype(f32)
    tails = [attn[:, 512:576], attn[:, 576:640], attn[:, 640:704], attn[:, 704:768]]
    for i in range(3):
        grad_attn[i, :, 0:128] = attn[:, 128 * i : 128 * i + 128]
        grad_attn[i, :, 128:192] = tails[i]
    grad_out[...] = jnp.concatenate([attn[:, 384:512], tails[3]], axis=1).T
    out = []
    for j in range(own):
        block = pl.ds(j * units, units)
        copies[2 * j].wait()
        copies[2 * j + 1].wait()
        patch_wide[block] = patch_low[block].astype(f32)
        for i, (src, dest) in enumerate(((result_low, result), (patch_wide, patch_grad))):
            copy = pltpu.make_async_copy(src.at[block], dest.at[block], out_sems.at[i, j])
            copy.start()
            out.append(copy)
    for copy in out:
        copy.wait()


def place(order, row_count, rows_all, up_sum, rest, all_total, part_total):
    shape = jax.ShapeDtypeStruct
    width = rows_all.shape[3]
    deep = rest.shape[2]
    vector = shape((width,), f32)
    return pl.pallas_call(
        place_kernel,
        out_shape=(
            shape((row_count // UNIT, UNIT, width), bf16), shape((row_count // UNIT, UNIT, width), f32), vector, vector,
            shape((3, deep, 192), f32), shape((2, 192), f32), shape((192, deep), f32), vector, vector, vector,
            shape((deep, width), f32), vector, shape((deep, width), f32), vector,
        ),
        in_specs=[SMEM, ANY] + [VMEM] * 4,
        out_specs=(ANY,) * 2 + (VMEM,) * 12,
        scratch_shapes=[
            pltpu.VMEM((row_count // UNIT, UNIT, width), bf16),
            pltpu.VMEM((row_count // UNIT, UNIT, width), bf16),
            pltpu.VMEM((row_count // UNIT, UNIT, width), f32),
            pltpu.SemaphoreType.DMA((2, row_count // BLOCK)),
            pltpu.SemaphoreType.DMA((2, row_count // BLOCK)),
        ],
        compiler_params=pltpu.CompilerParams(vmem_limit_bytes=LIMIT),
        name="place",
    )(order, rows_all, up_sum, rest, all_total, part_total)


def tree_shards(
    fsdp_count, patches, out_grad, block_order, first_gain, first_shift, attn_proj, attn_bias, out_proj, out_bias,
    second_gain, second_shift, up_proj, up_bias, down_proj, down_bias,
):
    middle = first_half(
        fsdp_count, block_order, patches, out_grad, attn_proj, out_proj, up_proj, down_proj.T, up_bias, attn_bias,
        first_gain, first_shift, second_gain, second_shift, out_bias, down_bias,
    )
    sums = second_half(fsdp_count, patches.shape[0], *middle, first_gain)
    outputs = list(place(block_order, patches.shape[0], *sums))
    outputs[0], outputs[1] = (rows.reshape(patches.shape) for rows in outputs[:2])
    outputs[12] = outputs[12].T
    return tuple(outputs)


def solution(mesh):
    fits = mesh.shape["context"] * 2 == BRANCHES and mesh.shape["tensor"] == 4 and mesh.shape["fsdp"] == 4
    body = partial(tree_shards, mesh.shape["fsdp"]) if fits else shards
    return jax.shard_map(
        body,
        mesh=mesh,
        in_specs=(
            P(("fsdp", "context"), None),
            P(("fsdp", "context"), None),
            P("fsdp", None),
            P(),
            P(),
            P(None, "fsdp", "tensor"),
            P(None, "tensor"),
            P("tensor", "fsdp"),
            P(),
            P(),
            P(),
            P("fsdp", "tensor"),
            P("tensor"),
            P("tensor", "fsdp"),
            P(),
        ),
        out_specs=(
            P(("fsdp", "context"), None),
            P(("fsdp", "context"), None),
            P(),
            P(),
            P(None, "fsdp", "tensor"),
            P(None, "tensor"),
            P("tensor", "fsdp"),
            P(),
            P(),
            P(),
            P("fsdp", "tensor"),
            P("tensor"),
            P("tensor", "fsdp"),
            P(),
        ),
        check_vma=False,
    )
```
